128 devices in a mesh: gx: 8 (over x, core), gy: 16 (over y, z).
Axes of the slice: x: 4, y: 4, z: 4, core: 2. Of those that a mesh axis runs over, the one named last changes fastest.
Arguments:
- state_prior: float32 [16, 16, 128, 1024], P(None, None, 'gy', 'gx'), may hold values from 0.1 to 3.6, as said below
- conductivity: float32 [16, 128, 1024], P(None, 'gy', 'gx'), may hold values from 0.25 to 1
- heat_input: bfloat16 [16, 16384, 128], P(None, ('gx', 'gy')), may hold values from 0.19921875 to 2
- owner_tile: int32 [16384, 1], P(('gx', 'gy')), may hold values from 0 to 127; in each aligned block of 128 rows (0 to 127, 128 to 255, ...) at most 2 rows name the same one
- voxel_list: int32 [16384, 128], P(('gx', 'gy')), may hold values from 0 to 2047
- pixel_cell: int32 [65536], P(('gx', 'gy')), may hold values from 0 to 1023
- observed: float32 [65536], P(('gx', 'gy')), may hold values from -6 to 6
- pixel_variance: float32 [65536], P(('gx', 'gy')), may hold values from 0.1 to 10
- pixel_noise: float32 [16, 65536], P(None, ('gx', 'gy')), may hold values from -6 to 6
Outputs:
- analysis: float32 [16, 16, 128, 1024], P(None, None, 'gy', 'gx')
The draws below stay inside these ranges and needn't reach their ends.
Inputs may be any that keep to these rules, and one draw needn't show every extreme that they name: `state_prior`: positive temperatures. `owner_tile`: in the rows of one device no tile is named more than 2 times. `voxel_list`: indices into the two top layers of the owner tile, flattened over layer, width cell and length cell. `pixel_cell`: indices into the top layer of the pixel's tile, flattened over width cell and length cell.
All inputs are finite; a program needn't handle non-finite values.
Results may differ from the reference program's by a relative error of at most 0.00055.
Values may be sent and summed in bfloat16 or wider, within the bound.
No kernel may reach another device: no remote copies, remote signals or barrier semaphores. Data moves between devices by JAX's collectives and lax.ppermute only.
A program may use at most 128 MiB of HBM per device.

```python
import math
import jax
import jax.numpy as jnp
import numpy as np
from jax import lax

M = 16
CX = 128
CY = 8
NZ = 16
SUBSTEPS = 6
BC = 128
CAP = 2
BLK_DEV = 128
PIX_DEV = 512
NX = 1024
NY = 128
BLOCKS = 16384
NPIX = 65536
N_GX = 8
N_GY = 16


def draw_state_prior(key, part):
    key = jax.random.fold_in(key, 11)
    along = (jnp.arange(NX, dtype=jnp.float32) / NX)[None, None, None, :]
    base = jax.random.uniform(key, (M, NZ, NY, NX), jnp.float32, 0.2, 1.2)
    return base * (1.0 + 2.0 * along)


def draw_pixel_variance(key, part):
    key = jax.random.fold_in(key, 23)
    along = jnp.arange(NPIX, dtype=jnp.float32) / NPIX
    base = jnp.exp(jax.random.uniform(key, (NPIX,), jnp.float32, jnp.log(0.5), jnp.log(5.0)))
    return base / (1.0 + 2.0 * along)


def touch_ends(array, rng, least, high):
    longest = array.shape.index(max(array.shape))
    spots = []
    for shift in (0, 1):
        where = [jax.random.randint(jax.random.fold_in(rng, axis), (), 0, length) for axis, length in enumerate(array.shape)]
        where[longest] = (where[longest] + shift) % array.shape[longest]
        spots.append(tuple(where))
    return array.at[spots[0]].set(least).at[spots[1]].set(high)


def level_of(own_key, extent, shards, low, largest):
    loudness = 1.0
    for dim, blocks in shards:
        steps = jax.random.uniform(jax.random.fold_in(jax.random.fold_in(own_key, 6), dim), (blocks,), jnp.float32, low / len(shards), largest / len(shards))
        loudness = loudness * jnp.repeat(jnp.exp(steps), extent[dim] // blocks).reshape((-1,) + (1,) * (len(extent) - 1 - dim))
    return loudness


def assign_block(rng, own, number, rows, amount, top, bound, lean):
    sequence = jax.random.permutation(rng, amount)
    packed, ordinary = shares(amount, rows * top, bound, lean, True), shares(amount, rows * top, bound, lean, False)
    places = jnp.arange(amount)

    def named(lengths, turn):
        used = int((lengths > 0).sum())
        fixed = max(1, used // 4)
        shifted = fixed + (places - fixed + turn * (used - fixed)) % max(1, amount - fixed)
        return jnp.zeros((amount,), jnp.int32).at[sequence[jnp.where(places < fixed, places, shifted)]].set(jnp.asarray(lengths, jnp.int32))

    lengths = jnp.where(number % 4 == 0, named(packed, number // 4), named(ordinary, number - number // 4 - 1))
    mixed = jax.random.permutation(jax.random.fold_in(own, 3), amount)
    giver, sink = mixed[0:amount // 2 * 2:2], mixed[1:amount // 2 * 2:2]
    slack = jnp.minimum(lengths[giver] - 1, bound - lengths[sink]) // 2
    slack = jnp.where((giver == sequence[0]) | (sink == sequence[0]) | (lengths[sink] == 0), 0, jnp.maximum(slack, 0))
    shifted = jax.random.randint(jax.random.fold_in(own, 4), (amount // 2,), 0, 1 << 20) % (slack + 1)
    lengths = lengths.at[giver].add(-shifted).at[sink].add(shifted)
    members = jnp.searchsorted(jnp.cumsum(lengths), jnp.arange(rows * top), side="right").astype(jnp.int32)
    table = members.reshape(top, rows).T
    table = table[jax.random.permutation(jax.random.fold_in(own, 1), rows)]
    turn = jax.random.randint(jax.random.fold_in(own, 2), (rows, 1), 0, top)
    return jnp.take_along_axis(table, (jnp.arange(top)[None, :] + turn) % top, axis=1)


def shares(count, total, most, lean, full):
    weights = [(1 << 20) // math.isqrt(standing ** lean) + 1 for standing in range(1, count + 1)]
    largest = most if full else min(most, max(-(-total // count), total * weights[0] // sum(weights)))
    least = 1 if total - largest >= count - 1 else 0
    counts, spare = [largest] + [least] * (count - 1), total - largest - least * (count - 1)
    while spare > 0:
        movable = [i for i in range(1, count) if counts[i] < largest] or [i for i in range(1, count) if counts[i] < most]
        whole, budget = sum([weights[i] for i in movable]), spare
        for i in movable:
            more = min(most - counts[i], max(1, budget * weights[i] // whole), spare)
            counts[i] = counts[i] + more
            spare = spare - more
    return np.array(counts)


def centred(own_key, shape, deviation, limit, split=(), kind=jnp.bfloat16):
    factor_of = level_of(own_key, shape, split, -0.22, 0.18) if split else 1.0
    drawn = jax.random.normal(own_key, shape, jnp.float32) * deviation * factor_of
    return jnp.minimum(jnp.maximum(drawn, -limit), limit).astype(kind)


def setup_inputs(seed: int = 0) -> dict:
    seeds = jax.random.split(jax.random.key(seed), 10)
    state_prior = draw_state_prior(jax.random.fold_in(seeds[9], 71), 0)
    conductivity = jnp.clip(jnp.exp(math.log(1.0) - 1.3862944 * jax.random.uniform(seeds[1], (NZ, NY, NX), jnp.float32) ** level_of(seeds[1], (NZ, NY, NX), ((1, 16), (2, 8)), -0.2, 0.2)), 0.25, 1.0)
    heat_input = jnp.clip(jnp.exp(math.log(2.0) - 2.306499 * jax.random.uniform(seeds[2], (M, BLOCKS, BC), jnp.float32) ** level_of(seeds[2], (M, BLOCKS, BC), ((1, 128),), -0.2, 0.2)), 0.19921875, 2.0).astype(jnp.bfloat16)
    owner_tile_keys = jax.random.split(jax.random.fold_in(seeds[3], 1), BLOCKS // BLK_DEV)
    owner_tile_turns = jax.random.permutation(jax.random.fold_in(seeds[3], 3), BLOCKS // BLK_DEV)
    owner_tile = jax.vmap(lambda own, number: assign_block(jax.random.fold_in(seeds[3], 2), own, number, BLK_DEV, N_GX * N_GY, 1, CAP, 2))(owner_tile_keys, owner_tile_turns).reshape((BLOCKS, 1))
    voxel_list = touch_ends(jax.random.randint(seeds[4], (BLOCKS, BC), 0, 2 * CX * CY), jax.random.fold_in(seeds[4], 1), 0, (2 * CX * CY) - 1).astype(jnp.int32)
    pixel_cell = touch_ends(jax.random.randint(seeds[5], (NPIX,), 0, CX * CY), jax.random.fold_in(seeds[5], 1), 0, (CX * CY) - 1).astype(jnp.int32)
    observed = centred(seeds[6], (NPIX,), 1.0, 6.0, ((0, 128),), jnp.float32)
    pixel_variance = draw_pixel_variance(jax.random.fold_in(seeds[9], 71), 0)
    pixel_noise = centred(seeds[8], (M, NPIX), 1.0, 6.0, ((1, 128),), jnp.float32)
    return {"state_prior": state_prior, "conductivity": conductivity, "heat_input": heat_input, "owner_tile": owner_tile, "voxel_list": voxel_list, "pixel_cell": pixel_cell, "observed": observed, "pixel_variance": pixel_variance, "pixel_noise": pixel_noise}


cool_rate = 0.1
stable_share = 0.9

def advance(padded, conduct, time_step):
    centre = padded[..., 1:-1, 1:-1]
    inner_k = conduct[..., 1:-1, 1:-1]
    lateral = 0.5 * (inner_k + conduct[..., 2:, 1:-1]) * (padded[..., 2:, 1:-1] - centre)
    lateral = lateral + 0.5 * (inner_k + conduct[..., :-2, 1:-1]) * (padded[..., :-2, 1:-1] - centre)
    lateral = lateral + 0.5 * (inner_k + conduct[..., 1:-1, 2:]) * (padded[..., 1:-1, 2:] - centre)
    lateral = lateral + 0.5 * (inner_k + conduct[..., 1:-1, :-2]) * (padded[..., 1:-1, :-2] - centre)
    vertical_flux = 0.5 * (inner_k[..., 1:, :, :] + inner_k[..., :-1, :, :]) * (centre[..., 1:, :, :] - centre[..., :-1, :, :])
    zero_face = jnp.zeros_like(vertical_flux[..., :1, :, :])
    vertical = jnp.concatenate([vertical_flux, zero_face], axis=-3) - jnp.concatenate([zero_face, vertical_flux], axis=-3)
    cooling = jnp.concatenate([cool_rate * centre[..., :1, :, :], jnp.zeros_like(centre[..., 1:, :, :])], axis=-3)
    return centre + time_step * (lateral + vertical - cooling)

def reference(state_prior, conductivity, heat_input, owner_tile, voxel_list, pixel_cell, observed, pixel_variance, pixel_noise):
    target_tile = owner_tile[:, 0]
    tile_x = target_tile // N_GY
    tile_y = target_tile % N_GY
    layer_idx = voxel_list // (CY * CX)
    width_idx = tile_y[:, None] * CY + voxel_list // CX % CY
    length_idx = tile_x[:, None] * CX + voxel_list % CX
    field_now = state_prior.at[:, layer_idx, width_idx, length_idx].add(heat_input.astype(jnp.float32))
    lateral_pad = ((0, 0), (1, 1), (1, 1))
    for substep in range(SUBSTEPS):
        peak_value = jnp.max(conductivity[None] * (1.0 + 0.25 * field_now * field_now))
        time_step = stable_share / (6.0 * peak_value + cool_rate)
        coef_pad = jnp.pad(conductivity, lateral_pad)

        def member_step(member_field):
            padded = jnp.pad(member_field, lateral_pad)
            return advance(padded, coef_pad * (1.0 + 0.25 * padded * padded), time_step)
        field_now = lax.map(member_step, field_now)
    pixel_ids = jnp.arange(NPIX, dtype=jnp.int32)
    device_of = pixel_ids // PIX_DEV
    seen_width = device_of % N_GY * CY + pixel_cell // CX
    seen_length = device_of // N_GY * CX + pixel_cell % CX
    seen = field_now[:, 0, seen_width, seen_length]
    spread = seen - lax.optimization_barrier(jnp.mean(seen, axis=0, keepdims=True))
    innovation = observed[None, :] + pixel_noise * jnp.sqrt(pixel_variance)[None, :] - seen
    weighted = spread / pixel_variance[None, :]
    cross = jnp.dot(weighted, spread.T, precision=lax.Precision.HIGHEST)
    target_sum = jnp.dot(weighted, innovation.T, precision=lax.Precision.HIGHEST)
    system = cross + (M - 1) * jnp.eye(M, dtype=jnp.float32)
    weights = jnp.linalg.solve(system, target_sum)
    flat_field = field_now.reshape(M, -1)
    anomalies = flat_field - lax.optimization_barrier(jnp.mean(flat_field, axis=0, keepdims=True))
    analysis = flat_field + jnp.einsum('kc,km->mc', anomalies, weights, precision=lax.Precision.HIGHEST)
    return analysis.reshape(field_now.shape)
```

```python
import functools

import jax
import jax.numpy as jnp
from jax import lax
from jax.experimental import pallas as pl
from jax.experimental.pallas import tpu as pltpu
from jax.sharding import PartitionSpec as P

SUBSTEPS = 6
CAP = 2
COOL = 0.1
SHARE = 0.9
F32 = jnp.float32
BF16 = jnp.bfloat16
VM = pltpu.VMEM
LIMIT = 48 * 1024 * 1024
NT = (((1,), (1,)), ((), ()))
BOTH = ("gx", "gy")

M, NZ, CY, CX = 16, 16, 8, 128
ROWS = 40


def vspec():
    return pl.BlockSpec(memory_space=pltpu.VMEM)


def params():
    return pltpu.CompilerParams(vmem_limit_bytes=LIMIT)


def lanes():
    return lax.broadcasted_iota(jnp.int32, (CY, CX), 1)


def rows():
    return lax.broadcasted_iota(jnp.int32, (CY, CX), 0)


def pack_kernel(owner, heat, voxel, out, wide, high, low, inverse):
    blocks = owner.shape[0]
    devices = out.shape[0]

    def clear(i, carry):
        inverse[i] = blocks
        return carry

    lax.fori_loop(0, devices * CAP, clear, 0, unroll=16)

    def place(b, carry):
        base = owner[b] * CAP
        base = base + jnp.where(inverse[base] != blocks, 1, 0)
        inverse[base] = b
        return carry

    lax.fori_loop(0, blocks, place, 0, unroll=8)

    def widen(m, carry):
        wide[m, 0:blocks, :] = heat[m].astype(F32)
        wide[m, blocks:, :] = jnp.zeros((8, CX), F32)
        return carry

    lax.fori_loop(0, M, widen, 0)
    cells = voxel[...]
    high[0:blocks, :] = (cells >> 7).astype(F32)
    high[blocks:, :] = jnp.zeros((8, CX), F32)
    low[0:blocks, :] = (cells & 127).astype(F32)
    low[blocks:, :] = jnp.zeros((8, CX), F32)
    row = rows()

    def emit(d, carry):
        first = inverse[d * CAP]
        second = inverse[d * CAP + 1]
        index = jnp.where(
            row == 0,
            high[pl.ds(first, 1), :],
            jnp.where(
                row == 1,
                high[pl.ds(second, 1), :],
                jnp.where(
                    row == 2,
                    low[pl.ds(first, 1), :],
                    jnp.where(row == 3, low[pl.ds(second, 1), :], 0.0),
                ),
            ),
        )
        chunk = jnp.concatenate(
            [
                wide[:, pl.ds(first, 1), :].reshape(M, CX),
                wide[:, pl.ds(second, 1), :].reshape(M, CX),
                index,
            ],
            axis=0,
        )
        out[d] = chunk.astype(BF16)
        return carry

    lax.fori_loop(0, devices, emit, 0, unroll=4)


def pack(owner, heat, voxel, devices):
    blocks = owner.shape[0]
    return pl.pallas_call(
        pack_kernel,
        out_shape=jax.ShapeDtypeStruct((devices, ROWS, CX), BF16),
        in_specs=[pl.BlockSpec(memory_space=pltpu.SMEM), vspec(), vspec()],
        out_specs=vspec(),
        scratch_shapes=[
            VM((M, blocks + 8, CX), F32),
            VM((blocks + 8, CX), F32),
            VM((blocks + 8, CX), F32),
            pltpu.SMEM((devices * CAP,), jnp.int32),
        ],
        compiler_params=params(),
        name="pack",
    )(owner, heat, voxel)


def pack_columns(field):
    lane = lanes()
    packed = jnp.zeros((CY, CX), F32)
    for z in range(NZ):
        packed = jnp.where((lane >> 1) == z, pltpu.roll(field[z], 2 * z + 1, axis=1), packed)
    return packed


def coef_kernel(conduct, half, eighth, cols, lo, hi):
    base = conduct[...]
    half[...] = 0.5 * base
    eighth[...] = 0.125 * base
    packed = pack_columns([0.5 * conduct[z] for z in range(NZ)])
    packed = packed + pltpu.roll(packed, 32, axis=1)
    cols[...] = packed + pltpu.roll(packed, 64, axis=1)
    for z0 in (0, 8):
        lo[z0 : z0 + 8, :] = 0.5 * conduct[z0 : z0 + 8, 0, :]
        hi[z0 : z0 + 8, :] = 0.5 * conduct[z0 : z0 + 8, CY - 1, :]


def coefs(conduct):
    whole = jax.ShapeDtypeStruct((NZ, CY, CX), F32)
    row = jax.ShapeDtypeStruct((NZ, CX), F32)
    return pl.pallas_call(
        coef_kernel,
        out_shape=[whole, whole, jax.ShapeDtypeStruct((CY, CX), F32), row, row],
        in_specs=[vspec()],
        out_specs=[vspec()] * 5,
        compiler_params=params(),
        name="coefs",
    )(conduct)


def finish_member(m, new, field, cols, lo, hi):
    lane = lanes()
    packed = pltpu.roll(pack_columns(new), 32 * (m % 4), axis=1)
    held = cols[m // 4]
    cols[m // 4] = jnp.where((lane >> 5) == m % 4, packed, held)
    for z0 in (0, 8):
        lo[m, z0 : z0 + 8, :] = field[m, z0 : z0 + 8, 0, :]
        hi[m, z0 : z0 + 8, :] = field[m, z0 : z0 + 8, CY - 1, :]


def spread_peak(peak, out):
    row = jnp.max(peak, axis=0, keepdims=True)
    for d in range(out.shape[0]):
        out[d] = row


EDGE_SHAPES = [
    jax.ShapeDtypeStruct((M, NZ, CY, CX), F32),
    jax.ShapeDtypeStruct((M // 4, CY, CX), F32),
    jax.ShapeDtypeStruct((M, NZ, CX), F32),
    jax.ShapeDtypeStruct((M, NZ, CX), F32),
]


def deposit_kernel(incoming, state, half, eighth, field, cols, lo, hi, peaks, total):
    sources = incoming.shape[0]
    group = 4
    place = lax.broadcasted_iota(jnp.int32, (CX, CX), 0).astype(F32).astype(BF16)
    zero = jnp.zeros((M, CX), BF16)
    total[...] = jnp.zeros_like(total)

    def one(g, carry):
        left = []
        right = []
        for s in range(group):
            source = g * group + s
            index = incoming[source, 32:40, :].astype(F32)
            for slot in range(CAP):
                heat = incoming[source, slot * M : (slot + 1) * M, :]
                layer = jnp.broadcast_to(index[slot : slot + 1, :], (M, CX)).astype(BF16)
                cell = jnp.broadcast_to(index[2 + slot : 3 + slot, :], (CX, CX)).astype(BF16)
                left.append(
                    jnp.concatenate(
                        [jnp.where(layer == h, heat, zero) for h in range(2 * CY)], axis=0
                    )
                )
                right.append(jnp.where(place == cell, 1.0, 0.0).astype(BF16))
        total[...] += lax.dot_general(
            jnp.concatenate(left, axis=1),
            jnp.concatenate(right, axis=1),
            NT,
            preferred_element_type=F32,
        )
        return carry

    lax.fori_loop(0, sources // group, one, 0)

    def member(m, peak):
        new = []
        for z in range(NZ):
            value = state[m, z]
            if z < 2:
                value = value + total[pl.ds(z * CY * M + m, CY, stride=M), :]
            field[m, z] = value
            peak = jnp.maximum(peak, half[z] + eighth[z] * (value * value))
            new.append(value)
        finish_member(m, new, field, cols, lo, hi)
        return peak

    peak = lax.fori_loop(0, M, member, jnp.zeros((CY, CX), F32))
    spread_peak(peak, peaks)


def deposit(incoming, state, half, eighth):
    devices = incoming.shape[0]
    return pl.pallas_call(
        deposit_kernel,
        out_shape=EDGE_SHAPES + [jax.ShapeDtypeStruct((devices, 1, CX), F32)],
        in_specs=[vspec()] * 4,
        out_specs=[vspec()] * 5,
        scratch_shapes=[VM((2 * CY * M, CX), F32)],
        compiler_params=params(),
        name="deposit",
    )(incoming, state, half, eighth)


def substep_kernel(
    last,
    field, cols, lo, hi,
    from_left, from_right, from_low, from_high,
    peaks,
    half, eighth, cols_k, lo_k, hi_k,
    left_k, right_k, low_k, high_k,
    *rest,
):
    if last:
        weight, data, out, sums, side, border, flat, flat_data = rest
    else:
        out, out_cols, out_lo, out_hi, out_peaks, side, border = rest
    lane = lanes()
    row = rows()
    even = (lane & 1) == 0
    edge_lane = (lane == 0) | (lane == CX - 1)
    not_last_lane = lane != CX - 1
    not_last_row = row != CY - 1

    peak = peaks[0]
    for d in range(1, peaks.shape[0]):
        peak = jnp.maximum(peak, peaks[d])
    peak = 2.0 * jnp.max(peak, axis=1, keepdims=True)
    step = jnp.broadcast_to(SHARE / (6.0 * peak + COOL), (CY, CX))

    own_k = cols_k[...]
    next_k = jnp.where(even, pltpu.roll(right_k[...], CX - 1, axis=1), pltpu.roll(left_k[...], 1, axis=1))
    for q in range(M // 4):
        own = cols[q]
        near = jnp.where(
            even, pltpu.roll(from_right[q], CX - 1, axis=1), pltpu.roll(from_left[q], 1, axis=1)
        )
        both = own_k * (1.0 + 0.25 * (own * own)) + next_k * (1.0 + 0.25 * (near * near))
        side[q] = both * (near - own)
    border[...] = jnp.zeros_like(border)

    def member(m, peak):
        for z0 in (0, 8):
            at = slice(z0, z0 + 8)
            for own_ref, near_ref, own_c, near_c, where in (
                (lo, from_low, lo_k, low_k, 0),
                (hi, from_high, hi_k, high_k, CY - 1),
            ):
                own = own_ref[m, at, :]
                near = near_ref[m, at, :]
                both = own_c[at, :] * (1.0 + 0.25 * (own * own)) + near_c[at, :] * (
                    1.0 + 0.25 * (near * near)
                )
                border[at, where, :] = both * (near - own)
        beside = pltpu.roll(side[m // 4], (CX - 32 * (m % 4)) % CX, axis=1)
        new = []
        u = field[m, 0]
        h = half[0] + eighth[0] * (u * u)
        flux_up = COOL * u
        for z in range(NZ):
            if z < NZ - 1:
                u_next = field[m, z + 1]
                h_next = half[z + 1] + eighth[z + 1] * (u_next * u_next)
                flux_down = (h + h_next) * (u_next - u)
            flux = (h + pltpu.roll(h, CX - 1, axis=1)) * (pltpu.roll(u, CX - 1, axis=1) - u)
            flux = jnp.where(not_last_lane, flux, 0.0)
            change = flux - pltpu.roll(flux, 1, axis=1)
            flux = (h + pltpu.roll(h, CY - 1, axis=0)) * (pltpu.roll(u, CY - 1, axis=0) - u)
            flux = jnp.where(not_last_row, flux, 0.0)
            change = change + (flux - pltpu.roll(flux, 1, axis=0))
            change = change + border[z]
            change = change + jnp.where(edge_lane, pltpu.roll(beside, CX - 1 - 2 * z, axis=1), 0.0)
            change = change - flux_up
            if z < NZ - 1:
                change = change + flux_down
            value = u + step * change
            out[m, z] = value
            if not last:
                peak = jnp.maximum(peak, half[z] + eighth[z] * (value * value))
                new.append(value)
            if z < NZ - 1:
                u, h, flux_up = u_next, h_next, flux_down
        if not last:
            finish_member(m, new, out, out_cols, out_lo, out_hi)
        return peak

    peak = lax.fori_loop(0, M, member, jnp.zeros((CY, CX), F32))
    if not last:
        spread_peak(peak, out_peaks)
        return

    grams = jnp.zeros((M, 2 * M), F32)
    for y in range(CY):
        for m in range(M):
            flat[m : m + 1, :] = out[m, 0, y : y + 1, :]
            flat_data[m : m + 1, :] = data[m, y : y + 1, :]
        seen = flat[...]
        w = weight[y : y + 1, :]
        spread = seen - jnp.mean(seen, axis=0, keepdims=True)
        both = jnp.concatenate([spread * w, flat_data[...] - seen * w], axis=0)
        grams = grams + lax.dot_general(
            spread, both, NT, precision=lax.Precision.HIGHEST, preferred_element_type=F32
        )
    grams = jnp.concatenate([grams, jnp.zeros((M, CX - 2 * M), F32)], axis=1)
    pair = grams[0:8] + pltpu.roll(grams[8:16], 32, axis=1)
    pair = jnp.where(lane < 64, pair, 0.0)
    quad = pair + pltpu.roll(pltpu.roll(pair, 64, axis=1), 4, axis=0)
    quad = quad[0:4]
    for d in range(sums.shape[0]):
        sums[d] = quad


def substep(field, edges, halos, peaks, coef, coef_halos, pixels=None):
    last = pixels is not None
    devices = peaks.shape[0]
    operands = [field, *edges, *halos, peaks, *coef, *coef_halos]
    scratch = [VM((M // 4, CY, CX), F32), VM((NZ, CY, CX), F32)]
    if last:
        operands += list(pixels)
        out_shape = [EDGE_SHAPES[0], jax.ShapeDtypeStruct((devices, 4, CX), F32)]
        scratch += [VM((M, CX), F32), VM((M, CX), F32)]
    else:
        out_shape = EDGE_SHAPES + [jax.ShapeDtypeStruct((devices, 1, CX), F32)]
    return pl.pallas_call(
        functools.partial(substep_kernel, last),
        out_shape=out_shape,
        in_specs=[vspec()] * len(operands),
        out_specs=[vspec()] * len(out_shape),
        scratch_shapes=scratch,
        compiler_params=params(),
        name="substep_last" if last else "substep",
    )(*operands)


def pixel_kernel(cell, observed, variance, noise, weight, data):
    pixels = cell.shape[1]
    place = cell[...]
    var = variance[...]
    inverse = 1.0 / var
    values = (observed[...] + noise[...] * jnp.sqrt(var)) * inverse
    stack = jnp.concatenate([values, jnp.broadcast_to(inverse, (8, pixels))], axis=0)
    width = place >> 7
    hot = jnp.where(
        lax.broadcasted_iota(jnp.int32, (CX, pixels), 0) == (place & 127), 1.0, 0.0
    ).astype(F32)
    for y in range(CY):
        part = lax.dot_general(
            jnp.where(width == y, stack, 0.0),
            hot,
            NT,
            precision=lax.Precision.HIGHEST,
            preferred_element_type=F32,
        )
        weight[y : y + 1, :] = part[M : M + 1, :]
        for m in range(M):
            data[m, y : y + 1, :] = part[m : m + 1, :]


def pixel_sums(cell, observed, variance, noise):
    return pl.pallas_call(
        pixel_kernel,
        out_shape=[
            jax.ShapeDtypeStruct((CY, CX), F32),
            jax.ShapeDtypeStruct((M, CY, CX), F32),
        ],
        in_specs=[vspec()] * 4,
        out_specs=[vspec()] * 2,
        compiler_params=params(),
        name="pixels",
    )(cell, observed, variance, noise)


def update_kernel(sums, field, out, weights):
    quad = sums[0]
    for d in range(1, sums.shape[0]):
        quad = quad + sums[d]
    lane = lanes()
    row = rows()
    quad = jnp.concatenate([quad, jnp.zeros_like(quad)], axis=0)
    pair = jnp.where(row < 4, quad, pltpu.roll(pltpu.roll(quad, 64, axis=1), 4, axis=0))
    system = jnp.concatenate([pair, pltpu.roll(pair, CX - 32, axis=1)], axis=0)
    tall = lax.broadcasted_iota(jnp.int32, (M, CX), 0)
    wide = lax.broadcasted_iota(jnp.int32, (M, CX), 1)
    system = jnp.where(tall == wide, system + (M - 1.0), system)
    for i in range(M):
        pivot = system[i : i + 1, :]
        pivot = pivot / pivot[:, i : i + 1]
        factor = jnp.where(tall == i, 0.0, jnp.broadcast_to(system[:, i : i + 1], (M, CX)))
        system = jnp.where(tall == i, pivot, system - factor * pivot)
    system = system - jnp.mean(system, axis=0, keepdims=True)
    for m in range(M):
        weights[m] = jnp.broadcast_to(system[:, M + m : M + m + 1], (M, CX))

    def layer(z, carry):
        prior = [field[k, z] for k in range(M)]
        for m in range(M):
            value = prior[m]
            for k in range(M):
                value = value + weights[m, k : k + 1, :] * prior[k]
            out[m, z] = value
        return carry

    lax.fori_loop(0, NZ, layer, 0)


def update(sums, field):
    return pl.pallas_call(
        update_kernel,
        out_shape=jax.ShapeDtypeStruct((M, NZ, CY, CX), F32),
        in_specs=[vspec()] * 2,
        out_specs=vspec(),
        scratch_shapes=[VM((M, M, CX), F32)],
        compiler_params=params(),
        name="update",
    )(sums, field)


def exchange(parts):
    return lax.all_to_all(parts, BOTH, split_axis=0, concat_axis=0, tiled=True)


def neighbours(to_right, to_left, to_high, to_low):
    def move(part, axis, ahead):
        count = lax.axis_size(axis)
        pairs = [(i, i + 1) if ahead else (i + 1, i) for i in range(count - 1)]
        return lax.ppermute(part, axis, pairs)

    return (
        move(to_right, "gx", True),
        move(to_left, "gx", False),
        move(to_high, "gy", True),
        move(to_low, "gy", False),
    )


def on_device(
    state_prior,
    conductivity,
    heat_input,
    owner_tile,
    voxel_list,
    pixel_cell,
    observed,
    pixel_variance,
    pixel_noise,
):
    devices = lax.axis_size("gx") * lax.axis_size("gy")
    pixels = pixel_cell.shape[0]
    outgoing = pack(owner_tile.reshape(-1), heat_input, voxel_list, devices)
    incoming = exchange(outgoing)
    half, eighth, cols_k, lo_k, hi_k = coefs(conductivity)
    coef = (half, eighth, cols_k, lo_k, hi_k)
    coef_halos = neighbours(cols_k, cols_k, hi_k, lo_k)
    seen = pixel_sums(
        pixel_cell.reshape(1, pixels),
        observed.reshape(1, pixels),
        pixel_variance.reshape(1, pixels),
        pixel_noise,
    )
    field, cols, lo, hi, peaks = deposit(incoming, state_prior, half, eighth)
    for s in range(SUBSTEPS):
        halos = neighbours(cols, cols, hi, lo)
        peaks = exchange(peaks)
        if s < SUBSTEPS - 1:
            field, cols, lo, hi, peaks = substep(
                field, (cols, lo, hi), halos, peaks, coef, coef_halos
            )
        else:
            field, sums = substep(field, (cols, lo, hi), halos, peaks, coef, coef_halos, seen)
    return update(exchange(sums), field)


def solution(mesh):
    in_specs = (
        P(None, None, "gy", "gx"),
        P(None, "gy", "gx"),
        P(None, BOTH, None),
        P(BOTH, None),
        P(BOTH, None),
        P(BOTH),
        P(BOTH),
        P(BOTH),
        P(None, BOTH),
    )
    out_specs = P(None, None, "gy", "gx")
    return jax.shard_map(
        on_device, mesh=mesh, in_specs=in_specs, out_specs=out_specs, check_vma=False
    )
```

```python
import functools

import jax
import jax.numpy as jnp
from jax import lax
from jax.experimental import pallas as pl
from jax.experimental.pallas import tpu as pltpu
from jax.sharding import PartitionSpec as P

SUBSTEPS = 6
CAP = 2
COOL = 0.1
SHARE = 0.9
F32 = jnp.float32
BF16 = jnp.bfloat16
VM = pltpu.VMEM
LIMIT = 48 * 1024 * 1024
NT = (((1,), (1,)), ((), ()))
BOTH = ("gx", "gy")

M, NZ, CY, CX = 16, 16, 8, 128
ROWS = 40


def vspec():
    return pl.BlockSpec(memory_space=pltpu.VMEM)


def params():
    return pltpu.CompilerParams(vmem_limit_bytes=LIMIT)


def lanes():
    return lax.broadcasted_iota(jnp.int32, (CY, CX), 1)


def rows():
    return lax.broadcasted_iota(jnp.int32, (CY, CX), 0)


def pack_kernel(owner, heat, voxel, out, wide, high, low, inverse):
    blocks = owner.shape[0]
    devices = out.shape[0]

    def clear(i, carry):
        inverse[i] = blocks
        return carry

    lax.fori_loop(0, devices * CAP, clear, 0, unroll=16)

    def place(b, carry):
        base = owner[b] * CAP
        base = base + jnp.where(inverse[base] != blocks, 1, 0)
        inverse[base] = b
        return carry

    lax.fori_loop(0, blocks, place, 0, unroll=8)

    def widen(m, carry):
        wide[m, 0:blocks, :] = heat[m].astype(F32)
        wide[m, blocks:, :] = jnp.zeros((8, CX), F32)
        return carry

    lax.fori_loop(0, M, widen, 0)
    cells = voxel[...]
    high[0:blocks, :] = (cells >> 7).astype(F32)
    high[blocks:, :] = jnp.zeros((8, CX), F32)
    low[0:blocks, :] = (cells & 127).astype(F32)
    low[blocks:, :] = jnp.zeros((8, CX), F32)
    row = rows()

    def emit(d, carry):
        first = inverse[d * CAP]
        second = inverse[d * CAP + 1]
        index = jnp.where(
            row == 0,
            high[pl.ds(first, 1), :],
            jnp.where(
                row == 1,
                high[pl.ds(second, 1), :],
                jnp.where(
                    row == 2,
                    low[pl.ds(first, 1), :],
                    jnp.where(row == 3, low[pl.ds(second, 1), :], 0.0),
                ),
            ),
        )
        chunk = jnp.concatenate(
            [
                wide[:, pl.ds(first, 1), :].reshape(M, CX),
                wide[:, pl.ds(second, 1), :].reshape(M, CX),
                index,
            ],
            axis=0,
        )
        out[d] = chunk.astype(BF16)
        return carry

    lax.fori_loop(0, devices, emit, 0, unroll=4)


def pack(owner, heat, voxel, devices):
    blocks = owner.shape[0]
    return pl.pallas_call(
        pack_kernel,
        out_shape=jax.ShapeDtypeStruct((devices, ROWS, CX), BF16),
        in_specs=[pl.BlockSpec(memory_space=pltpu.SMEM), vspec(), vspec()],
        out_specs=vspec(),
        scratch_shapes=[
            VM((M, blocks + 8, CX), F32),
            VM((blocks + 8, CX), F32),
            VM((blocks + 8, CX), F32),
            pltpu.SMEM((devices * CAP,), jnp.int32),
        ],
        compiler_params=params(),
        name="pack",
    )(owner, heat, voxel)


HALO = 6
YS = CY + 2 * HALO
XT = CX // 8 + 2
ZG = NZ // 2
OWN = jax.ShapeDtypeStruct((2, CY, XT - 2, 8, CX), F32)
ROWHALO = jax.ShapeDtypeStruct((2, HALO, XT - 2, 8, CX), F32)
WIDE = jax.ShapeDtypeStruct((2, YS, XT, 8, CX), F32)


def relayout_kernel(state, own, to_high, to_low):
    for zi in range(2):
        for y in range(CY):
            parts = [
                state[m0 : m0 + 8, 2 * group + zi, y, :] for group in range(ZG) for m0 in (0, 8)
            ]
            turned = (0.5 * jnp.concatenate(parts, axis=0)).T.reshape(XT - 2, 8, CX)
            own[zi, y] = turned
            if y >= CY - HALO:
                to_high[zi, y - (CY - HALO)] = turned
            if y < HALO:
                to_low[zi, y] = turned


def relayout(state):
    return pl.pallas_call(
        relayout_kernel,
        out_shape=[OWN, ROWHALO, ROWHALO],
        in_specs=[vspec()],
        out_specs=[vspec()] * 3,
        compiler_params=params(),
        name="relayout",
    )(state)


def side_kernel(own, low, high, to_left, to_right):
    for out, t in ((to_left, 0), (to_right, XT - 3)):
        for zi in range(2):
            for y in range(YS):
                if y < HALO:
                    out[zi, y] = low[zi, y, t]
                elif y < HALO + CY:
                    out[zi, y] = own[zi, y - HALO, t]
                else:
                    out[zi, y] = high[zi, y - HALO - CY, t]


def sides(own, low, high):
    shape = jax.ShapeDtypeStruct((2, YS, 8, CX), F32)
    return pl.pallas_call(
        side_kernel,
        out_shape=[shape, shape],
        in_specs=[vspec()] * 3,
        out_specs=[vspec()] * 2,
        compiler_params=params(),
        name="sides",
    )(own, low, high)


def coef_kernel(own, low, high, out, turned):
    for g, tiles in enumerate((low, own, high)):
        for t in range(3):
            turned[g, t] = (0.5 * tiles[t].reshape(CX, CX)).T
    source = lax.broadcasted_iota(jnp.int32, (CX, CX), 0)
    target = lax.broadcasted_iota(jnp.int32, (CX, CX), 1)

    def put(g, y0, yy):
        strip = jnp.concatenate([turned[g, 0, CX - 8 :, :], turned[g, 1], turned[g, 2, 0:8, :]], axis=0)
        for zi in range(2):
            wanted = (2 * (target >> 4) + zi) * CY + y0
            hot = jnp.where(source == wanted, 1.0, 0.0).astype(F32)
            part = jnp.dot(
                strip, hot, precision=lax.Precision.HIGHEST, preferred_element_type=F32
            )
            out[zi, yy] = part.reshape(XT, 8, CX)

    for y in range(HALO):
        put(0, y + CY - HALO, y)
    for y in range(CY):
        put(1, y, y + HALO)
    for y in range(HALO):
        put(2, y, y + HALO + CY)


def coefs(own, low, high):
    return pl.pallas_call(
        coef_kernel,
        out_shape=WIDE,
        in_specs=[vspec()] * 3,
        out_specs=vspec(),
        scratch_shapes=[VM((3, 3, CX, CX), F32)],
        compiler_params=params(),
        name="coefs",
    )(own, low, high)


def deposit_kernel(incoming, out, total):
    sources = incoming.shape[0]
    group = 4
    place = lax.broadcasted_iota(jnp.int32, (CX, CX), 0).astype(F32).astype(BF16)
    zero = jnp.zeros((M, CX), BF16)
    total[...] = jnp.zeros_like(total)

    def one(g, carry):
        left = []
        right = []
        for s in range(group):
            source = g * group + s
            index = incoming[source, 32:40, :].astype(F32)
            for slot in range(CAP):
                heat = incoming[source, slot * M : (slot + 1) * M, :]
                layer = jnp.broadcast_to(index[slot : slot + 1, :], (M, CX)).astype(BF16)
                cell = jnp.broadcast_to(index[2 + slot : 3 + slot, :], (CX, CX)).astype(BF16)
                left.append(
                    jnp.concatenate(
                        [jnp.where(layer == h, heat, zero) for h in range(2 * CY)], axis=0
                    )
                )
                right.append(jnp.where(place == cell, 1.0, 0.0).astype(BF16))
        total[...] += lax.dot_general(
            jnp.concatenate(left, axis=1),
            jnp.concatenate(right, axis=1),
            NT,
            preferred_element_type=F32,
        )
        return carry

    lax.fori_loop(0, sources // group, one, 0)
    for zi in range(2):
        out[zi] = (0.5 * total[zi * CX : (zi + 1) * CX, :]).T


def deposit(incoming):
    return pl.pallas_call(
        deposit_kernel,
        out_shape=jax.ShapeDtypeStruct((2, CX, CX), F32),
        in_specs=[vspec()],
        out_specs=vspec(),
        scratch_shapes=[VM((2 * CY * M, CX), F32)],
        compiler_params=params(),
        name="deposit",
    )(incoming)


def heat_side_kernel(low, own, high, to_left, to_right):
    for g, part in enumerate((low, own, high)):
        to_left[g] = part[:, 0:8, :]
        to_right[g] = part[:, CX - 8 :, :]


def heat_sides(low, own, high):
    shape = jax.ShapeDtypeStruct((3, 2, 8, CX), F32)
    return pl.pallas_call(
        heat_side_kernel,
        out_shape=[shape, shape],
        in_specs=[vspec()] * 3,
        out_specs=[vspec()] * 2,
        compiler_params=params(),
        name="heat_sides",
    )(low, own, high)


def heated_kernel(
    own, low, high, left, right, heat_low, heat_own, heat_high, heat_left, heat_right, coef, out, peaks
):
    top = lanes() < M
    peak = jnp.zeros((8, CX), F32)

    def row(g, heat, tile_of, y0, yy, peak, inner):
        shift = (CX - 16 * y0) % CX
        for zi in range(2):
            for t in range(XT):
                if t == 0:
                    prior, add = left[zi, yy], heat_left[g, zi]
                elif t == XT - 1:
                    prior, add = right[zi, yy], heat_right[g, zi]
                else:
                    prior, add = tile_of(zi, t - 1), heat[zi, 8 * t - 8 : 8 * t, :]
                if shift:
                    add = pltpu.roll(add, shift, axis=1)
                value = prior + jnp.where(top, add, 0.0)
                out[zi, yy, t] = value
                if inner and 0 < t < XT - 1:
                    c = coef[zi, yy, t]
                    peak = jnp.maximum(peak, c + c * (value * value))
        return peak

    for y in range(HALO):
        y0 = y + CY - HALO
        row(0, heat_low, lambda zi, t: low[zi, y, t], y0, y, peak, False)
    for y in range(CY):
        peak = row(1, heat_own, lambda zi, t: own[zi, y, t], y, y + HALO, peak, True)
    for y in range(HALO):
        row(2, heat_high, lambda zi, t: high[zi, y, t], y, y + HALO + CY, peak, False)
    spread_peak(peak, peaks)


def spread_peak(peak, out):
    row = jnp.max(peak, axis=0, keepdims=True)
    for d in range(out.shape[0]):
        out[d] = row


def heated(prior, halos, heat, coef, devices):
    operands = [*prior, *halos, *heat, coef]
    return pl.pallas_call(
        heated_kernel,
        out_shape=[WIDE, jax.ShapeDtypeStruct((devices, 1, CX), F32)],
        in_specs=[vspec()] * len(operands),
        out_specs=[vspec()] * 2,
        compiler_params=params(),
        name="heated",
    )(*operands)


def substep_kernel(number, inside, field, coef, peaks, *rest):
    last = number == SUBSTEPS - 1
    if last:
        weight, data, out, sums, above, below_h, flat = rest
    else:
        out, out_peaks, above, below_h = rest
    first, end = number + 1, YS - 1 - number
    lane = lanes()
    row = rows()
    last_row = row == 7
    first_row = row == 0
    inner_lane = lane < CX - M
    cooling = jnp.where(lane < M, COOL, 0.0)

    peak = peaks[0]
    for d in range(1, peaks.shape[0]):
        peak = jnp.maximum(peak, peaks[d])
    peak = 2.0 * jnp.max(peak, axis=(0, 1), keepdims=True)
    step = jnp.broadcast_to(SHARE / (6.0 * peak + COOL), (8, CX))

    def conduct(zi, y, t):
        u = field[zi, y, t]
        c = coef[zi, y, t]
        return u, c + c * (u * u)

    for zi in range(2):
        for t in range(XT):
            u, h = conduct(zi, first - 1, t)
            v, g = conduct(zi, first, t)
            above[zi, t] = (h + g) * (v - u)
            below_h[zi, t] = g

    def line(y, peak):
        kept = jnp.where(y < HALO, inside[2], jnp.where(y >= HALO + CY, inside[3], 1.0))
        mid = step * kept
        steps = [mid * inside[0]] + [mid] * (XT - 2) + [mid * inside[1]]
        top = jnp.zeros((8, CX), F32)

        def load(t):
            us = [field[zi, y, t] for zi in range(2)]
            hs = [below_h[zi, t] for zi in range(2)]
            return us, hs, [pltpu.roll(a, 7, axis=0) for a in us], [pltpu.roll(a, 7, axis=0) for a in hs]

        us, hs, ru, rh = load(0)
        carried = [jnp.zeros((8, CX), F32)] * 2
        for t in range(XT):
            if t < XT - 1:
                after = load(t + 1)
                next_u = [jnp.where(last_row, after[2][z], ru[z]) for z in range(2)]
                next_h = [jnp.where(last_row, after[3][z], rh[z]) for z in range(2)]
            else:
                next_u = [jnp.where(last_row, us[z], ru[z]) for z in range(2)]
                next_h = rh
            change = []
            for zi in range(2):
                u, h = us[zi], hs[zi]
                along = (h + next_h[zi]) * (next_u[zi] - u)
                turned = pltpu.roll(along, 1, axis=0)
                total = along - jnp.where(first_row, carried[zi], turned)
                carried[zi] = turned
                v, g = conduct(zi, y + 1, t)
                across = (h + g) * (v - u)
                total = total + (across - above[zi, t])
                above[zi, t] = across
                below_h[zi, t] = g
                change.append(total)
            within = (hs[0] + hs[1]) * (us[1] - us[0])
            between = (hs[1] + pltpu.roll(hs[0], CX - M, axis=1)) * (
                pltpu.roll(us[0], CX - M, axis=1) - us[1]
            )
            between = jnp.where(inner_lane, between, 0.0)
            change[0] = change[0] + (within - pltpu.roll(between, M, axis=1)) - cooling * us[0]
            change[1] = change[1] + (between - within)
            for zi in range(2):
                value = us[zi] + steps[t] * change[zi]
                if last:
                    if 0 < t < XT - 1:
                        out[zi, y - HALO, t - 1] = value
                else:
                    out[zi, y, t] = value
                    if 0 < t < XT - 1:
                        c = coef[zi, y, t]
                        top = jnp.maximum(top, c + c * (value * value))
            if t < XT - 1:
                us, hs, ru, rh = after
        own = jnp.where((y >= HALO) & (y < HALO + CY), 1.0, 0.0)
        return jnp.maximum(peak, top * own)

    peak = lax.fori_loop(first, end, line, jnp.zeros((8, CX), F32))
    if not last:
        spread_peak(peak, out_peaks)
        return

    grams = jnp.zeros((M, 2 * M), F32)
    for y in range(CY):
        seen = 2.0 * out[0, y].reshape(CX, CX).T[0:M, :]
        for m in range(M):
            flat[m : m + 1, :] = data[m, y : y + 1, :]
        w = weight[y : y + 1, :]
        spread = seen - jnp.mean(seen, axis=0, keepdims=True)
        both = jnp.concatenate([spread * w, flat[...] - seen * w], axis=0)
        grams = grams + lax.dot_general(
            spread, both, NT, precision=lax.Precision.HIGHEST, preferred_element_type=F32
        )
    grams = jnp.concatenate([grams, jnp.zeros((M, CX - 2 * M), F32)], axis=1)
    pair = grams[0:8] + pltpu.roll(grams[8:16], 32, axis=1)
    quad = pair + pltpu.roll(pltpu.roll(pair, 64, axis=1), 4, axis=0)
    quad = quad[0:4]
    for d in range(sums.shape[0]):
        sums[d] = quad


def substep(number, inside, field, coef, peaks, pixels):
    devices = peaks.shape[0]
    operands = [inside, field, coef, peaks]
    scratch = [VM((2, XT, 8, CX), F32), VM((2, XT, 8, CX), F32)]
    if number == SUBSTEPS - 1:
        operands += list(pixels)
        out_shape = [OWN, jax.ShapeDtypeStruct((devices, 4, CX), F32)]
        scratch += [VM((M, CX), F32)]
    else:
        out_shape = [WIDE, jax.ShapeDtypeStruct((devices, 1, CX), F32)]
    return pl.pallas_call(
        functools.partial(substep_kernel, number),
        out_shape=out_shape,
        in_specs=[pl.BlockSpec(memory_space=pltpu.SMEM)] + [vspec()] * (len(operands) - 1),
        out_specs=[vspec()] * 2,
        scratch_shapes=scratch,
        compiler_params=params(),
        name=f"substep_{number}",
    )(*operands)

def pixel_kernel(cell, observed, variance, noise, weight, data):
    pixels = cell.shape[1]
    place = cell[...]
    var = variance[...]
    inverse = 1.0 / var
    values = (observed[...] + noise[...] * jnp.sqrt(var)) * inverse
    stack = jnp.concatenate([values, jnp.broadcast_to(inverse, (8, pixels))], axis=0)
    width = place >> 7
    hot = jnp.where(
        lax.broadcasted_iota(jnp.int32, (CX, pixels), 0) == (place & 127), 1.0, 0.0
    ).astype(F32)
    for y in range(CY):
        part = lax.dot_general(
            jnp.where(width == y, stack, 0.0),
            hot,
            NT,
            precision=lax.Precision.HIGHEST,
            preferred_element_type=F32,
        )
        weight[y : y + 1, :] = part[M : M + 1, :]
        for m in range(M):
            data[m, y : y + 1, :] = part[m : m + 1, :]


def pixel_sums(cell, observed, variance, noise):
    return pl.pallas_call(
        pixel_kernel,
        out_shape=[
            jax.ShapeDtypeStruct((CY, CX), F32),
            jax.ShapeDtypeStruct((M, CY, CX), F32),
        ],
        in_specs=[vspec()] * 4,
        out_specs=[vspec()] * 2,
        compiler_params=params(),
        name="pixels",
    )(cell, observed, variance, noise)


def update_kernel(sums, field, out):
    quad = sums[0]
    for d in range(1, sums.shape[0]):
        quad = quad + sums[d]
    row = rows()
    quad = jnp.concatenate([quad, jnp.zeros_like(quad)], axis=0)
    pair = jnp.where(row < 4, quad, pltpu.roll(pltpu.roll(quad, 64, axis=1), 4, axis=0))
    system = jnp.concatenate([pair, pltpu.roll(pair, CX - 32, axis=1)], axis=0)
    tall = lax.broadcasted_iota(jnp.int32, (M, CX), 0)
    wide = lax.broadcasted_iota(jnp.int32, (M, CX), 1)
    system = jnp.where(tall == wide, system + (M - 1.0), system)
    for i in range(M):
        pivot = system[i : i + 1, :]
        pivot = pivot / pivot[:, i : i + 1]
        factor = jnp.where(tall == i, 0.0, jnp.broadcast_to(system[:, i : i + 1], (M, CX)))
        system = jnp.where(tall == i, pivot, system - factor * pivot)
    mixing = system - jnp.mean(system, axis=0, keepdims=True)
    mixing = pltpu.roll(mixing, CX - M, axis=1)
    mixing = jnp.where(wide < M, mixing + jnp.where(tall == wide, 1.0, 0.0), 0.0)
    for shift in (16, 32, 64):
        mixing = mixing + pltpu.roll(mixing, shift, axis=1)
    mixing = jnp.concatenate([mixing] * ZG, axis=0)
    tall = lax.broadcasted_iota(jnp.int32, (CX, CX), 0)
    wide = lax.broadcasted_iota(jnp.int32, (CX, CX), 1)
    mixing = jnp.where((tall >> 4) == (wide >> 4), 2.0 * mixing, 0.0).T
    for zi in range(2):
        for y in range(CY):
            part = lax.dot_general(
                mixing,
                field[zi, y].reshape(CX, CX),
                NT,
                precision=lax.Precision.HIGHEST,
                preferred_element_type=F32,
            )
            for group in range(ZG):
                for m0 in (0, 8):
                    at = group * M + m0
                    out[m0 : m0 + 8, 2 * group + zi, y, :] = part[at : at + 8, :]


def update(sums, field):
    return pl.pallas_call(
        update_kernel,
        out_shape=jax.ShapeDtypeStruct((M, NZ, CY, CX), F32),
        in_specs=[vspec()] * 2,
        out_specs=vspec(),
        compiler_params=params(),
        name="update",
    )(sums, field)


def exchange(parts):
    return lax.all_to_all(parts, BOTH, split_axis=0, concat_axis=0, tiled=True)


def move(part, axis, ahead):
    count = lax.axis_size(axis)
    pairs = [(i, i + 1) if ahead else (i + 1, i) for i in range(count - 1)]
    return lax.ppermute(part, axis, pairs)


def on_device(
    state_prior,
    conductivity,
    heat_input,
    owner_tile,
    voxel_list,
    pixel_cell,
    observed,
    pixel_variance,
    pixel_noise,
):
    devices = lax.axis_size("gx") * lax.axis_size("gy")
    pixels = pixel_cell.shape[0]
    outgoing = pack(owner_tile.reshape(-1), heat_input, voxel_list, devices)
    incoming = exchange(outgoing)

    gx, gy = lax.axis_index("gx"), lax.axis_index("gy")
    inside = jnp.stack(
        [gx > 0, gx < lax.axis_size("gx") - 1, gy > 0, gy < lax.axis_size("gy") - 1]
    ).astype(F32)
    own, to_high, to_low = relayout(state_prior)
    low, high = move(to_high, "gy", True), move(to_low, "gy", False)
    to_left, to_right = sides(own, low, high)
    left, right = move(to_right, "gx", True), move(to_left, "gx", False)

    tiles = jnp.stack(
        [move(conductivity, "gx", True), conductivity, move(conductivity, "gx", False)]
    )
    coef = coefs(tiles, move(tiles, "gy", True), move(tiles, "gy", False))
    seen = pixel_sums(
        pixel_cell.reshape(1, pixels),
        observed.reshape(1, pixels),
        pixel_variance.reshape(1, pixels),
        pixel_noise,
    )

    heat = deposit(incoming)
    heat_low, heat_high = move(heat, "gy", True), move(heat, "gy", False)
    to_left, to_right = heat_sides(heat_low, heat, heat_high)
    heat_left, heat_right = move(to_right, "gx", True), move(to_left, "gx", False)
    field, peaks = heated(
        (own, low, high),
        (left, right),
        (heat_low, heat, heat_high, heat_left, heat_right),
        coef,
        devices,
    )
    for number in range(SUBSTEPS):
        field, peaks = substep(number, inside, field, coef, exchange(peaks), seen)
    return update(exchange(peaks), field)


def solution(mesh):
    in_specs = (
        P(None, None, "gy", "gx"),
        P(None, "gy", "gx"),
        P(None, BOTH, None),
        P(BOTH, None),
        P(BOTH, None),
        P(BOTH),
        P(BOTH),
        P(BOTH),
        P(None, BOTH),
    )
    out_specs = P(None, None, "gy", "gx")
    return jax.shard_map(
        on_device, mesh=mesh, in_specs=in_specs, out_specs=out_specs, check_vma=False
    )
```

```python
import functools

import jax
import jax.numpy as jnp
from jax import lax
from jax.experimental import pallas as pl
from jax.experimental.pallas import tpu as pltpu
from jax.sharding import PartitionSpec as P

SUBSTEPS = 6
CAP = 2
COOL = 0.1
SHARE = 0.9
F32 = jnp.float32
BF16 = jnp.bfloat16
VM = pltpu.VMEM
LIMIT = 24 * 1024 * 1024
NT = (((1,), (1,)), ((), ()))
BOTH = ("gx", "gy")

M, NZ, CY, CX = 16, 16, 8, 128
ROWS = 40


def vspec():
    return pl.BlockSpec(memory_space=pltpu.VMEM)


def params():
    return pltpu.CompilerParams(vmem_limit_bytes=LIMIT)


def lanes():
    return lax.broadcasted_iota(jnp.int32, (CY, CX), 1)


def rows():
    return lax.broadcasted_iota(jnp.int32, (CY, CX), 0)


def pack_kernel(owner, heat, voxel, out, wide, high, low, inverse):
    blocks = owner.shape[0]
    devices = out.shape[0]

    def clear(i, carry):
        inverse[i] = blocks
        return carry

    lax.fori_loop(0, devices * CAP, clear, 0, unroll=16)

    def place(b, carry):
        base = owner[b] * CAP
        base = base + jnp.where(inverse[base] != blocks, 1, 0)
        inverse[base] = b
        return carry

    lax.fori_loop(0, blocks, place, 0, unroll=8)

    def widen(m, carry):
        wide[m, 0:blocks, :] = heat[m].astype(F32)
        wide[m, blocks:, :] = jnp.zeros((8, CX), F32)
        return carry

    lax.fori_loop(0, M, widen, 0)
    cells = voxel[...]
    high[0:blocks, :] = (cells >> 7).astype(F32)
    high[blocks:, :] = jnp.zeros((8, CX), F32)
    low[0:blocks, :] = (cells & 127).astype(F32)
    low[blocks:, :] = jnp.zeros((8, CX), F32)
    row = rows()

    def emit(d, carry):
        first = inverse[d * CAP]
        second = inverse[d * CAP + 1]
        index = jnp.where(
            row == 0,
            high[pl.ds(first, 1), :],
            jnp.where(
                row == 1,
                high[pl.ds(second, 1), :],
                jnp.where(
                    row == 2,
                    low[pl.ds(first, 1), :],
                    jnp.where(row == 3, low[pl.ds(second, 1), :], 0.0),
                ),
            ),
        )
        chunk = jnp.concatenate(
            [
                wide[:, pl.ds(first, 1), :].reshape(M, CX),
                wide[:, pl.ds(second, 1), :].reshape(M, CX),
                index,
            ],
            axis=0,
        )
        out[d] = chunk.astype(BF16)
        return carry

    lax.fori_loop(0, devices, emit, 0, unroll=4)


def pack(owner, heat, voxel, devices):
    blocks = owner.shape[0]
    return pl.pallas_call(
        pack_kernel,
        out_shape=jax.ShapeDtypeStruct((devices, ROWS, CX), BF16),
        in_specs=[pl.BlockSpec(memory_space=pltpu.SMEM), vspec(), vspec()],
        out_specs=vspec(),
        scratch_shapes=[
            VM((M, blocks + 8, CX), F32),
            VM((blocks + 8, CX), F32),
            VM((blocks + 8, CX), F32),
            pltpu.SMEM((devices * CAP,), jnp.int32),
        ],
        compiler_params=params(),
        name="pack",
    )(owner, heat, voxel)


HALO = 6
YS = CY + 2 * HALO
XT = CX // 8 + 2
ZG = NZ // 2
TOLERANCE = 1e-6
OWN = jax.ShapeDtypeStruct((2, CY, XT - 2, 8, CX), F32)
WIDE = jax.ShapeDtypeStruct((2, YS, XT, 8, CX), F32)
EDGE = 2 * HALO * (XT - 2)
SIDE = 2 * YS


def relayout_kernel(state, conduct, own, turned_c, to_high, to_low):
    turned = (0.5 * conduct[...].reshape(CX, CX)).T.reshape(XT - 2, 8, CX)
    turned_c[...] = turned
    to_high[EDGE:] = turned
    to_low[EDGE:] = turned
    for zi in range(2):
        for y in range(CY):
            parts = [
                state[m0 : m0 + 8, 2 * group + zi, y, :] for group in range(ZG) for m0 in (0, 8)
            ]
            turned = (0.5 * jnp.concatenate(parts, axis=0)).T.reshape(XT - 2, 8, CX)
            own[zi, y] = turned
            if y >= CY - HALO:
                at = (zi * HALO + y - (CY - HALO)) * (XT - 2)
                to_high[at : at + XT - 2] = turned
            if y < HALO:
                at = (zi * HALO + y) * (XT - 2)
                to_low[at : at + XT - 2] = turned


def relayout(state, conduct):
    edge = jax.ShapeDtypeStruct((EDGE + XT - 2, 8, CX), F32)
    return pl.pallas_call(
        relayout_kernel,
        out_shape=[OWN, jax.ShapeDtypeStruct((XT - 2, 8, CX), F32), edge, edge],
        in_specs=[vspec()] * 2,
        out_specs=[vspec()] * 4,
        compiler_params=params(),
        name="relayout",
    )(state, conduct)


def side_kernel(own, turned_c, low, high, to_left, to_right):
    for out, t in ((to_left, 0), (to_right, XT - 3)):
        for zi in range(2):
            for y in range(YS):
                if y < HALO:
                    part = low[(zi * HALO + y) * (XT - 2) + t]
                elif y < HALO + CY:
                    part = own[zi, y - HALO, t]
                else:
                    part = high[(zi * HALO + y - HALO - CY) * (XT - 2) + t]
                out[zi * YS + y] = part
        out[SIDE] = low[EDGE + t]
        out[SIDE + 1] = turned_c[t]
        out[SIDE + 2] = high[EDGE + t]


def sides(own, turned_c, low, high):
    shape = jax.ShapeDtypeStruct((SIDE + 3, 8, CX), F32)
    return pl.pallas_call(
        side_kernel,
        out_shape=[shape, shape],
        in_specs=[vspec()] * 4,
        out_specs=[vspec()] * 2,
        compiler_params=params(),
        name="sides",
    )(own, turned_c, low, high)


def coef_kernel(turned_c, low, high, left, right, out):
    source = lax.broadcasted_iota(jnp.int32, (CX, CX), 0)
    target = lax.broadcasted_iota(jnp.int32, (CX, CX), 1)
    strips = []
    for g in range(3):
        mid = (low[EDGE:], turned_c[...], high[EDGE:])[g].reshape(CX, CX)
        strips.append(jnp.concatenate([left[SIDE + g], mid, right[SIDE + g]], axis=0))

    def put(g, y0, yy):
        for zi in range(2):
            wanted = (2 * (target >> 4) + zi) * CY + y0
            hot = jnp.where(source == wanted, 1.0, 0.0).astype(F32)
            part = jnp.dot(
                strips[g], hot, precision=lax.Precision.HIGHEST, preferred_element_type=F32
            )
            out[zi, yy] = part.reshape(XT, 8, CX)

    for y in range(HALO):
        put(0, y + CY - HALO, y)
    for y in range(CY):
        put(1, y, y + HALO)
    for y in range(HALO):
        put(2, y, y + HALO + CY)


def coefs(turned_c, low, high, left, right):
    return pl.pallas_call(
        coef_kernel,
        out_shape=WIDE,
        in_specs=[vspec()] * 5,
        out_specs=vspec(),
        compiler_params=params(),
        name="coefs",
    )(turned_c, low, high, left, right)


def deposit_kernel(incoming, out, total):
    sources = incoming.shape[0]
    group = 4
    place = lax.broadcasted_iota(jnp.int32, (CX, CX), 0).astype(F32).astype(BF16)
    zero = jnp.zeros((M, CX), BF16)
    total[...] = jnp.zeros_like(total)

    def one(g, carry):
        left = []
        right = []
        for s in range(group):
            source = g * group + s
            index = incoming[source, 32:40, :].astype(F32)
            for slot in range(CAP):
                heat = incoming[source, slot * M : (slot + 1) * M, :]
                layer = jnp.broadcast_to(index[slot : slot + 1, :], (M, CX)).astype(BF16)
                cell = jnp.broadcast_to(index[2 + slot : 3 + slot, :], (CX, CX)).astype(BF16)
                left.append(
                    jnp.concatenate(
                        [jnp.where(layer == h, heat, zero) for h in range(2 * CY)], axis=0
                    )
                )
                right.append(jnp.where(place == cell, 1.0, 0.0).astype(BF16))
        total[...] += lax.dot_general(
            jnp.concatenate(left, axis=1),
            jnp.concatenate(right, axis=1),
            NT,
            preferred_element_type=F32,
        )
        return carry

    lax.fori_loop(0, sources // group, one, 0)
    for zi in range(2):
        out[zi] = (0.5 * total[zi * CX : (zi + 1) * CX, :]).T


def deposit(incoming):
    return pl.pallas_call(
        deposit_kernel,
        out_shape=jax.ShapeDtypeStruct((2, CX, CX), F32),
        in_specs=[vspec()],
        out_specs=vspec(),
        scratch_shapes=[VM((2 * CY * M, CX), F32)],
        compiler_params=params(),
        name="deposit",
    )(incoming)


def heat_side_kernel(low, own, high, to_left, to_right):
    for g, part in enumerate((low, own, high)):
        to_left[g] = part[:, 0:8, :]
        to_right[g] = part[:, CX - 8 :, :]


def heat_sides(low, own, high):
    shape = jax.ShapeDtypeStruct((3, 2, 8, CX), F32)
    return pl.pallas_call(
        heat_side_kernel,
        out_shape=[shape, shape],
        in_specs=[vspec()] * 3,
        out_specs=[vspec()] * 2,
        compiler_params=params(),
        name="heat_sides",
    )(low, own, high)


def columns_peak(value):
    for shift in (4, 2, 1):
        value = jnp.maximum(value, pltpu.roll(value, shift, axis=0))
    return value


def whole_peak(value):
    return jnp.broadcast_to(jnp.max(value, axis=(0, 1), keepdims=True), (8, CX))


def step_of(peak):
    return SHARE / (12.0 * peak + COOL)


def conductance(field, coef, zi, y, t):
    u = field[zi, y, t]
    c = coef[zi, y, t]
    return u, c + c * (u * u)


def own_row(y):
    return jnp.where((y >= HALO) & (y < HALO + CY), 1.0, 0.0)


def masks(inside, y):
    kept = jnp.where(y < HALO, inside[2], jnp.where(y >= HALO + CY, inside[3], 1.0))
    return [kept * inside[0]] + [kept] * (XT - 2) + [kept * inside[1]]


def sweep(field, coef, above, below_h, first, end, emit, carry):
    lane = lanes()
    row = rows()
    last_row = row == 7
    first_row = row == 0
    inner_lane = lane < CX - M
    cooling = jnp.where(lane < M, COOL, 0.0)

    for zi in range(2):
        for t in range(XT):
            u, h = conductance(field, coef, zi, first - 1, t)
            v, g = conductance(field, coef, zi, first, t)
            above[zi, t] = (h + g) * (v - u)
            below_h[zi, t] = g

    def line(y, state):
        def load(t):
            us = [field[zi, y, t] for zi in range(2)]
            hs = [below_h[zi, t] for zi in range(2)]
            return (
                us,
                hs,
                [pltpu.roll(a, 7, axis=0) for a in us],
                [pltpu.roll(a, 7, axis=0) for a in hs],
            )

        us, hs, ru, rh = load(0)
        carried = [jnp.zeros((8, CX), F32)] * 2
        for t in range(XT):
            if t < XT - 1:
                after = load(t + 1)
                next_u = [jnp.where(last_row, after[2][z], ru[z]) for z in range(2)]
                next_h = [jnp.where(last_row, after[3][z], rh[z]) for z in range(2)]
            else:
                next_u = [jnp.where(last_row, us[z], ru[z]) for z in range(2)]
                next_h = rh
            change = []
            for zi in range(2):
                u, h = us[zi], hs[zi]
                along = (h + next_h[zi]) * (next_u[zi] - u)
                turned = pltpu.roll(along, 1, axis=0)
                total = along - jnp.where(first_row, carried[zi], turned)
                carried[zi] = turned
                v, g = conductance(field, coef, zi, y + 1, t)
                across = (h + g) * (v - u)
                total = total + (across - above[zi, t])
                above[zi, t] = across
                below_h[zi, t] = g
                change.append(total)
            within = (hs[0] + hs[1]) * (us[1] - us[0])
            between = (hs[1] + pltpu.roll(hs[0], CX - M, axis=1)) * (
                pltpu.roll(us[0], CX - M, axis=1) - us[1]
            )
            between = jnp.where(inner_lane, between, 0.0)
            change[0] = change[0] + (within - pltpu.roll(between, M, axis=1)) - cooling * us[0]
            change[1] = change[1] + (between - within)
            state = emit(y, t, us, change, state)
            if t < XT - 1:
                us, hs, ru, rh = after
        return state

    return lax.fori_loop(first, end, line, carry)


def advance(field, coef, above, below_h, inside, step, first, end, put):
    def emit(y, t, us, change, peak):
        part = masks(inside, y)[t] * step
        own = own_row(y)
        for zi in range(2):
            value = us[zi] + part * change[zi]
            put(zi, y, t, value)
            if 0 < t < XT - 1:
                c = coef[zi, y, t]
                peak = jnp.maximum(peak, own * (c + c * (value * value)))
        return peak

    return sweep(field, coef, above, below_h, first, end, emit, jnp.zeros((8, CX), F32))


def propose(field, coef, above, below_h, inside, guess, first, end, changes, peak, late, out):
    def emit(y, t, us, change, best):
        part = masks(inside, y)[t]
        own = own_row(y)
        for zi in range(2):
            moved = change[zi] * part
            changes[zi, y, t] = moved
            if 0 < t < XT - 1:
                c = coef[zi, y, t]
                value = us[zi] + guess * moved
                rank = own * (c + c * (value * value))
                better = rank > best[0]
                best = tuple(
                    jnp.where(better, new, old)
                    for new, old in zip((rank, us[zi], moved, c), best)
                )
        return best

    best = sweep(
        field, coef, above, below_h, first, end, emit, (jnp.zeros((8, CX), F32),) * 4
    )
    for shift in (4, 2, 1):
        other = tuple(pltpu.roll(part, shift, axis=0) for part in best)
        better = other[0] > best[0]
        best = tuple(jnp.where(better, new, old) for new, old in zip(other, best))
    row = rows()
    head = jnp.where(lanes() < CX // 2, whole_peak(peak), whole_peak(late))
    chunk = jnp.where(
        row == 0, head, jnp.where(row == 1, best[1], jnp.where(row == 2, best[2], best[3]))
    )[0:4]
    for d in range(out.shape[0]):
        out[d] = chunk


def agree(parts):
    lane = lanes()
    now = jnp.zeros((8, CX), F32)
    for d in range(0, parts.shape[0], 8):
        now = jnp.maximum(now, parts[d : d + 8, 0, :])
    late = whole_peak(jnp.where(lane < CX // 2, 0.0, now))
    now = whole_peak(jnp.where(lane < CX // 2, now, 0.0))
    step = step_of(now)
    then = jnp.zeros((8, CX), F32)
    for d in range(0, parts.shape[0], 8):
        value = parts[d : d + 8, 1, :] + step * parts[d : d + 8, 2, :]
        c = parts[d : d + 8, 3, :]
        then = jnp.maximum(then, c + c * (value * value))
    return now, whole_peak(then), late


def differs(late, used):
    return jnp.where(late > used * (1.0 + TOLERANCE), 1.0, 0.0)


def heated_kernel(
    inside, own, low, high, left, right,
    heat_low, heat_own, heat_high, heat_left, heat_right,
    coef, out, changes, parts, above, below_h,
):
    top = lanes() < M
    peak = jnp.zeros((8, CX), F32)

    def row(g, heat, tile_of, y0, yy, peak):
        shift = (CX - 16 * y0) % CX
        for zi in range(2):
            for t in range(XT):
                if t == 0:
                    prior, add = left[zi * YS + yy], heat_left[g, zi]
                elif t == XT - 1:
                    prior, add = right[zi * YS + yy], heat_right[g, zi]
                else:
                    prior, add = tile_of(zi, t - 1), heat[zi, 8 * t - 8 : 8 * t, :]
                if shift:
                    add = pltpu.roll(add, shift, axis=1)
                value = prior + jnp.where(top, add, 0.0)
                out[zi, yy, t] = value
                if g == 1 and 0 < t < XT - 1:
                    c = coef[zi, yy, t]
                    peak = jnp.maximum(peak, c + c * (value * value))
        return peak

    def edge(ref, y):
        return lambda zi, t: ref[(zi * HALO + y) * (XT - 2) + t]

    for y in range(HALO):
        row(0, heat_low, edge(low, y), y + CY - HALO, y, peak)
    for y in range(CY):
        peak = row(1, heat_own, lambda zi, t: own[zi, y, t], y, y + HALO, peak)
    for y in range(HALO):
        row(2, heat_high, edge(high, y), y, y + HALO + CY, peak)
    guess = step_of(whole_peak(peak))
    zero = jnp.zeros((8, CX), F32)
    propose(out, coef, above, below_h, inside, guess, 1, YS - 1, changes, peak, zero, parts)


ROW = (2, XT, 8, CX)


def smem():
    return pl.BlockSpec(memory_space=pltpu.SMEM)


def heated(inside, prior, halos, heat, coef, devices):
    operands = [inside, *prior, *halos, *heat, coef]
    return pl.pallas_call(
        heated_kernel,
        out_shape=[WIDE, WIDE, jax.ShapeDtypeStruct((devices, 4, CX), F32)],
        in_specs=[smem()] + [vspec()] * (len(operands) - 1),
        out_specs=[vspec()] * 3,
        scratch_shapes=[VM(ROW, F32), VM(ROW, F32)],
        compiler_params=params(),
        name="heated",
    )(*operands)


def first_of_pair(field, changes, coef, step, first, end, out):
    def line(y, peak):
        own = own_row(y)
        top = jnp.zeros((8, CX), F32)
        for zi in range(2):
            for t in range(XT):
                value = field[zi, y, t] + step * changes[zi, y, t]
                out[zi, y, t] = value
                if 0 < t < XT - 1:
                    c = coef[zi, y, t]
                    top = jnp.maximum(top, c + c * (value * value))
        return jnp.maximum(peak, own * top)

    return lax.fori_loop(first, end, line, jnp.zeros((8, CX), F32))


def pair_kernel(
    number, inside, field, changes, coef, parts, status,
    out, out_changes, out_parts, out_status, middle, above, below_h,
):
    now, then, late = agree(parts)
    bad = status[1:2, :]
    if number:
        bad = jnp.maximum(bad, differs(late[0:1], status[0:1, :]))
    out_status[...] = jnp.where(rows() == 0, then, bad)
    seen = first_of_pair(field, changes, coef, step_of(now), number + 1, YS - 1 - number, middle)

    def put(zi, y, t, value):
        out[zi, y, t] = value

    step = step_of(then)
    peak = advance(
        middle, coef, above, below_h, inside, step, number + 2, YS - 2 - number, put
    )
    guess = jnp.minimum(step_of(whole_peak(peak)), 1.2 * step)
    propose(
        out, coef, above, below_h, inside, guess, number + 3, YS - 3 - number,
        out_changes, peak, seen, out_parts,
    )


STATUS = jax.ShapeDtypeStruct((8, CX), F32)


def pair(number, inside, field, changes, coef, parts, status):
    operands = [inside, field, changes, coef, parts, status]
    return pl.pallas_call(
        functools.partial(pair_kernel, number),
        out_shape=[WIDE, WIDE, jax.ShapeDtypeStruct(parts.shape, F32), STATUS],
        in_specs=[smem()] + [vspec()] * 5,
        out_specs=[vspec()] * 4,
        scratch_shapes=[VM(WIDE.shape, F32), VM(ROW, F32), VM(ROW, F32)],
        compiler_params=params(),
        name=f"pair_{number}",
    )(*operands)


def pixel_grams(field, weight, data, flat, late, sums):
    grams = jnp.zeros((M, 2 * M), F32)
    for y in range(CY):
        seen = 2.0 * field[0, y].reshape(CX, CX).T[0:M, :]
        for m in range(M):
            flat[m : m + 1, :] = data[m, y : y + 1, :]
        w = weight[y : y + 1, :]
        spread = seen - jnp.mean(seen, axis=0, keepdims=True)
        both = jnp.concatenate([spread * w, flat[...] - seen * w], axis=0)
        grams = grams + lax.dot_general(
            spread, both, NT, precision=lax.Precision.HIGHEST, preferred_element_type=F32
        )
    grams = jnp.concatenate([grams, jnp.zeros((M, CX - 2 * M), F32)], axis=1)
    two = grams[0:8] + pltpu.roll(grams[8:16], 32, axis=1)
    quad = two + pltpu.roll(pltpu.roll(two, 64, axis=1), 4, axis=0)
    quad = jnp.where((rows() == 0) & (lanes() == 1), whole_peak(late), quad)[0:4]
    for d in range(sums.shape[0]):
        sums[d] = quad


def last_kernel(
    inside, field, changes, coef, parts, status, weight, data,
    out, sums, out_status, middle, above, below_h, flat,
):
    number = SUBSTEPS - 2
    now, then, late = agree(parts)
    bad = jnp.maximum(status[1:2, :], differs(late[0:1], status[0:1, :]))
    out_status[...] = jnp.where(rows() == 0, then, bad)
    seen = first_of_pair(field, changes, coef, step_of(now), number + 1, YS - 1 - number, middle)

    def put(zi, y, t, value):
        if 0 < t < XT - 1:
            out[zi, y - HALO, t - 1] = value

    advance(middle, coef, above, below_h, inside, step_of(then), HALO, HALO + CY, put)
    pixel_grams(out, weight, data, flat, seen, sums)


def last(inside, field, changes, coef, parts, status, pixels):
    operands = [inside, field, changes, coef, parts, status, *pixels]
    return pl.pallas_call(
        last_kernel,
        out_shape=[OWN, jax.ShapeDtypeStruct(parts.shape, F32), STATUS],
        in_specs=[smem()] + [vspec()] * (len(operands) - 1),
        out_specs=[vspec()] * 3,
        scratch_shapes=[VM(WIDE.shape, F32), VM(ROW, F32), VM(ROW, F32), VM((M, CX), F32)],
        compiler_params=params(),
        name="last_pair",
    )(*operands)


def single_kernel(number, inside, field, coef, peaks, *rest):
    final = number == SUBSTEPS - 1
    if final:
        weight, data, out, sums, above, below_h, flat = rest
    else:
        out, out_peaks, above, below_h = rest
    peak = peaks[0]
    for d in range(1, peaks.shape[0]):
        peak = jnp.maximum(peak, peaks[d])
    step = step_of(whole_peak(peak))

    def put(zi, y, t, value):
        if not final:
            out[zi, y, t] = value
        elif 0 < t < XT - 1:
            out[zi, y - HALO, t - 1] = value

    peak = advance(field, coef, above, below_h, inside, step, number + 1, YS - 1 - number, put)
    if final:
        pixel_grams(out, weight, data, flat, jnp.zeros((8, CX), F32), sums)
    else:
        out_peaks[...] = jnp.broadcast_to(columns_peak(peak)[0:1].reshape(1, 1, CX), out_peaks.shape)


def single(number, inside, field, coef, peaks, pixels):
    devices = peaks.shape[0]
    operands = [inside, field, coef, peaks]
    scratch = [VM(ROW, F32), VM(ROW, F32)]
    if number == SUBSTEPS - 1:
        operands += list(pixels)
        out_shape = [OWN, jax.ShapeDtypeStruct((devices, 4, CX), F32)]
        scratch += [VM((M, CX), F32)]
    else:
        out_shape = [WIDE, jax.ShapeDtypeStruct((devices, 1, CX), F32)]
    return pl.pallas_call(
        functools.partial(single_kernel, number),
        out_shape=out_shape,
        in_specs=[smem()] + [vspec()] * (len(operands) - 1),
        out_specs=[vspec()] * 2,
        scratch_shapes=scratch,
        compiler_params=params(),
        name=f"single_{number}",
    )(*operands)


def pixel_kernel(cell, observed, variance, noise, weight, data):
    pixels = cell.shape[1]
    place = cell[...]
    var = variance[...]
    inverse = 1.0 / var
    values = (observed[...] + noise[...] * jnp.sqrt(var)) * inverse
    stack = jnp.concatenate([values, jnp.broadcast_to(inverse, (8, pixels))], axis=0)
    width = place >> 7
    hot = jnp.where(
        lax.broadcasted_iota(jnp.int32, (CX, pixels), 0) == (place & 127), 1.0, 0.0
    ).astype(F32)
    for y in range(CY):
        part = lax.dot_general(
            jnp.where(width == y, stack, 0.0),
            hot,
            NT,
            precision=lax.Precision.HIGHEST,
            preferred_element_type=F32,
        )
        weight[y : y + 1, :] = part[M : M + 1, :]
        for m in range(M):
            data[m, y : y + 1, :] = part[m : m + 1, :]


def pixel_sums(cell, observed, variance, noise):
    return pl.pallas_call(
        pixel_kernel,
        out_shape=[
            jax.ShapeDtypeStruct((CY, CX), F32),
            jax.ShapeDtypeStruct((M, CY, CX), F32),
        ],
        in_specs=[vspec()] * 4,
        out_specs=[vspec()] * 2,
        compiler_params=params(),
        name="pixels",
    )(cell, observed, variance, noise)


def update_kernel(sums, field, status, out, flag):
    quad = sums[0]
    late = quad
    for d in range(1, sums.shape[0]):
        quad = quad + sums[d]
        late = jnp.maximum(late, sums[d])
    late = jnp.broadcast_to(late[0:1, 1:2], (1, CX))
    bad = jnp.maximum(status[1:2, :], differs(late, status[0:1, :]))
    flag[0] = jnp.where(jnp.max(bad) > 0.0, 1, 0)
    row = rows()
    quad = jnp.concatenate([quad, jnp.zeros_like(quad)], axis=0)
    pair = jnp.where(row < 4, quad, pltpu.roll(pltpu.roll(quad, 64, axis=1), 4, axis=0))
    system = jnp.concatenate([pair, pltpu.roll(pair, CX - 32, axis=1)], axis=0)
    tall = lax.broadcasted_iota(jnp.int32, (M, CX), 0)
    wide = lax.broadcasted_iota(jnp.int32, (M, CX), 1)
    system = jnp.where(tall == wide, system + (M - 1.0), system)
    mirror = jnp.broadcast_to(system[1:2, 0:1], (M, CX))
    system = jnp.where((tall == 0) & (wide == 1), mirror, system)
    for i in range(M):
        pivot = system[i : i + 1, :]
        pivot = pivot / pivot[:, i : i + 1]
        factor = jnp.where(tall == i, 0.0, jnp.broadcast_to(system[:, i : i + 1], (M, CX)))
        system = jnp.where(tall == i, pivot, system - factor * pivot)
    mixing = system - jnp.mean(system, axis=0, keepdims=True)
    mixing = pltpu.roll(mixing, CX - M, axis=1)
    mixing = jnp.where(wide < M, mixing + jnp.where(tall == wide, 1.0, 0.0), 0.0)
    for shift in (16, 32, 64):
        mixing = mixing + pltpu.roll(mixing, shift, axis=1)
    mixing = jnp.concatenate([mixing] * ZG, axis=0)
    tall = lax.broadcasted_iota(jnp.int32, (CX, CX), 0)
    wide = lax.broadcasted_iota(jnp.int32, (CX, CX), 1)
    mixing = jnp.where((tall >> 4) == (wide >> 4), 2.0 * mixing, 0.0).T
    for zi in range(2):
        for y in range(CY):
            part = lax.dot_general(
                mixing,
                field[zi, y].reshape(CX, CX),
                NT,
                precision=lax.Precision.HIGHEST,
                preferred_element_type=F32,
            )
            for group in range(ZG):
                for m0 in (0, 8):
                    at = group * M + m0
                    out[m0 : m0 + 8, 2 * group + zi, y, :] = part[at : at + 8, :]


def update(sums, field, status):
    return pl.pallas_call(
        update_kernel,
        out_shape=[
            jax.ShapeDtypeStruct((M, NZ, CY, CX), F32),
            jax.ShapeDtypeStruct((1,), jnp.int32),
        ],
        in_specs=[vspec()] * 3,
        out_specs=[vspec(), smem()],
        compiler_params=params(),
        name="update",
    )(sums, field, status)


def exchange(parts):
    return lax.all_to_all(parts, BOTH, split_axis=0, concat_axis=0, tiled=True)


def move(part, axis, ahead):
    count = lax.axis_size(axis)
    pairs = [(i, i + 1) if ahead else (i + 1, i) for i in range(count - 1)]
    return lax.ppermute(part, axis, pairs)


def on_device(
    state_prior,
    conductivity,
    heat_input,
    owner_tile,
    voxel_list,
    pixel_cell,
    observed,
    pixel_variance,
    pixel_noise,
):
    devices = lax.axis_size("gx") * lax.axis_size("gy")
    pixels = pixel_cell.shape[0]
    outgoing = pack(owner_tile.reshape(-1), heat_input, voxel_list, devices)
    incoming = exchange(outgoing)

    gx, gy = lax.axis_index("gx"), lax.axis_index("gy")
    inside = jnp.stack(
        [gx > 0, gx < lax.axis_size("gx") - 1, gy > 0, gy < lax.axis_size("gy") - 1]
    ).astype(F32)
    own, turned_c, to_high, to_low = relayout(state_prior, conductivity)
    low, high = move(to_high, "gy", True), move(to_low, "gy", False)
    to_left, to_right = sides(own, turned_c, low, high)
    seen = pixel_sums(
        pixel_cell.reshape(1, pixels),
        observed.reshape(1, pixels),
        pixel_variance.reshape(1, pixels),
        pixel_noise,
    )
    incoming, to_left, to_right, inside, *seen = lax.optimization_barrier(
        (incoming, to_left, to_right, inside, *seen)
    )
    left, right = move(to_right, "gx", True), move(to_left, "gx", False)

    heat = deposit(incoming)
    heat_low, heat_high = move(heat, "gy", True), move(heat, "gy", False)
    to_left, to_right = heat_sides(heat_low, heat, heat_high)
    heat_left, heat_right = move(to_right, "gx", True), move(to_left, "gx", False)
    coef = coefs(turned_c, low, high, left, right)
    start, changes, parts = heated(
        inside,
        (own, low, high),
        (left, right),
        (heat_low, heat, heat_high, heat_left, heat_right),
        coef,
        devices,
    )
    field, status = start, jnp.zeros((8, CX), F32)
    for number in range(0, SUBSTEPS - 2, 2):
        field, changes, parts, status = pair(
            number, inside, field, changes, coef, exchange(parts), status
        )
    field, sums, status = last(inside, field, changes, coef, exchange(parts), status, seen)
    result, flag = update(exchange(sums), field, status)

    def again():
        peak = coef * (1.0 + start * start)
        peak = jnp.max(peak[:, HALO : HALO + CY, 1 : XT - 1])
        peaks = jnp.full((devices, 1, CX), peak)
        field = start
        for number in range(SUBSTEPS):
            field, peaks = single(number, inside, field, coef, exchange(peaks), seen)
        return update(exchange(peaks), field, jnp.ones((8, CX), F32))[0]

    return lax.cond(flag[0] > 0, again, lambda: result)


def solution(mesh):
    in_specs = (
        P(None, None, "gy", "gx"),
        P(None, "gy", "gx"),
        P(None, BOTH, None),
        P(BOTH, None),
        P(BOTH, None),
        P(BOTH),
        P(BOTH),
        P(BOTH),
        P(None, BOTH),
    )
    out_specs = P(None, None, "gy", "gx")
    return jax.shard_map(
        on_device, mesh=mesh, in_specs=in_specs, out_specs=out_specs, check_vma=False
    )
```

```python
import functools

import jax
import jax.numpy as jnp
from jax import lax
from jax.experimental import pallas as pl
from jax.experimental.pallas import tpu as pltpu
from jax.sharding import PartitionSpec as P

SUBSTEPS = 6
CAP = 2
COOL = 0.1
SHARE = 0.9
F32 = jnp.float32
BF16 = jnp.bfloat16
VM = pltpu.VMEM
LIMIT = 24 * 1024 * 1024
NT = (((1,), (1,)), ((), ()))
BOTH = ("gx", "gy")

M, NZ, CY, CX = 16, 16, 8, 128
ROWS = 40


def vspec():
    return pl.BlockSpec(memory_space=pltpu.VMEM)


def params():
    return pltpu.CompilerParams(vmem_limit_bytes=LIMIT)


def lanes():
    return lax.broadcasted_iota(jnp.int32, (CY, CX), 1)


def rows():
    return lax.broadcasted_iota(jnp.int32, (CY, CX), 0)


def pack_kernel(owner_far, heat_far, voxel_far, out, owner, heat, voxel, wide, high, low, inverse, sems):
    copies = [
        pltpu.make_async_copy(far, near, sems.at[i])
        for i, (far, near) in enumerate(
            ((owner_far, owner), (heat_far, heat), (voxel_far, voxel))
        )
    ]
    for copy in copies:
        copy.start()
    blocks = owner.shape[0]
    devices = out.shape[0]

    def clear(i, carry):
        inverse[i] = blocks
        return carry

    lax.fori_loop(0, devices * CAP, clear, 0, unroll=16)
    copies[0].wait()

    def place(b, carry):
        base = owner[b] * CAP
        base = base + jnp.where(inverse[base] != blocks, 1, 0)
        inverse[base] = b
        return carry

    lax.fori_loop(0, blocks, place, 0, unroll=8)
    copies[1].wait()
    copies[2].wait()

    def widen(m, carry):
        wide[m, 0:blocks, :] = heat[m].astype(F32)
        wide[m, blocks:, :] = jnp.zeros((8, CX), F32)
        return carry

    lax.fori_loop(0, M, widen, 0)
    cells = voxel[...]
    high[0:blocks, :] = (cells >> 7).astype(F32)
    high[blocks:, :] = jnp.zeros((8, CX), F32)
    low[0:blocks, :] = (cells & 127).astype(F32)
    low[blocks:, :] = jnp.zeros((8, CX), F32)
    row = rows()

    def emit(d, carry):
        first = inverse[d * CAP]
        second = inverse[d * CAP + 1]
        index = jnp.where(
            row == 0,
            high[pl.ds(first, 1), :],
            jnp.where(
                row == 1,
                high[pl.ds(second, 1), :],
                jnp.where(
                    row == 2,
                    low[pl.ds(first, 1), :],
                    jnp.where(row == 3, low[pl.ds(second, 1), :], 0.0),
                ),
            ),
        )
        chunk = jnp.concatenate(
            [
                wide[:, pl.ds(first, 1), :].reshape(M, CX),
                wide[:, pl.ds(second, 1), :].reshape(M, CX),
                index,
            ],
            axis=0,
        )
        out[d] = chunk.astype(BF16)
        return carry

    lax.fori_loop(0, devices, emit, 0, unroll=4)


def pack(owner, heat, voxel, devices):
    blocks = owner.shape[0]
    return pl.pallas_call(
        pack_kernel,
        out_shape=jax.ShapeDtypeStruct((devices, ROWS, CX), BF16),
        in_specs=[pl.BlockSpec(memory_space=pl.ANY)] * 3,
        out_specs=vspec(),
        scratch_shapes=[
            pltpu.SMEM((blocks,), jnp.int32),
            VM((M, blocks, CX), BF16),
            VM((blocks, CX), jnp.int32),
            VM((M, blocks + 8, CX), F32),
            VM((blocks + 8, CX), F32),
            VM((blocks + 8, CX), F32),
            pltpu.SMEM((devices * CAP,), jnp.int32),
            pltpu.SemaphoreType.DMA((3,)),
        ],
        compiler_params=params(),
        name="pack",
    )(owner, heat, voxel)


HALO = 6
YS = CY + 2 * HALO
XT = CX // 8 + 2
ZG = NZ // 2
TOLERANCE = 1e-6
OWN = jax.ShapeDtypeStruct((2, CY, XT - 2, 8, CX), F32)
WIDE = jax.ShapeDtypeStruct((2, YS, XT, 8, CX), F32)
EDGE = 2 * HALO * (XT - 2)
SIDE = 2 * YS


def relayout_kernel(state, own, to_high, to_low):
    for zi in range(2):
        for y in range(CY):
            parts = [
                state[m0 : m0 + 8, 2 * group + zi, y, :] for group in range(ZG) for m0 in (0, 8)
            ]
            turned = (0.5 * jnp.concatenate(parts, axis=0)).T.reshape(XT - 2, 8, CX)
            own[zi, y] = turned
            if y >= CY - HALO:
                at = (zi * HALO + y - (CY - HALO)) * (XT - 2)
                to_high[at : at + XT - 2] = turned
            if y < HALO:
                at = (zi * HALO + y) * (XT - 2)
                to_low[at : at + XT - 2] = turned


def relayout(state):
    edge = jax.ShapeDtypeStruct((EDGE, 8, CX), F32)
    return pl.pallas_call(
        relayout_kernel,
        out_shape=[OWN, edge, edge],
        in_specs=[vspec()],
        out_specs=[vspec()] * 3,
        compiler_params=params(),
        name="relayout",
    )(state)


def side_kernel(own, low, high, heat_low, heat_own, heat_high, to_left, to_right):
    for out, t in ((to_left, 0), (to_right, XT - 3)):
        for zi in range(2):
            for y in range(YS):
                if y < HALO:
                    part = low[(zi * HALO + y) * (XT - 2) + t]
                elif y < HALO + CY:
                    part = own[zi, y - HALO, t]
                else:
                    part = high[(zi * HALO + y - HALO - CY) * (XT - 2) + t]
                out[zi * YS + y] = part
        for g, heat in enumerate((heat_low, heat_own, heat_high)):
            for zi in range(2):
                out[SIDE + 2 * g + zi] = heat[zi, 8 * t : 8 * t + 8, :]


def sides(own, low, high, heat_low, heat_own, heat_high):
    shape = jax.ShapeDtypeStruct((SIDE + 6, 8, CX), F32)
    return pl.pallas_call(
        side_kernel,
        out_shape=[shape, shape],
        in_specs=[vspec()] * 6,
        out_specs=[vspec()] * 2,
        compiler_params=params(),
        name="sides",
    )(own, low, high, heat_low, heat_own, heat_high)


def strip_kernel(own, left, right, out):
    def turn(tile):
        return (0.5 * tile[...].reshape(CX, CX)).T

    out[0] = turn(left)[CX - 8 :, :]
    out[1 : XT - 1] = turn(own).reshape(XT - 2, 8, CX)
    out[XT - 1] = turn(right)[0:8, :]


def strip(own, left, right):
    return pl.pallas_call(
        strip_kernel,
        out_shape=jax.ShapeDtypeStruct((XT, 8, CX), F32),
        in_specs=[vspec()] * 3,
        out_specs=vspec(),
        compiler_params=params(),
        name="strip",
    )(own, left, right)


def coef_kernel(own, low, high, out):
    source = lax.broadcasted_iota(jnp.int32, (CX, CX), 0)
    target = lax.broadcasted_iota(jnp.int32, (CX, CX), 1)
    strips = [part[...].reshape(XT * 8, CX) for part in (low, own, high)]

    def put(g, y0, yy):
        for zi in range(2):
            wanted = (2 * (target >> 4) + zi) * CY + y0
            hot = jnp.where(source == wanted, 1.0, 0.0).astype(F32)
            part = jnp.dot(
                strips[g], hot, precision=lax.Precision.HIGHEST, preferred_element_type=F32
            )
            out[zi, yy] = part.reshape(XT, 8, CX)

    for y in range(HALO):
        put(0, y + CY - HALO, y)
    for y in range(CY):
        put(1, y, y + HALO)
    for y in range(HALO):
        put(2, y, y + HALO + CY)


def coefs(own, low, high):
    return pl.pallas_call(
        coef_kernel,
        out_shape=WIDE,
        in_specs=[vspec()] * 3,
        out_specs=vspec(),
        compiler_params=params(),
        name="coefs",
    )(own, low, high)


def deposit_kernel(incoming, out, total):
    sources = incoming.shape[0]
    group = 4
    place = lax.broadcasted_iota(jnp.int32, (CX, CX), 0).astype(F32).astype(BF16)
    zero = jnp.zeros((M, CX), BF16)
    total[...] = jnp.zeros_like(total)

    def one(g, carry):
        left = []
        right = []
        for s in range(group):
            source = g * group + s
            index = incoming[source, 32:40, :].astype(F32)
            for slot in range(CAP):
                heat = incoming[source, slot * M : (slot + 1) * M, :]
                layer = jnp.broadcast_to(index[slot : slot + 1, :], (M, CX)).astype(BF16)
                cell = jnp.broadcast_to(index[2 + slot : 3 + slot, :], (CX, CX)).astype(BF16)
                left.append(
                    jnp.concatenate(
                        [jnp.where(layer == h, heat, zero) for h in range(2 * CY)], axis=0
                    )
                )
                right.append(jnp.where(place == cell, 1.0, 0.0).astype(BF16))
        total[...] += lax.dot_general(
            jnp.concatenate(left, axis=1),
            jnp.concatenate(right, axis=1),
            NT,
            preferred_element_type=F32,
        )
        return carry

    lax.fori_loop(0, sources // group, one, 0)
    for zi in range(2):
        out[zi] = (0.5 * total[zi * CX : (zi + 1) * CX, :]).T


def deposit(incoming):
    return pl.pallas_call(
        deposit_kernel,
        out_shape=jax.ShapeDtypeStruct((2, CX, CX), F32),
        in_specs=[vspec()],
        out_specs=vspec(),
        scratch_shapes=[VM((2 * CY * M, CX), F32)],
        compiler_params=params(),
        name="deposit",
    )(incoming)


def columns_peak(value):
    for shift in (4, 2, 1):
        value = jnp.maximum(value, pltpu.roll(value, shift, axis=0))
    return value


def whole_peak(value):
    return jnp.broadcast_to(jnp.max(value, axis=(0, 1), keepdims=True), (8, CX))


def step_of(peak):
    return SHARE / (12.0 * peak + COOL)


def conductance(field, coef, zi, y, t):
    u = field[zi, y, t]
    c = coef[zi, y, t]
    return u, c + c * (u * u)


def own_row(y):
    return jnp.where((y >= HALO) & (y < HALO + CY), 1.0, 0.0)


def masks(inside, y):
    kept = jnp.where(y < HALO, inside[2], jnp.where(y >= HALO + CY, inside[3], 1.0))
    return [kept * inside[0]] + [kept] * (XT - 2) + [kept * inside[1]]


def sweep(field, coef, above, below_h, first, end, emit, carry):
    lane = lanes()
    row = rows()
    last_row = row == 7
    first_row = row == 0
    inner_lane = lane < CX - M
    cooling = jnp.where(lane < M, COOL, 0.0)

    for zi in range(2):
        for t in range(XT):
            u, h = conductance(field, coef, zi, first - 1, t)
            v, g = conductance(field, coef, zi, first, t)
            above[zi, t] = (h + g) * (v - u)
            below_h[zi, t] = g

    def line(y, state):
        def load(t):
            us = [field[zi, y, t] for zi in range(2)]
            hs = [below_h[zi, t] for zi in range(2)]
            return (
                us,
                hs,
                [pltpu.roll(a, 7, axis=0) for a in us],
                [pltpu.roll(a, 7, axis=0) for a in hs],
            )

        us, hs, ru, rh = load(0)
        carried = [jnp.zeros((8, CX), F32)] * 2
        for t in range(XT):
            if t < XT - 1:
                after = load(t + 1)
                next_u = [jnp.where(last_row, after[2][z], ru[z]) for z in range(2)]
                next_h = [jnp.where(last_row, after[3][z], rh[z]) for z in range(2)]
            else:
                next_u = [jnp.where(last_row, us[z], ru[z]) for z in range(2)]
                next_h = rh
            change = []
            for zi in range(2):
                u, h = us[zi], hs[zi]
                along = (h + next_h[zi]) * (next_u[zi] - u)
                turned = pltpu.roll(along, 1, axis=0)
                total = along - jnp.where(first_row, carried[zi], turned)
                carried[zi] = turned
                v, g = conductance(field, coef, zi, y + 1, t)
                across = (h + g) * (v - u)
                total = total + (across - above[zi, t])
                above[zi, t] = across
                below_h[zi, t] = g
                change.append(total)
            within = (hs[0] + hs[1]) * (us[1] - us[0])
            between = (hs[1] + pltpu.roll(hs[0], CX - M, axis=1)) * (
                pltpu.roll(us[0], CX - M, axis=1) - us[1]
            )
            between = jnp.where(inner_lane, between, 0.0)
            change[0] = change[0] + (within - pltpu.roll(between, M, axis=1)) - cooling * us[0]
            change[1] = change[1] + (between - within)
            state = emit(y, t, us, change, state)
            if t < XT - 1:
                us, hs, ru, rh = after
        return state

    return lax.fori_loop(first, end, line, carry)


def advance(field, coef, above, below_h, inside, step, first, end, put):
    def emit(y, t, us, change, peak):
        part = masks(inside, y)[t] * step
        own = own_row(y)
        for zi in range(2):
            value = us[zi] + part * change[zi]
            put(zi, y, t, value)
            if 0 < t < XT - 1:
                c = coef[zi, y, t]
                peak = jnp.maximum(peak, own * (c + c * (value * value)))
        return peak

    return sweep(field, coef, above, below_h, first, end, emit, jnp.zeros((8, CX), F32))


def propose(field, coef, above, below_h, inside, guess, first, end, changes, peak, late, out):
    def emit(y, t, us, change, best):
        part = masks(inside, y)[t]
        own = own_row(y)
        for zi in range(2):
            moved = change[zi] * part
            changes[zi, y, t] = moved
            if 0 < t < XT - 1:
                c = coef[zi, y, t]
                value = us[zi] + guess * moved
                rank = own * (c + c * (value * value))
                better = rank > best[0]
                best = tuple(
                    jnp.where(better, new, old)
                    for new, old in zip((rank, us[zi], moved, c), best)
                )
        return best

    best = sweep(
        field, coef, above, below_h, first, end, emit, (jnp.zeros((8, CX), F32),) * 4
    )
    for shift in (4, 2, 1):
        other = tuple(pltpu.roll(part, shift, axis=0) for part in best)
        better = other[0] > best[0]
        best = tuple(jnp.where(better, new, old) for new, old in zip(other, best))
    row = rows()
    head = jnp.where(lanes() < CX // 2, whole_peak(peak), whole_peak(late))
    chunk = jnp.where(
        row == 0, head, jnp.where(row == 1, best[1], jnp.where(row == 2, best[2], best[3]))
    )[0:4]
    for d in range(out.shape[0]):
        out[d] = chunk


def agree(parts):
    lane = lanes()
    now = jnp.zeros((8, CX), F32)
    for d in range(0, parts.shape[0], 8):
        now = jnp.maximum(now, parts[d : d + 8, 0, :])
    late = whole_peak(jnp.where(lane < CX // 2, 0.0, now))
    now = whole_peak(jnp.where(lane < CX // 2, now, 0.0))
    step = step_of(now)
    then = jnp.zeros((8, CX), F32)
    for d in range(0, parts.shape[0], 8):
        value = parts[d : d + 8, 1, :] + step * parts[d : d + 8, 2, :]
        c = parts[d : d + 8, 3, :]
        then = jnp.maximum(then, c + c * (value * value))
    return now, whole_peak(then), late


def differs(late, used):
    return jnp.where(late > used * (1.0 + TOLERANCE), 1.0, 0.0)


def heated_kernel(
    inside, own, low, high, left, right,
    heat_low, heat_own, heat_high,
    coef, out, changes, parts, above, below_h,
):
    top = lanes() < M
    peak = jnp.zeros((8, CX), F32)

    def row(g, heat, tile_of, y0, yy, peak):
        shift = (CX - 16 * y0) % CX
        for zi in range(2):
            for t in range(XT):
                if t == 0:
                    prior, add = left[zi * YS + yy], left[SIDE + 2 * g + zi]
                elif t == XT - 1:
                    prior, add = right[zi * YS + yy], right[SIDE + 2 * g + zi]
                else:
                    prior, add = tile_of(zi, t - 1), heat[zi, 8 * t - 8 : 8 * t, :]
                if shift:
                    add = pltpu.roll(add, shift, axis=1)
                value = prior + jnp.where(top, add, 0.0)
                out[zi, yy, t] = value
                if g == 1 and 0 < t < XT - 1:
                    c = coef[zi, yy, t]
                    peak = jnp.maximum(peak, c + c * (value * value))
        return peak

    def edge(ref, y):
        return lambda zi, t: ref[(zi * HALO + y) * (XT - 2) + t]

    for y in range(HALO):
        row(0, heat_low, edge(low, y), y + CY - HALO, y, peak)
    for y in range(CY):
        peak = row(1, heat_own, lambda zi, t: own[zi, y, t], y, y + HALO, peak)
    for y in range(HALO):
        row(2, heat_high, edge(high, y), y, y + HALO + CY, peak)
    guess = step_of(whole_peak(peak))
    zero = jnp.zeros((8, CX), F32)
    propose(out, coef, above, below_h, inside, guess, 1, YS - 1, changes, peak, zero, parts)


ROW = (2, XT, 8, CX)


def smem():
    return pl.BlockSpec(memory_space=pltpu.SMEM)


def heated(inside, prior, halos, heat, coef, devices):
    operands = [inside, *prior, *halos, *heat, coef]
    return pl.pallas_call(
        heated_kernel,
        out_shape=[WIDE, WIDE, jax.ShapeDtypeStruct((devices, 4, CX), F32)],
        in_specs=[smem()] + [vspec()] * (len(operands) - 1),
        out_specs=[vspec()] * 3,
        scratch_shapes=[VM(ROW, F32), VM(ROW, F32)],
        compiler_params=params(),
        name="heated",
    )(*operands)


def first_of_pair(field, changes, coef, step, first, end, out):
    def line(y, peak):
        own = own_row(y)
        top = jnp.zeros((8, CX), F32)
        for zi in range(2):
            for t in range(XT):
                value = field[zi, y, t] + step * changes[zi, y, t]
                out[zi, y, t] = value
                if 0 < t < XT - 1:
                    c = coef[zi, y, t]
                    top = jnp.maximum(top, c + c * (value * value))
        return jnp.maximum(peak, own * top)

    return lax.fori_loop(first, end, line, jnp.zeros((8, CX), F32))


def pair_kernel(
    number, inside, field, changes, coef, parts, status,
    out, out_changes, out_parts, out_status, middle, above, below_h,
):
    now, then, late = agree(parts)
    bad = status[1:2, :]
    if number:
        bad = jnp.maximum(bad, differs(late[0:1], status[0:1, :]))
    out_status[...] = jnp.where(rows() == 0, then, bad)
    seen = first_of_pair(field, changes, coef, step_of(now), number + 1, YS - 1 - number, middle)

    def put(zi, y, t, value):
        out[zi, y, t] = value

    step = step_of(then)
    peak = advance(
        middle, coef, above, below_h, inside, step, number + 2, YS - 2 - number, put
    )
    guess = jnp.minimum(step_of(whole_peak(peak)), 1.2 * step)
    propose(
        out, coef, above, below_h, inside, guess, number + 3, YS - 3 - number,
        out_changes, peak, seen, out_parts,
    )


STATUS = jax.ShapeDtypeStruct((8, CX), F32)


def pair(number, inside, field, changes, coef, parts, status):
    operands = [inside, field, changes, coef, parts, status]
    return pl.pallas_call(
        functools.partial(pair_kernel, number),
        out_shape=[WIDE, WIDE, jax.ShapeDtypeStruct(parts.shape, F32), STATUS],
        in_specs=[smem()] + [vspec()] * 5,
        out_specs=[vspec()] * 4,
        scratch_shapes=[VM(WIDE.shape, F32), VM(ROW, F32), VM(ROW, F32)],
        compiler_params=params(),
        name=f"pair_{number}",
    )(*operands)


def pixel_grams(field, weight, data, flat, late, sums):
    grams = jnp.zeros((M, 2 * M), F32)
    for y in range(CY):
        seen = 2.0 * field[0, y].reshape(CX, CX).T[0:M, :]
        for m in range(M):
            flat[m : m + 1, :] = data[m, y : y + 1, :]
        w = weight[y : y + 1, :]
        spread = seen - jnp.mean(seen, axis=0, keepdims=True)
        both = jnp.concatenate([spread * w, flat[...] - seen * w], axis=0)
        grams = grams + lax.dot_general(
            spread, both, NT, precision=lax.Precision.HIGHEST, preferred_element_type=F32
        )
    grams = jnp.concatenate([grams, jnp.zeros((M, CX - 2 * M), F32)], axis=1)
    two = grams[0:8] + pltpu.roll(grams[8:16], 32, axis=1)
    quad = two + pltpu.roll(pltpu.roll(two, 64, axis=1), 4, axis=0)
    quad = jnp.where((rows() == 0) & (lanes() == 1), whole_peak(late), quad)[0:4]
    for d in range(sums.shape[0]):
        sums[d] = quad


def last_kernel(
    inside, field, changes, coef, parts, status, weight, data,
    out, sums, out_status, middle, above, below_h, flat,
):
    number = SUBSTEPS - 2
    now, then, late = agree(parts)
    bad = jnp.maximum(status[1:2, :], differs(late[0:1], status[0:1, :]))
    out_status[...] = jnp.where(rows() == 0, then, bad)
    seen = first_of_pair(field, changes, coef, step_of(now), number + 1, YS - 1 - number, middle)

    def put(zi, y, t, value):
        if 0 < t < XT - 1:
            out[zi, y - HALO, t - 1] = value

    advance(middle, coef, above, below_h, inside, step_of(then), HALO, HALO + CY, put)
    pixel_grams(out, weight, data, flat, seen, sums)


def last(inside, field, changes, coef, parts, status, pixels):
    operands = [inside, field, changes, coef, parts, status, *pixels]
    return pl.pallas_call(
        last_kernel,
        out_shape=[OWN, jax.ShapeDtypeStruct(parts.shape, F32), STATUS],
        in_specs=[smem()] + [vspec()] * (len(operands) - 1),
        out_specs=[vspec()] * 3,
        scratch_shapes=[VM(WIDE.shape, F32), VM(ROW, F32), VM(ROW, F32), VM((M, CX), F32)],
        compiler_params=params(),
        name="last_pair",
    )(*operands)


def single_kernel(number, inside, field, coef, peaks, *rest):
    final = number == SUBSTEPS - 1
    if final:
        weight, data, out, sums, above, below_h, flat = rest
    else:
        out, out_peaks, above, below_h = rest
    peak = peaks[0]
    for d in range(1, peaks.shape[0]):
        peak = jnp.maximum(peak, peaks[d])
    step = step_of(whole_peak(peak))

    def put(zi, y, t, value):
        if not final:
            out[zi, y, t] = value
        elif 0 < t < XT - 1:
            out[zi, y - HALO, t - 1] = value

    peak = advance(field, coef, above, below_h, inside, step, number + 1, YS - 1 - number, put)
    if final:
        pixel_grams(out, weight, data, flat, jnp.zeros((8, CX), F32), sums)
    else:
        out_peaks[...] = jnp.broadcast_to(columns_peak(peak)[0:1].reshape(1, 1, CX), out_peaks.shape)


def single(number, inside, field, coef, peaks, pixels):
    devices = peaks.shape[0]
    operands = [inside, field, coef, peaks]
    scratch = [VM(ROW, F32), VM(ROW, F32)]
    if number == SUBSTEPS - 1:
        operands += list(pixels)
        out_shape = [OWN, jax.ShapeDtypeStruct((devices, 4, CX), F32)]
        scratch += [VM((M, CX), F32)]
    else:
        out_shape = [WIDE, jax.ShapeDtypeStruct((devices, 1, CX), F32)]
    return pl.pallas_call(
        functools.partial(single_kernel, number),
        out_shape=out_shape,
        in_specs=[smem()] + [vspec()] * (len(operands) - 1),
        out_specs=[vspec()] * 2,
        scratch_shapes=scratch,
        compiler_params=params(),
        name=f"single_{number}",
    )(*operands)


def pixel_kernel(cell, observed, variance, noise, weight, data):
    pixels = cell.shape[1]
    place = cell[...]
    var = variance[...]
    inverse = 1.0 / var
    values = (observed[...] + noise[...] * jnp.sqrt(var)) * inverse
    stack = jnp.concatenate([values, jnp.broadcast_to(inverse, (8, pixels))], axis=0)
    width = place >> 7
    hot = jnp.where(
        lax.broadcasted_iota(jnp.int32, (CX, pixels), 0) == (place & 127), 1.0, 0.0
    ).astype(F32)
    for y in range(CY):
        part = lax.dot_general(
            jnp.where(width == y, stack, 0.0),
            hot,
            NT,
            precision=lax.Precision.HIGHEST,
            preferred_element_type=F32,
        )
        weight[y : y + 1, :] = part[M : M + 1, :]
        for m in range(M):
            data[m, y : y + 1, :] = part[m : m + 1, :]


def pixel_sums(cell, observed, variance, noise):
    return pl.pallas_call(
        pixel_kernel,
        out_shape=[
            jax.ShapeDtypeStruct((CY, CX), F32),
            jax.ShapeDtypeStruct((M, CY, CX), F32),
        ],
        in_specs=[vspec()] * 4,
        out_specs=[vspec()] * 2,
        compiler_params=params(),
        name="pixels",
    )(cell, observed, variance, noise)


def update_kernel(sums, field, status, out, flag):
    quad = sums[0]
    late = quad
    for d in range(1, sums.shape[0]):
        quad = quad + sums[d]
        late = jnp.maximum(late, sums[d])
    late = jnp.broadcast_to(late[0:1, 1:2], (1, CX))
    bad = jnp.maximum(status[1:2, :], differs(late, status[0:1, :]))
    flag[0] = jnp.where(jnp.max(bad) > 0.0, 1, 0)
    row = rows()
    quad = jnp.concatenate([quad, jnp.zeros_like(quad)], axis=0)
    pair = jnp.where(row < 4, quad, pltpu.roll(pltpu.roll(quad, 64, axis=1), 4, axis=0))
    system = jnp.concatenate([pair, pltpu.roll(pair, CX - 32, axis=1)], axis=0)
    tall = lax.broadcasted_iota(jnp.int32, (M, CX), 0)
    wide = lax.broadcasted_iota(jnp.int32, (M, CX), 1)
    system = jnp.where(tall == wide, system + (M - 1.0), system)
    mirror = jnp.broadcast_to(system[1:2, 0:1], (M, CX))
    system = jnp.where((tall == 0) & (wide == 1), mirror, system)
    for i in range(M):
        pivot = system[i : i + 1, :]
        pivot = pivot / pivot[:, i : i + 1]
        factor = jnp.where(tall == i, 0.0, jnp.broadcast_to(system[:, i : i + 1], (M, CX)))
        system = jnp.where(tall == i, pivot, system - factor * pivot)
    mixing = system - jnp.mean(system, axis=0, keepdims=True)
    mixing = pltpu.roll(mixing, CX - M, axis=1)
    mixing = jnp.where(wide < M, mixing + jnp.where(tall == wide, 1.0, 0.0), 0.0)
    for shift in (16, 32, 64):
        mixing = mixing + pltpu.roll(mixing, shift, axis=1)
    mixing = jnp.concatenate([mixing] * ZG, axis=0)
    tall = lax.broadcasted_iota(jnp.int32, (CX, CX), 0)
    wide = lax.broadcasted_iota(jnp.int32, (CX, CX), 1)
    mixing = jnp.where((tall >> 4) == (wide >> 4), 2.0 * mixing, 0.0).T
    for zi in range(2):
        for y in range(CY):
            part = lax.dot_general(
                mixing,
                field[zi, y].reshape(CX, CX),
                NT,
                precision=lax.Precision.HIGHEST,
                preferred_element_type=F32,
            )
            for group in range(ZG):
                for m0 in (0, 8):
                    at = group * M + m0
                    out[m0 : m0 + 8, 2 * group + zi, y, :] = part[at : at + 8, :]


def update(sums, field, status):
    return pl.pallas_call(
        update_kernel,
        out_shape=[
            jax.ShapeDtypeStruct((M, NZ, CY, CX), F32),
            jax.ShapeDtypeStruct((1,), jnp.int32),
        ],
        in_specs=[vspec()] * 3,
        out_specs=[vspec(), smem()],
        compiler_params=params(),
        name="update",
    )(sums, field, status)


def exchange(parts):
    return lax.all_to_all(parts, BOTH, split_axis=0, concat_axis=0, tiled=True)


def move(part, axis, ahead):
    count = lax.axis_size(axis)
    pairs = [(i, i + 1) if ahead else (i + 1, i) for i in range(count - 1)]
    return lax.ppermute(part, axis, pairs)


def on_device(
    state_prior,
    conductivity,
    heat_input,
    owner_tile,
    voxel_list,
    pixel_cell,
    observed,
    pixel_variance,
    pixel_noise,
):
    devices = lax.axis_size("gx") * lax.axis_size("gy")
    pixels = pixel_cell.shape[0]
    outgoing = pack(owner_tile.reshape(-1), heat_input, voxel_list, devices)
    incoming = exchange(outgoing)

    gx, gy = lax.axis_index("gx"), lax.axis_index("gy")
    inside = jnp.stack(
        [gx > 0, gx < lax.axis_size("gx") - 1, gy > 0, gy < lax.axis_size("gy") - 1]
    ).astype(F32)
    left_c, right_c = move(conductivity, "gx", True), move(conductivity, "gx", False)
    strips = strip(conductivity, left_c, right_c)
    coef = coefs(strips, move(strips, "gy", True), move(strips, "gy", False))
    own, to_high, to_low = relayout(state_prior)
    low, high = move(to_high, "gy", True), move(to_low, "gy", False)
    seen = pixel_sums(
        pixel_cell.reshape(1, pixels),
        observed.reshape(1, pixels),
        pixel_variance.reshape(1, pixels),
        pixel_noise,
    )
    incoming, coef, own, inside, *seen = lax.optimization_barrier(
        (incoming, coef, own, inside, *seen)
    )
    heat = deposit(incoming)
    heat_low, heat_high = move(heat, "gy", True), move(heat, "gy", False)
    to_left, to_right = sides(own, low, high, heat_low, heat, heat_high)
    left, right = move(to_right, "gx", True), move(to_left, "gx", False)
    start, changes, parts = heated(
        inside, (own, low, high), (left, right), (heat_low, heat, heat_high), coef, devices
    )
    field, status = start, jnp.zeros((8, CX), F32)
    for number in range(0, SUBSTEPS - 2, 2):
        field, changes, parts, status = pair(
            number, inside, field, changes, coef, exchange(parts), status
        )
    field, sums, status = last(inside, field, changes, coef, exchange(parts), status, seen)
    result, flag = update(exchange(sums), field, status)

    def again():
        peak = coef * (1.0 + start * start)
        peak = jnp.max(peak[:, HALO : HALO + CY, 1 : XT - 1])
        peaks = jnp.full((devices, 1, CX), peak)
        field = start
        for number in range(SUBSTEPS):
            field, peaks = single(number, inside, field, coef, exchange(peaks), seen)
        return update(exchange(peaks), field, jnp.ones((8, CX), F32))[0]

    return lax.cond(flag[0] > 0, again, lambda: result)


def solution(mesh):
    in_specs = (
        P(None, None, "gy", "gx"),
        P(None, "gy", "gx"),
        P(None, BOTH, None),
        P(BOTH, None),
        P(BOTH, None),
        P(BOTH),
        P(BOTH),
        P(BOTH),
        P(None, BOTH),
    )
    out_specs = P(None, None, "gy", "gx")
    return jax.shard_map(
        on_device, mesh=mesh, in_specs=in_specs, out_specs=out_specs, check_vma=False
    )
```

```python
import functools

import jax
import jax.numpy as jnp
from jax import lax
from jax.experimental import pallas as pl
from jax.experimental.pallas import tpu as pltpu
from jax.sharding import PartitionSpec as P

SUBSTEPS = 6
CAP = 2
COOL = 0.1
SHARE = 0.9
F32 = jnp.float32
BF16 = jnp.bfloat16
VM = pltpu.VMEM
LIMIT = 24 * 1024 * 1024
NT = (((1,), (1,)), ((), ()))
BOTH = ("gx", "gy")

M, NZ, CY, CX = 16, 16, 8, 128
ROWS = 40


def vspec():
    return pl.BlockSpec(memory_space=pltpu.VMEM)


def params():
    return pltpu.CompilerParams(vmem_limit_bytes=LIMIT)


def lanes():
    return lax.broadcasted_iota(jnp.int32, (CY, CX), 1)


def rows():
    return lax.broadcasted_iota(jnp.int32, (CY, CX), 0)


def pack_kernel(owner_far, heat_far, voxel_far, out, owner, heat, voxel, wide, high, low, inverse, sems):
    copies = [
        pltpu.make_async_copy(far, near, sems.at[i])
        for i, (far, near) in enumerate(
            ((owner_far, owner), (heat_far, heat), (voxel_far, voxel))
        )
    ]
    for copy in copies:
        copy.start()
    blocks = owner.shape[0]
    devices = out.shape[0]

    def clear(i, carry):
        inverse[i] = blocks
        return carry

    lax.fori_loop(0, devices * CAP, clear, 0, unroll=16)
    copies[0].wait()

    def place(b, carry):
        base = owner[b] * CAP
        base = base + jnp.where(inverse[base] != blocks, 1, 0)
        inverse[base] = b
        return carry

    lax.fori_loop(0, blocks, place, 0, unroll=8)
    copies[1].wait()
    copies[2].wait()

    def widen(m, carry):
        wide[m, 0:blocks, :] = heat[m].astype(F32)
        wide[m, blocks:, :] = jnp.zeros((8, CX), F32)
        return carry

    lax.fori_loop(0, M, widen, 0)
    cells = voxel[...]
    high[0:blocks, :] = (cells >> 7).astype(F32)
    high[blocks:, :] = jnp.zeros((8, CX), F32)
    low[0:blocks, :] = (cells & 127).astype(F32)
    low[blocks:, :] = jnp.zeros((8, CX), F32)
    row = rows()

    def emit(d, carry):
        first = inverse[d * CAP]
        second = inverse[d * CAP + 1]
        index = jnp.where(
            row == 0,
            high[pl.ds(first, 1), :],
            jnp.where(
                row == 1,
                high[pl.ds(second, 1), :],
                jnp.where(
                    row == 2,
                    low[pl.ds(first, 1), :],
                    jnp.where(row == 3, low[pl.ds(second, 1), :], 0.0),
                ),
            ),
        )
        chunk = jnp.concatenate(
            [
                wide[:, pl.ds(first, 1), :].reshape(M, CX),
                wide[:, pl.ds(second, 1), :].reshape(M, CX),
                index,
            ],
            axis=0,
        )
        out[d] = chunk.astype(BF16)
        return carry

    lax.fori_loop(0, devices, emit, 0, unroll=4)


def pack(owner, heat, voxel, devices):
    blocks = owner.shape[0]
    return pl.pallas_call(
        pack_kernel,
        out_shape=jax.ShapeDtypeStruct((devices, ROWS, CX), BF16),
        in_specs=[pl.BlockSpec(memory_space=pl.ANY)] * 3,
        out_specs=vspec(),
        scratch_shapes=[
            pltpu.SMEM((blocks,), jnp.int32),
            VM((M, blocks, CX), BF16),
            VM((blocks, CX), jnp.int32),
            VM((M, blocks + 8, CX), F32),
            VM((blocks + 8, CX), F32),
            VM((blocks + 8, CX), F32),
            pltpu.SMEM((devices * CAP,), jnp.int32),
            pltpu.SemaphoreType.DMA((3,)),
        ],
        compiler_params=params(),
        name="pack",
    )(owner, heat, voxel)


HALO = 6
YS = CY + 2 * HALO
XT = CX // 8 + 2
ZG = NZ // 2
TOLERANCE = 1e-6
OWN = jax.ShapeDtypeStruct((2, CY, XT - 2, 8, CX), F32)
WIDE = jax.ShapeDtypeStruct((2, YS, XT, 8, CX), F32)
EDGE = 2 * HALO * (XT - 2)
SIDE = 2 * YS


def relayout_kernel(state, own, to_high, to_low, to_left, to_right):
    for zi in range(2):
        for y in range(CY):
            parts = [
                state[m0 : m0 + 8, 2 * group + zi, y, :] for group in range(ZG) for m0 in (0, 8)
            ]
            turned = (0.5 * jnp.concatenate(parts, axis=0)).T.reshape(XT - 2, 8, CX)
            own[zi, y] = turned
            to_left[zi * CY + y] = turned[0]
            to_right[zi * CY + y] = turned[XT - 3]
            if y >= CY - HALO:
                at = (zi * HALO + y - (CY - HALO)) * (XT - 2)
                to_high[at : at + XT - 2] = turned
            if y < HALO:
                at = (zi * HALO + y) * (XT - 2)
                to_low[at : at + XT - 2] = turned


def relayout(state):
    edge = jax.ShapeDtypeStruct((EDGE, 8, CX), F32)
    side = jax.ShapeDtypeStruct((2 * CY, 8, CX), F32)
    return pl.pallas_call(
        relayout_kernel,
        out_shape=[OWN, edge, edge, side, side],
        in_specs=[vspec()],
        out_specs=[vspec()] * 5,
        compiler_params=params(),
        name="relayout",
    )(state)


def strip_kernel(own, left, right, out):
    def turn(tile):
        return (0.5 * tile[...].reshape(CX, CX)).T

    out[0] = turn(left)[CX - 8 :, :]
    out[1 : XT - 1] = turn(own).reshape(XT - 2, 8, CX)
    out[XT - 1] = turn(right)[0:8, :]


def strip(own, left, right):
    return pl.pallas_call(
        strip_kernel,
        out_shape=jax.ShapeDtypeStruct((XT, 8, CX), F32),
        in_specs=[vspec()] * 3,
        out_specs=vspec(),
        compiler_params=params(),
        name="strip",
    )(own, left, right)


def coef_kernel(own, low, high, out):
    source = lax.broadcasted_iota(jnp.int32, (CX, CX), 0)
    target = lax.broadcasted_iota(jnp.int32, (CX, CX), 1)
    strips = [part[...].reshape(XT * 8, CX) for part in (low, own, high)]

    def put(g, y0, yy):
        for zi in range(2):
            wanted = (2 * (target >> 4) + zi) * CY + y0
            hot = jnp.where(source == wanted, 1.0, 0.0).astype(F32)
            part = jnp.dot(
                strips[g], hot, precision=lax.Precision.HIGHEST, preferred_element_type=F32
            )
            out[zi, yy] = part.reshape(XT, 8, CX)

    for y in range(HALO):
        put(0, y + CY - HALO, y)
    for y in range(CY):
        put(1, y, y + HALO)
    for y in range(HALO):
        put(2, y, y + HALO + CY)


def coefs(own, low, high):
    return pl.pallas_call(
        coef_kernel,
        out_shape=WIDE,
        in_specs=[vspec()] * 3,
        out_specs=vspec(),
        compiler_params=params(),
        name="coefs",
    )(own, low, high)


def deposit_kernel(incoming, out, to_left, to_right, total):
    sources = incoming.shape[0]
    group = 4
    place = lax.broadcasted_iota(jnp.int32, (CX, CX), 0).astype(F32).astype(BF16)
    zero = jnp.zeros((M, CX), BF16)
    total[...] = jnp.zeros_like(total)

    def one(g, carry):
        left = []
        right = []
        for s in range(group):
            source = g * group + s
            index = incoming[source, 32:40, :].astype(F32)
            for slot in range(CAP):
                heat = incoming[source, slot * M : (slot + 1) * M, :]
                layer = jnp.broadcast_to(index[slot : slot + 1, :], (M, CX)).astype(BF16)
                cell = jnp.broadcast_to(index[2 + slot : 3 + slot, :], (CX, CX)).astype(BF16)
                left.append(
                    jnp.concatenate(
                        [jnp.where(layer == h, heat, zero) for h in range(2 * CY)], axis=0
                    )
                )
                right.append(jnp.where(place == cell, 1.0, 0.0).astype(BF16))
        total[...] += lax.dot_general(
            jnp.concatenate(left, axis=1),
            jnp.concatenate(right, axis=1),
            NT,
            preferred_element_type=F32,
        )
        return carry

    lax.fori_loop(0, sources // group, one, 0)
    for zi in range(2):
        turned = (0.5 * total[zi * CX : (zi + 1) * CX, :]).T
        out[zi] = turned
        to_left[zi] = turned[0:8]
        to_right[zi] = turned[CX - 8 :]


def deposit(incoming):
    return pl.pallas_call(
        deposit_kernel,
        out_shape=[jax.ShapeDtypeStruct((2, rows_, CX), F32) for rows_ in (CX, 8, 8)],
        in_specs=[vspec()],
        out_specs=[vspec()] * 3,
        scratch_shapes=[VM((2 * CY * M, CX), F32)],
        compiler_params=params(),
        name="deposit",
    )(incoming)


def columns_peak(value):
    for shift in (4, 2, 1):
        value = jnp.maximum(value, pltpu.roll(value, shift, axis=0))
    return value


def whole_peak(value):
    return jnp.broadcast_to(jnp.max(value, axis=(0, 1), keepdims=True), (8, CX))


def step_of(peak):
    return SHARE / (12.0 * peak + COOL)


def conductance(field, coef, zi, y, t):
    u = field[zi, y, t]
    c = coef[zi, y, t]
    return u, c + c * (u * u)


def own_row(y):
    return jnp.where((y >= HALO) & (y < HALO + CY), 1.0, 0.0)


def masks(inside, y):
    kept = jnp.where(y < HALO, inside[2], jnp.where(y >= HALO + CY, inside[3], 1.0))
    return [kept * inside[0]] + [kept] * (XT - 2) + [kept * inside[1]]


def sweep(field, coef, above, below_h, first, end, emit, carry):
    lane = lanes()
    row = rows()
    last_row = row == 7
    first_row = row == 0
    inner_lane = lane < CX - M
    cooling = jnp.where(lane < M, COOL, 0.0)

    for zi in range(2):
        for t in range(XT):
            u, h = conductance(field, coef, zi, first - 1, t)
            v, g = conductance(field, coef, zi, first, t)
            above[zi, t] = (h + g) * (v - u)
            below_h[zi, t] = g

    def line(y, state):
        def load(t):
            us = [field[zi, y, t] for zi in range(2)]
            hs = [below_h[zi, t] for zi in range(2)]
            return (
                us,
                hs,
                [pltpu.roll(a, 7, axis=0) for a in us],
                [pltpu.roll(a, 7, axis=0) for a in hs],
            )

        us, hs, ru, rh = load(0)
        carried = [jnp.zeros((8, CX), F32)] * 2
        for t in range(XT):
            if t < XT - 1:
                after = load(t + 1)
                next_u = [jnp.where(last_row, after[2][z], ru[z]) for z in range(2)]
                next_h = [jnp.where(last_row, after[3][z], rh[z]) for z in range(2)]
            else:
                next_u = [jnp.where(last_row, us[z], ru[z]) for z in range(2)]
                next_h = rh
            change = []
            for zi in range(2):
                u, h = us[zi], hs[zi]
                along = (h + next_h[zi]) * (next_u[zi] - u)
                turned = pltpu.roll(along, 1, axis=0)
                total = along - jnp.where(first_row, carried[zi], turned)
                carried[zi] = turned
                v, g = conductance(field, coef, zi, y + 1, t)
                across = (h + g) * (v - u)
                total = total + (across - above[zi, t])
                above[zi, t] = across
                below_h[zi, t] = g
                change.append(total)
            within = (hs[0] + hs[1]) * (us[1] - us[0])
            between = (hs[1] + pltpu.roll(hs[0], CX - M, axis=1)) * (
                pltpu.roll(us[0], CX - M, axis=1) - us[1]
            )
            between = jnp.where(inner_lane, between, 0.0)
            change[0] = change[0] + (within - pltpu.roll(between, M, axis=1)) - cooling * us[0]
            change[1] = change[1] + (between - within)
            state = emit(y, t, us, change, state)
            if t < XT - 1:
                us, hs, ru, rh = after
        return state

    return lax.fori_loop(first, end, line, carry)


def advance(field, coef, above, below_h, inside, step, first, end, put):
    def emit(y, t, us, change, peak):
        part = masks(inside, y)[t] * step
        own = own_row(y)
        for zi in range(2):
            value = us[zi] + part * change[zi]
            put(zi, y, t, value)
            if 0 < t < XT - 1:
                c = coef[zi, y, t]
                peak = jnp.maximum(peak, own * (c + c * (value * value)))
        return peak

    return sweep(field, coef, above, below_h, first, end, emit, jnp.zeros((8, CX), F32))


def propose(field, coef, above, below_h, inside, guess, first, end, changes, peak, late, out):
    def emit(y, t, us, change, best):
        part = masks(inside, y)[t]
        own = own_row(y)
        for zi in range(2):
            moved = change[zi] * part
            if changes is not None:
                changes[zi, y, t] = moved
            if 0 < t < XT - 1:
                c = coef[zi, y, t]
                value = us[zi] + guess * moved
                rank = own * (c + c * (value * value))
                better = rank > best[0]
                best = tuple(
                    jnp.where(better, new, old)
                    for new, old in zip((rank, us[zi], moved, c), best)
                )
        return best

    best = sweep(
        field, coef, above, below_h, first, end, emit, (jnp.zeros((8, CX), F32),) * 4
    )
    for shift in (4, 2, 1):
        other = tuple(pltpu.roll(part, shift, axis=0) for part in best)
        better = other[0] > best[0]
        best = tuple(jnp.where(better, new, old) for new, old in zip(other, best))
    row = rows()
    head = jnp.where(lanes() < CX // 2, whole_peak(peak), whole_peak(late))
    chunk = jnp.where(
        row == 0, head, jnp.where(row == 1, best[1], jnp.where(row == 2, best[2], best[3]))
    )[0:4]
    for d in range(out.shape[0]):
        out[d] = chunk


def agree(parts):
    lane = lanes()
    now = jnp.zeros((8, CX), F32)
    for d in range(0, parts.shape[0], 8):
        now = jnp.maximum(now, parts[d : d + 8, 0, :])
    late = whole_peak(jnp.where(lane < CX // 2, 0.0, now))
    now = whole_peak(jnp.where(lane < CX // 2, now, 0.0))
    step = step_of(now)
    then = jnp.zeros((8, CX), F32)
    for d in range(0, parts.shape[0], 8):
        value = parts[d : d + 8, 1, :] + step * parts[d : d + 8, 2, :]
        c = parts[d : d + 8, 3, :]
        then = jnp.maximum(then, c + c * (value * value))
    return now, whole_peak(then), late


def differs(late, used):
    return jnp.where(late > used * (1.0 + TOLERANCE), 1.0, 0.0)


def heated_kernel(
    inside, own, low, high, left, right,
    heat_low, heat_own, heat_high, heat_left, heat_right,
    coef, out, parts, to_left, to_right, above, below_h,
):
    top = lanes() < M
    peak = jnp.zeros((8, CX), F32)

    def warm(prior, heat, y0):
        shift = (CX - 16 * y0) % CX
        if shift:
            heat = pltpu.roll(heat, shift, axis=1)
        return prior + jnp.where(top, heat, 0.0)

    def row(g, heat, tile_of, y0, yy, peak):
        for zi in range(2):
            for t in range(1, XT - 1):
                value = warm(tile_of(zi, t - 1), heat[zi, 8 * t - 8 : 8 * t, :], y0)
                out[zi, yy, t] = value
                if t == 1:
                    to_left[zi * YS + yy] = value
                if t == XT - 2:
                    to_right[zi * YS + yy] = value
                if g == 1:
                    c = coef[zi, yy, t]
                    peak = jnp.maximum(peak, c + c * (value * value))
            for t, ref, edge_heat in ((0, left, heat_left), (XT - 1, right, heat_right)):
                if g == 1:
                    out[zi, yy, t] = warm(ref[zi * CY + y0], edge_heat[zi], y0)
                else:
                    out[zi, yy, t] = jnp.zeros((8, CX), F32)
        return peak

    def edge(ref, y):
        return lambda zi, t: ref[(zi * HALO + y) * (XT - 2) + t]

    for y in range(HALO):
        row(0, heat_low, edge(low, y), y + CY - HALO, y, peak)
    for y in range(CY):
        peak = row(1, heat_own, lambda zi, t: own[zi, y, t], y, y + HALO, peak)
    for y in range(HALO):
        row(2, heat_high, edge(high, y), y, y + HALO + CY, peak)
    guess = step_of(whole_peak(peak))
    zero = jnp.zeros((8, CX), F32)
    propose(
        out, coef, above, below_h, inside, guess, HALO, HALO + CY, None, peak, zero, parts
    )


class Joined:
    def __init__(self, field, left, right):
        self.field, self.left, self.right = field, left, right

    def __getitem__(self, at):
        zi, y, t = at
        if t == 0:
            return self.left[zi * YS + y]
        if t == XT - 1:
            return self.right[zi * YS + y]
        return self.field[zi, y, t]


ROW = (2, XT, 8, CX)


def smem():
    return pl.BlockSpec(memory_space=pltpu.SMEM)


def heated(inside, prior, halos, heat, coef, devices):
    operands = [inside, *prior, *halos, *heat, coef]
    side = jax.ShapeDtypeStruct((SIDE, 8, CX), F32)
    return pl.pallas_call(
        heated_kernel,
        out_shape=[WIDE, jax.ShapeDtypeStruct((devices, 4, CX), F32), side, side],
        in_specs=[smem()] + [vspec()] * (len(operands) - 1),
        out_specs=[vspec()] * 4,
        scratch_shapes=[VM(ROW, F32), VM(ROW, F32)],
        compiler_params=params(),
        name="heated",
    )(*operands)


def first_of_pair(field, changes, coef, step, first, end, out):
    def line(y, peak):
        own = own_row(y)
        top = jnp.zeros((8, CX), F32)
        for zi in range(2):
            for t in range(XT):
                value = field[zi, y, t] + step * changes[zi, y, t]
                out[zi, y, t] = value
                if 0 < t < XT - 1:
                    c = coef[zi, y, t]
                    top = jnp.maximum(top, c + c * (value * value))
        return jnp.maximum(peak, own * top)

    return lax.fori_loop(first, end, line, jnp.zeros((8, CX), F32))


def first_pair_kernel(
    inside, field, left, right, coef, parts,
    out, out_changes, out_parts, out_status, middle, above, below_h,
):
    now, then, _ = agree(parts)
    out_status[...] = jnp.where(rows() == 0, then, 0.0)

    def put_middle(zi, y, t, value):
        middle[zi, y, t] = value

    seen = advance(
        Joined(field, left, right), coef, above, below_h, inside, step_of(now), 1, YS - 1, put_middle
    )
    second_of_pair(
        0, inside, middle, coef, step_of(then), seen, out, out_changes, out_parts, above, below_h
    )


def pair_kernel(
    number, inside, field, changes, coef, parts, status,
    out, out_changes, out_parts, out_status, middle, above, below_h,
):
    now, then, late = agree(parts)
    bad = jnp.maximum(status[1:2, :], differs(late[0:1], status[0:1, :]))
    out_status[...] = jnp.where(rows() == 0, then, bad)
    seen = first_of_pair(field, changes, coef, step_of(now), number + 1, YS - 1 - number, middle)
    second_of_pair(
        number, inside, middle, coef, step_of(then), seen,
        out, out_changes, out_parts, above, below_h,
    )


def second_of_pair(
    number, inside, middle, coef, step, seen, out, out_changes, out_parts, above, below_h
):
    def put(zi, y, t, value):
        out[zi, y, t] = value

    peak = advance(
        middle, coef, above, below_h, inside, step, number + 2, YS - 2 - number, put
    )
    guess = jnp.minimum(step_of(whole_peak(peak)), 1.2 * step)
    propose(
        out, coef, above, below_h, inside, guess, number + 3, YS - 3 - number,
        out_changes, peak, seen, out_parts,
    )


STATUS = jax.ShapeDtypeStruct((8, CX), F32)


def pair(number, kernel, operands, parts):
    return pl.pallas_call(
        kernel,
        out_shape=[WIDE, WIDE, jax.ShapeDtypeStruct(parts.shape, F32), STATUS],
        in_specs=[smem()] + [vspec()] * (len(operands) - 1),
        out_specs=[vspec()] * 4,
        scratch_shapes=[VM(WIDE.shape, F32), VM(ROW, F32), VM(ROW, F32)],
        compiler_params=params(),
        name=f"pair_{number}",
    )(*operands)


def first_pair(inside, start, coef, parts):
    return pair(0, first_pair_kernel, [inside, *start, coef, parts], parts)


def later_pair(number, inside, field, changes, coef, parts, status):
    operands = [inside, field, changes, coef, parts, status]
    return pair(number, functools.partial(pair_kernel, number), operands, parts)


def pixel_grams(field, weight, data, flat, late, sums):
    grams = jnp.zeros((M, 2 * M), F32)
    for y in range(CY):
        seen = 2.0 * field[0, y].reshape(CX, CX).T[0:M, :]
        for m in range(M):
            flat[m : m + 1, :] = data[m, y : y + 1, :]
        w = weight[y : y + 1, :]
        spread = seen - jnp.mean(seen, axis=0, keepdims=True)
        both = jnp.concatenate([spread * w, flat[...] - seen * w], axis=0)
        grams = grams + lax.dot_general(
            spread, both, NT, precision=lax.Precision.HIGHEST, preferred_element_type=F32
        )
    grams = jnp.concatenate([grams, jnp.zeros((M, CX - 2 * M), F32)], axis=1)
    two = grams[0:8] + pltpu.roll(grams[8:16], 32, axis=1)
    quad = two + pltpu.roll(pltpu.roll(two, 64, axis=1), 4, axis=0)
    quad = jnp.where((rows() == 0) & (lanes() == 1), whole_peak(late), quad)[0:4]
    for d in range(sums.shape[0]):
        sums[d] = quad


def last_kernel(
    inside, field, changes, coef, parts, status, weight, data,
    out, sums, out_status, middle, above, below_h, flat,
):
    number = SUBSTEPS - 2
    now, then, late = agree(parts)
    bad = jnp.maximum(status[1:2, :], differs(late[0:1], status[0:1, :]))
    out_status[...] = jnp.where(rows() == 0, then, bad)
    seen = first_of_pair(field, changes, coef, step_of(now), number + 1, YS - 1 - number, middle)

    def put(zi, y, t, value):
        if 0 < t < XT - 1:
            out[zi, y - HALO, t - 1] = value

    advance(middle, coef, above, below_h, inside, step_of(then), HALO, HALO + CY, put)
    pixel_grams(out, weight, data, flat, seen, sums)


def last(inside, field, changes, coef, parts, status, pixels):
    operands = [inside, field, changes, coef, parts, status, *pixels]
    return pl.pallas_call(
        last_kernel,
        out_shape=[OWN, jax.ShapeDtypeStruct(parts.shape, F32), STATUS],
        in_specs=[smem()] + [vspec()] * (len(operands) - 1),
        out_specs=[vspec()] * 3,
        scratch_shapes=[VM(WIDE.shape, F32), VM(ROW, F32), VM(ROW, F32), VM((M, CX), F32)],
        compiler_params=params(),
        name="last_pair",
    )(*operands)


def single_kernel(number, inside, coef, peaks, field, *rest):
    final = number == SUBSTEPS - 1
    if number == 0:
        field = Joined(field, *rest[:2])
        rest = rest[2:]
    if final:
        weight, data, out, sums, above, below_h, flat = rest
    else:
        out, out_peaks, above, below_h = rest
    peak = peaks[0]
    for d in range(1, peaks.shape[0]):
        peak = jnp.maximum(peak, peaks[d])
    step = step_of(whole_peak(peak))

    def put(zi, y, t, value):
        if not final:
            out[zi, y, t] = value
        elif 0 < t < XT - 1:
            out[zi, y - HALO, t - 1] = value

    peak = advance(field, coef, above, below_h, inside, step, number + 1, YS - 1 - number, put)
    if final:
        pixel_grams(out, weight, data, flat, jnp.zeros((8, CX), F32), sums)
    else:
        out_peaks[...] = jnp.broadcast_to(columns_peak(peak)[0:1].reshape(1, 1, CX), out_peaks.shape)


def single(number, inside, field, coef, peaks, pixels):
    devices = peaks.shape[0]
    operands = [inside, coef, peaks, *field]
    scratch = [VM(ROW, F32), VM(ROW, F32)]
    if number == SUBSTEPS - 1:
        operands += list(pixels)
        out_shape = [OWN, jax.ShapeDtypeStruct((devices, 4, CX), F32)]
        scratch += [VM((M, CX), F32)]
    else:
        out_shape = [WIDE, jax.ShapeDtypeStruct((devices, 1, CX), F32)]
    return pl.pallas_call(
        functools.partial(single_kernel, number),
        out_shape=out_shape,
        in_specs=[smem()] + [vspec()] * (len(operands) - 1),
        out_specs=[vspec()] * 2,
        scratch_shapes=scratch,
        compiler_params=params(),
        name=f"single_{number}",
    )(*operands)


def pixel_kernel(cell, observed, variance, noise, weight, data):
    pixels = cell.shape[1]
    place = cell[...]
    var = variance[...]
    inverse = 1.0 / var
    values = (observed[...] + noise[...] * jnp.sqrt(var)) * inverse
    stack = jnp.concatenate([values, jnp.broadcast_to(inverse, (8, pixels))], axis=0)
    width = place >> 7
    hot = jnp.where(
        lax.broadcasted_iota(jnp.int32, (CX, pixels), 0) == (place & 127), 1.0, 0.0
    ).astype(F32)
    for y in range(CY):
        part = lax.dot_general(
            jnp.where(width == y, stack, 0.0),
            hot,
            NT,
            precision=lax.Precision.HIGHEST,
            preferred_element_type=F32,
        )
        weight[y : y + 1, :] = part[M : M + 1, :]
        for m in range(M):
            data[m, y : y + 1, :] = part[m : m + 1, :]


def pixel_sums(cell, observed, variance, noise):
    return pl.pallas_call(
        pixel_kernel,
        out_shape=[
            jax.ShapeDtypeStruct((CY, CX), F32),
            jax.ShapeDtypeStruct((M, CY, CX), F32),
        ],
        in_specs=[vspec()] * 4,
        out_specs=[vspec()] * 2,
        compiler_params=params(),
        name="pixels",
    )(cell, observed, variance, noise)


def update_kernel(sums, field, status, out, flag):
    quad = sums[0]
    late = quad
    for d in range(1, sums.shape[0]):
        quad = quad + sums[d]
        late = jnp.maximum(late, sums[d])
    late = jnp.broadcast_to(late[0:1, 1:2], (1, CX))
    bad = jnp.maximum(status[1:2, :], differs(late, status[0:1, :]))
    flag[0] = jnp.where(jnp.max(bad) > 0.0, 1, 0)
    row = rows()
    quad = jnp.concatenate([quad, jnp.zeros_like(quad)], axis=0)
    pair = jnp.where(row < 4, quad, pltpu.roll(pltpu.roll(quad, 64, axis=1), 4, axis=0))
    system = jnp.concatenate([pair, pltpu.roll(pair, CX - 32, axis=1)], axis=0)
    tall = lax.broadcasted_iota(jnp.int32, (M, CX), 0)
    wide = lax.broadcasted_iota(jnp.int32, (M, CX), 1)
    system = jnp.where(tall == wide, system + (M - 1.0), system)
    mirror = jnp.broadcast_to(system[1:2, 0:1], (M, CX))
    system = jnp.where((tall == 0) & (wide == 1), mirror, system)
    for i in range(M):
        pivot = system[i : i + 1, :]
        pivot = pivot / pivot[:, i : i + 1]
        factor = jnp.where(tall == i, 0.0, jnp.broadcast_to(system[:, i : i + 1], (M, CX)))
        system = jnp.where(tall == i, pivot, system - factor * pivot)
    mixing = system - jnp.mean(system, axis=0, keepdims=True)
    mixing = pltpu.roll(mixing, CX - M, axis=1)
    mixing = jnp.where(wide < M, mixing + jnp.where(tall == wide, 1.0, 0.0), 0.0)
    for shift in (16, 32, 64):
        mixing = mixing + pltpu.roll(mixing, shift, axis=1)
    mixing = jnp.concatenate([mixing] * ZG, axis=0)
    tall = lax.broadcasted_iota(jnp.int32, (CX, CX), 0)
    wide = lax.broadcasted_iota(jnp.int32, (CX, CX), 1)
    mixing = jnp.where((tall >> 4) == (wide >> 4), 2.0 * mixing, 0.0).T
    for zi in range(2):
        for y in range(CY):
            part = lax.dot_general(
                mixing,
                field[zi, y].reshape(CX, CX),
                NT,
                precision=lax.Precision.HIGHEST,
                preferred_element_type=F32,
            )
            for group in range(ZG):
                for m0 in (0, 8):
                    at = group * M + m0
                    out[m0 : m0 + 8, 2 * group + zi, y, :] = part[at : at + 8, :]


def update(sums, field, status):
    return pl.pallas_call(
        update_kernel,
        out_shape=[
            jax.ShapeDtypeStruct((M, NZ, CY, CX), F32),
            jax.ShapeDtypeStruct((1,), jnp.int32),
        ],
        in_specs=[vspec()] * 3,
        out_specs=[vspec(), smem()],
        compiler_params=params(),
        name="update",
    )(sums, field, status)


def exchange(parts):
    return lax.all_to_all(parts, BOTH, split_axis=0, concat_axis=0, tiled=True)


def move(part, axis, ahead):
    count = lax.axis_size(axis)
    pairs = [(i, i + 1) if ahead else (i + 1, i) for i in range(count - 1)]
    return lax.ppermute(part, axis, pairs)


def on_device(
    state_prior,
    conductivity,
    heat_input,
    owner_tile,
    voxel_list,
    pixel_cell,
    observed,
    pixel_variance,
    pixel_noise,
):
    devices = lax.axis_size("gx") * lax.axis_size("gy")
    pixels = pixel_cell.shape[0]
    outgoing = pack(owner_tile.reshape(-1), heat_input, voxel_list, devices)
    incoming = exchange(outgoing)

    gx, gy = lax.axis_index("gx"), lax.axis_index("gy")
    inside = jnp.stack(
        [gx > 0, gx < lax.axis_size("gx") - 1, gy > 0, gy < lax.axis_size("gy") - 1]
    ).astype(F32)
    left_c, right_c = move(conductivity, "gx", True), move(conductivity, "gx", False)
    strips = strip(conductivity, left_c, right_c)
    coef = coefs(strips, move(strips, "gy", True), move(strips, "gy", False))
    state_prior, strips = lax.optimization_barrier((state_prior, strips))
    own, to_high, to_low, to_left, to_right = relayout(state_prior)
    low, high = move(to_high, "gy", True), move(to_low, "gy", False)
    left, right = move(to_right, "gx", True), move(to_left, "gx", False)
    seen = pixel_sums(
        pixel_cell.reshape(1, pixels),
        observed.reshape(1, pixels),
        pixel_variance.reshape(1, pixels),
        pixel_noise,
    )
    incoming, coef, own, left, right, inside, *seen = lax.optimization_barrier(
        (incoming, coef, own, left, right, inside, *seen)
    )
    heat, to_left, to_right = deposit(incoming)
    heat_low, heat_high = move(heat, "gy", True), move(heat, "gy", False)
    heat_left, heat_right = move(to_right, "gx", True), move(to_left, "gx", False)
    start, parts, to_left, to_right = heated(
        inside,
        (own, low, high),
        (left, right),
        (heat_low, heat, heat_high, heat_left, heat_right),
        coef,
        devices,
    )
    start = (start, move(to_right, "gx", True), move(to_left, "gx", False))
    field, changes, parts, status = first_pair(inside, start, coef, exchange(parts))
    for number in range(2, SUBSTEPS - 2, 2):
        field, changes, parts, status = later_pair(
            number, inside, field, changes, coef, exchange(parts), status
        )
    field, sums, status = last(inside, field, changes, coef, exchange(parts), status, seen)
    result, flag = update(exchange(sums), field, status)

    def again():
        peak = coef * (1.0 + start[0] * start[0])
        peak = jnp.max(peak[:, HALO : HALO + CY, 1 : XT - 1])
        peaks = jnp.full((devices, 1, CX), peak)
        field = start
        for number in range(SUBSTEPS):
            field, peaks = single(number, inside, field, coef, exchange(peaks), seen)
            field = (field,)
        return update(exchange(peaks), field[0], jnp.ones((8, CX), F32))[0]

    return lax.cond(flag[0] > 0, again, lambda: result)


def solution(mesh):
    in_specs = (
        P(None, None, "gy", "gx"),
        P(None, "gy", "gx"),
        P(None, BOTH, None),
        P(BOTH, None),
        P(BOTH, None),
        P(BOTH),
        P(BOTH),
        P(BOTH),
        P(None, BOTH),
    )
    out_specs = P(None, None, "gy", "gx")
    return jax.shard_map(
        on_device, mesh=mesh, in_specs=in_specs, out_specs=out_specs, check_vma=False
    )
```

```python
import functools

import jax
import jax.numpy as jnp
from jax import lax
from jax.experimental import pallas as pl
from jax.experimental.pallas import tpu as pltpu
from jax.sharding import PartitionSpec as P

SUBSTEPS = 6
CAP = 2
COOL = 0.1
SHARE = 0.9
F32 = jnp.float32
BF16 = jnp.bfloat16
VM = pltpu.VMEM
LIMIT = 24 * 1024 * 1024
NT = (((1,), (1,)), ((), ()))
BOTH = ("gx", "gy")

M, NZ, CY, CX = 16, 16, 8, 128
ROWS = 40


def vspec():
    return pl.BlockSpec(memory_space=pltpu.VMEM)


def params():
    return pltpu.CompilerParams(vmem_limit_bytes=LIMIT)


def lanes():
    return lax.broadcasted_iota(jnp.int32, (CY, CX), 1)


def rows():
    return lax.broadcasted_iota(jnp.int32, (CY, CX), 0)


def pack_kernel(owner_far, heat_far, voxel_far, out, owner, heat, voxel, wide, high, low, inverse, sems):
    copies = [
        pltpu.make_async_copy(far, near, sems.at[i])
        for i, (far, near) in enumerate(
            ((owner_far, owner), (heat_far, heat), (voxel_far, voxel))
        )
    ]
    for copy in copies:
        copy.start()
    blocks = owner.shape[0]
    devices = out.shape[0]

    def clear(i, carry):
        inverse[i] = blocks
        return carry

    lax.fori_loop(0, devices * CAP, clear, 0, unroll=16)
    copies[0].wait()

    def place(b, carry):
        base = owner[b] * CAP
        base = base + jnp.where(inverse[base] != blocks, 1, 0)
        inverse[base] = b
        return carry

    lax.fori_loop(0, blocks, place, 0, unroll=8)
    copies[1].wait()
    copies[2].wait()

    def widen(m, carry):
        wide[m, 0:blocks, :] = heat[m].astype(F32)
        wide[m, blocks:, :] = jnp.zeros((8, CX), F32)
        return carry

    lax.fori_loop(0, M, widen, 0)
    cells = voxel[...]
    high[0:blocks, :] = (cells >> 7).astype(F32)
    high[blocks:, :] = jnp.zeros((8, CX), F32)
    low[0:blocks, :] = (cells & 127).astype(F32)
    low[blocks:, :] = jnp.zeros((8, CX), F32)
    row = rows()

    def emit(d, carry):
        first = inverse[d * CAP]
        second = inverse[d * CAP + 1]
        index = jnp.where(
            row == 0,
            high[pl.ds(first, 1), :],
            jnp.where(
                row == 1,
                high[pl.ds(second, 1), :],
                jnp.where(
                    row == 2,
                    low[pl.ds(first, 1), :],
                    jnp.where(row == 3, low[pl.ds(second, 1), :], 0.0),
                ),
            ),
        )
        chunk = jnp.concatenate(
            [
                wide[:, pl.ds(first, 1), :].reshape(M, CX),
                wide[:, pl.ds(second, 1), :].reshape(M, CX),
                index,
            ],
            axis=0,
        )
        out[d] = chunk.astype(BF16)
        return carry

    lax.fori_loop(0, devices, emit, 0, unroll=4)


def pack(owner, heat, voxel, devices):
    blocks = owner.shape[0]
    return pl.pallas_call(
        pack_kernel,
        out_shape=jax.ShapeDtypeStruct((devices, ROWS, CX), BF16),
        in_specs=[pl.BlockSpec(memory_space=pl.ANY)] * 3,
        out_specs=vspec(),
        scratch_shapes=[
            pltpu.SMEM((blocks,), jnp.int32),
            VM((M, blocks, CX), BF16),
            VM((blocks, CX), jnp.int32),
            VM((M, blocks + 8, CX), F32),
            VM((blocks + 8, CX), F32),
            VM((blocks + 8, CX), F32),
            pltpu.SMEM((devices * CAP,), jnp.int32),
            pltpu.SemaphoreType.DMA((3,)),
        ],
        compiler_params=params(),
        name="pack",
    )(owner, heat, voxel)


HALO = 6
YS = CY + 2 * HALO
XT = CX // 8 + 2
ZG = NZ // 2
TOLERANCE = 1e-6
OWN = jax.ShapeDtypeStruct((2, CY, CX, CX), F32)
XS = 8 * XT
WIDE = jax.ShapeDtypeStruct((2, YS, XS, CX), F32)
EDGE = 2 * HALO * (XT - 2)
SIDE = 2 * YS


def relayout_kernel(state, conduct, own, turned_c, to_high, to_low):
    turned = (0.5 * conduct[...].reshape(CX, CX)).T.reshape(XT - 2, 8, CX)
    turned_c[...] = turned
    to_high[EDGE:] = turned
    to_low[EDGE:] = turned
    for zi in range(2):
        for y in range(CY):
            parts = [
                state[m0 : m0 + 8, 2 * group + zi, y, :] for group in range(ZG) for m0 in (0, 8)
            ]
            turned = (0.5 * jnp.concatenate(parts, axis=0)).T
            own[zi, y] = turned
            turned = turned.reshape(XT - 2, 8, CX)
            if y >= CY - HALO:
                at = (zi * HALO + y - (CY - HALO)) * (XT - 2)
                to_high[at : at + XT - 2] = turned
            if y < HALO:
                at = (zi * HALO + y) * (XT - 2)
                to_low[at : at + XT - 2] = turned


def relayout(state, conduct):
    edge = jax.ShapeDtypeStruct((EDGE + XT - 2, 8, CX), F32)
    return pl.pallas_call(
        relayout_kernel,
        out_shape=[OWN, jax.ShapeDtypeStruct((XT - 2, 8, CX), F32), edge, edge],
        in_specs=[vspec()] * 2,
        out_specs=[vspec()] * 4,
        compiler_params=params(),
        name="relayout",
    )(state, conduct)


def side_kernel(own, turned_c, low, high, to_left, to_right):
    for out, t in ((to_left, 0), (to_right, XT - 3)):
        for zi in range(2):
            for y in range(YS):
                if y < HALO:
                    part = low[(zi * HALO + y) * (XT - 2) + t]
                elif y < HALO + CY:
                    part = own[zi, y - HALO, 8 * t : 8 * t + 8, :]
                else:
                    part = high[(zi * HALO + y - HALO - CY) * (XT - 2) + t]
                out[zi * YS + y] = part
        out[SIDE] = low[EDGE + t]
        out[SIDE + 1] = turned_c[t]
        out[SIDE + 2] = high[EDGE + t]


def sides(own, turned_c, low, high):
    shape = jax.ShapeDtypeStruct((SIDE + 3, 8, CX), F32)
    return pl.pallas_call(
        side_kernel,
        out_shape=[shape, shape],
        in_specs=[vspec()] * 4,
        out_specs=[vspec()] * 2,
        compiler_params=params(),
        name="sides",
    )(own, turned_c, low, high)


def coef_kernel(turned_c, low, high, left, right, out):
    source = lax.broadcasted_iota(jnp.int32, (CX, CX), 0)
    target = lax.broadcasted_iota(jnp.int32, (CX, CX), 1)
    strips = []
    for g in range(3):
        mid = (low[EDGE:], turned_c[...], high[EDGE:])[g].reshape(CX, CX)
        strips.append(jnp.concatenate([left[SIDE + g], mid, right[SIDE + g]], axis=0))

    def put(g, y0, yy):
        for zi in range(2):
            wanted = (2 * (target >> 4) + zi) * CY + y0
            hot = jnp.where(source == wanted, 1.0, 0.0).astype(F32)
            part = jnp.dot(
                strips[g], hot, precision=lax.Precision.HIGHEST, preferred_element_type=F32
            )
            out[zi, yy] = part

    for y in range(HALO):
        put(0, y + CY - HALO, y)
    for y in range(CY):
        put(1, y, y + HALO)
    for y in range(HALO):
        put(2, y, y + HALO + CY)


def coefs(turned_c, low, high, left, right):
    return pl.pallas_call(
        coef_kernel,
        out_shape=WIDE,
        in_specs=[vspec()] * 5,
        out_specs=vspec(),
        compiler_params=params(),
        name="coefs",
    )(turned_c, low, high, left, right)


def deposit_kernel(incoming, out, total):
    sources = incoming.shape[0]
    group = 32
    place = lax.broadcasted_iota(jnp.int32, (CX, CX), 0).astype(F32).astype(BF16)
    zero = jnp.zeros((M, CX), BF16)
    total[...] = jnp.zeros_like(total)

    def one(g, carry):
        left = []
        right = []
        for s in range(group):
            source = g * group + s
            index = incoming[source, 32:40, :].astype(F32)
            for slot in range(CAP):
                heat = incoming[source, slot * M : (slot + 1) * M, :]
                layer = jnp.broadcast_to(index[slot : slot + 1, :], (M, CX)).astype(BF16)
                cell = jnp.broadcast_to(index[2 + slot : 3 + slot, :], (CX, CX)).astype(BF16)
                left.append(
                    jnp.concatenate(
                        [jnp.where(layer == h, heat, zero) for h in range(2 * CY)], axis=0
                    )
                )
                right.append(jnp.where(place == cell, 1.0, 0.0).astype(BF16))
        total[...] += lax.dot_general(
            jnp.concatenate(left, axis=1),
            jnp.concatenate(right, axis=1),
            NT,
            preferred_element_type=F32,
        )
        return carry

    lax.fori_loop(0, sources // group, one, 0)
    for zi in range(2):
        out[zi] = (0.5 * total[zi * CX : (zi + 1) * CX, :]).T


def deposit(incoming):
    return pl.pallas_call(
        deposit_kernel,
        out_shape=jax.ShapeDtypeStruct((2, CX, CX), F32),
        in_specs=[vspec()],
        out_specs=vspec(),
        scratch_shapes=[VM((2 * CY * M, CX), F32)],
        compiler_params=params(),
        name="deposit",
    )(incoming)


def heat_side_kernel(low, own, high, to_left, to_right):
    for g, part in enumerate((low, own, high)):
        to_left[g] = part[:, 0:8, :]
        to_right[g] = part[:, CX - 8 :, :]


def heat_sides(low, own, high):
    shape = jax.ShapeDtypeStruct((3, 2, 8, CX), F32)
    return pl.pallas_call(
        heat_side_kernel,
        out_shape=[shape, shape],
        in_specs=[vspec()] * 3,
        out_specs=[vspec()] * 2,
        compiler_params=params(),
        name="heat_sides",
    )(low, own, high)


def whole_peak(value):
    return jnp.broadcast_to(jnp.max(value, axis=(0, 1), keepdims=True), (8, CX))


def step_of(peak):
    return SHARE / (12.0 * peak + COOL)


def tile(t):
    return slice(8 * t, 8 * t + 8)


def half_conductance(c, u):
    return c + c * (u * u)


def segments(inside, first, end):
    parts = []
    if first < HALO:
        parts.append((first, HALO, False, inside[2]))
    parts.append((max(first, HALO), min(end, HALO + CY), True, None))
    if end > HALO + CY:
        parts.append((HALO + CY, end, False, inside[3]))
    return parts


def mask_of(inside, row_mask, t):
    if t == 0:
        return inside[0] if row_mask is None else inside[0] * row_mask
    if t == XT - 1:
        return inside[1] if row_mask is None else inside[1] * row_mask
    return row_mask


def sweep(field, half, above, inside, first, end, emit, carry):
    lane = lanes()
    row = rows()
    last_row = row == 7
    first_row = row == 0
    inner_lane = lane < CX - M
    cooling = jnp.where(lane < M, COOL, 0.0)

    for zi in range(2):
        for t in range(XT):
            s = tile(t)
            above[zi, t] = (half[zi, first - 1, s, :] + half[zi, first, s, :]) * (
                field[zi, first, s, :] - field[zi, first - 1, s, :]
            )

    def line(own, row_mask, y, state):
        carried = [jnp.zeros((8, CX), F32)] * 2
        for t in range(XT):
            s = tile(t)
            us = [field[zi, y, s, :] for zi in range(2)]
            hs = [half[zi, y, s, :] for zi in range(2)]
            change = []
            for zi in range(2):
                u, h = us[zi], hs[zi]
                if t < XT - 1:
                    after = slice(8 * t + 1, 8 * t + 9)
                    u_after, h_after = field[zi, y, after, :], half[zi, y, after, :]
                else:
                    u_after = jnp.where(last_row, u, pltpu.roll(u, 7, axis=0))
                    h_after = pltpu.roll(h, 7, axis=0)
                along = (h + h_after) * (u_after - u)
                turned = pltpu.roll(along, 1, axis=0)
                total = along - jnp.where(first_row, carried[zi], turned)
                carried[zi] = turned
                across = (h + half[zi, y + 1, s, :]) * (field[zi, y + 1, s, :] - u)
                total = total + (across - above[zi, t])
                above[zi, t] = across
                change.append(total)
            within = (hs[0] + hs[1]) * (us[1] - us[0])
            between = (hs[1] + pltpu.roll(hs[0], CX - M, axis=1)) * (
                pltpu.roll(us[0], CX - M, axis=1) - us[1]
            )
            between = jnp.where(inner_lane, between, 0.0)
            change[0] = change[0] + (within - pltpu.roll(between, M, axis=1)) - cooling * us[0]
            change[1] = change[1] + (between - within)
            state = emit(y, t, us, change, own, mask_of(inside, row_mask, t), state)
        return state

    for start, stop, own, row_mask in segments(inside, first, end):
        carry = lax.fori_loop(start, stop, functools.partial(line, own, row_mask), carry)
    return carry


def advance(field, half, coef, above, inside, step, first, end, put):
    def emit(y, t, us, change, own, mask, peak):
        part = step if mask is None else step * mask
        for zi in range(2):
            value = us[zi] + part * change[zi]
            after = half_conductance(coef[zi, y, tile(t), :], value)
            put(zi, y, t, value, after)
            if own and 0 < t < XT - 1:
                peak = jnp.maximum(peak, after)
        return peak

    return sweep(field, half, above, inside, first, end, emit, jnp.zeros((8, CX), F32))


def propose(field, half, coef, above, inside, guess, first, end, changes, peak, late, out):
    def emit(y, t, us, change, own, mask, best):
        for zi in range(2):
            moved = change[zi] if mask is None else change[zi] * mask
            changes[zi, y, tile(t), :] = moved
            if own and 0 < t < XT - 1:
                c = coef[zi, y, tile(t), :]
                rank = half_conductance(c, us[zi] + guess * moved)
                better = rank > best[0]
                best = tuple(
                    jnp.where(better, new, old)
                    for new, old in zip((rank, us[zi], moved, c), best)
                )
        return best

    best = sweep(
        field, half, above, inside, first, end, emit, (jnp.zeros((8, CX), F32),) * 4
    )
    for shift, axis in ((4, 0), (2, 0), (1, 0), (64, 1), (32, 1)):
        other = tuple(pltpu.roll(part, shift, axis=axis) for part in best)
        better = other[0] > best[0]
        best = tuple(jnp.where(better, new, old) for new, old in zip(other, best))
    part = lanes() >> 4
    chunk = jnp.where(part == 6, whole_peak(peak), whole_peak(late))
    for place, value in ((2, best[3]), (1, best[2]), (0, best[1])):
        chunk = jnp.where((part >> 1) == place, value, chunk)
    for d in range(0, out.shape[0], 8):
        out[d : d + 8, 0, :] = chunk


def agree(parts):
    part = lanes() >> 4
    rows_of = [parts[d : d + 8, 0, :] for d in range(0, parts.shape[0], 8)]
    most = rows_of[0]
    for value in rows_of[1:]:
        most = jnp.maximum(most, value)
    now = whole_peak(jnp.where(part == 6, most, 0.0))
    late = whole_peak(jnp.where(part == 7, most, 0.0))
    step = step_of(now)
    then = jnp.zeros((8, CX), F32)
    for value in rows_of:
        moved = pltpu.roll(value, CX - 32, axis=1)
        c = pltpu.roll(value, CX - 64, axis=1)
        then = jnp.maximum(then, half_conductance(c, value + step * moved))
    return now, whole_peak(jnp.where(part < 2, then, 0.0)), late


def differs(late, used):
    return jnp.where(late > used * (1.0 + TOLERANCE), 1.0, 0.0)


def heated_kernel(
    inside, own, low, high, left, right,
    heat_low, heat_own, heat_high, heat_left, heat_right,
    coef, out, changes, parts, half, above,
):
    top = lanes() < M
    peak = jnp.zeros((8, CX), F32)

    def row(g, heat, tile_of, y0, yy, peak):
        shift = (CX - 16 * y0) % CX
        for zi in range(2):
            for t in range(XT):
                if t == 0:
                    prior, add = left[zi * YS + yy], heat_left[g, zi]
                elif t == XT - 1:
                    prior, add = right[zi * YS + yy], heat_right[g, zi]
                else:
                    prior, add = tile_of(zi, t - 1), heat[zi, tile(t - 1), :]
                if shift:
                    add = pltpu.roll(add, shift, axis=1)
                value = prior + jnp.where(top, add, 0.0)
                after = half_conductance(coef[zi, yy, tile(t), :], value)
                out[zi, yy, tile(t), :] = value
                half[zi, yy, tile(t), :] = after
                if g == 1 and 0 < t < XT - 1:
                    peak = jnp.maximum(peak, after)
        return peak

    def edge(ref, y):
        return lambda zi, t: ref[(zi * HALO + y) * (XT - 2) + t]

    for y in range(HALO):
        row(0, heat_low, edge(low, y), y + CY - HALO, y, peak)
    for y in range(CY):
        peak = row(1, heat_own, lambda zi, t: own[zi, y, tile(t), :], y, y + HALO, peak)
    for y in range(HALO):
        row(2, heat_high, edge(high, y), y, y + HALO + CY, peak)
    guess = step_of(whole_peak(peak))
    zero = jnp.zeros((8, CX), F32)
    propose(out, half, coef, above, inside, guess, 1, YS - 1, changes, peak, zero, parts)


ROW = (2, XT, 8, CX)


def smem():
    return pl.BlockSpec(memory_space=pltpu.SMEM)


def heated(inside, prior, halos, heat, coef, devices):
    operands = [inside, *prior, *halos, *heat, coef]
    return pl.pallas_call(
        heated_kernel,
        out_shape=[WIDE, WIDE, jax.ShapeDtypeStruct((devices, 1, CX), F32)],
        in_specs=[smem()] + [vspec()] * (len(operands) - 1),
        out_specs=[vspec()] * 3,
        scratch_shapes=[VM(WIDE.shape, F32), VM(ROW, F32)],
        compiler_params=params(),
        name="heated",
    )(*operands)


def first_of_pair(field, changes, coef, step, first, end, out, half):
    def line(y, peak):
        top = jnp.zeros((8, CX), F32)
        for zi in range(2):
            for t in range(XT):
                value = field[zi, y, tile(t), :] + step * changes[zi, y, tile(t), :]
                after = half_conductance(coef[zi, y, tile(t), :], value)
                out[zi, y, tile(t), :] = value
                half[zi, y, tile(t), :] = after
                if 0 < t < XT - 1:
                    top = jnp.maximum(top, after)
        own = jnp.where((y >= HALO) & (y < HALO + CY), 1.0, 0.0)
        return jnp.maximum(peak, own * top)

    return lax.fori_loop(first, end, line, jnp.zeros((8, CX), F32))


def pair_kernel(
    number, inside, field, changes, coef, parts, status,
    out, out_changes, out_parts, out_status, middle, half, next_half, above,
):
    now, then, late = agree(parts)
    bad = status[1:2, :]
    if number:
        bad = jnp.maximum(bad, differs(late[0:1], status[0:1, :]))
    out_status[...] = jnp.where(rows() == 0, then, bad)
    seen = first_of_pair(
        field, changes, coef, step_of(now), number + 1, YS - 1 - number, middle, half
    )

    def put(zi, y, t, value, after):
        out[zi, y, tile(t), :] = value
        next_half[zi, y, tile(t), :] = after

    step = step_of(then)
    peak = advance(
        middle, half, coef, above, inside, step, number + 2, YS - 2 - number, put
    )
    guess = jnp.minimum(step_of(whole_peak(peak)), 1.2 * step)
    propose(
        out, next_half, coef, above, inside, guess, number + 3, YS - 3 - number,
        out_changes, peak, seen, out_parts,
    )


STATUS = jax.ShapeDtypeStruct((8, CX), F32)


def pair(number, inside, field, changes, coef, parts, status):
    operands = [inside, field, changes, coef, parts, status]
    return pl.pallas_call(
        functools.partial(pair_kernel, number),
        out_shape=[WIDE, WIDE, jax.ShapeDtypeStruct(parts.shape, F32), STATUS],
        in_specs=[smem()] + [vspec()] * 5,
        out_specs=[vspec()] * 4,
        scratch_shapes=[VM(WIDE.shape, F32)] * 3 + [VM(ROW, F32)],
        compiler_params=params(),
        name=f"pair_{number}",
    )(*operands)


def pixel_grams(field, weight, data, flat, late, sums):
    grams = jnp.zeros((M, 2 * M), F32)
    for y in range(CY):
        seen = 2.0 * field[0, y].T[0:M, :]
        for m in range(M):
            flat[m : m + 1, :] = data[m, y : y + 1, :]
        w = weight[y : y + 1, :]
        spread = seen - jnp.mean(seen, axis=0, keepdims=True)
        both = jnp.concatenate([spread * w, flat[...] - seen * w], axis=0)
        grams = grams + lax.dot_general(
            spread, both, NT, precision=lax.Precision.HIGHEST, preferred_element_type=F32
        )
    grams = jnp.concatenate([grams, jnp.zeros((M, CX - 2 * M), F32)], axis=1)
    two = grams[0:8] + pltpu.roll(grams[8:16], 32, axis=1)
    quad = two + pltpu.roll(pltpu.roll(two, 64, axis=1), 4, axis=0)
    quad = jnp.where((rows() == 0) & (lanes() == 1), whole_peak(late), quad)[0:4]
    for d in range(sums.shape[0]):
        sums[d] = quad


def last_kernel(
    inside, field, changes, coef, parts, status, weight, data,
    out, sums, out_status, middle, half, above, flat,
):
    number = SUBSTEPS - 2
    now, then, late = agree(parts)
    bad = jnp.maximum(status[1:2, :], differs(late[0:1], status[0:1, :]))
    out_status[...] = jnp.where(rows() == 0, then, bad)
    seen = first_of_pair(
        field, changes, coef, step_of(now), number + 1, YS - 1 - number, middle, half
    )

    def put(zi, y, t, value, after):
        if 0 < t < XT - 1:
            out[zi, y - HALO, tile(t - 1), :] = value

    advance(middle, half, coef, above, inside, step_of(then), HALO, HALO + CY, put)
    pixel_grams(out, weight, data, flat, seen, sums)


def last(inside, field, changes, coef, parts, status, pixels):
    operands = [inside, field, changes, coef, parts, status, *pixels]
    return pl.pallas_call(
        last_kernel,
        out_shape=[OWN, jax.ShapeDtypeStruct((parts.shape[0], 4, CX), F32), STATUS],
        in_specs=[smem()] + [vspec()] * (len(operands) - 1),
        out_specs=[vspec()] * 3,
        scratch_shapes=[VM(WIDE.shape, F32)] * 2 + [VM(ROW, F32), VM((M, CX), F32)],
        compiler_params=params(),
        name="last_pair",
    )(*operands)


def single_kernel(number, inside, field, coef, peaks, *rest):
    final = number == SUBSTEPS - 1
    if final:
        weight, data, out, sums, half, above, flat = rest
    else:
        out, out_peaks, half, above = rest
    peak = peaks[0]
    for d in range(1, peaks.shape[0]):
        peak = jnp.maximum(peak, peaks[d])
    step = step_of(whole_peak(peak))

    def fill(y, carry):
        for zi in range(2):
            half[zi, y] = half_conductance(coef[zi, y], field[zi, y])
        return carry

    lax.fori_loop(number, YS - number, fill, 0)

    def put(zi, y, t, value, after):
        if not final:
            out[zi, y, tile(t), :] = value
        elif 0 < t < XT - 1:
            out[zi, y - HALO, tile(t - 1), :] = value

    peak = advance(field, half, coef, above, inside, step, number + 1, YS - 1 - number, put)
    if final:
        pixel_grams(out, weight, data, flat, jnp.zeros((8, CX), F32), sums)
    else:
        peak = whole_peak(peak)
        for d in range(0, out_peaks.shape[0], 8):
            out_peaks[d : d + 8, 0, :] = peak


def single(number, inside, field, coef, peaks, pixels):
    devices = peaks.shape[0]
    operands = [inside, field, coef, peaks]
    scratch = [VM(WIDE.shape, F32), VM(ROW, F32)]
    if number == SUBSTEPS - 1:
        operands += list(pixels)
        out_shape = [OWN, jax.ShapeDtypeStruct((devices, 4, CX), F32)]
        scratch += [VM((M, CX), F32)]
    else:
        out_shape = [WIDE, jax.ShapeDtypeStruct((devices, 1, CX), F32)]
    return pl.pallas_call(
        functools.partial(single_kernel, number),
        out_shape=out_shape,
        in_specs=[smem()] + [vspec()] * (len(operands) - 1),
        out_specs=[vspec()] * 2,
        scratch_shapes=scratch,
        compiler_params=params(),
        name=f"single_{number}",
    )(*operands)


def pixel_kernel(cell, observed, variance, noise, weight, data):
    pixels = cell.shape[1]
    place = cell[...]
    var = variance[...]
    inverse = 1.0 / var
    values = (observed[...] + noise[...] * jnp.sqrt(var)) * inverse
    stack = jnp.concatenate([values, jnp.broadcast_to(inverse, (8, pixels))], axis=0)
    width = place >> 7
    hot = jnp.where(
        lax.broadcasted_iota(jnp.int32, (CX, pixels), 0) == (place & 127), 1.0, 0.0
    ).astype(F32)
    for y in range(CY):
        part = lax.dot_general(
            jnp.where(width == y, stack, 0.0),
            hot,
            NT,
            precision=lax.Precision.HIGHEST,
            preferred_element_type=F32,
        )
        weight[y : y + 1, :] = part[M : M + 1, :]
        for m in range(M):
            data[m, y : y + 1, :] = part[m : m + 1, :]


def pixel_sums(cell, observed, variance, noise):
    return pl.pallas_call(
        pixel_kernel,
        out_shape=[
            jax.ShapeDtypeStruct((CY, CX), F32),
            jax.ShapeDtypeStruct((M, CY, CX), F32),
        ],
        in_specs=[vspec()] * 4,
        out_specs=[vspec()] * 2,
        compiler_params=params(),
        name="pixels",
    )(cell, observed, variance, noise)


def update_kernel(sums, field, status, out, flag):
    quad = sums[0]
    late = quad
    for d in range(1, sums.shape[0]):
        quad = quad + sums[d]
        late = jnp.maximum(late, sums[d])
    late = jnp.broadcast_to(late[0:1, 1:2], (1, CX))
    bad = jnp.maximum(status[1:2, :], differs(late, status[0:1, :]))
    flag[0] = jnp.where(jnp.max(bad) > 0.0, 1, 0)
    row = rows()
    quad = jnp.concatenate([quad, jnp.zeros_like(quad)], axis=0)
    pair = jnp.where(row < 4, quad, pltpu.roll(pltpu.roll(quad, 64, axis=1), 4, axis=0))
    system = jnp.concatenate([pair, pltpu.roll(pair, CX - 32, axis=1)], axis=0)
    tall = lax.broadcasted_iota(jnp.int32, (M, CX), 0)
    wide = lax.broadcasted_iota(jnp.int32, (M, CX), 1)
    system = jnp.where(tall == wide, system + (M - 1.0), system)
    mirror = jnp.broadcast_to(system[1:2, 0:1], (M, CX))
    system = jnp.where((tall == 0) & (wide == 1), mirror, system)
    for i in range(M):
        pivot = system[i : i + 1, :]
        pivot = pivot / pivot[:, i : i + 1]
        factor = jnp.where(tall == i, 0.0, jnp.broadcast_to(system[:, i : i + 1], (M, CX)))
        system = jnp.where(tall == i, pivot, system - factor * pivot)
    mixing = system - jnp.mean(system, axis=0, keepdims=True)
    mixing = pltpu.roll(mixing, CX - M, axis=1)
    mixing = jnp.where(wide < M, mixing + jnp.where(tall == wide, 1.0, 0.0), 0.0)
    for shift in (16, 32, 64):
        mixing = mixing + pltpu.roll(mixing, shift, axis=1)
    mixing = jnp.concatenate([mixing] * ZG, axis=0)
    tall = lax.broadcasted_iota(jnp.int32, (CX, CX), 0)
    wide = lax.broadcasted_iota(jnp.int32, (CX, CX), 1)
    mixing = jnp.where((tall >> 4) == (wide >> 4), 2.0 * mixing, 0.0).T
    for zi in range(2):
        for y in range(CY):
            part = lax.dot_general(
                mixing,
                field[zi, y],
                NT,
                precision=lax.Precision.HIGHEST,
                preferred_element_type=F32,
            )
            for group in range(ZG):
                for m0 in (0, 8):
                    at = group * M + m0
                    out[m0 : m0 + 8, 2 * group + zi, y, :] = part[at : at + 8, :]


def update(sums, field, status):
    return pl.pallas_call(
        update_kernel,
        out_shape=[
            jax.ShapeDtypeStruct((M, NZ, CY, CX), F32),
            jax.ShapeDtypeStruct((1,), jnp.int32),
        ],
        in_specs=[vspec()] * 3,
        out_specs=[vspec(), smem()],
        compiler_params=params(),
        name="update",
    )(sums, field, status)


def exchange(parts):
    return lax.all_to_all(parts, BOTH, split_axis=0, concat_axis=0, tiled=True)


def move(part, axis, ahead):
    count = lax.axis_size(axis)
    pairs = [(i, i + 1) if ahead else (i + 1, i) for i in range(count - 1)]
    return lax.ppermute(part, axis, pairs)


def on_device(
    state_prior,
    conductivity,
    heat_input,
    owner_tile,
    voxel_list,
    pixel_cell,
    observed,
    pixel_variance,
    pixel_noise,
):
    devices = lax.axis_size("gx") * lax.axis_size("gy")
    pixels = pixel_cell.shape[0]
    gx, gy = lax.axis_index("gx"), lax.axis_index("gy")
    inside = jnp.stack(
        [gx > 0, gx < lax.axis_size("gx") - 1, gy > 0, gy < lax.axis_size("gy") - 1]
    ).astype(F32)
    own, turned_c, to_high, to_low = relayout(state_prior, conductivity)
    own, owner_tile, to_high, to_low = lax.optimization_barrier((own, owner_tile, to_high, to_low))
    low, high = move(to_high, "gy", True), move(to_low, "gy", False)
    incoming = exchange(pack(owner_tile.reshape(-1), heat_input, voxel_list, devices))
    to_left, to_right = sides(own, turned_c, low, high)
    seen = pixel_sums(
        pixel_cell.reshape(1, pixels),
        observed.reshape(1, pixels),
        pixel_variance.reshape(1, pixels),
        pixel_noise,
    )
    incoming, to_left, to_right, inside, *seen = lax.optimization_barrier(
        (incoming, to_left, to_right, inside, *seen)
    )
    left, right = move(to_right, "gx", True), move(to_left, "gx", False)

    heat = deposit(incoming)
    heat_low, heat_high = move(heat, "gy", True), move(heat, "gy", False)
    to_left, to_right = heat_sides(heat_low, heat, heat_high)
    heat_left, heat_right = move(to_right, "gx", True), move(to_left, "gx", False)
    coef = coefs(turned_c, low, high, left, right)
    start, changes, parts = heated(
        inside,
        (own, low, high),
        (left, right),
        (heat_low, heat, heat_high, heat_left, heat_right),
        coef,
        devices,
    )
    field, status = start, jnp.zeros((8, CX), F32)
    for number in range(0, SUBSTEPS - 2, 2):
        field, changes, parts, status = pair(
            number, inside, field, changes, coef, exchange(parts), status
        )
    field, sums, status = last(inside, field, changes, coef, exchange(parts), status, seen)
    result, flag = update(exchange(sums), field, status)

    def again():
        peak = coef * (1.0 + start * start)
        peak = jnp.max(peak[:, HALO : HALO + CY, 8 : XS - 8])
        peaks = jnp.full((devices, 1, CX), peak)
        field = start
        for number in range(SUBSTEPS):
            field, peaks = single(number, inside, field, coef, exchange(peaks), seen)
        return update(exchange(peaks), field, jnp.ones((8, CX), F32))[0]

    return lax.cond(flag[0] > 0, again, lambda: result)


def solution(mesh):
    in_specs = (
        P(None, None, "gy", "gx"),
        P(None, "gy", "gx"),
        P(None, BOTH, None),
        P(BOTH, None),
        P(BOTH, None),
        P(BOTH),
        P(BOTH),
        P(BOTH),
        P(None, BOTH),
    )
    out_specs = P(None, None, "gy", "gx")
    return jax.shard_map(
        on_device, mesh=mesh, in_specs=in_specs, out_specs=out_specs, check_vma=False
    )
```

```python
import functools

import jax
import jax.numpy as jnp
from jax import lax
from jax.experimental import pallas as pl
from jax.experimental.pallas import tpu as pltpu
from jax.sharding import PartitionSpec as P

SUBSTEPS = 6
CAP = 2
COOL = 0.1
SHARE = 0.9
F32 = jnp.float32
BF16 = jnp.bfloat16
VM = pltpu.VMEM
LIMIT = 24 * 1024 * 1024
NT = (((1,), (1,)), ((), ()))
BOTH = ("gx", "gy")

M, NZ, CY, CX = 16, 16, 8, 128
ROWS = 40


def vspec():
    return pl.BlockSpec(memory_space=pltpu.VMEM)


def params():
    return pltpu.CompilerParams(vmem_limit_bytes=LIMIT)


def lanes():
    return lax.broadcasted_iota(jnp.int32, (CY, CX), 1)


def rows():
    return lax.broadcasted_iota(jnp.int32, (CY, CX), 0)


def pack_kernel(owner_far, heat_far, voxel_far, out, owner, heat, voxel, wide, high, low, inverse, sems):
    copies = [
        pltpu.make_async_copy(far, near, sems.at[i])
        for i, (far, near) in enumerate(
            ((owner_far, owner), (heat_far, heat), (voxel_far, voxel))
        )
    ]
    for copy in copies:
        copy.start()
    blocks = owner.shape[0]
    devices = out.shape[0]

    def clear(i, carry):
        inverse[i] = blocks
        return carry

    lax.fori_loop(0, devices * CAP, clear, 0, unroll=16)
    copies[0].wait()

    def place(b, carry):
        base = owner[b] * CAP
        base = base + jnp.where(inverse[base] != blocks, 1, 0)
        inverse[base] = b
        return carry

    lax.fori_loop(0, blocks, place, 0, unroll=8)
    copies[1].wait()
    copies[2].wait()

    def widen(m, carry):
        wide[m, 0:blocks, :] = heat[m].astype(F32)
        wide[m, blocks:, :] = jnp.zeros((8, CX), F32)
        return carry

    lax.fori_loop(0, M, widen, 0)
    cells = voxel[...]
    high[0:blocks, :] = (cells >> 7).astype(F32)
    high[blocks:, :] = jnp.zeros((8, CX), F32)
    low[0:blocks, :] = (cells & 127).astype(F32)
    low[blocks:, :] = jnp.zeros((8, CX), F32)
    row = rows()

    def emit(d, carry):
        first = inverse[d * CAP]
        second = inverse[d * CAP + 1]
        index = jnp.where(
            row == 0,
            high[pl.ds(first, 1), :],
            jnp.where(
                row == 1,
                high[pl.ds(second, 1), :],
                jnp.where(
                    row == 2,
                    low[pl.ds(first, 1), :],
                    jnp.where(row == 3, low[pl.ds(second, 1), :], 0.0),
                ),
            ),
        )
        chunk = jnp.concatenate(
            [
                wide[:, pl.ds(first, 1), :].reshape(M, CX),
                wide[:, pl.ds(second, 1), :].reshape(M, CX),
                index,
            ],
            axis=0,
        )
        out[d] = chunk.astype(BF16)
        return carry

    lax.fori_loop(0, devices, emit, 0, unroll=4)


def pack(owner, heat, voxel, devices):
    blocks = owner.shape[0]
    return pl.pallas_call(
        pack_kernel,
        out_shape=jax.ShapeDtypeStruct((devices, ROWS, CX), BF16),
        in_specs=[pl.BlockSpec(memory_space=pl.ANY)] * 3,
        out_specs=vspec(),
        scratch_shapes=[
            pltpu.SMEM((blocks,), jnp.int32),
            VM((M, blocks, CX), BF16),
            VM((blocks, CX), jnp.int32),
            VM((M, blocks + 8, CX), F32),
            VM((blocks + 8, CX), F32),
            VM((blocks + 8, CX), F32),
            pltpu.SMEM((devices * CAP,), jnp.int32),
            pltpu.SemaphoreType.DMA((3,)),
        ],
        compiler_params=params(),
        name="pack",
    )(owner, heat, voxel)


HALO = 6
YS = CY + 2 * HALO
XT = CX // 8 + 2
ZG = NZ // 2
TOLERANCE = 1e-6
OWN = jax.ShapeDtypeStruct((2, CY, CX, CX), F32)
XS = 8 * XT
WIDE = jax.ShapeDtypeStruct((2, YS, XS, CX), F32)
EDGE = 2 * HALO * (XT - 2)
SIDE = 2 * YS


def relayout_kernel(state, conduct, own, turned_c, to_high, to_low):
    turned = (0.5 * conduct[...].reshape(CX, CX)).T.reshape(XT - 2, 8, CX)
    turned_c[...] = turned
    to_high[EDGE:] = turned
    to_low[EDGE:] = turned
    for zi in range(2):
        for y in range(CY):
            parts = [
                state[m0 : m0 + 8, 2 * group + zi, y, :] for group in range(ZG) for m0 in (0, 8)
            ]
            turned = (0.5 * jnp.concatenate(parts, axis=0)).T
            own[zi, y] = turned
            turned = turned.reshape(XT - 2, 8, CX)
            if y >= CY - HALO:
                at = (zi * HALO + y - (CY - HALO)) * (XT - 2)
                to_high[at : at + XT - 2] = turned
            if y < HALO:
                at = (zi * HALO + y) * (XT - 2)
                to_low[at : at + XT - 2] = turned


def relayout(state, conduct):
    edge = jax.ShapeDtypeStruct((EDGE + XT - 2, 8, CX), F32)
    return pl.pallas_call(
        relayout_kernel,
        out_shape=[OWN, jax.ShapeDtypeStruct((XT - 2, 8, CX), F32), edge, edge],
        in_specs=[vspec()] * 2,
        out_specs=[vspec()] * 4,
        compiler_params=params(),
        name="relayout",
    )(state, conduct)


def side_kernel(own, turned_c, low, high, heat_low, heat_own, heat_high, to_left, to_right):
    for out, t in ((to_left, 0), (to_right, XT - 3)):
        for zi in range(2):
            for y in range(YS):
                if y < HALO:
                    part = low[(zi * HALO + y) * (XT - 2) + t]
                elif y < HALO + CY:
                    part = own[zi, y - HALO, 8 * t : 8 * t + 8, :]
                else:
                    part = high[(zi * HALO + y - HALO - CY) * (XT - 2) + t]
                out[zi * YS + y] = part
        out[SIDE] = low[EDGE + t]
        out[SIDE + 1] = turned_c[t]
        out[SIDE + 2] = high[EDGE + t]
        for g, heat in enumerate((heat_low, heat_own, heat_high)):
            for zi in range(2):
                out[SIDE + 3 + 2 * g + zi] = heat[zi, 8 * t : 8 * t + 8, :]


def sides(own, turned_c, low, high, heat_low, heat_own, heat_high):
    shape = jax.ShapeDtypeStruct((SIDE + 9, 8, CX), F32)
    return pl.pallas_call(
        side_kernel,
        out_shape=[shape, shape],
        in_specs=[vspec()] * 7,
        out_specs=[vspec()] * 2,
        compiler_params=params(),
        name="sides",
    )(own, turned_c, low, high, heat_low, heat_own, heat_high)


def placed(strip, zi, y0):
    source = lax.broadcasted_iota(jnp.int32, (CX, CX), 0)
    target = lax.broadcasted_iota(jnp.int32, (CX, CX), 1)
    hot = jnp.where(source == (2 * (target >> 4) + zi) * CY + y0, 1.0, 0.0).astype(F32)
    return jnp.dot(strip, hot, precision=lax.Precision.HIGHEST, preferred_element_type=F32)


def halo_row(g, y0):
    row = y0 + HALO + (g - 1) * CY
    return row if 0 <= row < YS else None


def coef_kernel(own, low, high, out):
    strip = jnp.concatenate(
        [low[EDGE:].reshape(CX, CX), own[...].reshape(CX, CX), high[EDGE:].reshape(CX, CX)], axis=0
    )
    for zi in range(2):
        for y0 in range(CY):
            part = placed(strip, zi, y0)
            for g in range(3):
                row = halo_row(g, y0)
                if row is not None:
                    out[zi, row] = part[g * CX : (g + 1) * CX, :]


def coefs(own, low, high):
    return pl.pallas_call(
        coef_kernel,
        out_shape=jax.ShapeDtypeStruct((2, YS, CX, CX), F32),
        in_specs=[vspec()] * 3,
        out_specs=vspec(),
        compiler_params=params(),
        name="coefs",
    )(own, low, high)


def deposit_kernel(incoming, out, total):
    sources = incoming.shape[0]
    group = 32
    place = lax.broadcasted_iota(jnp.int32, (CX, CX), 0).astype(F32).astype(BF16)
    zero = jnp.zeros((M, CX), BF16)
    total[...] = jnp.zeros_like(total)

    def one(g, carry):
        left = []
        right = []
        for s in range(group):
            source = g * group + s
            index = incoming[source, 32:40, :].astype(F32)
            for slot in range(CAP):
                heat = incoming[source, slot * M : (slot + 1) * M, :]
                layer = jnp.broadcast_to(index[slot : slot + 1, :], (M, CX)).astype(BF16)
                cell = jnp.broadcast_to(index[2 + slot : 3 + slot, :], (CX, CX)).astype(BF16)
                left.append(
                    jnp.concatenate(
                        [jnp.where(layer == h, heat, zero) for h in range(2 * CY)], axis=0
                    )
                )
                right.append(jnp.where(place == cell, 1.0, 0.0).astype(BF16))
        total[...] += lax.dot_general(
            jnp.concatenate(left, axis=1),
            jnp.concatenate(right, axis=1),
            NT,
            preferred_element_type=F32,
        )
        return carry

    lax.fori_loop(0, sources // group, one, 0)
    for zi in range(2):
        out[zi] = (0.5 * total[zi * CX : (zi + 1) * CX, :]).T


def deposit(incoming):
    return pl.pallas_call(
        deposit_kernel,
        out_shape=jax.ShapeDtypeStruct((2, CX, CX), F32),
        in_specs=[vspec()],
        out_specs=vspec(),
        scratch_shapes=[VM((2 * CY * M, CX), F32)],
        compiler_params=params(),
        name="deposit",
    )(incoming)


def whole_peak(value):
    return jnp.broadcast_to(jnp.max(value, axis=(0, 1), keepdims=True), (8, CX))


def step_of(peak):
    return SHARE / (12.0 * peak + COOL)


def tile(t):
    return slice(8 * t, 8 * t + 8)


def half_conductance(c, u):
    return c + c * (u * u)


def segments(inside, first, end):
    parts = []
    if first < HALO:
        parts.append((first, HALO, False, inside[2]))
    parts.append((max(first, HALO), min(end, HALO + CY), True, None))
    if end > HALO + CY:
        parts.append((HALO + CY, end, False, inside[3]))
    return parts


def mask_of(inside, row_mask, t):
    if t == 0:
        return inside[0] if row_mask is None else inside[0] * row_mask
    if t == XT - 1:
        return inside[1] if row_mask is None else inside[1] * row_mask
    return row_mask


def sweep(field, half, above, inside, first, end, emit, carry):
    lane = lanes()
    row = rows()
    last_row = row == 7
    first_row = row == 0
    inner_lane = lane < CX - M
    cooling = jnp.where(lane < M, COOL, 0.0)

    for zi in range(2):
        for t in range(XT):
            s = tile(t)
            above[zi, t] = (half[zi, first - 1, s, :] + half[zi, first, s, :]) * (
                field[zi, first, s, :] - field[zi, first - 1, s, :]
            )

    def line(own, row_mask, y, state):
        carried = [jnp.zeros((8, CX), F32)] * 2
        for t in range(XT):
            s = tile(t)
            us = [field[zi, y, s, :] for zi in range(2)]
            hs = [half[zi, y, s, :] for zi in range(2)]
            change = []
            for zi in range(2):
                u, h = us[zi], hs[zi]
                if t < XT - 1:
                    after = slice(8 * t + 1, 8 * t + 9)
                    u_after, h_after = field[zi, y, after, :], half[zi, y, after, :]
                else:
                    u_after = jnp.where(last_row, u, pltpu.roll(u, 7, axis=0))
                    h_after = pltpu.roll(h, 7, axis=0)
                along = (h + h_after) * (u_after - u)
                turned = pltpu.roll(along, 1, axis=0)
                total = along - jnp.where(first_row, carried[zi], turned)
                carried[zi] = turned
                across = (h + half[zi, y + 1, s, :]) * (field[zi, y + 1, s, :] - u)
                total = total + (across - above[zi, t])
                above[zi, t] = across
                change.append(total)
            within = (hs[0] + hs[1]) * (us[1] - us[0])
            between = (hs[1] + pltpu.roll(hs[0], CX - M, axis=1)) * (
                pltpu.roll(us[0], CX - M, axis=1) - us[1]
            )
            between = jnp.where(inner_lane, between, 0.0)
            change[0] = change[0] + (within - pltpu.roll(between, M, axis=1)) - cooling * us[0]
            change[1] = change[1] + (between - within)
            state = emit(y, t, us, change, own, mask_of(inside, row_mask, t), state)
        return state

    for start, stop, own, row_mask in segments(inside, first, end):
        carry = lax.fori_loop(start, stop, functools.partial(line, own, row_mask), carry)
    return carry


def advance(field, half, coef, above, inside, step, first, end, put):
    def emit(y, t, us, change, own, mask, peak):
        part = step if mask is None else step * mask
        for zi in range(2):
            value = us[zi] + part * change[zi]
            after = half_conductance(coef[zi, y, tile(t), :], value)
            put(zi, y, t, value, after)
            if own and 0 < t < XT - 1:
                peak = jnp.maximum(peak, after)
        return peak

    return sweep(field, half, above, inside, first, end, emit, jnp.zeros((8, CX), F32))


def propose(field, half, coef, above, inside, guess, first, end, changes, peak, late, out):
    def emit(y, t, us, change, own, mask, best):
        for zi in range(2):
            moved = change[zi] if mask is None else change[zi] * mask
            changes[zi, y, tile(t), :] = moved
            if own and 0 < t < XT - 1:
                c = coef[zi, y, tile(t), :]
                rank = half_conductance(c, us[zi] + guess * moved)
                better = rank > best[0]
                best = tuple(
                    jnp.where(better, new, old)
                    for new, old in zip((rank, us[zi], moved, c), best)
                )
        return best

    best = sweep(
        field, half, above, inside, first, end, emit, (jnp.zeros((8, CX), F32),) * 4
    )
    for shift, axis in ((4, 0), (2, 0), (1, 0), (64, 1), (32, 1)):
        other = tuple(pltpu.roll(part, shift, axis=axis) for part in best)
        better = other[0] > best[0]
        best = tuple(jnp.where(better, new, old) for new, old in zip(other, best))
    part = lanes() >> 4
    chunk = jnp.where(part == 6, whole_peak(peak), whole_peak(late))
    for place, value in ((2, best[3]), (1, best[2]), (0, best[1])):
        chunk = jnp.where((part >> 1) == place, value, chunk)
    for d in range(0, out.shape[0], 8):
        out[d : d + 8, 0, :] = chunk


def agree(parts):
    part = lanes() >> 4
    rows_of = [parts[d : d + 8, 0, :] for d in range(0, parts.shape[0], 8)]
    most = rows_of[0]
    for value in rows_of[1:]:
        most = jnp.maximum(most, value)
    now = whole_peak(jnp.where(part == 6, most, 0.0))
    late = whole_peak(jnp.where(part == 7, most, 0.0))
    step = step_of(now)
    then = jnp.zeros((8, CX), F32)
    for value in rows_of:
        moved = pltpu.roll(value, CX - 32, axis=1)
        c = pltpu.roll(value, CX - 64, axis=1)
        then = jnp.maximum(then, half_conductance(c, value + step * moved))
    return now, whole_peak(jnp.where(part < 2, then, 0.0)), late


def differs(late, used):
    return jnp.where(late > used * (1.0 + TOLERANCE), 1.0, 0.0)


def heated_kernel(
    inside, own, low, high, left, right,
    heat_low, heat_own, heat_high,
    coef_main, out, coef, changes, parts, half, above,
):
    top = lanes() < M
    peak = jnp.zeros((8, CX), F32)

    strip = jnp.concatenate(
        [side[SIDE + g] for g in range(3) for side in (left, right)], axis=0
    )
    for zi in range(2):
        for y0 in range(CY):
            part = placed(strip, zi, y0)
            for g in range(3):
                at = halo_row(g, y0)
                if at is not None:
                    coef[zi, at, tile(0), :] = part[16 * g : 16 * g + 8, :]
                    coef[zi, at, tile(XT - 1), :] = part[16 * g + 8 : 16 * g + 16, :]

    def row(g, heat, tile_of, y0, yy, peak):
        shift = (CX - 16 * y0) % CX
        for zi in range(2):
            for t in range(XT):
                if t == 0:
                    prior, add = left[zi * YS + yy], left[SIDE + 3 + 2 * g + zi]
                elif t == XT - 1:
                    prior, add = right[zi * YS + yy], right[SIDE + 3 + 2 * g + zi]
                else:
                    prior, add = tile_of(zi, t - 1), heat[zi, tile(t - 1), :]
                if shift:
                    add = pltpu.roll(add, shift, axis=1)
                value = prior + jnp.where(top, add, 0.0)
                if 0 < t < XT - 1:
                    c = coef_main[zi, yy, tile(t - 1), :]
                    coef[zi, yy, tile(t), :] = c
                else:
                    c = coef[zi, yy, tile(t), :]
                after = half_conductance(c, value)
                out[zi, yy, tile(t), :] = value
                half[zi, yy, tile(t), :] = after
                if g == 1 and 0 < t < XT - 1:
                    peak = jnp.maximum(peak, after)
        return peak

    def edge(ref, y):
        return lambda zi, t: ref[(zi * HALO + y) * (XT - 2) + t]

    for y in range(HALO):
        row(0, heat_low, edge(low, y), y + CY - HALO, y, peak)
    for y in range(CY):
        peak = row(1, heat_own, lambda zi, t: own[zi, y, tile(t), :], y, y + HALO, peak)
    for y in range(HALO):
        row(2, heat_high, edge(high, y), y, y + HALO + CY, peak)
    guess = step_of(whole_peak(peak))
    zero = jnp.zeros((8, CX), F32)
    propose(out, half, coef, above, inside, guess, 1, YS - 1, changes, peak, zero, parts)


ROW = (2, XT, 8, CX)


def smem():
    return pl.BlockSpec(memory_space=pltpu.SMEM)


def heated(inside, prior, halos, heat, coef, devices):
    operands = [inside, *prior, *halos, *heat, coef]
    return pl.pallas_call(
        heated_kernel,
        out_shape=[WIDE, WIDE, WIDE, jax.ShapeDtypeStruct((devices, 1, CX), F32)],
        in_specs=[smem()] + [vspec()] * (len(operands) - 1),
        out_specs=[vspec()] * 4,
        scratch_shapes=[VM(WIDE.shape, F32), VM(ROW, F32)],
        compiler_params=params(),
        name="heated",
    )(*operands)


def first_of_pair(field, changes, coef, step, first, end, out, half):
    def line(y, peak):
        top = jnp.zeros((8, CX), F32)
        for zi in range(2):
            for t in range(XT):
                value = field[zi, y, tile(t), :] + step * changes[zi, y, tile(t), :]
                after = half_conductance(coef[zi, y, tile(t), :], value)
                out[zi, y, tile(t), :] = value
                half[zi, y, tile(t), :] = after
                if 0 < t < XT - 1:
                    top = jnp.maximum(top, after)
        own = jnp.where((y >= HALO) & (y < HALO + CY), 1.0, 0.0)
        return jnp.maximum(peak, own * top)

    return lax.fori_loop(first, end, line, jnp.zeros((8, CX), F32))


def pair_kernel(
    number, inside, field, changes, coef, parts, status,
    out, out_changes, out_parts, out_status, middle, half, next_half, above,
):
    now, then, late = agree(parts)
    bad = status[1:2, :]
    if number:
        bad = jnp.maximum(bad, differs(late[0:1], status[0:1, :]))
    out_status[...] = jnp.where(rows() == 0, then, bad)
    seen = first_of_pair(
        field, changes, coef, step_of(now), number + 1, YS - 1 - number, middle, half
    )

    def put(zi, y, t, value, after):
        out[zi, y, tile(t), :] = value
        next_half[zi, y, tile(t), :] = after

    step = step_of(then)
    peak = advance(
        middle, half, coef, above, inside, step, number + 2, YS - 2 - number, put
    )
    guess = jnp.minimum(step_of(whole_peak(peak)), 1.2 * step)
    propose(
        out, next_half, coef, above, inside, guess, number + 3, YS - 3 - number,
        out_changes, peak, seen, out_parts,
    )


STATUS = jax.ShapeDtypeStruct((8, CX), F32)


def pair(number, inside, field, changes, coef, parts, status):
    operands = [inside, field, changes, coef, parts, status]
    return pl.pallas_call(
        functools.partial(pair_kernel, number),
        out_shape=[WIDE, WIDE, jax.ShapeDtypeStruct(parts.shape, F32), STATUS],
        in_specs=[smem()] + [vspec()] * 5,
        out_specs=[vspec()] * 4,
        scratch_shapes=[VM(WIDE.shape, F32)] * 3 + [VM(ROW, F32)],
        compiler_params=params(),
        name=f"pair_{number}",
    )(*operands)


def pixel_grams(field, weight, data, flat, late, sums):
    grams = jnp.zeros((M, 2 * M), F32)
    for y in range(CY):
        seen = 2.0 * field[0, y].T[0:M, :]
        for m in range(M):
            flat[m : m + 1, :] = data[m, y : y + 1, :]
        w = weight[y : y + 1, :]
        spread = seen - jnp.mean(seen, axis=0, keepdims=True)
        both = jnp.concatenate([spread * w, flat[...] - seen * w], axis=0)
        grams = grams + lax.dot_general(
            spread, both, NT, precision=lax.Precision.HIGHEST, preferred_element_type=F32
        )
    grams = jnp.concatenate([grams, jnp.zeros((M, CX - 2 * M), F32)], axis=1)
    two = grams[0:8] + pltpu.roll(grams[8:16], 32, axis=1)
    quad = two + pltpu.roll(pltpu.roll(two, 64, axis=1), 4, axis=0)
    quad = jnp.where((rows() == 0) & (lanes() == 1), whole_peak(late), quad)[0:4]
    for d in range(sums.shape[0]):
        sums[d] = quad


def last_kernel(
    inside, field, changes, coef, parts, status, weight, data,
    out, sums, out_status, middle, half, above, flat,
):
    number = SUBSTEPS - 2
    now, then, late = agree(parts)
    bad = jnp.maximum(status[1:2, :], differs(late[0:1], status[0:1, :]))
    out_status[...] = jnp.where(rows() == 0, then, bad)
    seen = first_of_pair(
        field, changes, coef, step_of(now), number + 1, YS - 1 - number, middle, half
    )

    def put(zi, y, t, value, after):
        if 0 < t < XT - 1:
            out[zi, y - HALO, tile(t - 1), :] = value

    advance(middle, half, coef, above, inside, step_of(then), HALO, HALO + CY, put)
    pixel_grams(out, weight, data, flat, seen, sums)


def last(inside, field, changes, coef, parts, status, pixels):
    operands = [inside, field, changes, coef, parts, status, *pixels]
    return pl.pallas_call(
        last_kernel,
        out_shape=[OWN, jax.ShapeDtypeStruct((parts.shape[0], 4, CX), F32), STATUS],
        in_specs=[smem()] + [vspec()] * (len(operands) - 1),
        out_specs=[vspec()] * 3,
        scratch_shapes=[VM(WIDE.shape, F32)] * 2 + [VM(ROW, F32), VM((M, CX), F32)],
        compiler_params=params(),
        name="last_pair",
    )(*operands)


def single_kernel(number, inside, field, coef, peaks, *rest):
    final = number == SUBSTEPS - 1
    if final:
        weight, data, out, sums, half, above, flat = rest
    else:
        out, out_peaks, half, above = rest
    peak = peaks[0]
    for d in range(1, peaks.shape[0]):
        peak = jnp.maximum(peak, peaks[d])
    step = step_of(whole_peak(peak))

    def fill(y, carry):
        for zi in range(2):
            half[zi, y] = half_conductance(coef[zi, y], field[zi, y])
        return carry

    lax.fori_loop(number, YS - number, fill, 0)

    def put(zi, y, t, value, after):
        if not final:
            out[zi, y, tile(t), :] = value
        elif 0 < t < XT - 1:
            out[zi, y - HALO, tile(t - 1), :] = value

    peak = advance(field, half, coef, above, inside, step, number + 1, YS - 1 - number, put)
    if final:
        pixel_grams(out, weight, data, flat, jnp.zeros((8, CX), F32), sums)
    else:
        peak = whole_peak(peak)
        for d in range(0, out_peaks.shape[0], 8):
            out_peaks[d : d + 8, 0, :] = peak


def single(number, inside, field, coef, peaks, pixels):
    devices = peaks.shape[0]
    operands = [inside, field, coef, peaks]
    scratch = [VM(WIDE.shape, F32), VM(ROW, F32)]
    if number == SUBSTEPS - 1:
        operands += list(pixels)
        out_shape = [OWN, jax.ShapeDtypeStruct((devices, 4, CX), F32)]
        scratch += [VM((M, CX), F32)]
    else:
        out_shape = [WIDE, jax.ShapeDtypeStruct((devices, 1, CX), F32)]
    return pl.pallas_call(
        functools.partial(single_kernel, number),
        out_shape=out_shape,
        in_specs=[smem()] + [vspec()] * (len(operands) - 1),
        out_specs=[vspec()] * 2,
        scratch_shapes=scratch,
        compiler_params=params(),
        name=f"single_{number}",
    )(*operands)


def pixel_kernel(cell, observed, variance, noise, weight, data):
    pixels = cell.shape[1]
    place = cell[...]
    var = variance[...]
    inverse = 1.0 / var
    values = (observed[...] + noise[...] * jnp.sqrt(var)) * inverse
    stack = jnp.concatenate([values, jnp.broadcast_to(inverse, (8, pixels))], axis=0)
    width = place >> 7
    hot = jnp.where(
        lax.broadcasted_iota(jnp.int32, (CX, pixels), 0) == (place & 127), 1.0, 0.0
    ).astype(F32)
    for y in range(CY):
        part = lax.dot_general(
            jnp.where(width == y, stack, 0.0),
            hot,
            NT,
            precision=lax.Precision.HIGHEST,
            preferred_element_type=F32,
        )
        weight[y : y + 1, :] = part[M : M + 1, :]
        for m in range(M):
            data[m, y : y + 1, :] = part[m : m + 1, :]


def pixel_sums(cell, observed, variance, noise):
    return pl.pallas_call(
        pixel_kernel,
        out_shape=[
            jax.ShapeDtypeStruct((CY, CX), F32),
            jax.ShapeDtypeStruct((M, CY, CX), F32),
        ],
        in_specs=[vspec()] * 4,
        out_specs=[vspec()] * 2,
        compiler_params=params(),
        name="pixels",
    )(cell, observed, variance, noise)


def update_kernel(sums, field, status, out, flag):
    quad = sums[0]
    late = quad
    for d in range(1, sums.shape[0]):
        quad = quad + sums[d]
        late = jnp.maximum(late, sums[d])
    late = jnp.broadcast_to(late[0:1, 1:2], (1, CX))
    bad = jnp.maximum(status[1:2, :], differs(late, status[0:1, :]))
    flag[0] = jnp.where(jnp.max(bad) > 0.0, 1, 0)
    row = rows()
    quad = jnp.concatenate([quad, jnp.zeros_like(quad)], axis=0)
    pair = jnp.where(row < 4, quad, pltpu.roll(pltpu.roll(quad, 64, axis=1), 4, axis=0))
    system = jnp.concatenate([pair, pltpu.roll(pair, CX - 32, axis=1)], axis=0)
    tall = lax.broadcasted_iota(jnp.int32, (M, CX), 0)
    wide = lax.broadcasted_iota(jnp.int32, (M, CX), 1)
    system = jnp.where(tall == wide, system + (M - 1.0), system)
    mirror = jnp.broadcast_to(system[1:2, 0:1], (M, CX))
    system = jnp.where((tall == 0) & (wide == 1), mirror, system)
    for i in range(M):
        pivot = system[i : i + 1, :]
        pivot = pivot / pivot[:, i : i + 1]
        factor = jnp.where(tall == i, 0.0, jnp.broadcast_to(system[:, i : i + 1], (M, CX)))
        system = jnp.where(tall == i, pivot, system - factor * pivot)
    mixing = system - jnp.mean(system, axis=0, keepdims=True)
    mixing = pltpu.roll(mixing, CX - M, axis=1)
    mixing = jnp.where(wide < M, mixing + jnp.where(tall == wide, 1.0, 0.0), 0.0)
    for shift in (16, 32, 64):
        mixing = mixing + pltpu.roll(mixing, shift, axis=1)
    mixing = jnp.concatenate([mixing] * ZG, axis=0)
    tall = lax.broadcasted_iota(jnp.int32, (CX, CX), 0)
    wide = lax.broadcasted_iota(jnp.int32, (CX, CX), 1)
    mixing = jnp.where((tall >> 4) == (wide >> 4), 2.0 * mixing, 0.0).T
    for zi in range(2):
        for y in range(CY):
            part = lax.dot_general(
                mixing,
                field[zi, y],
                NT,
                precision=lax.Precision.HIGHEST,
                preferred_element_type=F32,
            )
            for group in range(ZG):
                for m0 in (0, 8):
                    at = group * M + m0
                    out[m0 : m0 + 8, 2 * group + zi, y, :] = part[at : at + 8, :]


def update(sums, field, status):
    return pl.pallas_call(
        update_kernel,
        out_shape=[
            jax.ShapeDtypeStruct((M, NZ, CY, CX), F32),
            jax.ShapeDtypeStruct((1,), jnp.int32),
        ],
        in_specs=[vspec()] * 3,
        out_specs=[vspec(), smem()],
        compiler_params=params(),
        name="update",
    )(sums, field, status)


def exchange(parts):
    return lax.all_to_all(parts, BOTH, split_axis=0, concat_axis=0, tiled=True)


def move(part, axis, ahead):
    count = lax.axis_size(axis)
    pairs = [(i, i + 1) if ahead else (i + 1, i) for i in range(count - 1)]
    return lax.ppermute(part, axis, pairs)


def on_device(
    state_prior,
    conductivity,
    heat_input,
    owner_tile,
    voxel_list,
    pixel_cell,
    observed,
    pixel_variance,
    pixel_noise,
):
    devices = lax.axis_size("gx") * lax.axis_size("gy")
    pixels = pixel_cell.shape[0]
    gx, gy = lax.axis_index("gx"), lax.axis_index("gy")
    inside = jnp.stack(
        [gx > 0, gx < lax.axis_size("gx") - 1, gy > 0, gy < lax.axis_size("gy") - 1]
    ).astype(F32)
    incoming = exchange(pack(owner_tile.reshape(-1), heat_input, voxel_list, devices))
    own, turned_c, to_high, to_low = relayout(state_prior, conductivity)
    low, high = move(to_high, "gy", True), move(to_low, "gy", False)
    seen = pixel_sums(
        pixel_cell.reshape(1, pixels),
        observed.reshape(1, pixels),
        pixel_variance.reshape(1, pixels),
        pixel_noise,
    )
    incoming, own, inside, *seen = lax.optimization_barrier((incoming, own, inside, *seen))
    heat = deposit(incoming)
    heat_low, heat_high = move(heat, "gy", True), move(heat, "gy", False)
    to_left, to_right = sides(own, turned_c, low, high, heat_low, heat, heat_high)
    left, right = move(to_right, "gx", True), move(to_left, "gx", False)
    start, coef, changes, parts = heated(
        inside,
        (own, low, high),
        (left, right),
        (heat_low, heat, heat_high),
        coefs(turned_c, low, high),
        devices,
    )
    field, status = start, jnp.zeros((8, CX), F32)
    for number in range(0, SUBSTEPS - 2, 2):
        field, changes, parts, status = pair(
            number, inside, field, changes, coef, exchange(parts), status
        )
    field, sums, status = last(inside, field, changes, coef, exchange(parts), status, seen)
    result, flag = update(exchange(sums), field, status)

    def again():
        peak = coef * (1.0 + start * start)
        peak = jnp.max(peak[:, HALO : HALO + CY, 8 : XS - 8])
        peaks = jnp.full((devices, 1, CX), peak)
        field = start
        for number in range(SUBSTEPS):
            field, peaks = single(number, inside, field, coef, exchange(peaks), seen)
        return update(exchange(peaks), field, jnp.ones((8, CX), F32))[0]

    return lax.cond(flag[0] > 0, again, lambda: result)


def solution(mesh):
    in_specs = (
        P(None, None, "gy", "gx"),
        P(None, "gy", "gx"),
        P(None, BOTH, None),
        P(BOTH, None),
        P(BOTH, None),
        P(BOTH),
        P(BOTH),
        P(BOTH),
        P(None, BOTH),
    )
    out_specs = P(None, None, "gy", "gx")
    return jax.shard_map(
        on_device, mesh=mesh, in_specs=in_specs, out_specs=out_specs, check_vma=False
    )
```

```python
import functools

import jax
import jax.numpy as jnp
from jax import lax
from jax.experimental import pallas as pl
from jax.experimental.pallas import tpu as pltpu
from jax.sharding import PartitionSpec as P

SUBSTEPS = 6
CAP = 2
COOL = 0.1
SHARE = 0.9
F32 = jnp.float32
BF16 = jnp.bfloat16
VM = pltpu.VMEM
LIMIT = 32 * 1024 * 1024
NT = (((1,), (1,)), ((), ()))
BOTH = ("gx", "gy")

M, NZ, CY, CX = 16, 16, 8, 128
ROWS = 40


def vspec():
    return pl.BlockSpec(memory_space=pltpu.VMEM)


def params():
    return pltpu.CompilerParams(vmem_limit_bytes=LIMIT)


def lanes():
    return lax.broadcasted_iota(jnp.int32, (CY, CX), 1)


def rows():
    return lax.broadcasted_iota(jnp.int32, (CY, CX), 0)


def pack_kernel(owner_far, heat_far, voxel_far, out, owner, heat, voxel, wide, high, low, inverse, sems):
    copies = [
        pltpu.make_async_copy(far, near, sems.at[i])
        for i, (far, near) in enumerate(
            ((owner_far, owner), (heat_far, heat), (voxel_far, voxel))
        )
    ]
    for copy in copies:
        copy.start()
    blocks = owner.shape[0]
    devices = out.shape[0]

    def clear(i, carry):
        inverse[i] = blocks
        return carry

    lax.fori_loop(0, devices * CAP, clear, 0, unroll=16)
    copies[0].wait()

    def place(b, carry):
        base = owner[b] * CAP
        base = base + jnp.where(inverse[base] != blocks, 1, 0)
        inverse[base] = b
        return carry

    lax.fori_loop(0, blocks, place, 0, unroll=8)
    copies[1].wait()
    copies[2].wait()

    def widen(m, carry):
        wide[m, 0:blocks, :] = heat[m].astype(F32)
        wide[m, blocks:, :] = jnp.zeros((8, CX), F32)
        return carry

    lax.fori_loop(0, M, widen, 0)
    cells = voxel[...]
    high[0:blocks, :] = (cells >> 7).astype(F32)
    high[blocks:, :] = jnp.zeros((8, CX), F32)
    low[0:blocks, :] = (cells & 127).astype(F32)
    low[blocks:, :] = jnp.zeros((8, CX), F32)
    row = rows()

    def emit(d, carry):
        first = inverse[d * CAP]
        second = inverse[d * CAP + 1]
        index = jnp.where(
            row == 0,
            high[pl.ds(first, 1), :],
            jnp.where(
                row == 1,
                high[pl.ds(second, 1), :],
                jnp.where(
                    row == 2,
                    low[pl.ds(first, 1), :],
                    jnp.where(row == 3, low[pl.ds(second, 1), :], 0.0),
                ),
            ),
        )
        chunk = jnp.concatenate(
            [
                wide[:, pl.ds(first, 1), :].reshape(M, CX),
                wide[:, pl.ds(second, 1), :].reshape(M, CX),
                index,
            ],
            axis=0,
        )
        out[d] = chunk.astype(BF16)
        return carry

    lax.fori_loop(0, devices, emit, 0, unroll=4)


def pack(owner, heat, voxel, devices):
    blocks = owner.shape[0]
    return pl.pallas_call(
        pack_kernel,
        out_shape=jax.ShapeDtypeStruct((devices, ROWS, CX), BF16),
        in_specs=[pl.BlockSpec(memory_space=pltpu.HBM)] * 3,
        out_specs=vspec(),
        scratch_shapes=[
            pltpu.SMEM((blocks,), jnp.int32),
            VM((M, blocks, CX), BF16),
            VM((blocks, CX), jnp.int32),
            VM((M, blocks + 8, CX), F32),
            VM((blocks + 8, CX), F32),
            VM((blocks + 8, CX), F32),
            pltpu.SMEM((devices * CAP,), jnp.int32),
            pltpu.SemaphoreType.DMA((3,)),
        ],
        compiler_params=params(),
        name="pack",
    )(owner, heat, voxel)


HALO = 6
YS = CY + 2 * HALO
XT = CX // 8 + 2
ZG = NZ // 2
TOLERANCE = 1e-6
OWN = jax.ShapeDtypeStruct((2, CY, CX, CX), F32)
XS = 8 * XT
WIDE = jax.ShapeDtypeStruct((2, YS, XS, CX), F32)
EDGE = 2 * HALO * (XT - 2)
SIDE = 2 * YS


def relayout_kernel(
    state, conduct, own, turned_c, to_high, to_low, edge_left, edge_right, top, quiet
):
    turned = (0.5 * conduct[...].reshape(CX, CX)).T.reshape(XT - 2, 8, CX)
    turned_c[...] = turned
    to_high[EDGE:] = turned
    to_low[EDGE:] = turned
    peak = jnp.zeros((8, CX), F32)
    for zi in range(2):
        for y in range(CY):
            parts = []
            for group in range(ZG):
                layer = 2 * group + zi
                c = 0.5 * conduct[layer, y : y + 1, :]
                for m0 in (0, 8):
                    part = 0.5 * state[m0 : m0 + 8, layer, y, :]
                    parts.append(part)
                    if group:
                        peak = jnp.maximum(peak, c + c * (part * part))
            turned = jnp.concatenate(parts, axis=0).T
            own[zi, y] = turned
            turned = turned.reshape(XT - 2, 8, CX)
            edge_left[zi * CY + y] = turned[0]
            edge_right[zi * CY + y] = turned[XT - 3]
            if y >= CY - HALO:
                at = (zi * HALO + y - (CY - HALO)) * (XT - 2)
                to_high[at : at + XT - 2] = turned
            if y < HALO:
                at = (zi * HALO + y) * (XT - 2)
                to_low[at : at + XT - 2] = turned
    quiet[...] = peak
    for m in range(M):
        for zi in range(2):
            top[m, zi] = 0.5 * state[m, zi]


def relayout(state, conduct):
    edge = jax.ShapeDtypeStruct((EDGE + XT - 2, 8, CX), F32)
    side = jax.ShapeDtypeStruct((2 * CY, 8, CX), F32)
    return pl.pallas_call(
        relayout_kernel,
        out_shape=[
            OWN,
            jax.ShapeDtypeStruct((XT - 2, 8, CX), F32),
            edge,
            edge,
            side,
            side,
            jax.ShapeDtypeStruct((M, 2, CY, CX), F32),
            jax.ShapeDtypeStruct((8, CX), F32),
        ],
        in_specs=[vspec()] * 2,
        out_specs=[vspec()] * 8,
        compiler_params=params(),
        name="relayout",
    )(state, conduct)


def side_kernel(
    edge_left, edge_right, turned_c, low, high, heat_low, heat_own, heat_high, to_left, to_right
):
    for out, edge, t in ((to_left, edge_left, 0), (to_right, edge_right, XT - 3)):
        for zi in range(2):
            for y in range(YS):
                if y < HALO:
                    part = low[(zi * HALO + y) * (XT - 2) + t]
                elif y < HALO + CY:
                    part = edge[zi * CY + y - HALO]
                else:
                    part = high[(zi * HALO + y - HALO - CY) * (XT - 2) + t]
                out[zi * YS + y] = part
        out[SIDE] = low[EDGE + t]
        out[SIDE + 1] = turned_c[t]
        out[SIDE + 2] = high[EDGE + t]
        for g, heat in enumerate((heat_low, heat_own, heat_high)):
            for zi in range(2):
                out[SIDE + 3 + 2 * g + zi] = heat[zi, 8 * t : 8 * t + 8, :]


def sides(*operands):
    shape = jax.ShapeDtypeStruct((SIDE + 9, 8, CX), F32)
    return pl.pallas_call(
        side_kernel,
        out_shape=[shape, shape],
        in_specs=[vspec()] * len(operands),
        out_specs=[vspec()] * 2,
        compiler_params=params(),
        name="sides",
    )(*operands)


def placed(strip, zi, y0):
    source = lax.broadcasted_iota(jnp.int32, (CX, CX), 0)
    target = lax.broadcasted_iota(jnp.int32, (CX, CX), 1)
    hot = jnp.where(source == (2 * (target >> 4) + zi) * CY + y0, 1.0, 0.0).astype(F32)
    return jnp.dot(strip, hot, precision=lax.Precision.HIGHEST, preferred_element_type=F32)


def halo_row(g, y0):
    row = y0 + HALO + (g - 1) * CY
    return row if 0 <= row < YS else None


def coef_kernel(own, low, high, out):
    strip = jnp.concatenate(
        [low[EDGE:].reshape(CX, CX), own[...].reshape(CX, CX), high[EDGE:].reshape(CX, CX)], axis=0
    )
    for zi in range(2):
        for y0 in range(CY):
            part = placed(strip, zi, y0)
            for g in range(3):
                row = halo_row(g, y0)
                if row is not None:
                    out[zi, row] = part[g * CX : (g + 1) * CX, :]


def coefs(own, low, high):
    return pl.pallas_call(
        coef_kernel,
        out_shape=jax.ShapeDtypeStruct((2, YS, CX, CX), F32),
        in_specs=[vspec()] * 3,
        out_specs=vspec(),
        compiler_params=params(),
        name="coefs",
    )(own, low, high)


def deposit_kernel(incoming, top, conduct, quiet, out, peaks, total):
    sources = incoming.shape[0]
    group = 32
    place = lax.broadcasted_iota(jnp.int32, (CX, CX), 0).astype(F32).astype(BF16)
    zero = jnp.zeros((M, CX), BF16)
    total[...] = jnp.zeros_like(total)

    def one(g, carry):
        left = []
        right = []
        for s in range(group):
            source = g * group + s
            index = incoming[source, 32:40, :].astype(F32)
            for slot in range(CAP):
                heat = incoming[source, slot * M : (slot + 1) * M, :]
                layer = jnp.broadcast_to(index[slot : slot + 1, :], (M, CX)).astype(BF16)
                cell = jnp.broadcast_to(index[2 + slot : 3 + slot, :], (CX, CX)).astype(BF16)
                left.append(
                    jnp.concatenate(
                        [jnp.where(layer == h, heat, zero) for h in range(2 * CY)], axis=0
                    )
                )
                right.append(jnp.where(place == cell, 1.0, 0.0).astype(BF16))
        total[...] += lax.dot_general(
            jnp.concatenate(left, axis=1),
            jnp.concatenate(right, axis=1),
            NT,
            preferred_element_type=F32,
        )
        return carry

    lax.fori_loop(0, sources // group, one, 0)
    for zi in range(2):
        out[zi] = (0.5 * total[zi * CX : (zi + 1) * CX, :]).T
    peak = quiet[...]
    for zi in range(2):
        c = 0.5 * conduct[zi]
        for m in range(M):
            value = top[m, zi] + 0.5 * total[pl.ds(zi * CX + m, CY, stride=M), :]
            peak = jnp.maximum(peak, c + c * (value * value))
    send_row(whole_peak(peak), peaks)


def send_row(row, out):
    for d in range(0, out.shape[0], 8):
        out[d : d + 8, 0, :] = row


def deposit(incoming, top, conduct, quiet):
    devices = incoming.shape[0]
    return pl.pallas_call(
        deposit_kernel,
        out_shape=[
            jax.ShapeDtypeStruct((2, CX, CX), F32),
            jax.ShapeDtypeStruct((devices, 1, CX), F32),
        ],
        in_specs=[vspec()] * 4,
        out_specs=[vspec()] * 2,
        scratch_shapes=[VM((2 * CY * M, CX), F32)],
        compiler_params=params(),
        name="deposit",
    )(incoming, top, conduct, quiet)


def whole_peak(value):
    return jnp.broadcast_to(jnp.max(value, axis=(0, 1), keepdims=True), (8, CX))


def step_of(peak):
    return SHARE / (12.0 * peak + COOL)


def tile(t):
    return slice(8 * t, 8 * t + 8)


def half_conductance(c, u):
    return c + c * (u * u)


def segments(inside, first, end):
    parts = []
    if first < HALO:
        parts.append((first, HALO, False, inside[2]))
    parts.append((max(first, HALO), min(end, HALO + CY), True, None))
    if end > HALO + CY:
        parts.append((HALO + CY, end, False, inside[3]))
    return parts


def mask_of(inside, row_mask, t):
    if t == 0:
        return inside[0] if row_mask is None else inside[0] * row_mask
    if t == XT - 1:
        return inside[1] if row_mask is None else inside[1] * row_mask
    return row_mask


def sweep(field, half, above, inside, first, end, emit, carry):
    lane = lanes()
    row = rows()
    last_row = row == 7
    first_row = row == 0
    inner_lane = lane < CX - M
    cooling = jnp.where(lane < M, COOL, 0.0)

    for zi in range(2):
        for t in range(XT):
            s = tile(t)
            above[zi, t] = (half[zi, first - 1, s, :] + half[zi, first, s, :]) * (
                field[zi, first, s, :] - field[zi, first - 1, s, :]
            )

    def line(own, row_mask, y, state):
        carried = [jnp.zeros((8, CX), F32)] * 2
        for t in range(XT):
            s = tile(t)
            us = [field[zi, y, s, :] for zi in range(2)]
            hs = [half[zi, y, s, :] for zi in range(2)]
            change = []
            for zi in range(2):
                u, h = us[zi], hs[zi]
                if t < XT - 1:
                    after = slice(8 * t + 1, 8 * t + 9)
                    u_after, h_after = field[zi, y, after, :], half[zi, y, after, :]
                else:
                    u_after = jnp.where(last_row, u, pltpu.roll(u, 7, axis=0))
                    h_after = pltpu.roll(h, 7, axis=0)
                along = (h + h_after) * (u_after - u)
                turned = pltpu.roll(along, 1, axis=0)
                total = along - jnp.where(first_row, carried[zi], turned)
                carried[zi] = turned
                across = (h + half[zi, y + 1, s, :]) * (field[zi, y + 1, s, :] - u)
                total = total + (across - above[zi, t])
                above[zi, t] = across
                change.append(total)
            within = (hs[0] + hs[1]) * (us[1] - us[0])
            between = (hs[1] + pltpu.roll(hs[0], CX - M, axis=1)) * (
                pltpu.roll(us[0], CX - M, axis=1) - us[1]
            )
            between = jnp.where(inner_lane, between, 0.0)
            change[0] = change[0] + (within - pltpu.roll(between, M, axis=1)) - cooling * us[0]
            change[1] = change[1] + (between - within)
            state = emit(y, t, us, change, own, mask_of(inside, row_mask, t), state)
        return state

    for start, stop, own, row_mask in segments(inside, first, end):
        carry = lax.fori_loop(start, stop, functools.partial(line, own, row_mask), carry)
    return carry


def advance(field, half, coef, above, inside, step, first, end, put):
    def emit(y, t, us, change, own, mask, peak):
        part = step if mask is None else step * mask
        for zi in range(2):
            value = us[zi] + part * change[zi]
            after = half_conductance(coef[zi, y, tile(t), :], value)
            put(zi, y, t, value, after)
            if own and 0 < t < XT - 1:
                peak = jnp.maximum(peak, after)
        return peak

    return sweep(field, half, above, inside, first, end, emit, jnp.zeros((8, CX), F32))


def propose(field, half, coef, above, inside, guess, first, end, changes, peak, late, out):
    def emit(y, t, us, change, own, mask, best):
        for zi in range(2):
            moved = change[zi] if mask is None else change[zi] * mask
            changes[zi, y, tile(t), :] = moved
            if own and 0 < t < XT - 1:
                c = coef[zi, y, tile(t), :]
                rank = half_conductance(c, us[zi] + guess * moved)
                better = rank > best[0]
                best = tuple(
                    jnp.where(better, new, old)
                    for new, old in zip((rank, us[zi], moved, c), best)
                )
        return best

    best = sweep(
        field, half, above, inside, first, end, emit, (jnp.zeros((8, CX), F32),) * 4
    )
    for shift, axis in ((4, 0), (2, 0), (1, 0), (64, 1), (32, 1)):
        other = tuple(pltpu.roll(part, shift, axis=axis) for part in best)
        better = other[0] > best[0]
        best = tuple(jnp.where(better, new, old) for new, old in zip(other, best))
    part = lanes() >> 4
    chunk = jnp.where(part == 6, whole_peak(peak), whole_peak(late))
    for place, value in ((2, best[3]), (1, best[2]), (0, best[1])):
        chunk = jnp.where((part >> 1) == place, value, chunk)
    send_row(chunk, out)


def gather_rows(parts):
    return [parts[d : d + 8, 0, :] for d in range(0, parts.shape[0], 8)]


def largest(values):
    most = values[0]
    for value in values[1:]:
        most = jnp.maximum(most, value)
    return most


def agree(parts):
    part = lanes() >> 4
    rows_of = gather_rows(parts)
    most = largest(rows_of)
    now = whole_peak(jnp.where(part == 6, most, 0.0))
    late = whole_peak(jnp.where(part == 7, most, 0.0))
    step = step_of(now)
    then = jnp.zeros((8, CX), F32)
    for value in rows_of:
        moved = pltpu.roll(value, CX - 32, axis=1)
        c = pltpu.roll(value, CX - 64, axis=1)
        then = jnp.maximum(then, half_conductance(c, value + step * moved))
    return now, whole_peak(jnp.where(part < 2, then, 0.0)), late


def differs(late, used):
    return jnp.where(late > used * (1.0 + TOLERANCE), 1.0, 0.0)


def heated_kernel(
    inside, own, low, high, left, right,
    heat_low, heat_own, heat_high,
    coef_main, peaks, out, coef, changes, parts, start, half, next_half, above,
):
    top = lanes() < M

    strip = jnp.concatenate(
        [side[SIDE + g] for g in range(3) for side in (left, right)], axis=0
    )
    for zi in range(2):
        for y0 in range(CY):
            part = placed(strip, zi, y0)
            for g in range(3):
                at = halo_row(g, y0)
                if at is not None:
                    coef[zi, at, tile(0), :] = part[16 * g : 16 * g + 8, :]
                    coef[zi, at, tile(XT - 1), :] = part[16 * g + 8 : 16 * g + 16, :]

    def row(g, heat, tile_of, y0, yy):
        shift = (CX - 16 * y0) % CX
        for zi in range(2):
            for t in range(XT):
                if t == 0:
                    prior, add = left[zi * YS + yy], left[SIDE + 3 + 2 * g + zi]
                elif t == XT - 1:
                    prior, add = right[zi * YS + yy], right[SIDE + 3 + 2 * g + zi]
                else:
                    prior, add = tile_of(zi, t - 1), heat[zi, tile(t - 1), :]
                if shift:
                    add = pltpu.roll(add, shift, axis=1)
                value = prior + jnp.where(top, add, 0.0)
                if 0 < t < XT - 1:
                    c = coef_main[zi, yy, tile(t - 1), :]
                    coef[zi, yy, tile(t), :] = c
                else:
                    c = coef[zi, yy, tile(t), :]
                after = half_conductance(c, value)
                start[zi, yy, tile(t), :] = value
                half[zi, yy, tile(t), :] = after

    def edge(ref, y):
        return lambda zi, t: ref[(zi * HALO + y) * (XT - 2) + t]

    for y in range(HALO):
        row(0, heat_low, edge(low, y), y + CY - HALO, y)
    for y in range(CY):
        row(1, heat_own, lambda zi, t: own[zi, y, tile(t), :], y, y + HALO)
    for y in range(HALO):
        row(2, heat_high, edge(high, y), y, y + HALO + CY)

    def put(zi, y, t, value, after):
        out[zi, y, tile(t), :] = value
        next_half[zi, y, tile(t), :] = after

    step = step_of(whole_peak(largest(gather_rows(peaks))))
    peak = advance(start, half, coef, above, inside, step, 1, YS - 1, put)
    guess = jnp.minimum(step_of(whole_peak(peak)), 2.0 * step)
    zero = jnp.zeros((8, CX), F32)
    propose(
        out, next_half, coef, above, inside, guess, 2, YS - 2, changes, peak, zero, parts
    )


ROW = (2, XT, 8, CX)


def smem():
    return pl.BlockSpec(memory_space=pltpu.SMEM)


def heated(inside, prior, halos, heat, coef, peaks):
    operands = [inside, *prior, *halos, *heat, coef, peaks]
    return pl.pallas_call(
        heated_kernel,
        out_shape=[WIDE, WIDE, WIDE, jax.ShapeDtypeStruct(peaks.shape, F32)],
        in_specs=[smem()] + [vspec()] * (len(operands) - 1),
        out_specs=[vspec()] * 4,
        scratch_shapes=[VM(WIDE.shape, F32)] * 3 + [VM(ROW, F32)],
        compiler_params=params(),
        name="heated",
    )(*operands)


def first_of_pair(field, changes, coef, step, first, end, out, half):
    def line(y, peak):
        top = jnp.zeros((8, CX), F32)
        for zi in range(2):
            for t in range(XT):
                value = field[zi, y, tile(t), :] + step * changes[zi, y, tile(t), :]
                after = half_conductance(coef[zi, y, tile(t), :], value)
                out[zi, y, tile(t), :] = value
                half[zi, y, tile(t), :] = after
                if 0 < t < XT - 1:
                    top = jnp.maximum(top, after)
        own = jnp.where((y >= HALO) & (y < HALO + CY), 1.0, 0.0)
        return jnp.maximum(peak, own * top)

    return lax.fori_loop(first, end, line, jnp.zeros((8, CX), F32))


def pair_kernel(
    number, inside, field, changes, coef, parts,
    out, out_changes, out_parts, status, middle, half, next_half, above,
):
    now, then, _ = agree(parts)
    status[...] = jnp.where(rows() == 0, then, 0.0)
    seen = first_of_pair(
        field, changes, coef, step_of(now), number + 1, YS - 1 - number, middle, half
    )

    def put(zi, y, t, value, after):
        out[zi, y, tile(t), :] = value
        next_half[zi, y, tile(t), :] = after

    step = step_of(then)
    peak = advance(
        middle, half, coef, above, inside, step, number + 2, YS - 2 - number, put
    )
    guess = jnp.minimum(step_of(whole_peak(peak)), 1.2 * step)
    propose(
        out, next_half, coef, above, inside, guess, number + 3, YS - 3 - number,
        out_changes, peak, seen, out_parts,
    )


STATUS = jax.ShapeDtypeStruct((8, CX), F32)


def pair(number, inside, field, changes, coef, parts):
    operands = [inside, field, changes, coef, parts]
    return pl.pallas_call(
        functools.partial(pair_kernel, number),
        out_shape=[WIDE, WIDE, jax.ShapeDtypeStruct(parts.shape, F32), STATUS],
        in_specs=[smem()] + [vspec()] * 4,
        out_specs=[vspec()] * 4,
        scratch_shapes=[VM(WIDE.shape, F32)] * 3 + [VM(ROW, F32)],
        compiler_params=params(),
        name=f"pair_{number}",
    )(*operands)


def closing(
    field, half, above, inside, weight, data, peak, late, out, out_changes, sums, flat
):
    def emit(y, t, us, change, own, mask, state):
        if 0 < t < XT - 1:
            for zi in range(2):
                out[zi, y - HALO, tile(t - 1), :] = us[zi]
                out_changes[zi, y - HALO, tile(t - 1), :] = change[zi]
        return state

    sweep(field, half, above, inside, HALO, HALO + CY, emit, 0)
    grams = jnp.zeros((5 * CY, 3 * M), F32)
    for y in range(CY):
        w = weight[y : y + 1, :]
        for m in range(M):
            flat[m : m + 1, :] = data[m, y : y + 1, :]
        means = []
        spreads = []
        for part in (out, out_changes):
            seen = 2.0 * part[0, y].T[0:M, :]
            mean = jnp.mean(seen, axis=0, keepdims=True)
            means.append(mean)
            spreads.append(seen - mean)
        left = jnp.concatenate(spreads + means + [jnp.zeros((6, CX), F32)], axis=0)
        right = jnp.concatenate([part * w for part in spreads] + [flat[...]], axis=0)
        grams = grams + lax.dot_general(
            left, right, NT, precision=lax.Precision.HIGHEST, preferred_element_type=F32
        )
    grams = jnp.concatenate([grams, jnp.zeros((5 * CY, CX - 3 * M), F32)], axis=1)
    tall = lax.broadcasted_iota(jnp.int32, (M, CX), 0)
    wide = lax.broadcasted_iota(jnp.int32, (M, CX), 1)
    first, second, means = grams[0:M], grams[M : 2 * M], grams[2 * M : 2 * M + 8]

    def block(part, at):
        return jnp.where(wide < M, pltpu.roll(part, (CX - M * at) % CX, axis=1), 0.0)

    def lone(part, row, at):
        moved = pltpu.roll(part, (CX - M * at) % CX, axis=1) if at else part
        return jnp.broadcast_to(moved[row : row + 1, :], (M, CX))

    tops = [
        lone(means, 0, 1) + lone(means, 1, 0),
        lone(means, 0, 0),
        lone(means, 1, 1),
    ]
    blocks = [
        jnp.where(tall < wide, block(first, 0), block(second, 1)),
        block(first, 1) + block(second, 0),
        block(first, 2),
        block(second, 2),
    ]
    scalar = jnp.where(wide == 0, whole_peak(peak)[0:1], whole_peak(late)[0:1])
    blocks[0] = jnp.where(tall == wide, scalar, blocks[0])
    for i, top in enumerate(tops):
        blocks[i + 1] = jnp.where(tall == 0, jnp.where(wide < M, top, 0.0), blocks[i + 1])
    packed = blocks[0]
    for i in range(1, 4):
        packed = packed + pltpu.roll(blocks[i], M * i, axis=1)
    packed = packed[0:8] + pltpu.roll(packed[8:16], CX // 2, axis=1)
    for d in range(sums.shape[0]):
        sums[d] = packed


def last_kernel(
    inside, field, changes, coef, parts, status, weight, data,
    out, out_changes, sums, out_status, middle, half, near, near_half, above, flat,
):
    number = SUBSTEPS - 3
    now, then, late = agree(parts)
    bad = differs(late[0:1], status[0:1, :])
    out_status[...] = jnp.where(rows() == 0, then, bad)
    seen = first_of_pair(
        field, changes, coef, step_of(now), number + 1, YS - 1 - number, middle, half
    )

    def put(zi, y, t, value, after):
        near[zi, y, tile(t), :] = value
        near_half[zi, y, tile(t), :] = after

    peak = advance(
        middle, half, coef, above, inside, step_of(then), number + 2, YS - 2 - number, put
    )
    closing(
        near, near_half, above, inside, weight, data, peak, seen, out, out_changes, sums, flat
    )


def sums_shape(devices):
    return jax.ShapeDtypeStruct((devices, 8, CX), F32)


def last(inside, field, changes, coef, parts, status, pixels):
    operands = [inside, field, changes, coef, parts, status, *pixels]
    return pl.pallas_call(
        last_kernel,
        out_shape=[OWN, OWN, sums_shape(parts.shape[0]), STATUS],
        in_specs=[smem()] + [vspec()] * (len(operands) - 1),
        out_specs=[vspec()] * 4,
        scratch_shapes=[VM(WIDE.shape, F32)] * 4 + [VM(ROW, F32), VM((M, CX), F32)],
        compiler_params=params(),
        name="last_pair",
    )(*operands)


def fill_half(field, coef, half, first, end):
    def fill(y, carry):
        for zi in range(2):
            half[zi, y] = half_conductance(coef[zi, y], field[zi, y])
        return carry

    lax.fori_loop(first, end, fill, 0)


def single_kernel(number, inside, field, coef, peaks, out, out_peaks, half, above):
    step = step_of(whole_peak(largest(gather_rows(peaks))))
    fill_half(field, coef, half, number, YS - number)

    def put(zi, y, t, value, after):
        out[zi, y, tile(t), :] = value

    peak = advance(field, half, coef, above, inside, step, number + 1, YS - 1 - number, put)
    send_row(whole_peak(peak), out_peaks)


def single(number, inside, field, coef, peaks):
    return pl.pallas_call(
        functools.partial(single_kernel, number),
        out_shape=[WIDE, jax.ShapeDtypeStruct(peaks.shape, F32)],
        in_specs=[smem()] + [vspec()] * 3,
        out_specs=[vspec()] * 2,
        scratch_shapes=[VM(WIDE.shape, F32), VM(ROW, F32)],
        compiler_params=params(),
        name=f"single_{number}",
    )(inside, field, coef, peaks)


def closing_kernel(
    inside, field, coef, peaks, weight, data, out, out_changes, sums, half, above, flat
):
    fill_half(field, coef, half, HALO - 1, HALO + CY + 1)
    peak = peaks[0:8, 0, :]
    closing(
        field, half, above, inside, weight, data, peak, jnp.zeros((8, CX), F32),
        out, out_changes, sums, flat,
    )


def close(inside, field, coef, peaks, pixels):
    operands = [inside, field, coef, peaks, *pixels]
    return pl.pallas_call(
        closing_kernel,
        out_shape=[OWN, OWN, sums_shape(peaks.shape[0])],
        in_specs=[smem()] + [vspec()] * (len(operands) - 1),
        out_specs=[vspec()] * 3,
        scratch_shapes=[VM(WIDE.shape, F32), VM(ROW, F32), VM((M, CX), F32)],
        compiler_params=params(),
        name="closing",
    )(*operands)


def pixel_kernel(cell, observed, variance, noise, weight, data):
    pixels = cell.shape[1]
    place = cell[...]
    var = variance[...]
    inverse = 1.0 / var
    values = (observed[...] + noise[...] * jnp.sqrt(var)) * inverse
    stack = jnp.concatenate([values, jnp.broadcast_to(inverse, (8, pixels))], axis=0)
    width = place >> 7
    hot = jnp.where(
        lax.broadcasted_iota(jnp.int32, (CX, pixels), 0) == (place & 127), 1.0, 0.0
    ).astype(F32)
    for y in range(CY):
        part = lax.dot_general(
            jnp.where(width == y, stack, 0.0),
            hot,
            NT,
            precision=lax.Precision.HIGHEST,
            preferred_element_type=F32,
        )
        weight[y : y + 1, :] = part[M : M + 1, :]
        for m in range(M):
            data[m, y : y + 1, :] = part[m : m + 1, :]


def pixel_sums(cell, observed, variance, noise):
    return pl.pallas_call(
        pixel_kernel,
        out_shape=[
            jax.ShapeDtypeStruct((CY, CX), F32),
            jax.ShapeDtypeStruct((M, CY, CX), F32),
        ],
        in_specs=[vspec()] * 4,
        out_specs=[vspec()] * 2,
        compiler_params=params(),
        name="pixels",
    )(cell, observed, variance, noise)


def update_kernel(sums, field, changes, status, out, flag):
    total = sums[0]
    most = total
    for d in range(1, sums.shape[0]):
        total = total + sums[d]
        most = jnp.maximum(most, sums[d])
    step = step_of(jnp.broadcast_to(most[0:1, 0:1], (1, CX)))
    late = jnp.broadcast_to(most[1:2, 1:2], (1, CX))
    bad = jnp.maximum(status[1:2, :], differs(late, status[0:1, :]))
    flag[0] = jnp.where(jnp.max(bad) > 0.0, 1, 0)

    tall = lax.broadcasted_iota(jnp.int32, (M, CX), 0)
    wide = lax.broadcasted_iota(jnp.int32, (M, CX), 1)
    packed = jnp.concatenate([total, pltpu.roll(total, CX // 2, axis=1)], axis=0)

    def block(at):
        return jnp.where(wide < M, pltpu.roll(packed, (CX - M * at) % CX, axis=1), 0.0)

    def whole(part):
        rest = jnp.where(tall == 0, 0.0, part)
        first = -jnp.sum(rest, axis=0, keepdims=True)
        return jnp.where(tall == 0, first, rest), part[0:1, :]

    def balanced(part):
        part = jnp.where((tall == wide) | (wide >= M), 0.0, part)
        return jnp.where(tall == wide, -jnp.sum(part, axis=1, keepdims=True), part)

    corner = block(0)
    mirror = jnp.concatenate([corner, jnp.zeros((CX - M, CX), F32)], axis=0).T[0:M, :]
    square = balanced(jnp.where(tall < wide, corner, mirror))
    square_c = balanced(jnp.where(tall > wide, corner, mirror))
    mixed, mean_1 = whole(block(1))
    data, mean_0 = whole(block(2))
    data_c, mean_2 = whole(block(3))
    cross = square + step * (mixed + step * square_c)
    mean = mean_0 + step * (mean_1 + step * mean_2)
    mean = jnp.sum(jnp.where(tall == wide, mean, 0.0), axis=1, keepdims=True)
    target = jnp.where(wide < M, data + step * data_c - cross - mean, 0.0)
    system = jnp.where(tall == wide, cross + (M - 1.0), cross)
    system = system + pltpu.roll(target, M, axis=1)
    for i in range(M):
        pivot = system[i : i + 1, :]
        pivot = pivot / pivot[:, i : i + 1]
        factor = jnp.where(tall == i, 0.0, jnp.broadcast_to(system[:, i : i + 1], (M, CX)))
        system = jnp.where(tall == i, pivot, system - factor * pivot)
    mixing = system - jnp.mean(system, axis=0, keepdims=True)
    mixing = pltpu.roll(mixing, CX - M, axis=1)
    mixing = jnp.where(wide < M, mixing + jnp.where(tall == wide, 1.0, 0.0), 0.0)
    for shift in (16, 32, 64):
        mixing = mixing + pltpu.roll(mixing, shift, axis=1)
    mixing = jnp.concatenate([mixing] * ZG, axis=0)
    tall = lax.broadcasted_iota(jnp.int32, (CX, CX), 0)
    wide = lax.broadcasted_iota(jnp.int32, (CX, CX), 1)
    mixing = jnp.where((tall >> 4) == (wide >> 4), 2.0 * mixing, 0.0).T
    for zi in range(2):
        for y in range(CY):
            part = lax.dot_general(
                mixing,
                field[zi, y] + step * changes[zi, y],
                NT,
                precision=lax.Precision.HIGHEST,
                preferred_element_type=F32,
            )
            for group in range(ZG):
                for m0 in (0, 8):
                    at = group * M + m0
                    out[m0 : m0 + 8, 2 * group + zi, y, :] = part[at : at + 8, :]


def update(sums, field, changes, status):
    return pl.pallas_call(
        update_kernel,
        out_shape=[
            jax.ShapeDtypeStruct((M, NZ, CY, CX), F32),
            jax.ShapeDtypeStruct((1,), jnp.int32),
        ],
        in_specs=[vspec()] * 4,
        out_specs=[vspec(), smem()],
        compiler_params=params(),
        name="update",
    )(sums, field, changes, status)


def exchange(parts):
    return lax.all_to_all(parts, BOTH, split_axis=0, concat_axis=0, tiled=True)


def move(part, axis, ahead):
    count = lax.axis_size(axis)
    pairs = [(i, i + 1) if ahead else (i + 1, i) for i in range(count - 1)]
    return lax.ppermute(part, axis, pairs)


def on_device(
    state_prior,
    conductivity,
    heat_input,
    owner_tile,
    voxel_list,
    pixel_cell,
    observed,
    pixel_variance,
    pixel_noise,
):
    devices = lax.axis_size("gx") * lax.axis_size("gy")
    pixels = pixel_cell.shape[0]
    gx, gy = lax.axis_index("gx"), lax.axis_index("gy")
    inside = jnp.stack(
        [gx > 0, gx < lax.axis_size("gx") - 1, gy > 0, gy < lax.axis_size("gy") - 1]
    ).astype(F32)
    incoming = exchange(pack(owner_tile.reshape(-1), heat_input, voxel_list, devices))
    own, turned_c, to_high, to_low, edge_left, edge_right, top, quiet = relayout(
        state_prior, conductivity
    )
    low, high = move(to_high, "gy", True), move(to_low, "gy", False)
    seen = pixel_sums(
        pixel_cell.reshape(1, pixels),
        observed.reshape(1, pixels),
        pixel_variance.reshape(1, pixels),
        pixel_noise,
    )
    incoming, own, top, inside, *seen = lax.optimization_barrier(
        (incoming, own, top, inside, *seen)
    )
    heat, peaks = deposit(incoming, top, conductivity, quiet)
    heat_low, heat_high = move(heat, "gy", True), move(heat, "gy", False)
    peaks = exchange(peaks)
    to_left, to_right = sides(
        edge_left, edge_right, turned_c, low, high, heat_low, heat, heat_high
    )
    left, right = move(to_right, "gx", True), move(to_left, "gx", False)
    start, coef, changes, parts = heated(
        inside,
        (own, low, high),
        (left, right),
        (heat_low, heat, heat_high),
        coefs(turned_c, low, high),
        peaks,
    )
    field, changes, parts, status = pair(1, inside, start, changes, coef, exchange(parts))
    field, changes, sums, status = last(
        inside, field, changes, coef, exchange(parts), status, seen
    )
    result, flag = update(exchange(sums), field, changes, status)

    def again():
        peak = coef * (1.0 + start * start)
        peaks = jnp.full((devices, 1, CX), jnp.max(peak[:, HALO : HALO + CY, 8 : XS - 8]))
        field = start
        for number in range(1, SUBSTEPS - 1):
            field, peaks = single(number, inside, field, coef, exchange(peaks))
        field, changes, sums = close(inside, field, coef, peaks, seen)
        return update(exchange(sums), field, changes, jnp.ones((8, CX), F32))[0]

    return lax.cond(flag[0] > 0, again, lambda: result)


def solution(mesh):
    in_specs = (
        P(None, None, "gy", "gx"),
        P(None, "gy", "gx"),
        P(None, BOTH, None),
        P(BOTH, None),
        P(BOTH, None),
        P(BOTH),
        P(BOTH),
        P(BOTH),
        P(None, BOTH),
    )
    out_specs = P(None, None, "gy", "gx")
    return jax.shard_map(
        on_device, mesh=mesh, in_specs=in_specs, out_specs=out_specs, check_vma=False
    )
```

```python
import functools

import jax
import jax.numpy as jnp
from jax import lax
from jax.experimental import pallas as pl
from jax.experimental.pallas import tpu as pltpu
from jax.sharding import PartitionSpec as P

SUBSTEPS = 6
CAP = 2
COOL = 0.1
SHARE = 0.9
F32 = jnp.float32
BF16 = jnp.bfloat16
VM = pltpu.VMEM
LIMIT = 32 * 1024 * 1024
NT = (((1,), (1,)), ((), ()))
BOTH = ("gx", "gy")

M, NZ, CY, CX = 16, 16, 8, 128
ROWS = 40


def vspec():
    return pl.BlockSpec(memory_space=pltpu.VMEM)


def hspec():
    return pl.BlockSpec(memory_space=pltpu.HBM)


def far(*arrays):
    return [pltpu.with_memory_space_constraint(array, pltpu.HBM) for array in arrays]


def fetch(sems, pairs):
    copies = [
        pltpu.make_async_copy(source, target, sems.at[i])
        for i, (source, target) in enumerate(pairs)
    ]
    for copy in copies:
        copy.start()
    return copies


def params():
    return pltpu.CompilerParams(vmem_limit_bytes=LIMIT)


def lanes():
    return lax.broadcasted_iota(jnp.int32, (CY, CX), 1)


def rows():
    return lax.broadcasted_iota(jnp.int32, (CY, CX), 0)


def pack_kernel(owner_far, heat_far, voxel_far, out, owner, heat, voxel, wide, high, low, inverse, sems):
    copies = fetch(sems, ((owner_far, owner), (heat_far, heat), (voxel_far, voxel)))
    blocks = owner.shape[0]
    devices = out.shape[0]

    def clear(i, carry):
        inverse[i] = blocks
        return carry

    lax.fori_loop(0, devices * CAP, clear, 0, unroll=16)
    copies[0].wait()

    def place(b, carry):
        base = owner[b] * CAP
        base = base + jnp.where(inverse[base] != blocks, 1, 0)
        inverse[base] = b
        return carry

    lax.fori_loop(0, blocks, place, 0, unroll=8)
    copies[1].wait()
    copies[2].wait()

    def widen(m, carry):
        wide[m, 0:blocks, :] = heat[m].astype(F32)
        wide[m, blocks:, :] = jnp.zeros((8, CX), F32)
        return carry

    lax.fori_loop(0, M, widen, 0)
    cells = voxel[...]
    high[0:blocks, :] = (cells >> 7).astype(F32)
    high[blocks:, :] = jnp.zeros((8, CX), F32)
    low[0:blocks, :] = (cells & 127).astype(F32)
    low[blocks:, :] = jnp.zeros((8, CX), F32)
    row = rows()

    def emit(d, carry):
        first = inverse[d * CAP]
        second = inverse[d * CAP + 1]
        index = jnp.where(
            row == 0,
            high[pl.ds(first, 1), :],
            jnp.where(
                row == 1,
                high[pl.ds(second, 1), :],
                jnp.where(
                    row == 2,
                    low[pl.ds(first, 1), :],
                    jnp.where(row == 3, low[pl.ds(second, 1), :], 0.0),
                ),
            ),
        )
        chunk = jnp.concatenate(
            [
                wide[:, pl.ds(first, 1), :].reshape(M, CX),
                wide[:, pl.ds(second, 1), :].reshape(M, CX),
                index,
            ],
            axis=0,
        )
        out[d] = chunk.astype(BF16)
        return carry

    lax.fori_loop(0, devices, emit, 0, unroll=4)


def pack(owner, heat, voxel, devices):
    blocks = owner.shape[0]
    return pl.pallas_call(
        pack_kernel,
        out_shape=jax.ShapeDtypeStruct((devices, ROWS, CX), BF16),
        in_specs=[hspec()] * 3,
        out_specs=vspec(),
        scratch_shapes=[
            pltpu.SMEM((blocks,), jnp.int32),
            VM((M, blocks, CX), BF16),
            VM((blocks, CX), jnp.int32),
            VM((M, blocks + 8, CX), F32),
            VM((blocks + 8, CX), F32),
            VM((blocks + 8, CX), F32),
            pltpu.SMEM((devices * CAP,), jnp.int32),
            pltpu.SemaphoreType.DMA((3,)),
        ],
        compiler_params=params(),
        name="pack",
    )(*far(owner, heat, voxel))


HALO = 6
YS = CY + 2 * HALO
XT = CX // 8 + 2
ZG = NZ // 2
TOLERANCE = 1e-6
OWN = jax.ShapeDtypeStruct((2, CY, CX, CX), F32)
XS = 8 * XT
WIDE = jax.ShapeDtypeStruct((2, YS, XS, CX), F32)
EDGE = 2 * HALO
SIDE = 2 * YS


def relayout_kernel(
    state, conduct, own, turned_c, to_high, to_low, edge_left, edge_right, top, quiet
):
    turned = (0.5 * conduct[...].reshape(CX, CX)).T.reshape(XT - 2, 8, CX)
    turned_c[...] = turned
    to_high[EDGE] = turned
    to_low[EDGE] = turned
    peak = jnp.zeros((8, CX), F32)
    for zi in range(2):
        for y in range(CY):
            parts = []
            for group in range(ZG):
                layer = 2 * group + zi
                c = 0.5 * conduct[layer, y : y + 1, :]
                for m0 in (0, 8):
                    part = 0.5 * state[m0 : m0 + 8, layer, y, :]
                    parts.append(part)
                    if group:
                        peak = jnp.maximum(peak, c + c * (part * part))
            turned = jnp.concatenate(parts, axis=0).T
            own[zi, y] = turned
            turned = turned.reshape(XT - 2, 8, CX)
            edge_left[zi * CY + y] = turned[0]
            edge_right[zi * CY + y] = turned[XT - 3]
            if y >= CY - HALO:
                to_high[zi * HALO + y - (CY - HALO)] = turned
            if y < HALO:
                to_low[zi * HALO + y] = turned
    quiet[...] = peak
    for m in range(M):
        for zi in range(2):
            top[m, zi] = 0.5 * state[m, zi]


def relayout(state, conduct):
    edge = jax.ShapeDtypeStruct((EDGE + 1, XT - 2, 8, CX), F32)
    side = jax.ShapeDtypeStruct((2 * CY, 8, CX), F32)
    return pl.pallas_call(
        relayout_kernel,
        out_shape=[
            OWN,
            jax.ShapeDtypeStruct((XT - 2, 8, CX), F32),
            edge,
            edge,
            side,
            side,
            jax.ShapeDtypeStruct((M, 2, CY, CX), F32),
            jax.ShapeDtypeStruct((8, CX), F32),
        ],
        in_specs=[vspec()] * 2,
        out_specs=[vspec()] * 8,
        compiler_params=params(),
        name="relayout",
    )(state, conduct)


def side_kernel(
    edge_left, edge_right, turned_c, low, high, heat_low, heat_own, heat_high,
    to_left, to_right, sems,
):
    pairs = []
    for out, edge, t in ((to_left, edge_left, 0), (to_right, edge_right, XT - 3)):
        for zi in range(2):
            at, rows_at = zi * YS, slice(zi * HALO, zi * HALO + HALO)
            pairs += [
                (low.at[rows_at, t], out.at[at : at + HALO]),
                (edge.at[zi * CY : zi * CY + CY], out.at[at + HALO : at + HALO + CY]),
                (high.at[rows_at, t], out.at[at + HALO + CY : at + YS]),
            ]
            for g, heat in enumerate((heat_low, heat_own, heat_high)):
                pairs.append((heat.at[zi, 8 * t : 8 * t + 8, :], out.at[SIDE + 3 + 2 * g + zi]))
        for g, part in enumerate((low.at[EDGE, t], turned_c.at[t], high.at[EDGE, t])):
            pairs.append((part, out.at[SIDE + g]))
    for copy in fetch(sems, pairs):
        copy.wait()


def sides(*operands):
    shape = jax.ShapeDtypeStruct((SIDE + 9, 8, CX), F32)
    return pl.pallas_call(
        side_kernel,
        out_shape=[shape, shape],
        in_specs=[hspec()] * len(operands),
        out_specs=[vspec()] * 2,
        scratch_shapes=[pltpu.SemaphoreType.DMA((30,))],
        compiler_params=params(),
        name="sides",
    )(*far(*operands))


def placed(strip, zi, y0):
    source = lax.broadcasted_iota(jnp.int32, (CX, CX), 0)
    target = lax.broadcasted_iota(jnp.int32, (CX, CX), 1)
    hot = jnp.where(source == (2 * (target >> 4) + zi) * CY + y0, 1.0, 0.0).astype(F32)
    return jnp.dot(strip, hot, precision=lax.Precision.HIGHEST, preferred_element_type=F32)


def halo_row(g, y0):
    row = y0 + HALO + (g - 1) * CY
    return row if 0 <= row < YS else None


def coef_kernel(own, low, high, out, tiles, sems):
    pairs = ((low.at[EDGE], tiles.at[0]), (own, tiles.at[1]), (high.at[EDGE], tiles.at[2]))
    for copy in fetch(sems, pairs):
        copy.wait()
    strip = tiles[...].reshape(3 * CX, CX)
    for zi in range(2):
        for y0 in range(CY):
            part = placed(strip, zi, y0)
            for g in range(3):
                row = halo_row(g, y0)
                if row is not None:
                    out[zi, row] = part[g * CX : (g + 1) * CX, :]


def coefs(own, low, high):
    return pl.pallas_call(
        coef_kernel,
        out_shape=jax.ShapeDtypeStruct((2, YS, CX, CX), F32),
        in_specs=[hspec()] * 3,
        out_specs=vspec(),
        scratch_shapes=[VM((3, XT - 2, 8, CX), F32), pltpu.SemaphoreType.DMA((3,))],
        compiler_params=params(),
        name="coefs",
    )(*far(own, low, high))


def deposit_kernel(
    incoming, top_far, conduct_far, quiet_far, out, peaks, total, top, conduct, quiet, sems
):
    copies = fetch(sems, ((top_far, top), (conduct_far.at[0:2], conduct), (quiet_far, quiet)))
    sources = incoming.shape[0]
    group = 32
    place = lax.broadcasted_iota(jnp.int32, (CX, CX), 0).astype(F32).astype(BF16)
    zero = jnp.zeros((M, CX), BF16)
    total[...] = jnp.zeros_like(total)

    def one(g, carry):
        left = []
        right = []
        for s in range(group):
            source = g * group + s
            index = incoming[source, 32:40, :].astype(F32)
            for slot in range(CAP):
                heat = incoming[source, slot * M : (slot + 1) * M, :]
                layer = jnp.broadcast_to(index[slot : slot + 1, :], (M, CX)).astype(BF16)
                cell = jnp.broadcast_to(index[2 + slot : 3 + slot, :], (CX, CX)).astype(BF16)
                left.append(
                    jnp.concatenate(
                        [jnp.where(layer == h, heat, zero) for h in range(2 * CY)], axis=0
                    )
                )
                right.append(jnp.where(place == cell, 1.0, 0.0).astype(BF16))
        total[...] += lax.dot_general(
            jnp.concatenate(left, axis=1),
            jnp.concatenate(right, axis=1),
            NT,
            preferred_element_type=F32,
        )
        return carry

    lax.fori_loop(0, sources // group, one, 0)
    for zi in range(2):
        out[zi] = (0.5 * total[zi * CX : (zi + 1) * CX, :]).T
    for copy in copies:
        copy.wait()
    peak = quiet[...]
    for zi in range(2):
        c = 0.5 * conduct[zi]
        for m in range(M):
            value = top[m, zi] + 0.5 * total[pl.ds(zi * CX + m, CY, stride=M), :]
            peak = jnp.maximum(peak, c + c * (value * value))
    send_row(whole_peak(peak), peaks)


def send_row(row, out):
    for d in range(0, out.shape[0], 8):
        out[d : d + 8, 0, :] = row


def deposit(incoming, top, conduct, quiet):
    devices = incoming.shape[0]
    return pl.pallas_call(
        deposit_kernel,
        out_shape=[
            jax.ShapeDtypeStruct((2, CX, CX), F32),
            jax.ShapeDtypeStruct((devices, 1, CX), F32),
        ],
        in_specs=[vspec()] + [hspec()] * 3,
        out_specs=[vspec()] * 2,
        scratch_shapes=[
            VM((2 * CY * M, CX), F32),
            VM(top.shape, F32),
            VM((2, CY, CX), F32),
            VM(quiet.shape, F32),
            pltpu.SemaphoreType.DMA((3,)),
        ],
        compiler_params=params(),
        name="deposit",
    )(incoming, *far(top, conduct, quiet))


def whole_peak(value):
    return jnp.broadcast_to(jnp.max(value, axis=(0, 1), keepdims=True), (8, CX))


def step_of(peak):
    return SHARE / (12.0 * peak + COOL)


def tile(t):
    return slice(8 * t, 8 * t + 8)


def half_conductance(c, u):
    return c + c * (u * u)


def segments(inside, first, end):
    parts = []
    if first < HALO:
        parts.append((first, HALO, False, inside[2]))
    parts.append((max(first, HALO), min(end, HALO + CY), True, None))
    if end > HALO + CY:
        parts.append((HALO + CY, end, False, inside[3]))
    return parts


def mask_of(inside, row_mask, t):
    if t == 0:
        return inside[0] if row_mask is None else inside[0] * row_mask
    if t == XT - 1:
        return inside[1] if row_mask is None else inside[1] * row_mask
    return row_mask


def sweep(field, half, above, inside, first, end, emit, carry):
    lane = lanes()
    row = rows()
    last_row = row == 7
    first_row = row == 0
    inner_lane = lane < CX - M
    cooling = jnp.where(lane < M, COOL, 0.0)

    for zi in range(2):
        for t in range(XT):
            s = tile(t)
            above[zi, t] = (half[zi, first - 1, s, :] + half[zi, first, s, :]) * (
                field[zi, first, s, :] - field[zi, first - 1, s, :]
            )

    def line(own, row_mask, y, state):
        carried = [jnp.zeros((8, CX), F32)] * 2
        for t in range(XT):
            s = tile(t)
            us = [field[zi, y, s, :] for zi in range(2)]
            hs = [half[zi, y, s, :] for zi in range(2)]
            change = []
            for zi in range(2):
                u, h = us[zi], hs[zi]
                if t < XT - 1:
                    after = slice(8 * t + 1, 8 * t + 9)
                    u_after, h_after = field[zi, y, after, :], half[zi, y, after, :]
                else:
                    u_after = jnp.where(last_row, u, pltpu.roll(u, 7, axis=0))
                    h_after = pltpu.roll(h, 7, axis=0)
                along = (h + h_after) * (u_after - u)
                turned = pltpu.roll(along, 1, axis=0)
                total = along - jnp.where(first_row, carried[zi], turned)
                carried[zi] = turned
                across = (h + half[zi, y + 1, s, :]) * (field[zi, y + 1, s, :] - u)
                total = total + (across - above[zi, t])
                above[zi, t] = across
                change.append(total)
            within = (hs[0] + hs[1]) * (us[1] - us[0])
            between = (hs[1] + pltpu.roll(hs[0], CX - M, axis=1)) * (
                pltpu.roll(us[0], CX - M, axis=1) - us[1]
            )
            between = jnp.where(inner_lane, between, 0.0)
            change[0] = change[0] + (within - pltpu.roll(between, M, axis=1)) - cooling * us[0]
            change[1] = change[1] + (between - within)
            state = emit(y, t, us, change, own, mask_of(inside, row_mask, t), state)
        return state

    for start, stop, own, row_mask in segments(inside, first, end):
        carry = lax.fori_loop(start, stop, functools.partial(line, own, row_mask), carry)
    return carry


def advance(field, half, coef, above, inside, step, first, end, put):
    def emit(y, t, us, change, own, mask, peak):
        part = step if mask is None else step * mask
        for zi in range(2):
            value = us[zi] + part * change[zi]
            after = half_conductance(coef[zi, y, tile(t), :], value)
            put(zi, y, t, value, after)
            if own and 0 < t < XT - 1:
                peak = jnp.maximum(peak, after)
        return peak

    return sweep(field, half, above, inside, first, end, emit, jnp.zeros((8, CX), F32))


def propose(field, half, coef, above, inside, guess, first, end, changes, peak, late, out):
    def emit(y, t, us, change, own, mask, best):
        for zi in range(2):
            moved = change[zi] if mask is None else change[zi] * mask
            changes[zi, y, tile(t), :] = moved
            if own and 0 < t < XT - 1:
                c = coef[zi, y, tile(t), :]
                rank = half_conductance(c, us[zi] + guess * moved)
                better = rank > best[0]
                best = tuple(
                    jnp.where(better, new, old)
                    for new, old in zip((rank, us[zi], moved, c), best)
                )
        return best

    best = sweep(
        field, half, above, inside, first, end, emit, (jnp.zeros((8, CX), F32),) * 4
    )
    for shift, axis in ((4, 0), (2, 0), (1, 0), (64, 1), (32, 1)):
        other = tuple(pltpu.roll(part, shift, axis=axis) for part in best)
        better = other[0] > best[0]
        best = tuple(jnp.where(better, new, old) for new, old in zip(other, best))
    part = lanes() >> 4
    chunk = jnp.where(part == 6, whole_peak(peak), whole_peak(late))
    for place, value in ((2, best[3]), (1, best[2]), (0, best[1])):
        chunk = jnp.where((part >> 1) == place, value, chunk)
    send_row(chunk, out)


def gather_rows(parts):
    return [parts[d : d + 8, 0, :] for d in range(0, parts.shape[0], 8)]


def largest(values):
    most = values[0]
    for value in values[1:]:
        most = jnp.maximum(most, value)
    return most


def agree(parts):
    part = lanes() >> 4
    rows_of = gather_rows(parts)
    most = largest(rows_of)
    now = whole_peak(jnp.where(part == 6, most, 0.0))
    late = whole_peak(jnp.where(part == 7, most, 0.0))
    step = step_of(now)
    then = jnp.zeros((8, CX), F32)
    for value in rows_of:
        moved = pltpu.roll(value, CX - 32, axis=1)
        c = pltpu.roll(value, CX - 64, axis=1)
        then = jnp.maximum(then, half_conductance(c, value + step * moved))
    return now, whole_peak(jnp.where(part < 2, then, 0.0)), late


def differs(late, used):
    return jnp.where(late > used * (1.0 + TOLERANCE), 1.0, 0.0)


def heated_kernel(
    inside, peaks, own_far, low_far, high_far, left_far, right_far,
    heat_low_far, heat_own_far, heat_high_far, coef_far,
    out, coef, changes, parts, start, half, next_half, above,
    own, low, high, left, right, heat_low, heat_own, heat_high, coef_main, sems,
):
    spans = (slice(0, HALO), slice(HALO, HALO + CY), slice(HALO + CY, YS))
    copies = fetch(
        sems,
        [
            (left_far, left),
            (right_far, right),
            (heat_low_far, heat_low),
            (low_far.at[0:EDGE], low),
            (coef_far.at[:, spans[0]], coef_main.at[:, spans[0]]),
            (heat_own_far, heat_own),
            (own_far, own),
            (coef_far.at[:, spans[1]], coef_main.at[:, spans[1]]),
            (heat_high_far, heat_high),
            (high_far.at[0:EDGE], high),
            (coef_far.at[:, spans[2]], coef_main.at[:, spans[2]]),
        ],
    )
    top = lanes() < M
    for copy in copies[0:2]:
        copy.wait()

    strip = jnp.concatenate(
        [side[SIDE + g] for g in range(3) for side in (left, right)], axis=0
    )
    for zi in range(2):
        for y0 in range(CY):
            part = placed(strip, zi, y0)
            for g in range(3):
                at = halo_row(g, y0)
                if at is not None:
                    coef[zi, at, tile(0), :] = part[16 * g : 16 * g + 8, :]
                    coef[zi, at, tile(XT - 1), :] = part[16 * g + 8 : 16 * g + 16, :]

    def row(g, heat, tile_of, y0, yy):
        shift = (CX - 16 * y0) % CX
        for zi in range(2):
            for t in range(XT):
                if t == 0:
                    prior, add = left[zi * YS + yy], left[SIDE + 3 + 2 * g + zi]
                elif t == XT - 1:
                    prior, add = right[zi * YS + yy], right[SIDE + 3 + 2 * g + zi]
                else:
                    prior, add = tile_of(zi, t - 1), heat[zi, tile(t - 1), :]
                if shift:
                    add = pltpu.roll(add, shift, axis=1)
                value = prior + jnp.where(top, add, 0.0)
                if 0 < t < XT - 1:
                    c = coef_main[zi, yy, tile(t - 1), :]
                    coef[zi, yy, tile(t), :] = c
                else:
                    c = coef[zi, yy, tile(t), :]
                after = half_conductance(c, value)
                start[zi, yy, tile(t), :] = value
                half[zi, yy, tile(t), :] = after

    def edge(ref, y):
        return lambda zi, t: ref[zi * HALO + y, t]

    for copy in copies[2:5]:
        copy.wait()
    for y in range(HALO):
        row(0, heat_low, edge(low, y), y + CY - HALO, y)
    for copy in copies[5:8]:
        copy.wait()
    for y in range(CY):
        row(1, heat_own, lambda zi, t: own[zi, y, tile(t), :], y, y + HALO)
    for copy in copies[8:11]:
        copy.wait()
    for y in range(HALO):
        row(2, heat_high, edge(high, y), y, y + HALO + CY)

    def put(zi, y, t, value, after):
        out[zi, y, tile(t), :] = value
        next_half[zi, y, tile(t), :] = after

    step = step_of(whole_peak(largest(gather_rows(peaks))))
    peak = advance(start, half, coef, above, inside, step, 1, YS - 1, put)
    guess = jnp.minimum(step_of(whole_peak(peak)), 2.0 * step)
    zero = jnp.zeros((8, CX), F32)
    propose(
        out, next_half, coef, above, inside, guess, 2, YS - 2, changes, peak, zero, parts
    )


ROW = (2, XT, 8, CX)


def smem():
    return pl.BlockSpec(memory_space=pltpu.SMEM)


def heated(inside, prior, halos, heat, coef, peaks):
    operands = far(*prior, *halos, *heat, coef)
    edge = VM((EDGE, XT - 2, 8, CX), F32)
    return pl.pallas_call(
        heated_kernel,
        out_shape=[WIDE, WIDE, WIDE, jax.ShapeDtypeStruct(peaks.shape, F32)],
        in_specs=[smem(), vspec()] + [hspec()] * len(operands),
        out_specs=[vspec()] * 4,
        scratch_shapes=[VM(WIDE.shape, F32)] * 3
        + [VM(ROW, F32), VM(OWN.shape, F32), edge, edge]
        + [VM(part.shape, F32) for part in (*halos, *heat, coef)]
        + [pltpu.SemaphoreType.DMA((11,))],
        compiler_params=params(),
        name="heated",
    )(inside, peaks, *operands)


def first_of_pair(field, changes, coef, step, first, end, out, half):
    def line(y, peak):
        top = jnp.zeros((8, CX), F32)
        for zi in range(2):
            for t in range(XT):
                value = field[zi, y, tile(t), :] + step * changes[zi, y, tile(t), :]
                after = half_conductance(coef[zi, y, tile(t), :], value)
                out[zi, y, tile(t), :] = value
                half[zi, y, tile(t), :] = after
                if 0 < t < XT - 1:
                    top = jnp.maximum(top, after)
        own = jnp.where((y >= HALO) & (y < HALO + CY), 1.0, 0.0)
        return jnp.maximum(peak, own * top)

    return lax.fori_loop(first, end, line, jnp.zeros((8, CX), F32))


def pair_kernel(
    number, inside, field, changes, coef, parts,
    out, out_changes, out_parts, status, middle, half, next_half, above,
):
    now, then, _ = agree(parts)
    status[...] = jnp.where(rows() == 0, then, 0.0)
    seen = first_of_pair(
        field, changes, coef, step_of(now), number + 1, YS - 1 - number, middle, half
    )

    def put(zi, y, t, value, after):
        out[zi, y, tile(t), :] = value
        next_half[zi, y, tile(t), :] = after

    step = step_of(then)
    peak = advance(
        middle, half, coef, above, inside, step, number + 2, YS - 2 - number, put
    )
    guess = jnp.minimum(step_of(whole_peak(peak)), 1.2 * step)
    propose(
        out, next_half, coef, above, inside, guess, number + 3, YS - 3 - number,
        out_changes, peak, seen, out_parts,
    )


STATUS = jax.ShapeDtypeStruct((8, CX), F32)


def pair(number, inside, field, changes, coef, parts):
    operands = [inside, field, changes, coef, parts]
    return pl.pallas_call(
        functools.partial(pair_kernel, number),
        out_shape=[WIDE, WIDE, jax.ShapeDtypeStruct(parts.shape, F32), STATUS],
        in_specs=[smem()] + [vspec()] * 4,
        out_specs=[vspec()] * 4,
        scratch_shapes=[VM(WIDE.shape, F32)] * 3 + [VM(ROW, F32)],
        compiler_params=params(),
        name=f"pair_{number}",
    )(*operands)


def closing(
    field, half, above, inside, weight, data, peak, late, out, out_changes, sums, flat
):
    def emit(y, t, us, change, own, mask, state):
        if 0 < t < XT - 1:
            for zi in range(2):
                out[zi, y - HALO, tile(t - 1), :] = us[zi]
                out_changes[zi, y - HALO, tile(t - 1), :] = change[zi]
        return state

    sweep(field, half, above, inside, HALO, HALO + CY, emit, 0)
    grams = jnp.zeros((5 * CY, 3 * M), F32)
    for y in range(CY):
        w = weight[y : y + 1, :]
        for m in range(M):
            flat[m : m + 1, :] = data[m, y : y + 1, :]
        means = []
        spreads = []
        for part in (out, out_changes):
            seen = 2.0 * part[0, y].T[0:M, :]
            mean = jnp.mean(seen, axis=0, keepdims=True)
            means.append(mean)
            spreads.append(seen - mean)
        left = jnp.concatenate(spreads + means + [jnp.zeros((6, CX), F32)], axis=0)
        right = jnp.concatenate([part * w for part in spreads] + [flat[...]], axis=0)
        grams = grams + lax.dot_general(
            left, right, NT, precision=lax.Precision.HIGHEST, preferred_element_type=F32
        )
    grams = jnp.concatenate([grams, jnp.zeros((5 * CY, CX - 3 * M), F32)], axis=1)
    tall = lax.broadcasted_iota(jnp.int32, (M, CX), 0)
    wide = lax.broadcasted_iota(jnp.int32, (M, CX), 1)
    first, second, means = grams[0:M], grams[M : 2 * M], grams[2 * M : 2 * M + 8]

    def block(part, at):
        return jnp.where(wide < M, pltpu.roll(part, (CX - M * at) % CX, axis=1), 0.0)

    def lone(part, row, at):
        moved = pltpu.roll(part, (CX - M * at) % CX, axis=1) if at else part
        return jnp.broadcast_to(moved[row : row + 1, :], (M, CX))

    tops = [
        lone(means, 0, 1) + lone(means, 1, 0),
        lone(means, 0, 0),
        lone(means, 1, 1),
    ]
    blocks = [
        jnp.where(tall < wide, block(first, 0), block(second, 1)),
        block(first, 1) + block(second, 0),
        block(first, 2),
        block(second, 2),
    ]
    scalar = jnp.where(wide == 0, whole_peak(peak)[0:1], whole_peak(late)[0:1])
    blocks[0] = jnp.where(tall == wide, scalar, blocks[0])
    for i, top in enumerate(tops):
        blocks[i + 1] = jnp.where(tall == 0, jnp.where(wide < M, top, 0.0), blocks[i + 1])
    packed = blocks[0]
    for i in range(1, 4):
        packed = packed + pltpu.roll(blocks[i], M * i, axis=1)
    packed = packed[0:8] + pltpu.roll(packed[8:16], CX // 2, axis=1)
    for d in range(sums.shape[0]):
        sums[d] = packed


def last_kernel(
    inside, field, changes, coef, parts, status, weight_far, data_far,
    out, out_changes, sums, out_status,
    middle, half, near, near_half, above, flat, weight, data, sems,
):
    copies = fetch(sems, ((weight_far, weight), (data_far, data)))
    number = SUBSTEPS - 3
    now, then, late = agree(parts)
    bad = differs(late[0:1], status[0:1, :])
    out_status[...] = jnp.where(rows() == 0, then, bad)
    seen = first_of_pair(
        field, changes, coef, step_of(now), number + 1, YS - 1 - number, middle, half
    )

    def put(zi, y, t, value, after):
        near[zi, y, tile(t), :] = value
        near_half[zi, y, tile(t), :] = after

    peak = advance(
        middle, half, coef, above, inside, step_of(then), number + 2, YS - 2 - number, put
    )
    for copy in copies:
        copy.wait()
    closing(
        near, near_half, above, inside, weight, data, peak, seen, out, out_changes, sums, flat
    )


def sums_shape(devices):
    return jax.ShapeDtypeStruct((devices, 8, CX), F32)


def last(inside, field, changes, coef, parts, status, pixels):
    operands = [inside, field, changes, coef, parts, status, *far(*pixels)]
    return pl.pallas_call(
        last_kernel,
        out_shape=[OWN, OWN, sums_shape(parts.shape[0]), STATUS],
        in_specs=[smem()] + [vspec()] * 5 + [hspec()] * 2,
        out_specs=[vspec()] * 4,
        scratch_shapes=[VM(WIDE.shape, F32)] * 4
        + [VM(ROW, F32), VM((M, CX), F32)]
        + [VM(part.shape, F32) for part in pixels]
        + [pltpu.SemaphoreType.DMA((2,))],
        compiler_params=params(),
        name="last_pair",
    )(*operands)


def fill_half(field, coef, half, first, end):
    def fill(y, carry):
        for zi in range(2):
            half[zi, y] = half_conductance(coef[zi, y], field[zi, y])
        return carry

    lax.fori_loop(first, end, fill, 0)


def single_kernel(number, inside, field, coef, peaks, out, out_peaks, half, above):
    step = step_of(whole_peak(largest(gather_rows(peaks))))
    fill_half(field, coef, half, number, YS - number)

    def put(zi, y, t, value, after):
        out[zi, y, tile(t), :] = value

    peak = advance(field, half, coef, above, inside, step, number + 1, YS - 1 - number, put)
    send_row(whole_peak(peak), out_peaks)


def single(number, inside, field, coef, peaks):
    return pl.pallas_call(
        functools.partial(single_kernel, number),
        out_shape=[WIDE, jax.ShapeDtypeStruct(peaks.shape, F32)],
        in_specs=[smem()] + [vspec()] * 3,
        out_specs=[vspec()] * 2,
        scratch_shapes=[VM(WIDE.shape, F32), VM(ROW, F32)],
        compiler_params=params(),
        name=f"single_{number}",
    )(inside, field, coef, peaks)


def closing_kernel(
    inside, field, coef, peaks, weight, data, out, out_changes, sums, half, above, flat
):
    fill_half(field, coef, half, HALO - 1, HALO + CY + 1)
    peak = peaks[0:8, 0, :]
    closing(
        field, half, above, inside, weight, data, peak, jnp.zeros((8, CX), F32),
        out, out_changes, sums, flat,
    )


def close(inside, field, coef, peaks, pixels):
    operands = [inside, field, coef, peaks, *pixels]
    return pl.pallas_call(
        closing_kernel,
        out_shape=[OWN, OWN, sums_shape(peaks.shape[0])],
        in_specs=[smem()] + [vspec()] * (len(operands) - 1),
        out_specs=[vspec()] * 3,
        scratch_shapes=[VM(WIDE.shape, F32), VM(ROW, F32), VM((M, CX), F32)],
        compiler_params=params(),
        name="closing",
    )(*operands)


def pixel_kernel(cell, observed, variance, noise, weight, data):
    pixels = cell.shape[1]
    place = cell[...]
    var = variance[...]
    inverse = 1.0 / var
    values = (observed[...] + noise[...] * jnp.sqrt(var)) * inverse
    stack = jnp.concatenate([values, jnp.broadcast_to(inverse, (8, pixels))], axis=0)
    width = place >> 7
    hot = jnp.where(
        lax.broadcasted_iota(jnp.int32, (CX, pixels), 0) == (place & 127), 1.0, 0.0
    ).astype(F32)
    for y in range(CY):
        part = lax.dot_general(
            jnp.where(width == y, stack, 0.0),
            hot,
            NT,
            precision=lax.Precision.HIGHEST,
            preferred_element_type=F32,
        )
        weight[y : y + 1, :] = part[M : M + 1, :]
        for m in range(M):
            data[m, y : y + 1, :] = part[m : m + 1, :]


def pixel_sums(cell, observed, variance, noise):
    return pl.pallas_call(
        pixel_kernel,
        out_shape=[
            jax.ShapeDtypeStruct((CY, CX), F32),
            jax.ShapeDtypeStruct((M, CY, CX), F32),
        ],
        in_specs=[vspec()] * 4,
        out_specs=[vspec()] * 2,
        compiler_params=params(),
        name="pixels",
    )(cell, observed, variance, noise)


def update_kernel(sums, field, changes, status, out, flag):
    total = sums[0]
    most = total
    for d in range(1, sums.shape[0]):
        total = total + sums[d]
        most = jnp.maximum(most, sums[d])
    step = step_of(jnp.broadcast_to(most[0:1, 0:1], (1, CX)))
    late = jnp.broadcast_to(most[1:2, 1:2], (1, CX))
    bad = jnp.maximum(status[1:2, :], differs(late, status[0:1, :]))
    flag[0] = jnp.where(jnp.max(bad) > 0.0, 1, 0)

    tall = lax.broadcasted_iota(jnp.int32, (M, CX), 0)
    wide = lax.broadcasted_iota(jnp.int32, (M, CX), 1)
    packed = jnp.concatenate([total, pltpu.roll(total, CX // 2, axis=1)], axis=0)

    def block(at):
        return jnp.where(wide < M, pltpu.roll(packed, (CX - M * at) % CX, axis=1), 0.0)

    def whole(part):
        rest = jnp.where(tall == 0, 0.0, part)
        first = -jnp.sum(rest, axis=0, keepdims=True)
        return jnp.where(tall == 0, first, rest), part[0:1, :]

    def balanced(part):
        part = jnp.where((tall == wide) | (wide >= M), 0.0, part)
        return jnp.where(tall == wide, -jnp.sum(part, axis=1, keepdims=True), part)

    corner = block(0)
    mirror = jnp.concatenate([corner, jnp.zeros((CX - M, CX), F32)], axis=0).T[0:M, :]
    square = balanced(jnp.where(tall < wide, corner, mirror))
    square_c = balanced(jnp.where(tall > wide, corner, mirror))
    mixed, mean_1 = whole(block(1))
    data, mean_0 = whole(block(2))
    data_c, mean_2 = whole(block(3))
    cross = square + step * (mixed + step * square_c)
    mean = mean_0 + step * (mean_1 + step * mean_2)
    mean = jnp.sum(jnp.where(tall == wide, mean, 0.0), axis=1, keepdims=True)
    target = jnp.where(wide < M, data + step * data_c - cross - mean, 0.0)
    system = jnp.where(tall == wide, cross + (M - 1.0), cross)
    system = system + pltpu.roll(target, M, axis=1)
    for i in range(M):
        pivot = system[i : i + 1, :]
        pivot = pivot / pivot[:, i : i + 1]
        factor = jnp.where(tall == i, 0.0, jnp.broadcast_to(system[:, i : i + 1], (M, CX)))
        system = jnp.where(tall == i, pivot, system - factor * pivot)
    mixing = system - jnp.mean(system, axis=0, keepdims=True)
    mixing = pltpu.roll(mixing, CX - M, axis=1)
    mixing = jnp.where(wide < M, mixing + jnp.where(tall == wide, 1.0, 0.0), 0.0)
    for shift in (16, 32, 64):
        mixing = mixing + pltpu.roll(mixing, shift, axis=1)
    mixing = jnp.concatenate([mixing] * ZG, axis=0)
    tall = lax.broadcasted_iota(jnp.int32, (CX, CX), 0)
    wide = lax.broadcasted_iota(jnp.int32, (CX, CX), 1)
    mixing = jnp.where((tall >> 4) == (wide >> 4), 2.0 * mixing, 0.0).T
    for zi in range(2):
        for y in range(CY):
            part = lax.dot_general(
                mixing,
                field[zi, y] + step * changes[zi, y],
                NT,
                precision=lax.Precision.HIGHEST,
                preferred_element_type=F32,
            )
            for group in range(ZG):
                for m0 in (0, 8):
                    at = group * M + m0
                    out[m0 : m0 + 8, 2 * group + zi, y, :] = part[at : at + 8, :]


def update(sums, field, changes, status):
    return pl.pallas_call(
        update_kernel,
        out_shape=[
            jax.ShapeDtypeStruct((M, NZ, CY, CX), F32),
            jax.ShapeDtypeStruct((1,), jnp.int32),
        ],
        in_specs=[vspec()] * 4,
        out_specs=[vspec(), smem()],
        compiler_params=params(),
        name="update",
    )(sums, field, changes, status)


def exchange(parts):
    return lax.all_to_all(parts, BOTH, split_axis=0, concat_axis=0, tiled=True)


def move(part, axis, ahead):
    count = lax.axis_size(axis)
    pairs = [(i, i + 1) if ahead else (i + 1, i) for i in range(count - 1)]
    return lax.ppermute(part, axis, pairs)


def on_device(
    state_prior,
    conductivity,
    heat_input,
    owner_tile,
    voxel_list,
    pixel_cell,
    observed,
    pixel_variance,
    pixel_noise,
):
    devices = lax.axis_size("gx") * lax.axis_size("gy")
    pixels = pixel_cell.shape[0]
    gx, gy = lax.axis_index("gx"), lax.axis_index("gy")
    inside = jnp.stack(
        [gx > 0, gx < lax.axis_size("gx") - 1, gy > 0, gy < lax.axis_size("gy") - 1]
    ).astype(F32)
    incoming = exchange(pack(owner_tile.reshape(-1), heat_input, voxel_list, devices))
    own, turned_c, to_high, to_low, edge_left, edge_right, top, quiet = relayout(
        state_prior, conductivity
    )
    low, high = move(to_high, "gy", True), move(to_low, "gy", False)
    seen = pixel_sums(
        pixel_cell.reshape(1, pixels),
        observed.reshape(1, pixels),
        pixel_variance.reshape(1, pixels),
        pixel_noise,
    )
    incoming, own, top, inside, *seen = lax.optimization_barrier(
        (incoming, own, top, inside, *seen)
    )
    heat, peaks = deposit(incoming, top, conductivity, quiet)
    heat_low, heat_high = move(heat, "gy", True), move(heat, "gy", False)
    peaks = exchange(peaks)
    to_left, to_right = sides(
        edge_left, edge_right, turned_c, low, high, heat_low, heat, heat_high
    )
    left, right = move(to_right, "gx", True), move(to_left, "gx", False)
    start, coef, changes, parts = heated(
        inside,
        (own, low, high),
        (left, right),
        (heat_low, heat, heat_high),
        coefs(turned_c, low, high),
        peaks,
    )
    field, changes, parts, status = pair(1, inside, start, changes, coef, exchange(parts))
    field, changes, sums, status = last(
        inside, field, changes, coef, exchange(parts), status, seen
    )
    result, flag = update(exchange(sums), field, changes, status)

    def again():
        peak = coef * (1.0 + start * start)
        peaks = jnp.full((devices, 1, CX), jnp.max(peak[:, HALO : HALO + CY, 8 : XS - 8]))
        field = start
        for number in range(1, SUBSTEPS - 1):
            field, peaks = single(number, inside, field, coef, exchange(peaks))
        field, changes, sums = close(inside, field, coef, peaks, seen)
        return update(exchange(sums), field, changes, jnp.ones((8, CX), F32))[0]

    return lax.cond(flag[0] > 0, again, lambda: result)


def solution(mesh):
    in_specs = (
        P(None, None, "gy", "gx"),
        P(None, "gy", "gx"),
        P(None, BOTH, None),
        P(BOTH, None),
        P(BOTH, None),
        P(BOTH),
        P(BOTH),
        P(BOTH),
        P(None, BOTH),
    )
    out_specs = P(None, None, "gy", "gx")
    return jax.shard_map(
        on_device, mesh=mesh, in_specs=in_specs, out_specs=out_specs, check_vma=False
    )
```

```python
import functools

import jax
import jax.numpy as jnp
from jax import lax
from jax.experimental import pallas as pl
from jax.experimental.pallas import tpu as pltpu
from jax.sharding import PartitionSpec as P

SUBSTEPS = 6
CAP = 2
COOL = 0.1
SHARE = 0.9
F32 = jnp.float32
BF16 = jnp.bfloat16
VM = pltpu.VMEM
LIMIT = 32 * 1024 * 1024
NT = (((1,), (1,)), ((), ()))
BOTH = ("gx", "gy")

M, NZ, CY, CX = 16, 16, 8, 128
ROWS = 40


def vspec():
    return pl.BlockSpec(memory_space=pltpu.VMEM)


def hspec():
    return pl.BlockSpec(memory_space=pltpu.HBM)


def far(*arrays):
    return [pltpu.with_memory_space_constraint(array, pltpu.HBM) for array in arrays]


def kept(shape):
    return pltpu.HBM(tuple(shape), F32)


def fetch(sems, pairs):
    copies = [
        pltpu.make_async_copy(source, target, sems.at[i])
        for i, (source, target) in enumerate(pairs)
    ]
    for copy in copies:
        copy.start()
    return copies


def params():
    return pltpu.CompilerParams(vmem_limit_bytes=LIMIT)


def lanes():
    return lax.broadcasted_iota(jnp.int32, (CY, CX), 1)


def rows():
    return lax.broadcasted_iota(jnp.int32, (CY, CX), 0)


def pack_kernel(owner_far, heat_far, voxel_far, out, owner, heat, voxel, wide, high, low, inverse, sems):
    copies = fetch(sems, ((owner_far, owner), (heat_far, heat), (voxel_far, voxel)))
    blocks = owner.shape[0]
    devices = out.shape[0]

    def clear(i, carry):
        inverse[i] = blocks
        return carry

    lax.fori_loop(0, devices * CAP, clear, 0, unroll=16)
    copies[0].wait()

    def place(b, carry):
        base = owner[b] * CAP
        base = base + jnp.where(inverse[base] != blocks, 1, 0)
        inverse[base] = b
        return carry

    lax.fori_loop(0, blocks, place, 0, unroll=8)
    copies[1].wait()
    copies[2].wait()

    def widen(m, carry):
        wide[m, 0:blocks, :] = heat[m].astype(F32)
        wide[m, blocks:, :] = jnp.zeros((8, CX), F32)
        return carry

    lax.fori_loop(0, M, widen, 0)
    cells = voxel[...]
    high[0:blocks, :] = (cells >> 7).astype(F32)
    high[blocks:, :] = jnp.zeros((8, CX), F32)
    low[0:blocks, :] = (cells & 127).astype(F32)
    low[blocks:, :] = jnp.zeros((8, CX), F32)
    row = rows()

    def emit(d, carry):
        first = inverse[d * CAP]
        second = inverse[d * CAP + 1]
        index = jnp.where(
            row == 0,
            high[pl.ds(first, 1), :],
            jnp.where(
                row == 1,
                high[pl.ds(second, 1), :],
                jnp.where(
                    row == 2,
                    low[pl.ds(first, 1), :],
                    jnp.where(row == 3, low[pl.ds(second, 1), :], 0.0),
                ),
            ),
        )
        chunk = jnp.concatenate(
            [
                wide[:, pl.ds(first, 1), :].reshape(M, CX),
                wide[:, pl.ds(second, 1), :].reshape(M, CX),
                index,
            ],
            axis=0,
        )
        out[d] = chunk.astype(BF16)
        return carry

    lax.fori_loop(0, devices, emit, 0, unroll=4)


def pack(owner, heat, voxel, devices):
    blocks = owner.shape[0]
    return pl.pallas_call(
        pack_kernel,
        out_shape=jax.ShapeDtypeStruct((devices, ROWS, CX), BF16),
        in_specs=[hspec()] * 3,
        out_specs=vspec(),
        scratch_shapes=[
            pltpu.SMEM((blocks,), jnp.int32),
            VM((M, blocks, CX), BF16),
            VM((blocks, CX), jnp.int32),
            VM((M, blocks + 8, CX), F32),
            VM((blocks + 8, CX), F32),
            VM((blocks + 8, CX), F32),
            pltpu.SMEM((devices * CAP,), jnp.int32),
            pltpu.SemaphoreType.DMA((3,)),
        ],
        compiler_params=params(),
        name="pack",
    )(*far(owner, heat, voxel))


HALO = 6
YS = CY + 2 * HALO
XT = CX // 8 + 2
ZG = NZ // 2
TOLERANCE = 1e-6
OWN = jax.ShapeDtypeStruct((2, CY, CX, CX), F32)
XS = 8 * XT
WIDE = jax.ShapeDtypeStruct((2, YS, XS, CX), F32)
EDGE = 2 * HALO
SIDE = 2 * YS


def relayout_kernel(
    state, conduct, own, turned_c, to_high, to_low, edge_left, edge_right, top, quiet
):
    turned = (0.5 * conduct[...].reshape(CX, CX)).T.reshape(XT - 2, 8, CX)
    turned_c[...] = turned
    to_high[EDGE] = turned
    to_low[EDGE] = turned
    peak = jnp.zeros((8, CX), F32)
    for zi in range(2):
        for y in range(CY):
            parts = []
            for group in range(ZG):
                layer = 2 * group + zi
                c = 0.5 * conduct[layer, y : y + 1, :]
                for m0 in (0, 8):
                    part = 0.5 * state[m0 : m0 + 8, layer, y, :]
                    parts.append(part)
                    if group:
                        peak = jnp.maximum(peak, c + c * (part * part))
            turned = jnp.concatenate(parts, axis=0).T
            own[zi, y] = turned
            turned = turned.reshape(XT - 2, 8, CX)
            edge_left[zi * CY + y] = turned[0]
            edge_right[zi * CY + y] = turned[XT - 3]
            if y >= CY - HALO:
                to_high[zi * HALO + y - (CY - HALO)] = turned
            if y < HALO:
                to_low[zi * HALO + y] = turned
    quiet[...] = peak
    for m in range(M):
        for zi in range(2):
            top[m, zi] = 0.5 * state[m, zi]


def relayout(state, conduct):
    edge = kept((EDGE + 1, XT - 2, 8, CX))
    side = kept((2 * CY, 8, CX))
    return pl.pallas_call(
        relayout_kernel,
        out_shape=[
            kept(OWN.shape),
            kept((XT - 2, 8, CX)),
            edge,
            edge,
            side,
            side,
            kept((M, 2, CY, CX)),
            kept((8, CX)),
        ],
        in_specs=[vspec()] * 2,
        out_specs=[vspec()] * 8,
        compiler_params=params(),
        name="relayout",
    )(state, conduct)


def side_kernel(
    edge_left, edge_right, turned_c, low, high, heat_low, heat_own, heat_high,
    to_left, to_right, sems,
):
    pairs = []
    for out, edge, t in ((to_left, edge_left, 0), (to_right, edge_right, XT - 3)):
        for zi in range(2):
            at, rows_at = zi * YS, slice(zi * HALO, zi * HALO + HALO)
            pairs += [
                (low.at[rows_at, t], out.at[at : at + HALO]),
                (edge.at[zi * CY : zi * CY + CY], out.at[at + HALO : at + HALO + CY]),
                (high.at[rows_at, t], out.at[at + HALO + CY : at + YS]),
            ]
            for g, heat in enumerate((heat_low, heat_own, heat_high)):
                pairs.append((heat.at[zi, 8 * t : 8 * t + 8, :], out.at[SIDE + 3 + 2 * g + zi]))
        for g, part in enumerate((low.at[EDGE, t], turned_c.at[t], high.at[EDGE, t])):
            pairs.append((part, out.at[SIDE + g]))
    for copy in fetch(sems, pairs):
        copy.wait()


def sides(*operands):
    shape = jax.ShapeDtypeStruct((SIDE + 9, 8, CX), F32)
    return pl.pallas_call(
        side_kernel,
        out_shape=[shape, shape],
        in_specs=[hspec()] * len(operands),
        out_specs=[vspec()] * 2,
        scratch_shapes=[pltpu.SemaphoreType.DMA((30,))],
        compiler_params=params(),
        name="sides",
    )(*far(*operands))


def placed(strip, zi, y0):
    source = lax.broadcasted_iota(jnp.int32, (CX, CX), 0)
    target = lax.broadcasted_iota(jnp.int32, (CX, CX), 1)
    hot = jnp.where(source == (2 * (target >> 4) + zi) * CY + y0, 1.0, 0.0).astype(F32)
    return jnp.dot(strip, hot, precision=lax.Precision.HIGHEST, preferred_element_type=F32)


def halo_row(g, y0):
    row = y0 + HALO + (g - 1) * CY
    return row if 0 <= row < YS else None


def coef_kernel(own, low, high, out, tiles, sems):
    pairs = ((low.at[EDGE], tiles.at[0]), (own, tiles.at[1]), (high.at[EDGE], tiles.at[2]))
    for copy in fetch(sems, pairs):
        copy.wait()
    strip = tiles[...].reshape(3 * CX, CX)
    for zi in range(2):
        for y0 in range(CY):
            part = placed(strip, zi, y0)
            for g in range(3):
                row = halo_row(g, y0)
                if row is not None:
                    out[zi, row] = part[g * CX : (g + 1) * CX, :]


def coefs(own, low, high):
    return pl.pallas_call(
        coef_kernel,
        out_shape=jax.ShapeDtypeStruct((2, YS, CX, CX), F32),
        in_specs=[hspec()] * 3,
        out_specs=vspec(),
        scratch_shapes=[VM((3, XT - 2, 8, CX), F32), pltpu.SemaphoreType.DMA((3,))],
        compiler_params=params(),
        name="coefs",
    )(*far(own, low, high))


def deposit_kernel(
    incoming, top_far, conduct_far, quiet_far, out, peaks, total, top, conduct, quiet, sems
):
    copies = fetch(sems, ((top_far, top), (conduct_far.at[0:2], conduct), (quiet_far, quiet)))
    sources = incoming.shape[0]
    group = 32
    place = lax.broadcasted_iota(jnp.int32, (CX, CX), 0).astype(F32).astype(BF16)
    zero = jnp.zeros((M, CX), BF16)
    total[...] = jnp.zeros_like(total)

    def one(g, carry):
        left = []
        right = []
        for s in range(group):
            source = g * group + s
            index = incoming[source, 32:40, :].astype(F32)
            for slot in range(CAP):
                heat = incoming[source, slot * M : (slot + 1) * M, :]
                layer = jnp.broadcast_to(index[slot : slot + 1, :], (M, CX)).astype(BF16)
                cell = jnp.broadcast_to(index[2 + slot : 3 + slot, :], (CX, CX)).astype(BF16)
                left.append(
                    jnp.concatenate(
                        [jnp.where(layer == h, heat, zero) for h in range(2 * CY)], axis=0
                    )
                )
                right.append(jnp.where(place == cell, 1.0, 0.0).astype(BF16))
        total[...] += lax.dot_general(
            jnp.concatenate(left, axis=1),
            jnp.concatenate(right, axis=1),
            NT,
            preferred_element_type=F32,
        )
        return carry

    lax.fori_loop(0, sources // group, one, 0)
    for zi in range(2):
        out[zi] = (0.5 * total[zi * CX : (zi + 1) * CX, :]).T
    for copy in copies:
        copy.wait()
    peak = quiet[...]
    for zi in range(2):
        c = 0.5 * conduct[zi]
        for m in range(M):
            value = top[m, zi] + 0.5 * total[pl.ds(zi * CX + m, CY, stride=M), :]
            peak = jnp.maximum(peak, c + c * (value * value))
    send_row(whole_peak(peak), peaks)


def send_row(row, out):
    for d in range(0, out.shape[0], 8):
        out[d : d + 8, 0, :] = row


def deposit(incoming, top, conduct, quiet):
    devices = incoming.shape[0]
    return pl.pallas_call(
        deposit_kernel,
        out_shape=[
            kept((2, CX, CX)),
            jax.ShapeDtypeStruct((devices, 1, CX), F32),
        ],
        in_specs=[vspec()] + [hspec()] * 3,
        out_specs=[vspec()] * 2,
        scratch_shapes=[
            VM((2 * CY * M, CX), F32),
            VM(top.shape, F32),
            VM((2, CY, CX), F32),
            VM(quiet.shape, F32),
            pltpu.SemaphoreType.DMA((3,)),
        ],
        compiler_params=params(),
        name="deposit",
    )(incoming, *far(top, conduct, quiet))


def whole_peak(value):
    return jnp.broadcast_to(jnp.max(value, axis=(0, 1), keepdims=True), (8, CX))


def step_of(peak):
    return SHARE / (12.0 * peak + COOL)


def tile(t):
    return slice(8 * t, 8 * t + 8)


def half_conductance(c, u):
    return c + c * (u * u)


def segments(inside, first, end):
    parts = []
    if first < HALO:
        parts.append((first, HALO, False, inside[2]))
    parts.append((max(first, HALO), min(end, HALO + CY), True, None))
    if end > HALO + CY:
        parts.append((HALO + CY, end, False, inside[3]))
    return parts


def mask_of(inside, row_mask, t):
    if t == 0:
        return inside[0] if row_mask is None else inside[0] * row_mask
    if t == XT - 1:
        return inside[1] if row_mask is None else inside[1] * row_mask
    return row_mask


def sweep(field, half, above, inside, first, end, emit, carry):
    lane = lanes()
    row = rows()
    last_row = row == 7
    first_row = row == 0
    inner_lane = lane < CX - M
    cooling = jnp.where(lane < M, COOL, 0.0)

    for zi in range(2):
        for t in range(XT):
            s = tile(t)
            above[zi, t] = (half[zi, first - 1, s, :] + half[zi, first, s, :]) * (
                field[zi, first, s, :] - field[zi, first - 1, s, :]
            )

    def line(own, row_mask, y, state):
        carried = [jnp.zeros((8, CX), F32)] * 2
        for t in range(XT):
            s = tile(t)
            us = [field[zi, y, s, :] for zi in range(2)]
            hs = [half[zi, y, s, :] for zi in range(2)]
            change = []
            for zi in range(2):
                u, h = us[zi], hs[zi]
                if t < XT - 1:
                    after = slice(8 * t + 1, 8 * t + 9)
                    u_after, h_after = field[zi, y, after, :], half[zi, y, after, :]
                else:
                    u_after = jnp.where(last_row, u, pltpu.roll(u, 7, axis=0))
                    h_after = pltpu.roll(h, 7, axis=0)
                along = (h + h_after) * (u_after - u)
                turned = pltpu.roll(along, 1, axis=0)
                total = along - jnp.where(first_row, carried[zi], turned)
                carried[zi] = turned
                across = (h + half[zi, y + 1, s, :]) * (field[zi, y + 1, s, :] - u)
                total = total + (across - above[zi, t])
                above[zi, t] = across
                change.append(total)
            within = (hs[0] + hs[1]) * (us[1] - us[0])
            between = (hs[1] + pltpu.roll(hs[0], CX - M, axis=1)) * (
                pltpu.roll(us[0], CX - M, axis=1) - us[1]
            )
            between = jnp.where(inner_lane, between, 0.0)
            change[0] = change[0] + (within - pltpu.roll(between, M, axis=1)) - cooling * us[0]
            change[1] = change[1] + (between - within)
            state = emit(y, t, us, change, own, mask_of(inside, row_mask, t), state)
        return state

    for start, stop, own, row_mask in segments(inside, first, end):
        carry = lax.fori_loop(start, stop, functools.partial(line, own, row_mask), carry)
    return carry


def advance(field, half, coef, above, inside, step, first, end, put):
    def emit(y, t, us, change, own, mask, peak):
        part = step if mask is None else step * mask
        for zi in range(2):
            value = us[zi] + part * change[zi]
            after = half_conductance(coef[zi, y, tile(t), :], value)
            put(zi, y, t, value, after)
            if own and 0 < t < XT - 1:
                peak = jnp.maximum(peak, after)
        return peak

    return sweep(field, half, above, inside, first, end, emit, jnp.zeros((8, CX), F32))


def propose(field, half, coef, above, inside, guess, first, end, changes, peak, late, out):
    def emit(y, t, us, change, own, mask, best):
        for zi in range(2):
            moved = change[zi] if mask is None else change[zi] * mask
            changes[zi, y, tile(t), :] = moved
            if own and 0 < t < XT - 1:
                c = coef[zi, y, tile(t), :]
                rank = half_conductance(c, us[zi] + guess * moved)
                better = rank > best[0]
                best = tuple(
                    jnp.where(better, new, old)
                    for new, old in zip((rank, us[zi], moved, c), best)
                )
        return best

    best = sweep(
        field, half, above, inside, first, end, emit, (jnp.zeros((8, CX), F32),) * 4
    )
    for shift, axis in ((4, 0), (2, 0), (1, 0), (64, 1), (32, 1)):
        other = tuple(pltpu.roll(part, shift, axis=axis) for part in best)
        better = other[0] > best[0]
        best = tuple(jnp.where(better, new, old) for new, old in zip(other, best))
    part = lanes() >> 4
    chunk = jnp.where(part == 6, whole_peak(peak), whole_peak(late))
    for place, value in ((2, best[3]), (1, best[2]), (0, best[1])):
        chunk = jnp.where((part >> 1) == place, value, chunk)
    send_row(chunk, out)


def gather_rows(parts):
    return [parts[d : d + 8, 0, :] for d in range(0, parts.shape[0], 8)]


def largest(values):
    most = values[0]
    for value in values[1:]:
        most = jnp.maximum(most, value)
    return most


def agree(parts):
    part = lanes() >> 4
    rows_of = gather_rows(parts)
    most = largest(rows_of)
    now = whole_peak(jnp.where(part == 6, most, 0.0))
    late = whole_peak(jnp.where(part == 7, most, 0.0))
    step = step_of(now)
    then = jnp.zeros((8, CX), F32)
    for value in rows_of:
        moved = pltpu.roll(value, CX - 32, axis=1)
        c = pltpu.roll(value, CX - 64, axis=1)
        then = jnp.maximum(then, half_conductance(c, value + step * moved))
    return now, whole_peak(jnp.where(part < 2, then, 0.0)), late


def differs(late, used):
    return jnp.where(late > used * (1.0 + TOLERANCE), 1.0, 0.0)


def heated_kernel(
    inside, peaks, left, right, coef_main, own_far, low_far, high_far,
    heat_low_far, heat_own_far, heat_high_far,
    out, coef, changes, parts, start, half, next_half, above,
    own, low, high, heat_low, heat_own, heat_high, sems,
):
    copies = fetch(
        sems,
        [
            (heat_low_far, heat_low),
            (low_far.at[0:EDGE], low),
            (heat_own_far, heat_own),
            (own_far, own),
            (heat_high_far, heat_high),
            (high_far.at[0:EDGE], high),
        ],
    )
    top = lanes() < M

    strip = jnp.concatenate(
        [side[SIDE + g] for g in range(3) for side in (left, right)], axis=0
    )
    for zi in range(2):
        for y0 in range(CY):
            part = placed(strip, zi, y0)
            for g in range(3):
                at = halo_row(g, y0)
                if at is not None:
                    coef[zi, at, tile(0), :] = part[16 * g : 16 * g + 8, :]
                    coef[zi, at, tile(XT - 1), :] = part[16 * g + 8 : 16 * g + 16, :]

    def row(g, heat, tile_of, y0, yy):
        shift = (CX - 16 * y0) % CX
        for zi in range(2):
            for t in range(XT):
                if t == 0:
                    prior, add = left[zi * YS + yy], left[SIDE + 3 + 2 * g + zi]
                elif t == XT - 1:
                    prior, add = right[zi * YS + yy], right[SIDE + 3 + 2 * g + zi]
                else:
                    prior, add = tile_of(zi, t - 1), heat[zi, tile(t - 1), :]
                if shift:
                    add = pltpu.roll(add, shift, axis=1)
                value = prior + jnp.where(top, add, 0.0)
                if 0 < t < XT - 1:
                    c = coef_main[zi, yy, tile(t - 1), :]
                    coef[zi, yy, tile(t), :] = c
                else:
                    c = coef[zi, yy, tile(t), :]
                after = half_conductance(c, value)
                start[zi, yy, tile(t), :] = value
                half[zi, yy, tile(t), :] = after

    def edge(ref, y):
        return lambda zi, t: ref[zi * HALO + y, t]

    for copy in copies[0:2]:
        copy.wait()
    for y in range(HALO):
        row(0, heat_low, edge(low, y), y + CY - HALO, y)
    for copy in copies[2:4]:
        copy.wait()
    for y in range(CY):
        row(1, heat_own, lambda zi, t: own[zi, y, tile(t), :], y, y + HALO)
    for copy in copies[4:6]:
        copy.wait()
    for y in range(HALO):
        row(2, heat_high, edge(high, y), y, y + HALO + CY)

    def put(zi, y, t, value, after):
        out[zi, y, tile(t), :] = value
        next_half[zi, y, tile(t), :] = after

    step = step_of(whole_peak(largest(gather_rows(peaks))))
    peak = advance(start, half, coef, above, inside, step, 1, YS - 1, put)
    guess = jnp.minimum(step_of(whole_peak(peak)), 2.0 * step)
    zero = jnp.zeros((8, CX), F32)
    propose(
        out, next_half, coef, above, inside, guess, 2, YS - 2, changes, peak, zero, parts
    )


ROW = (2, XT, 8, CX)


def smem():
    return pl.BlockSpec(memory_space=pltpu.SMEM)


def heated(inside, prior, halos, heat, coef, peaks):
    near = [inside, peaks, *halos, coef]
    operands = far(*prior, *heat)
    edge = VM((EDGE, XT - 2, 8, CX), F32)
    return pl.pallas_call(
        heated_kernel,
        out_shape=[WIDE, WIDE, WIDE, jax.ShapeDtypeStruct(peaks.shape, F32)],
        in_specs=[smem()] + [vspec()] * 4 + [hspec()] * len(operands),
        out_specs=[vspec()] * 4,
        scratch_shapes=[VM(WIDE.shape, F32)] * 3
        + [VM(ROW, F32), VM(OWN.shape, F32), edge, edge]
        + [VM(part.shape, F32) for part in heat]
        + [pltpu.SemaphoreType.DMA((6,))],
        compiler_params=params(),
        name="heated",
    )(*near, *operands)


def first_of_pair(field, changes, coef, step, first, end, out, half):
    def line(y, peak):
        top = jnp.zeros((8, CX), F32)
        for zi in range(2):
            for t in range(XT):
                value = field[zi, y, tile(t), :] + step * changes[zi, y, tile(t), :]
                after = half_conductance(coef[zi, y, tile(t), :], value)
                out[zi, y, tile(t), :] = value
                half[zi, y, tile(t), :] = after
                if 0 < t < XT - 1:
                    top = jnp.maximum(top, after)
        own = jnp.where((y >= HALO) & (y < HALO + CY), 1.0, 0.0)
        return jnp.maximum(peak, own * top)

    return lax.fori_loop(first, end, line, jnp.zeros((8, CX), F32))


def pair_kernel(
    number, inside, field, changes, coef, parts,
    out, out_changes, out_parts, status, middle, half, next_half, above,
):
    now, then, _ = agree(parts)
    status[...] = jnp.where(rows() == 0, then, 0.0)
    seen = first_of_pair(
        field, changes, coef, step_of(now), number + 1, YS - 1 - number, middle, half
    )

    def put(zi, y, t, value, after):
        out[zi, y, tile(t), :] = value
        next_half[zi, y, tile(t), :] = after

    step = step_of(then)
    peak = advance(
        middle, half, coef, above, inside, step, number + 2, YS - 2 - number, put
    )
    guess = jnp.minimum(step_of(whole_peak(peak)), 1.2 * step)
    propose(
        out, next_half, coef, above, inside, guess, number + 3, YS - 3 - number,
        out_changes, peak, seen, out_parts,
    )


STATUS = jax.ShapeDtypeStruct((8, CX), F32)


def pair(number, inside, field, changes, coef, parts):
    operands = [inside, field, changes, coef, parts]
    return pl.pallas_call(
        functools.partial(pair_kernel, number),
        out_shape=[WIDE, WIDE, jax.ShapeDtypeStruct(parts.shape, F32), STATUS],
        in_specs=[smem()] + [vspec()] * 4,
        out_specs=[vspec()] * 4,
        scratch_shapes=[VM(WIDE.shape, F32)] * 3 + [VM(ROW, F32)],
        compiler_params=params(),
        name=f"pair_{number}",
    )(*operands)


def closing(
    field, half, above, inside, weight, data, peak, late, out, out_changes, sums, flat
):
    def emit(y, t, us, change, own, mask, state):
        if 0 < t < XT - 1:
            for zi in range(2):
                out[zi, y - HALO, tile(t - 1), :] = us[zi]
                out_changes[zi, y - HALO, tile(t - 1), :] = change[zi]
        return state

    sweep(field, half, above, inside, HALO, HALO + CY, emit, 0)
    grams = jnp.zeros((5 * CY, 3 * M), F32)
    for y in range(CY):
        w = weight[y : y + 1, :]
        for m in range(M):
            flat[m : m + 1, :] = data[m, y : y + 1, :]
        means = []
        spreads = []
        for part in (out, out_changes):
            seen = 2.0 * part[0, y].T[0:M, :]
            mean = jnp.mean(seen, axis=0, keepdims=True)
            means.append(mean)
            spreads.append(seen - mean)
        left = jnp.concatenate(spreads + means + [jnp.zeros((6, CX), F32)], axis=0)
        right = jnp.concatenate([part * w for part in spreads] + [flat[...]], axis=0)
        grams = grams + lax.dot_general(
            left, right, NT, precision=lax.Precision.HIGHEST, preferred_element_type=F32
        )
    grams = jnp.concatenate([grams, jnp.zeros((5 * CY, CX - 3 * M), F32)], axis=1)
    tall = lax.broadcasted_iota(jnp.int32, (M, CX), 0)
    wide = lax.broadcasted_iota(jnp.int32, (M, CX), 1)
    first, second, means = grams[0:M], grams[M : 2 * M], grams[2 * M : 2 * M + 8]

    def block(part, at):
        return jnp.where(wide < M, pltpu.roll(part, (CX - M * at) % CX, axis=1), 0.0)

    def lone(part, row, at):
        moved = pltpu.roll(part, (CX - M * at) % CX, axis=1) if at else part
        return jnp.broadcast_to(moved[row : row + 1, :], (M, CX))

    tops = [
        lone(means, 0, 1) + lone(means, 1, 0),
        lone(means, 0, 0),
        lone(means, 1, 1),
    ]
    blocks = [
        jnp.where(tall < wide, block(first, 0), block(second, 1)),
        block(first, 1) + block(second, 0),
        block(first, 2),
        block(second, 2),
    ]
    scalar = jnp.where(wide == 0, whole_peak(peak)[0:1], whole_peak(late)[0:1])
    blocks[0] = jnp.where(tall == wide, scalar, blocks[0])
    for i, top in enumerate(tops):
        blocks[i + 1] = jnp.where(tall == 0, jnp.where(wide < M, top, 0.0), blocks[i + 1])
    packed = blocks[0]
    for i in range(1, 4):
        packed = packed + pltpu.roll(blocks[i], M * i, axis=1)
    packed = packed[0:8] + pltpu.roll(packed[8:16], CX // 2, axis=1)
    for d in range(sums.shape[0]):
        sums[d] = packed


def last_kernel(
    inside, field, changes, coef, parts, status, weight_far, data_far,
    out, out_changes, sums, out_status,
    middle, half, near, near_half, above, flat, weight, data, sems,
):
    copies = fetch(sems, ((weight_far, weight), (data_far, data)))
    number = SUBSTEPS - 3
    now, then, late = agree(parts)
    bad = differs(late[0:1], status[0:1, :])
    out_status[...] = jnp.where(rows() == 0, then, bad)
    seen = first_of_pair(
        field, changes, coef, step_of(now), number + 1, YS - 1 - number, middle, half
    )

    def put(zi, y, t, value, after):
        near[zi, y, tile(t), :] = value
        near_half[zi, y, tile(t), :] = after

    peak = advance(
        middle, half, coef, above, inside, step_of(then), number + 2, YS - 2 - number, put
    )
    for copy in copies:
        copy.wait()
    closing(
        near, near_half, above, inside, weight, data, peak, seen, out, out_changes, sums, flat
    )


def sums_shape(devices):
    return jax.ShapeDtypeStruct((devices, 8, CX), F32)


def last(inside, field, changes, coef, parts, status, pixels):
    operands = [inside, field, changes, coef, parts, status, *far(*pixels)]
    return pl.pallas_call(
        last_kernel,
        out_shape=[OWN, OWN, sums_shape(parts.shape[0]), STATUS],
        in_specs=[smem()] + [vspec()] * 5 + [hspec()] * 2,
        out_specs=[vspec()] * 4,
        scratch_shapes=[VM(WIDE.shape, F32)] * 4
        + [VM(ROW, F32), VM((M, CX), F32)]
        + [VM(part.shape, F32) for part in pixels]
        + [pltpu.SemaphoreType.DMA((2,))],
        compiler_params=params(),
        name="last_pair",
    )(*operands)


def fill_half(field, coef, half, first, end):
    def fill(y, carry):
        for zi in range(2):
            half[zi, y] = half_conductance(coef[zi, y], field[zi, y])
        return carry

    lax.fori_loop(first, end, fill, 0)


def single_kernel(number, inside, field, coef, peaks, out, out_peaks, half, above):
    step = step_of(whole_peak(largest(gather_rows(peaks))))
    fill_half(field, coef, half, number, YS - number)

    def put(zi, y, t, value, after):
        out[zi, y, tile(t), :] = value

    peak = advance(field, half, coef, above, inside, step, number + 1, YS - 1 - number, put)
    send_row(whole_peak(peak), out_peaks)


def single(number, inside, field, coef, peaks):
    return pl.pallas_call(
        functools.partial(single_kernel, number),
        out_shape=[WIDE, jax.ShapeDtypeStruct(peaks.shape, F32)],
        in_specs=[smem()] + [vspec()] * 3,
        out_specs=[vspec()] * 2,
        scratch_shapes=[VM(WIDE.shape, F32), VM(ROW, F32)],
        compiler_params=params(),
        name=f"single_{number}",
    )(inside, field, coef, peaks)


def closing_kernel(
    inside, field, coef, peaks, weight, data, out, out_changes, sums, half, above, flat
):
    fill_half(field, coef, half, HALO - 1, HALO + CY + 1)
    peak = peaks[0:8, 0, :]
    closing(
        field, half, above, inside, weight, data, peak, jnp.zeros((8, CX), F32),
        out, out_changes, sums, flat,
    )


def close(inside, field, coef, peaks, pixels):
    operands = [inside, field, coef, peaks, *pixels]
    return pl.pallas_call(
        closing_kernel,
        out_shape=[OWN, OWN, sums_shape(peaks.shape[0])],
        in_specs=[smem()] + [vspec()] * (len(operands) - 1),
        out_specs=[vspec()] * 3,
        scratch_shapes=[VM(WIDE.shape, F32), VM(ROW, F32), VM((M, CX), F32)],
        compiler_params=params(),
        name="closing",
    )(*operands)


def pixel_kernel(cell, observed, variance, noise, weight, data):
    pixels = cell.shape[1]
    place = cell[...]
    var = variance[...]
    inverse = 1.0 / var
    values = (observed[...] + noise[...] * jnp.sqrt(var)) * inverse
    stack = jnp.concatenate([values, jnp.broadcast_to(inverse, (8, pixels))], axis=0)
    width = place >> 7
    hot = jnp.where(
        lax.broadcasted_iota(jnp.int32, (CX, pixels), 0) == (place & 127), 1.0, 0.0
    ).astype(F32)
    for y in range(CY):
        part = lax.dot_general(
            jnp.where(width == y, stack, 0.0),
            hot,
            NT,
            precision=lax.Precision.HIGHEST,
            preferred_element_type=F32,
        )
        weight[y : y + 1, :] = part[M : M + 1, :]
        for m in range(M):
            data[m, y : y + 1, :] = part[m : m + 1, :]


def pixel_sums(cell, observed, variance, noise):
    return pl.pallas_call(
        pixel_kernel,
        out_shape=[kept((CY, CX)), kept((M, CY, CX))],
        in_specs=[vspec()] * 4,
        out_specs=[vspec()] * 2,
        compiler_params=params(),
        name="pixels",
    )(cell, observed, variance, noise)


def update_kernel(sums, field, changes, status, out, flag):
    total = sums[0]
    most = total
    for d in range(1, sums.shape[0]):
        total = total + sums[d]
        most = jnp.maximum(most, sums[d])
    step = step_of(jnp.broadcast_to(most[0:1, 0:1], (1, CX)))
    late = jnp.broadcast_to(most[1:2, 1:2], (1, CX))
    bad = jnp.maximum(status[1:2, :], differs(late, status[0:1, :]))
    flag[0] = jnp.where(jnp.max(bad) > 0.0, 1, 0)

    tall = lax.broadcasted_iota(jnp.int32, (M, CX), 0)
    wide = lax.broadcasted_iota(jnp.int32, (M, CX), 1)
    packed = jnp.concatenate([total, pltpu.roll(total, CX // 2, axis=1)], axis=0)

    def block(at):
        return jnp.where(wide < M, pltpu.roll(packed, (CX - M * at) % CX, axis=1), 0.0)

    def whole(part):
        rest = jnp.where(tall == 0, 0.0, part)
        first = -jnp.sum(rest, axis=0, keepdims=True)
        return jnp.where(tall == 0, first, rest), part[0:1, :]

    def balanced(part):
        part = jnp.where((tall == wide) | (wide >= M), 0.0, part)
        return jnp.where(tall == wide, -jnp.sum(part, axis=1, keepdims=True), part)

    corner = block(0)
    mirror = jnp.concatenate([corner, jnp.zeros((CX - M, CX), F32)], axis=0).T[0:M, :]
    square = balanced(jnp.where(tall < wide, corner, mirror))
    square_c = balanced(jnp.where(tall > wide, corner, mirror))
    mixed, mean_1 = whole(block(1))
    data, mean_0 = whole(block(2))
    data_c, mean_2 = whole(block(3))
    cross = square + step * (mixed + step * square_c)
    mean = mean_0 + step * (mean_1 + step * mean_2)
    mean = jnp.sum(jnp.where(tall == wide, mean, 0.0), axis=1, keepdims=True)
    target = jnp.where(wide < M, data + step * data_c - cross - mean, 0.0)
    system = jnp.where(tall == wide, cross + (M - 1.0), cross)
    system = system + pltpu.roll(target, M, axis=1)
    for i in range(M):
        pivot = system[i : i + 1, :]
        pivot = pivot / pivot[:, i : i + 1]
        factor = jnp.where(tall == i, 0.0, jnp.broadcast_to(system[:, i : i + 1], (M, CX)))
        system = jnp.where(tall == i, pivot, system - factor * pivot)
    mixing = system - jnp.mean(system, axis=0, keepdims=True)
    mixing = pltpu.roll(mixing, CX - M, axis=1)
    mixing = jnp.where(wide < M, mixing + jnp.where(tall == wide, 1.0, 0.0), 0.0)
    for shift in (16, 32, 64):
        mixing = mixing + pltpu.roll(mixing, shift, axis=1)
    mixing = jnp.concatenate([mixing] * ZG, axis=0)
    tall = lax.broadcasted_iota(jnp.int32, (CX, CX), 0)
    wide = lax.broadcasted_iota(jnp.int32, (CX, CX), 1)
    mixing = jnp.where((tall >> 4) == (wide >> 4), 2.0 * mixing, 0.0).T
    for zi in range(2):
        for y in range(CY):
            part = lax.dot_general(
                mixing,
                field[zi, y] + step * changes[zi, y],
                NT,
                precision=lax.Precision.HIGHEST,
                preferred_element_type=F32,
            )
            for group in range(ZG):
                for m0 in (0, 8):
                    at = group * M + m0
                    out[m0 : m0 + 8, 2 * group + zi, y, :] = part[at : at + 8, :]


def update(sums, field, changes, status):
    return pl.pallas_call(
        update_kernel,
        out_shape=[
            jax.ShapeDtypeStruct((M, NZ, CY, CX), F32),
            jax.ShapeDtypeStruct((1,), jnp.int32),
        ],
        in_specs=[vspec()] * 4,
        out_specs=[vspec(), smem()],
        compiler_params=params(),
        name="update",
    )(sums, field, changes, status)


def exchange(parts):
    return lax.all_to_all(parts, BOTH, split_axis=0, concat_axis=0, tiled=True)


def move(part, axis, ahead):
    count = lax.axis_size(axis)
    pairs = [(i, i + 1) if ahead else (i + 1, i) for i in range(count - 1)]
    return lax.ppermute(part, axis, pairs)


def on_device(
    state_prior,
    conductivity,
    heat_input,
    owner_tile,
    voxel_list,
    pixel_cell,
    observed,
    pixel_variance,
    pixel_noise,
):
    devices = lax.axis_size("gx") * lax.axis_size("gy")
    pixels = pixel_cell.shape[0]
    gx, gy = lax.axis_index("gx"), lax.axis_index("gy")
    inside = jnp.stack(
        [gx > 0, gx < lax.axis_size("gx") - 1, gy > 0, gy < lax.axis_size("gy") - 1]
    ).astype(F32)
    incoming = exchange(pack(owner_tile.reshape(-1), heat_input, voxel_list, devices))
    own, turned_c, to_high, to_low, edge_left, edge_right, top, quiet = relayout(
        state_prior, conductivity
    )
    low, high = move(to_high, "gy", True), move(to_low, "gy", False)
    seen = pixel_sums(
        pixel_cell.reshape(1, pixels),
        observed.reshape(1, pixels),
        pixel_variance.reshape(1, pixels),
        pixel_noise,
    )
    incoming, own, top, inside, *seen = lax.optimization_barrier(
        (incoming, own, top, inside, *seen)
    )
    heat, peaks = deposit(incoming, top, conductivity, quiet)
    heat_low, heat_high = move(heat, "gy", True), move(heat, "gy", False)
    low, high, heat_low, heat_high, peaks = lax.optimization_barrier(
        (low, high, heat_low, heat_high, exchange(peaks))
    )
    to_left, to_right = sides(
        edge_left, edge_right, turned_c, low, high, heat_low, heat, heat_high
    )
    left, right = move(to_right, "gx", True), move(to_left, "gx", False)
    start, coef, changes, parts = heated(
        inside,
        (own, low, high),
        (left, right),
        (heat_low, heat, heat_high),
        coefs(turned_c, low, high),
        peaks,
    )
    field, changes, parts, status = pair(1, inside, start, changes, coef, exchange(parts))
    field, changes, sums, status = last(
        inside, field, changes, coef, exchange(parts), status, seen
    )
    result, flag = update(exchange(sums), field, changes, status)

    def again():
        peak = coef * (1.0 + start * start)
        peaks = jnp.full((devices, 1, CX), jnp.max(peak[:, HALO : HALO + CY, 8 : XS - 8]))
        field = start
        for number in range(1, SUBSTEPS - 1):
            field, peaks = single(number, inside, field, coef, exchange(peaks))
        field, changes, sums = close(inside, field, coef, peaks, seen)
        return update(exchange(sums), field, changes, jnp.ones((8, CX), F32))[0]

    return lax.cond(flag[0] > 0, again, lambda: result)


def solution(mesh):
    in_specs = (
        P(None, None, "gy", "gx"),
        P(None, "gy", "gx"),
        P(None, BOTH, None),
        P(BOTH, None),
        P(BOTH, None),
        P(BOTH),
        P(BOTH),
        P(BOTH),
        P(None, BOTH),
    )
    out_specs = P(None, None, "gy", "gx")
    return jax.shard_map(
        on_device, mesh=mesh, in_specs=in_specs, out_specs=out_specs, check_vma=False
    )
```

```python
import functools

import jax
import jax.numpy as jnp
from jax import lax
from jax.experimental import pallas as pl
from jax.experimental.pallas import tpu as pltpu
from jax.sharding import PartitionSpec as P

SUBSTEPS = 6
CAP = 2
COOL = 0.1
SHARE = 0.9
F32 = jnp.float32
BF16 = jnp.bfloat16
VM = pltpu.VMEM
LIMIT = 32 * 1024 * 1024
NT = (((1,), (1,)), ((), ()))
BOTH = ("gx", "gy")

M, NZ, CY, CX = 16, 16, 8, 128
ROWS = 40


def vspec():
    return pl.BlockSpec(memory_space=pltpu.VMEM)


def hspec():
    return pl.BlockSpec(memory_space=pltpu.HBM)


def far(*arrays):
    return [pltpu.with_memory_space_constraint(array, pltpu.HBM) for array in arrays]


def kept(shape):
    return pltpu.HBM(tuple(shape), F32)


def fetch(sems, pairs):
    copies = [
        pltpu.make_async_copy(source, target, sems.at[i])
        for i, (source, target) in enumerate(pairs)
    ]
    for copy in copies:
        copy.start()
    return copies


def params():
    return pltpu.CompilerParams(vmem_limit_bytes=LIMIT)


def lanes():
    return lax.broadcasted_iota(jnp.int32, (CY, CX), 1)


def rows():
    return lax.broadcasted_iota(jnp.int32, (CY, CX), 0)


def pack_kernel(owner_far, heat_far, voxel_far, out, owner, heat, voxel, wide, high, low, inverse, sems):
    copies = fetch(sems, ((owner_far, owner), (heat_far, heat), (voxel_far, voxel)))
    blocks = owner.shape[0]
    devices = out.shape[0]

    def clear(i, carry):
        inverse[i] = blocks
        return carry

    lax.fori_loop(0, devices * CAP, clear, 0, unroll=16)
    copies[0].wait()

    def place(b, carry):
        base = owner[b] * CAP
        base = base + jnp.where(inverse[base] != blocks, 1, 0)
        inverse[base] = b
        return carry

    lax.fori_loop(0, blocks, place, 0, unroll=8)
    copies[1].wait()
    copies[2].wait()

    def widen(m, carry):
        wide[m, 0:blocks, :] = heat[m].astype(F32)
        wide[m, blocks:, :] = jnp.zeros((8, CX), F32)
        return carry

    lax.fori_loop(0, M, widen, 0)
    cells = voxel[...]
    high[0:blocks, :] = (cells >> 7).astype(F32)
    high[blocks:, :] = jnp.zeros((8, CX), F32)
    low[0:blocks, :] = (cells & 127).astype(F32)
    low[blocks:, :] = jnp.zeros((8, CX), F32)
    row = rows()

    def emit(d, carry):
        first = inverse[d * CAP]
        second = inverse[d * CAP + 1]
        index = jnp.where(
            row == 0,
            high[pl.ds(first, 1), :],
            jnp.where(
                row == 1,
                high[pl.ds(second, 1), :],
                jnp.where(
                    row == 2,
                    low[pl.ds(first, 1), :],
                    jnp.where(row == 3, low[pl.ds(second, 1), :], 0.0),
                ),
            ),
        )
        chunk = jnp.concatenate(
            [
                wide[:, pl.ds(first, 1), :].reshape(M, CX),
                wide[:, pl.ds(second, 1), :].reshape(M, CX),
                index,
            ],
            axis=0,
        )
        out[d] = chunk.astype(BF16)
        return carry

    lax.fori_loop(0, devices, emit, 0, unroll=16)


def pack(owner, heat, voxel, devices):
    blocks = owner.shape[0]
    return pl.pallas_call(
        pack_kernel,
        out_shape=jax.ShapeDtypeStruct((devices, ROWS, CX), BF16),
        in_specs=[hspec()] * 3,
        out_specs=vspec(),
        scratch_shapes=[
            pltpu.SMEM((blocks,), jnp.int32),
            VM((M, blocks, CX), BF16),
            VM((blocks, CX), jnp.int32),
            VM((M, blocks + 8, CX), F32),
            VM((blocks + 8, CX), F32),
            VM((blocks + 8, CX), F32),
            pltpu.SMEM((devices * CAP,), jnp.int32),
            pltpu.SemaphoreType.DMA((3,)),
        ],
        compiler_params=params(),
        name="pack",
    )(*far(owner, heat, voxel))


HALO = 6
YS = CY + 2 * HALO
XT = CX // 8 + 2
ZG = NZ // 2
TOLERANCE = 1e-6
OWN = jax.ShapeDtypeStruct((2, CY, CX, CX), F32)
XS = 8 * XT
WIDE = jax.ShapeDtypeStruct((2, YS, XS, CX), F32)
EDGE = 2 * HALO
SIDE = 2 * YS


def relayout_kernel(
    state, conduct, own, turned_c, to_high, to_low, edge_left, edge_right, top, quiet
):
    turned = (0.5 * conduct[...].reshape(CX, CX)).T.reshape(XT - 2, 8, CX)
    turned_c[...] = turned
    to_high[EDGE] = turned
    to_low[EDGE] = turned
    peak = jnp.zeros((8, CX), F32)
    for zi in range(2):
        for y in range(CY):
            parts = []
            for group in range(ZG):
                layer = 2 * group + zi
                c = 0.5 * conduct[layer, y : y + 1, :]
                for m0 in (0, 8):
                    part = 0.5 * state[m0 : m0 + 8, layer, y, :]
                    parts.append(part)
                    if group:
                        peak = jnp.maximum(peak, c + c * (part * part))
            turned = jnp.concatenate(parts, axis=0).T
            own[zi, y] = turned
            turned = turned.reshape(XT - 2, 8, CX)
            edge_left[zi * CY + y] = turned[0]
            edge_right[zi * CY + y] = turned[XT - 3]
            if y >= CY - HALO:
                to_high[zi * HALO + y - (CY - HALO)] = turned
            if y < HALO:
                to_low[zi * HALO + y] = turned
    quiet[...] = peak
    for m in range(M):
        for zi in range(2):
            top[m, zi] = 0.5 * state[m, zi]


def relayout(state, conduct):
    edge = kept((EDGE + 1, XT - 2, 8, CX))
    side = kept((2 * CY, 8, CX))
    return pl.pallas_call(
        relayout_kernel,
        out_shape=[
            kept(OWN.shape),
            kept((XT - 2, 8, CX)),
            edge,
            edge,
            side,
            side,
            kept((M, 2, CY, CX)),
            kept((8, CX)),
        ],
        in_specs=[vspec()] * 2,
        out_specs=[vspec()] * 8,
        compiler_params=params(),
        name="relayout",
    )(state, conduct)


def side_kernel(
    edge_left, edge_right, turned_c, low, high, heat_low, heat_own, heat_high,
    to_left, to_right, sems,
):
    pairs = []
    for out, edge, t in ((to_left, edge_left, 0), (to_right, edge_right, XT - 3)):
        for zi in range(2):
            at, rows_at = zi * YS, slice(zi * HALO, zi * HALO + HALO)
            pairs += [
                (low.at[rows_at, t], out.at[at : at + HALO]),
                (edge.at[zi * CY : zi * CY + CY], out.at[at + HALO : at + HALO + CY]),
                (high.at[rows_at, t], out.at[at + HALO + CY : at + YS]),
            ]
            for g, heat in enumerate((heat_low, heat_own, heat_high)):
                pairs.append((heat.at[zi, 8 * t : 8 * t + 8, :], out.at[SIDE + 3 + 2 * g + zi]))
        for g, part in enumerate((low.at[EDGE, t], turned_c.at[t], high.at[EDGE, t])):
            pairs.append((part, out.at[SIDE + g]))
    for copy in fetch(sems, pairs):
        copy.wait()


def sides(*operands):
    shape = jax.ShapeDtypeStruct((SIDE + 9, 8, CX), F32)
    return pl.pallas_call(
        side_kernel,
        out_shape=[shape, shape],
        in_specs=[hspec()] * len(operands),
        out_specs=[vspec()] * 2,
        scratch_shapes=[pltpu.SemaphoreType.DMA((30,))],
        compiler_params=params(),
        name="sides",
    )(*far(*operands))


def split(strip):
    parts = []
    for _ in range(3):
        part = strip.astype(BF16)
        parts.append(part)
        strip = strip - part.astype(F32)
    return jnp.concatenate(parts, axis=1)


def placed(parts, zi, y0):
    source = lax.broadcasted_iota(jnp.int32, (CX, CX), 0)
    target = lax.broadcasted_iota(jnp.int32, (CX, CX), 1)
    hot = jnp.where(source == (2 * (target >> 4) + zi) * CY + y0, 1.0, 0.0).astype(BF16)
    hot = jnp.concatenate([hot] * 3, axis=0)
    return jnp.dot(parts, hot, preferred_element_type=F32)


def halo_row(g, y0):
    row = y0 + HALO + (g - 1) * CY
    return row if 0 <= row < YS else None


def coef_kernel(own, low, high, out, tiles, sems):
    pairs = ((low.at[EDGE], tiles.at[0]), (own, tiles.at[1]), (high.at[EDGE], tiles.at[2]))
    for copy in fetch(sems, pairs):
        copy.wait()
    strip = split(tiles[...].reshape(3 * CX, CX))
    for zi in range(2):
        for y0 in range(CY):
            part = placed(strip, zi, y0)
            for g in range(3):
                row = halo_row(g, y0)
                if row is not None:
                    out[zi, row] = part[g * CX : (g + 1) * CX, :]


def coefs(own, low, high):
    return pl.pallas_call(
        coef_kernel,
        out_shape=jax.ShapeDtypeStruct((2, YS, CX, CX), F32),
        in_specs=[hspec()] * 3,
        out_specs=vspec(),
        scratch_shapes=[VM((3, XT - 2, 8, CX), F32), pltpu.SemaphoreType.DMA((3,))],
        compiler_params=params(),
        name="coefs",
    )(*far(own, low, high))


def deposit_kernel(
    incoming, top_far, conduct_far, quiet_far, out, peaks, total, top, conduct, quiet, sems
):
    copies = fetch(sems, ((top_far, top), (conduct_far.at[0:2], conduct), (quiet_far, quiet)))
    sources = incoming.shape[0]
    group = 32
    place = lax.broadcasted_iota(jnp.int32, (CX, CX), 0).astype(F32).astype(BF16)
    zero = jnp.zeros((M, CX), BF16)
    total[...] = jnp.zeros_like(total)

    def one(g, carry):
        left = []
        right = []
        for s in range(group):
            source = g * group + s
            index = incoming[source, 32:40, :].astype(F32)
            for slot in range(CAP):
                heat = incoming[source, slot * M : (slot + 1) * M, :]
                layer = jnp.broadcast_to(index[slot : slot + 1, :], (M, CX)).astype(BF16)
                cell = jnp.broadcast_to(index[2 + slot : 3 + slot, :], (CX, CX)).astype(BF16)
                left.append(
                    jnp.concatenate(
                        [jnp.where(layer == h, heat, zero) for h in range(2 * CY)], axis=0
                    )
                )
                right.append(jnp.where(place == cell, 1.0, 0.0).astype(BF16))
        total[...] += lax.dot_general(
            jnp.concatenate(left, axis=1),
            jnp.concatenate(right, axis=1),
            NT,
            preferred_element_type=F32,
        )
        return carry

    lax.fori_loop(0, sources // group, one, 0)
    for zi in range(2):
        out[zi] = (0.5 * total[zi * CX : (zi + 1) * CX, :]).T
    for copy in copies:
        copy.wait()
    peak = quiet[...]
    for zi in range(2):
        c = 0.5 * conduct[zi]
        for m in range(M):
            value = top[m, zi] + 0.5 * total[pl.ds(zi * CX + m, CY, stride=M), :]
            peak = jnp.maximum(peak, c + c * (value * value))
    send_row(whole_peak(peak), peaks)


def send_row(row, out):
    for d in range(0, out.shape[0], 8):
        out[d : d + 8, 0, :] = row


def deposit(incoming, top, conduct, quiet):
    devices = incoming.shape[0]
    return pl.pallas_call(
        deposit_kernel,
        out_shape=[
            kept((2, CX, CX)),
            jax.ShapeDtypeStruct((devices, 1, CX), F32),
        ],
        in_specs=[vspec()] + [hspec()] * 3,
        out_specs=[vspec()] * 2,
        scratch_shapes=[
            VM((2 * CY * M, CX), F32),
            VM(top.shape, F32),
            VM((2, CY, CX), F32),
            VM(quiet.shape, F32),
            pltpu.SemaphoreType.DMA((3,)),
        ],
        compiler_params=params(),
        name="deposit",
    )(incoming, *far(top, conduct, quiet))


def whole_peak(value):
    return jnp.broadcast_to(jnp.max(value, axis=(0, 1), keepdims=True), (8, CX))


def step_of(peak):
    return SHARE / (12.0 * peak + COOL)


def tile(t):
    return slice(8 * t, 8 * t + 8)


def half_conductance(c, u):
    return c + c * (u * u)


def segments(inside, first, end):
    parts = []
    if first < HALO:
        parts.append((first, HALO, False, inside[2]))
    parts.append((max(first, HALO), min(end, HALO + CY), True, None))
    if end > HALO + CY:
        parts.append((HALO + CY, end, False, inside[3]))
    return parts


def mask_of(inside, row_mask, t):
    if t == 0:
        return inside[0] if row_mask is None else inside[0] * row_mask
    if t == XT - 1:
        return inside[1] if row_mask is None else inside[1] * row_mask
    return row_mask


def sweep(field, half, above, inside, first, end, emit, carry):
    lane = lanes()
    row = rows()
    last_row = row == 7
    first_row = row == 0
    inner_lane = lane < CX - M
    outer_lane = lane >= M
    cooling = jnp.where(lane < M, COOL, 0.0)

    for zi in range(2):
        for t in range(XT):
            s = tile(t)
            above[zi, t] = (half[zi, first - 1, s, :] + half[zi, first, s, :]) * (
                field[zi, first, s, :] - field[zi, first - 1, s, :]
            )

    def line(own, row_mask, y, state):
        for t in range(XT):
            s = tile(t)
            us = [field[zi, y, s, :] for zi in range(2)]
            hs = [half[zi, y, s, :] for zi in range(2)]
            change = []
            for zi in range(2):
                u, h = us[zi], hs[zi]
                if t < XT - 1:
                    after = slice(8 * t + 1, 8 * t + 9)
                    u_after, h_after = field[zi, y, after, :], half[zi, y, after, :]
                else:
                    u_after = jnp.where(last_row, u, pltpu.roll(u, 7, axis=0))
                    h_after = pltpu.roll(h, 7, axis=0)
                if t:
                    before = slice(8 * t - 1, 8 * t + 7)
                    u_before, h_before = field[zi, y, before, :], half[zi, y, before, :]
                else:
                    u_before = jnp.where(first_row, u, pltpu.roll(u, 1, axis=0))
                    h_before = pltpu.roll(h, 1, axis=0)
                total = (h + h_after) * (u_after - u) + (h + h_before) * (u_before - u)
                across = (h + half[zi, y + 1, s, :]) * (field[zi, y + 1, s, :] - u)
                total = total + (across - above[zi, t])
                above[zi, t] = across
                change.append(total)
            within = (hs[0] + hs[1]) * (us[1] - us[0])
            between = (hs[1] + pltpu.roll(hs[0], CX - M, axis=1)) * (
                pltpu.roll(us[0], CX - M, axis=1) - us[1]
            )
            between = jnp.where(inner_lane, between, 0.0)
            below = (hs[0] + pltpu.roll(hs[1], M, axis=1)) * (us[0] - pltpu.roll(us[1], M, axis=1))
            below = jnp.where(outer_lane, below, 0.0)
            change[0] = change[0] + (within - below) - cooling * us[0]
            change[1] = change[1] + (between - within)
            state = emit(y, t, us, change, own, mask_of(inside, row_mask, t), state)
        return state

    for start, stop, own, row_mask in segments(inside, first, end):
        carry = lax.fori_loop(start, stop, functools.partial(line, own, row_mask), carry)
    return carry


def advance(field, half, coef, above, inside, step, first, end, put):
    def emit(y, t, us, change, own, mask, peak):
        part = step if mask is None else step * mask
        for zi in range(2):
            value = us[zi] + part * change[zi]
            after = half_conductance(coef[zi, y, tile(t), :], value)
            put(zi, y, t, value, after)
            if own and 0 < t < XT - 1:
                peak = jnp.maximum(peak, after)
        return peak

    return sweep(field, half, above, inside, first, end, emit, jnp.zeros((8, CX), F32))


def propose(field, half, coef, above, inside, guess, first, end, changes, peak, late, out):
    def emit(y, t, us, change, own, mask, best):
        for zi in range(2):
            moved = change[zi] if mask is None else change[zi] * mask
            changes[zi, y, tile(t), :] = moved
            if own and 0 < t < XT - 1:
                c = coef[zi, y, tile(t), :]
                rank = half_conductance(c, us[zi] + guess * moved)
                better = rank > best[0]
                best = tuple(
                    jnp.where(better, new, old)
                    for new, old in zip((rank, us[zi], moved, c), best)
                )
        return best

    best = sweep(
        field, half, above, inside, first, end, emit, (jnp.zeros((8, CX), F32),) * 4
    )
    for shift, axis in ((4, 0), (2, 0), (1, 0), (64, 1), (32, 1)):
        other = tuple(pltpu.roll(part, shift, axis=axis) for part in best)
        better = other[0] > best[0]
        best = tuple(jnp.where(better, new, old) for new, old in zip(other, best))
    part = lanes() >> 4
    chunk = jnp.where(part == 6, whole_peak(peak), whole_peak(late))
    for place, value in ((2, best[3]), (1, best[2]), (0, best[1])):
        chunk = jnp.where((part >> 1) == place, value, chunk)
    send_row(chunk, out)


def gather_rows(parts):
    return [parts[d : d + 8, 0, :] for d in range(0, parts.shape[0], 8)]


def largest(values):
    most = values[0]
    for value in values[1:]:
        most = jnp.maximum(most, value)
    return most


def agree(parts):
    part = lanes() >> 4
    rows_of = gather_rows(parts)
    most = largest(rows_of)
    now = whole_peak(jnp.where(part == 6, most, 0.0))
    late = whole_peak(jnp.where(part == 7, most, 0.0))
    step = step_of(now)
    then = jnp.zeros((8, CX), F32)
    for value in rows_of:
        moved = pltpu.roll(value, CX - 32, axis=1)
        c = pltpu.roll(value, CX - 64, axis=1)
        then = jnp.maximum(then, half_conductance(c, value + step * moved))
    return now, whole_peak(jnp.where(part < 2, then, 0.0)), late


def differs(late, used):
    return jnp.where(late > used * (1.0 + TOLERANCE), 1.0, 0.0)


def heated_kernel(
    inside, peaks, left, right, coef_main, own_far, low_far, high_far,
    heat_low_far, heat_own_far, heat_high_far,
    out, coef, changes, parts, start, half, next_half, above,
    own, low, high, heat_low, heat_own, heat_high, sems,
):
    copies = fetch(
        sems,
        [
            (heat_low_far, heat_low),
            (low_far.at[0:EDGE], low),
            (heat_own_far, heat_own),
            (own_far, own),
            (heat_high_far, heat_high),
            (high_far.at[0:EDGE], high),
        ],
    )
    top = lanes() < M

    strip = split(
        jnp.concatenate([side[SIDE + g] for g in range(3) for side in (left, right)], axis=0)
    )
    for zi in range(2):
        for y0 in range(CY):
            part = placed(strip, zi, y0)
            for g in range(3):
                at = halo_row(g, y0)
                if at is not None:
                    coef[zi, at, tile(0), :] = part[16 * g : 16 * g + 8, :]
                    coef[zi, at, tile(XT - 1), :] = part[16 * g + 8 : 16 * g + 16, :]

    def row(g, heat, tile_of, y0, yy):
        shift = (CX - 16 * y0) % CX
        for zi in range(2):
            for t in range(XT):
                if t == 0:
                    prior, add = left[zi * YS + yy], left[SIDE + 3 + 2 * g + zi]
                elif t == XT - 1:
                    prior, add = right[zi * YS + yy], right[SIDE + 3 + 2 * g + zi]
                else:
                    prior, add = tile_of(zi, t - 1), heat[zi, tile(t - 1), :]
                if shift:
                    add = pltpu.roll(add, shift, axis=1)
                value = prior + jnp.where(top, add, 0.0)
                if 0 < t < XT - 1:
                    c = coef_main[zi, yy, tile(t - 1), :]
                    coef[zi, yy, tile(t), :] = c
                else:
                    c = coef[zi, yy, tile(t), :]
                after = half_conductance(c, value)
                start[zi, yy, tile(t), :] = value
                half[zi, yy, tile(t), :] = after

    def edge(ref, y):
        return lambda zi, t: ref[zi * HALO + y, t]

    for copy in copies[0:2]:
        copy.wait()
    for y in range(HALO):
        row(0, heat_low, edge(low, y), y + CY - HALO, y)
    for copy in copies[2:4]:
        copy.wait()
    for y in range(CY):
        row(1, heat_own, lambda zi, t: own[zi, y, tile(t), :], y, y + HALO)
    for copy in copies[4:6]:
        copy.wait()
    for y in range(HALO):
        row(2, heat_high, edge(high, y), y, y + HALO + CY)

    def put(zi, y, t, value, after):
        out[zi, y, tile(t), :] = value
        next_half[zi, y, tile(t), :] = after

    step = step_of(whole_peak(largest(gather_rows(peaks))))
    peak = advance(start, half, coef, above, inside, step, 1, YS - 1, put)
    guess = jnp.minimum(step_of(whole_peak(peak)), 2.0 * step)
    zero = jnp.zeros((8, CX), F32)
    propose(
        out, next_half, coef, above, inside, guess, 2, YS - 2, changes, peak, zero, parts
    )


ROW = (2, XT, 8, CX)


def smem():
    return pl.BlockSpec(memory_space=pltpu.SMEM)


def heated(inside, prior, halos, heat, coef, peaks):
    near = [inside, peaks, *halos, coef]
    operands = far(*prior, *heat)
    edge = VM((EDGE, XT - 2, 8, CX), F32)
    return pl.pallas_call(
        heated_kernel,
        out_shape=[WIDE, WIDE, WIDE, jax.ShapeDtypeStruct(peaks.shape, F32)],
        in_specs=[smem()] + [vspec()] * 4 + [hspec()] * len(operands),
        out_specs=[vspec()] * 4,
        scratch_shapes=[VM(WIDE.shape, F32)] * 3
        + [VM(ROW, F32), VM(OWN.shape, F32), edge, edge]
        + [VM(part.shape, F32) for part in heat]
        + [pltpu.SemaphoreType.DMA((6,))],
        compiler_params=params(),
        name="heated",
    )(*near, *operands)


def first_of_pair(field, changes, coef, step, first, end, out, half):
    def line(y, peak):
        top = jnp.zeros((8, CX), F32)
        for zi in range(2):
            for t in range(XT):
                value = field[zi, y, tile(t), :] + step * changes[zi, y, tile(t), :]
                after = half_conductance(coef[zi, y, tile(t), :], value)
                out[zi, y, tile(t), :] = value
                half[zi, y, tile(t), :] = after
                if 0 < t < XT - 1:
                    top = jnp.maximum(top, after)
        own = jnp.where((y >= HALO) & (y < HALO + CY), 1.0, 0.0)
        return jnp.maximum(peak, own * top)

    return lax.fori_loop(first, end, line, jnp.zeros((8, CX), F32))


def pair_kernel(
    number, inside, field, changes, coef, parts,
    out, out_changes, out_parts, status, middle, half, next_half, above,
):
    now, then, _ = agree(parts)
    status[...] = jnp.where(rows() == 0, then, 0.0)
    seen = first_of_pair(
        field, changes, coef, step_of(now), number + 1, YS - 1 - number, middle, half
    )

    def put(zi, y, t, value, after):
        out[zi, y, tile(t), :] = value
        next_half[zi, y, tile(t), :] = after

    step = step_of(then)
    peak = advance(
        middle, half, coef, above, inside, step, number + 2, YS - 2 - number, put
    )
    guess = jnp.minimum(step_of(whole_peak(peak)), 1.2 * step)
    propose(
        out, next_half, coef, above, inside, guess, number + 3, YS - 3 - number,
        out_changes, peak, seen, out_parts,
    )


STATUS = jax.ShapeDtypeStruct((8, CX), F32)


def pair(number, inside, field, changes, coef, parts):
    operands = [inside, field, changes, coef, parts]
    return pl.pallas_call(
        functools.partial(pair_kernel, number),
        out_shape=[WIDE, WIDE, jax.ShapeDtypeStruct(parts.shape, F32), STATUS],
        in_specs=[smem()] + [vspec()] * 4,
        out_specs=[vspec()] * 4,
        scratch_shapes=[VM(WIDE.shape, F32)] * 3 + [VM(ROW, F32)],
        compiler_params=params(),
        name=f"pair_{number}",
    )(*operands)


def closing(
    field, half, above, inside, weight, data, peak, late, out, out_changes, sums, flat
):
    def emit(y, t, us, change, own, mask, state):
        if 0 < t < XT - 1:
            for zi in range(2):
                out[zi, y - HALO, tile(t - 1), :] = us[zi]
                out_changes[zi, y - HALO, tile(t - 1), :] = change[zi]
        return state

    sweep(field, half, above, inside, HALO, HALO + CY, emit, 0)
    lefts, rights = [], []
    for y in range(CY):
        w = weight[y : y + 1, :]
        for m in range(M):
            flat[m : m + 1, :] = data[m, y : y + 1, :]
        means = []
        spreads = []
        for part in (out, out_changes):
            seen = 2.0 * part[0, y].T[0:M, :]
            mean = jnp.mean(seen, axis=0, keepdims=True)
            means.append(mean)
            spreads.append(seen - mean)
        lefts.append(jnp.concatenate(spreads + means + [jnp.zeros((6, CX), F32)], axis=0))
        rights.append(jnp.concatenate([part * w for part in spreads] + [flat[...]], axis=0))
    grams = lax.dot_general(
        jnp.concatenate(lefts, axis=1),
        jnp.concatenate(rights, axis=1),
        NT,
        precision=lax.Precision.HIGHEST,
        preferred_element_type=F32,
    )
    grams = jnp.concatenate([grams, jnp.zeros((5 * CY, CX - 3 * M), F32)], axis=1)
    tall = lax.broadcasted_iota(jnp.int32, (M, CX), 0)
    wide = lax.broadcasted_iota(jnp.int32, (M, CX), 1)
    first, second, means = grams[0:M], grams[M : 2 * M], grams[2 * M : 2 * M + 8]

    def block(part, at):
        return jnp.where(wide < M, pltpu.roll(part, (CX - M * at) % CX, axis=1), 0.0)

    def lone(part, row, at):
        moved = pltpu.roll(part, (CX - M * at) % CX, axis=1) if at else part
        return jnp.broadcast_to(moved[row : row + 1, :], (M, CX))

    tops = [
        lone(means, 0, 1) + lone(means, 1, 0),
        lone(means, 0, 0),
        lone(means, 1, 1),
    ]
    blocks = [
        jnp.where(tall < wide, block(first, 0), block(second, 1)),
        block(first, 1) + block(second, 0),
        block(first, 2),
        block(second, 2),
    ]
    scalar = jnp.where(wide == 0, whole_peak(peak)[0:1], whole_peak(late)[0:1])
    blocks[0] = jnp.where(tall == wide, scalar, blocks[0])
    for i, top in enumerate(tops):
        blocks[i + 1] = jnp.where(tall == 0, jnp.where(wide < M, top, 0.0), blocks[i + 1])
    packed = blocks[0]
    for i in range(1, 4):
        packed = packed + pltpu.roll(blocks[i], M * i, axis=1)
    packed = packed[0:8] + pltpu.roll(packed[8:16], CX // 2, axis=1)
    for d in range(sums.shape[0]):
        sums[d] = packed


def last_kernel(
    inside, field, changes, coef, parts, status, weight_far, data_far,
    out, out_changes, sums, out_status,
    middle, half, near, near_half, above, flat, weight, data, sems,
):
    copies = fetch(sems, ((weight_far, weight), (data_far, data)))
    number = SUBSTEPS - 3
    now, then, late = agree(parts)
    bad = differs(late[0:1], status[0:1, :])
    out_status[...] = jnp.where(rows() == 0, then, bad)
    seen = first_of_pair(
        field, changes, coef, step_of(now), number + 1, YS - 1 - number, middle, half
    )

    def put(zi, y, t, value, after):
        near[zi, y, tile(t), :] = value
        near_half[zi, y, tile(t), :] = after

    peak = advance(
        middle, half, coef, above, inside, step_of(then), number + 2, YS - 2 - number, put
    )
    for copy in copies:
        copy.wait()
    closing(
        near, near_half, above, inside, weight, data, peak, seen, out, out_changes, sums, flat
    )


def sums_shape(devices):
    return jax.ShapeDtypeStruct((devices, 8, CX), F32)


def last(inside, field, changes, coef, parts, status, pixels):
    operands = [inside, field, changes, coef, parts, status, *far(*pixels)]
    return pl.pallas_call(
        last_kernel,
        out_shape=[OWN, OWN, sums_shape(parts.shape[0]), STATUS],
        in_specs=[smem()] + [vspec()] * 5 + [hspec()] * 2,
        out_specs=[vspec()] * 4,
        scratch_shapes=[VM(WIDE.shape, F32)] * 4
        + [VM(ROW, F32), VM((M, CX), F32)]
        + [VM(part.shape, F32) for part in pixels]
        + [pltpu.SemaphoreType.DMA((2,))],
        compiler_params=params(),
        name="last_pair",
    )(*operands)


def fill_half(field, coef, half, first, end):
    def fill(y, carry):
        for zi in range(2):
            half[zi, y] = half_conductance(coef[zi, y], field[zi, y])
        return carry

    lax.fori_loop(first, end, fill, 0)


def single_kernel(number, inside, field, coef, peaks, out, out_peaks, half, above):
    step = step_of(whole_peak(largest(gather_rows(peaks))))
    fill_half(field, coef, half, number, YS - number)

    def put(zi, y, t, value, after):
        out[zi, y, tile(t), :] = value

    peak = advance(field, half, coef, above, inside, step, number + 1, YS - 1 - number, put)
    send_row(whole_peak(peak), out_peaks)


def single(number, inside, field, coef, peaks):
    return pl.pallas_call(
        functools.partial(single_kernel, number),
        out_shape=[WIDE, jax.ShapeDtypeStruct(peaks.shape, F32)],
        in_specs=[smem()] + [vspec()] * 3,
        out_specs=[vspec()] * 2,
        scratch_shapes=[VM(WIDE.shape, F32), VM(ROW, F32)],
        compiler_params=params(),
        name=f"single_{number}",
    )(inside, field, coef, peaks)


def closing_kernel(
    inside, field, coef, peaks, weight, data, out, out_changes, sums, half, above, flat
):
    fill_half(field, coef, half, HALO - 1, HALO + CY + 1)
    peak = peaks[0:8, 0, :]
    closing(
        field, half, above, inside, weight, data, peak, jnp.zeros((8, CX), F32),
        out, out_changes, sums, flat,
    )


def close(inside, field, coef, peaks, pixels):
    operands = [inside, field, coef, peaks, *pixels]
    return pl.pallas_call(
        closing_kernel,
        out_shape=[OWN, OWN, sums_shape(peaks.shape[0])],
        in_specs=[smem()] + [vspec()] * (len(operands) - 1),
        out_specs=[vspec()] * 3,
        scratch_shapes=[VM(WIDE.shape, F32), VM(ROW, F32), VM((M, CX), F32)],
        compiler_params=params(),
        name="closing",
    )(*operands)


def pixel_kernel(cell, observed, variance, noise, weight, data):
    pixels = cell.shape[1]
    place = cell[...]
    var = variance[...]
    inverse = 1.0 / var
    values = (observed[...] + noise[...] * jnp.sqrt(var)) * inverse
    stack = jnp.concatenate([values, jnp.broadcast_to(inverse, (8, pixels))], axis=0)
    width = place >> 7
    hot = jnp.where(
        lax.broadcasted_iota(jnp.int32, (CX, pixels), 0) == (place & 127), 1.0, 0.0
    ).astype(F32)
    for y in range(CY):
        part = lax.dot_general(
            jnp.where(width == y, stack, 0.0),
            hot,
            NT,
            precision=lax.Precision.HIGHEST,
            preferred_element_type=F32,
        )
        weight[y : y + 1, :] = part[M : M + 1, :]
        for m in range(M):
            data[m, y : y + 1, :] = part[m : m + 1, :]


def pixel_sums(cell, observed, variance, noise):
    return pl.pallas_call(
        pixel_kernel,
        out_shape=[kept((CY, CX)), kept((M, CY, CX))],
        in_specs=[vspec()] * 4,
        out_specs=[vspec()] * 2,
        compiler_params=params(),
        name="pixels",
    )(cell, observed, variance, noise)


def update_kernel(sums, field, changes, status, out, flag):
    total = sums[0]
    most = total
    for d in range(1, sums.shape[0]):
        total = total + sums[d]
        most = jnp.maximum(most, sums[d])
    step = step_of(jnp.broadcast_to(most[0:1, 0:1], (1, CX)))
    late = jnp.broadcast_to(most[1:2, 1:2], (1, CX))
    bad = jnp.maximum(status[1:2, :], differs(late, status[0:1, :]))
    flag[0] = jnp.where(jnp.max(bad) > 0.0, 1, 0)

    tall = lax.broadcasted_iota(jnp.int32, (M, CX), 0)
    wide = lax.broadcasted_iota(jnp.int32, (M, CX), 1)
    packed = jnp.concatenate([total, pltpu.roll(total, CX // 2, axis=1)], axis=0)

    def block(at):
        return jnp.where(wide < M, pltpu.roll(packed, (CX - M * at) % CX, axis=1), 0.0)

    def whole(part):
        rest = jnp.where(tall == 0, 0.0, part)
        first = -jnp.sum(rest, axis=0, keepdims=True)
        return jnp.where(tall == 0, first, rest), part[0:1, :]

    def balanced(part):
        part = jnp.where((tall == wide) | (wide >= M), 0.0, part)
        return jnp.where(tall == wide, -jnp.sum(part, axis=1, keepdims=True), part)

    corner = block(0)
    mirror = jnp.concatenate([corner, jnp.zeros((CX - M, CX), F32)], axis=0).T[0:M, :]
    square = balanced(jnp.where(tall < wide, corner, mirror))
    square_c = balanced(jnp.where(tall > wide, corner, mirror))
    mixed, mean_1 = whole(block(1))
    data, mean_0 = whole(block(2))
    data_c, mean_2 = whole(block(3))
    cross = square + step * (mixed + step * square_c)
    mean = mean_0 + step * (mean_1 + step * mean_2)
    mean = jnp.sum(jnp.where(tall == wide, mean, 0.0), axis=1, keepdims=True)
    target = jnp.where(wide < M, data + step * data_c - cross - mean, 0.0)
    system = jnp.where(tall == wide, cross + (M - 1.0), cross)
    columns = [jnp.broadcast_to(system[:, i : i + 1], (M, CX)) for i in range(M)]
    for i in range(M):
        pivot = 1.0 / columns[i][i : i + 1, :]
        factor = jnp.where(tall == i, 0.0, columns[i] * pivot)
        for j in range(i + 1, M):
            columns[j] = columns[j] - factor * columns[j][i : i + 1, :]
        target = target - factor * target[i : i + 1, :]
    for i in range(M):
        target = jnp.where(tall == i, target / columns[i], target)
    mixing = target - jnp.mean(target, axis=0, keepdims=True)
    mixing = jnp.where(wide < M, mixing + jnp.where(tall == wide, 1.0, 0.0), 0.0)
    for shift in (16, 32, 64):
        mixing = mixing + pltpu.roll(mixing, shift, axis=1)
    mixing = jnp.concatenate([mixing] * ZG, axis=0)
    tall = lax.broadcasted_iota(jnp.int32, (CX, CX), 0)
    wide = lax.broadcasted_iota(jnp.int32, (CX, CX), 1)
    mixing = jnp.where((tall >> 4) == (wide >> 4), 2.0 * mixing, 0.0).T
    mixing_high = mixing.astype(BF16)
    mixing_low = (mixing - mixing_high.astype(F32)).astype(BF16)
    mixing = jnp.concatenate([mixing_high, mixing_low, mixing_high], axis=1)
    for zi in range(2):
        for y in range(CY):
            prior = field[zi, y] + step * changes[zi, y]
            high = prior.astype(BF16)
            low = (prior - high.astype(F32)).astype(BF16)
            part = lax.dot_general(
                mixing,
                jnp.concatenate([high, high, low], axis=1),
                NT,
                preferred_element_type=F32,
            )
            for group in range(ZG):
                for m0 in (0, 8):
                    at = group * M + m0
                    out[m0 : m0 + 8, 2 * group + zi, y, :] = part[at : at + 8, :]


def update(sums, field, changes, status):
    return pl.pallas_call(
        update_kernel,
        out_shape=[
            jax.ShapeDtypeStruct((M, NZ, CY, CX), F32),
            jax.ShapeDtypeStruct((1,), jnp.int32),
        ],
        in_specs=[vspec()] * 4,
        out_specs=[vspec(), smem()],
        compiler_params=params(),
        name="update",
    )(sums, field, changes, status)


def exchange(parts):
    return lax.all_to_all(parts, BOTH, split_axis=0, concat_axis=0, tiled=True)


def move(part, axis, ahead):
    count = lax.axis_size(axis)
    pairs = [(i, i + 1) if ahead else (i + 1, i) for i in range(count - 1)]
    return lax.ppermute(part, axis, pairs)


def on_device(
    state_prior,
    conductivity,
    heat_input,
    owner_tile,
    voxel_list,
    pixel_cell,
    observed,
    pixel_variance,
    pixel_noise,
):
    devices = lax.axis_size("gx") * lax.axis_size("gy")
    pixels = pixel_cell.shape[0]
    gx, gy = lax.axis_index("gx"), lax.axis_index("gy")
    inside = jnp.stack(
        [gx > 0, gx < lax.axis_size("gx") - 1, gy > 0, gy < lax.axis_size("gy") - 1]
    ).astype(F32)
    incoming = exchange(pack(owner_tile.reshape(-1), heat_input, voxel_list, devices))
    own, turned_c, to_high, to_low, edge_left, edge_right, top, quiet = relayout(
        state_prior, conductivity
    )
    low, high = move(to_high, "gy", True), move(to_low, "gy", False)
    seen = pixel_sums(
        pixel_cell.reshape(1, pixels),
        observed.reshape(1, pixels),
        pixel_variance.reshape(1, pixels),
        pixel_noise,
    )
    incoming, own, top, inside, *seen = lax.optimization_barrier(
        (incoming, own, top, inside, *seen)
    )
    heat, peaks = deposit(incoming, top, conductivity, quiet)
    heat_low, heat_high = move(heat, "gy", True), move(heat, "gy", False)
    low, high, heat_low, heat_high, peaks = lax.optimization_barrier(
        (low, high, heat_low, heat_high, exchange(peaks))
    )
    to_left, to_right = sides(
        edge_left, edge_right, turned_c, low, high, heat_low, heat, heat_high
    )
    left, right = move(to_right, "gx", True), move(to_left, "gx", False)
    start, coef, changes, parts = heated(
        inside,
        (own, low, high),
        (left, right),
        (heat_low, heat, heat_high),
        coefs(turned_c, low, high),
        peaks,
    )
    field, changes, parts, status = pair(1, inside, start, changes, coef, exchange(parts))
    field, changes, sums, status = last(
        inside, field, changes, coef, exchange(parts), status, seen
    )
    result, flag = update(exchange(sums), field, changes, status)

    def again():
        peak = coef * (1.0 + start * start)
        peaks = jnp.full((devices, 1, CX), jnp.max(peak[:, HALO : HALO + CY, 8 : XS - 8]))
        field = start
        for number in range(1, SUBSTEPS - 1):
            field, peaks = single(number, inside, field, coef, exchange(peaks))
        field, changes, sums = close(inside, field, coef, peaks, seen)
        return update(exchange(sums), field, changes, jnp.ones((8, CX), F32))[0]

    return lax.cond(flag[0] > 0, again, lambda: result)


def solution(mesh):
    in_specs = (
        P(None, None, "gy", "gx"),
        P(None, "gy", "gx"),
        P(None, BOTH, None),
        P(BOTH, None),
        P(BOTH, None),
        P(BOTH),
        P(BOTH),
        P(BOTH),
        P(None, BOTH),
    )
    out_specs = P(None, None, "gy", "gx")
    return jax.shard_map(
        on_device, mesh=mesh, in_specs=in_specs, out_specs=out_specs, check_vma=False
    )
```

```python
import functools

import jax
import jax.numpy as jnp
from jax import lax
from jax.experimental import pallas as pl
from jax.experimental.pallas import tpu as pltpu
from jax.sharding import PartitionSpec as P

SUBSTEPS = 6
CAP = 2
COOL = 0.1
SHARE = 0.9
F32 = jnp.float32
BF16 = jnp.bfloat16
VM = pltpu.VMEM
LIMIT = 32 * 1024 * 1024
NT = (((1,), (1,)), ((), ()))
BOTH = ("gx", "gy")

M, NZ, CY, CX = 16, 16, 8, 128
ROWS = 40


def vspec():
    return pl.BlockSpec(memory_space=pltpu.VMEM)


def hspec():
    return pl.BlockSpec(memory_space=pltpu.HBM)


def far(*arrays):
    return [pltpu.with_memory_space_constraint(array, pltpu.HBM) for array in arrays]


def kept(shape):
    return pltpu.HBM(tuple(shape), F32)


def fetch(sems, pairs):
    copies = [
        pltpu.make_async_copy(source, target, sems.at[i])
        for i, (source, target) in enumerate(pairs)
    ]
    for copy in copies:
        copy.start()
    return copies


def params():
    return pltpu.CompilerParams(vmem_limit_bytes=LIMIT)


def lanes():
    return lax.broadcasted_iota(jnp.int32, (CY, CX), 1)


def rows():
    return lax.broadcasted_iota(jnp.int32, (CY, CX), 0)


PARTS = 4


def pack_kernel(
    owner_far, heat_far, voxel_far, out_far,
    out, owner, heat, voxel, wide, high, low, inverse, sems, out_sems,
):
    copies = fetch(sems, ((owner_far, owner), (heat_far, heat), (voxel_far, voxel)))
    blocks = owner.shape[0]
    devices = out.shape[0]

    def clear(i, carry):
        inverse[i] = blocks
        return carry

    lax.fori_loop(0, devices * CAP, clear, 0, unroll=16)
    copies[0].wait()

    def place(b, carry):
        base = owner[b] * CAP
        base = base + jnp.where(inverse[base] != blocks, 1, 0)
        inverse[base] = b
        return carry

    lax.fori_loop(0, blocks, place, 0, unroll=8)
    copies[1].wait()
    copies[2].wait()

    def widen(m, carry):
        wide[m, 0:blocks, :] = heat[m].astype(F32)
        wide[m, blocks:, :] = jnp.zeros((8, CX), F32)
        return carry

    lax.fori_loop(0, M, widen, 0)
    cells = voxel[...]
    high[0:blocks, :] = (cells >> 7).astype(F32)
    high[blocks:, :] = jnp.zeros((8, CX), F32)
    low[0:blocks, :] = (cells & 127).astype(F32)
    low[blocks:, :] = jnp.zeros((8, CX), F32)
    row = rows()

    def emit(d, carry):
        first = inverse[d * CAP]
        second = inverse[d * CAP + 1]
        index = jnp.where(
            row == 0,
            high[pl.ds(first, 1), :],
            jnp.where(
                row == 1,
                high[pl.ds(second, 1), :],
                jnp.where(
                    row == 2,
                    low[pl.ds(first, 1), :],
                    jnp.where(row == 3, low[pl.ds(second, 1), :], 0.0),
                ),
            ),
        )
        chunk = jnp.concatenate(
            [
                wide[:, pl.ds(first, 1), :].reshape(M, CX),
                wide[:, pl.ds(second, 1), :].reshape(M, CX),
                index,
            ],
            axis=0,
        )
        out[d] = chunk.astype(BF16)
        return carry

    share = devices // PARTS
    sent = []
    for part in range(PARTS):
        lax.fori_loop(part * share, (part + 1) * share, emit, 0, unroll=16)
        at = pl.ds(part * share, share)
        copy = pltpu.make_async_copy(out.at[at], out_far.at[at], out_sems.at[part])
        copy.start()
        sent.append(copy)
    for copy in sent:
        copy.wait()


def pack(owner, heat, voxel, devices):
    blocks = owner.shape[0]
    return pl.pallas_call(
        pack_kernel,
        out_shape=pltpu.HBM((devices, ROWS, CX), BF16),
        in_specs=[hspec()] * 3,
        out_specs=hspec(),
        scratch_shapes=[
            VM((devices, ROWS, CX), BF16),
            pltpu.SMEM((blocks,), jnp.int32),
            VM((M, blocks, CX), BF16),
            VM((blocks, CX), jnp.int32),
            VM((M, blocks + 8, CX), F32),
            VM((blocks + 8, CX), F32),
            VM((blocks + 8, CX), F32),
            pltpu.SMEM((devices * CAP,), jnp.int32),
            pltpu.SemaphoreType.DMA((3,)),
            pltpu.SemaphoreType.DMA((PARTS,)),
        ],
        compiler_params=params(),
        name="pack",
    )(*far(owner, heat, voxel))


HALO = 6
YS = CY + 2 * HALO
XT = CX // 8 + 2
ZG = NZ // 2
TOLERANCE = 1e-6
OWN = jax.ShapeDtypeStruct((2, CY, CX, CX), F32)
XS = 8 * XT
WIDE = jax.ShapeDtypeStruct((2, YS, XS, CX), F32)
EDGE = 2 * HALO
SIDE = 2 * YS


def layout_block(state, zi, y):
    parts = [state[m0 : m0 + 8, 2 * group + zi, y, :] for group in range(ZG) for m0 in (0, 8)]
    return (0.5 * jnp.concatenate(parts, axis=0)).T


def rim_kernel(state, conduct, turned_c, to_high, to_low):
    turned = (0.5 * conduct[...].reshape(CX, CX)).T.reshape(XT - 2, 8, CX)
    turned_c[...] = turned
    to_high[EDGE] = turned
    to_low[EDGE] = turned
    for zi in range(2):
        for y in range(CY):
            turned = layout_block(state, zi, y).reshape(XT - 2, 8, CX)
            if y >= CY - HALO:
                to_high[zi * HALO + y - (CY - HALO)] = turned
            if y < HALO:
                to_low[zi * HALO + y] = turned


def rims(state, conduct):
    edge = kept((EDGE + 1, XT - 2, 8, CX))
    return pl.pallas_call(
        rim_kernel,
        out_shape=[kept((XT - 2, 8, CX)), edge, edge],
        in_specs=[vspec()] * 2,
        out_specs=[vspec()] * 3,
        compiler_params=params(),
        name="rims",
    )(state, conduct)


def relayout_kernel(state, conduct, own, edge_left, edge_right, top, quiet):
    peak = jnp.zeros((8, CX), F32)
    for zi in range(2):
        for y in range(CY):
            turned = layout_block(state, zi, y)
            own[zi, y] = turned
            edge_left[zi * CY + y] = turned[0:8]
            edge_right[zi * CY + y] = turned[CX - 8 :]
    for z in range(2, NZ):
        c = 0.5 * conduct[z]
        for m in range(M):
            value = 0.5 * state[m, z]
            peak = jnp.maximum(peak, c + c * (value * value))
    quiet[...] = peak
    for m in range(M):
        for zi in range(2):
            top[m, zi] = 0.5 * state[m, zi]


def relayout(state, conduct):
    side = kept((2 * CY, 8, CX))
    return pl.pallas_call(
        relayout_kernel,
        out_shape=[kept(OWN.shape), side, side, kept((M, 2, CY, CX)), kept((8, CX))],
        in_specs=[vspec()] * 2,
        out_specs=[vspec()] * 5,
        compiler_params=params(),
        name="relayout",
    )(state, conduct)


def side_kernel(
    edge_left, edge_right, turned_c, low, high, heat_low, heat_own, heat_high,
    to_left, to_right, sems,
):
    pairs = []
    for out, edge, t in ((to_left, edge_left, 0), (to_right, edge_right, XT - 3)):
        for zi in range(2):
            at, rows_at = zi * YS, slice(zi * HALO, zi * HALO + HALO)
            pairs += [
                (low.at[rows_at, t], out.at[at : at + HALO]),
                (edge.at[zi * CY : zi * CY + CY], out.at[at + HALO : at + HALO + CY]),
                (high.at[rows_at, t], out.at[at + HALO + CY : at + YS]),
            ]
            for g, heat in enumerate((heat_low, heat_own, heat_high)):
                pairs.append((heat.at[zi, 8 * t : 8 * t + 8, :], out.at[SIDE + 3 + 2 * g + zi]))
        for g, part in enumerate((low.at[EDGE, t], turned_c.at[t], high.at[EDGE, t])):
            pairs.append((part, out.at[SIDE + g]))
    for copy in fetch(sems, pairs):
        copy.wait()


def sides(*operands):
    shape = jax.ShapeDtypeStruct((SIDE + 9, 8, CX), F32)
    return pl.pallas_call(
        side_kernel,
        out_shape=[shape, shape],
        in_specs=[hspec()] * len(operands),
        out_specs=[vspec()] * 2,
        scratch_shapes=[pltpu.SemaphoreType.DMA((30,))],
        compiler_params=params(),
        name="sides",
    )(*far(*operands))


def split(strip):
    parts = []
    for _ in range(3):
        part = strip.astype(BF16)
        parts.append(part)
        strip = strip - part.astype(F32)
    return jnp.concatenate(parts, axis=1)


def placed(parts, zi, y0):
    source = lax.broadcasted_iota(jnp.int32, (CX, CX), 0)
    target = lax.broadcasted_iota(jnp.int32, (CX, CX), 1)
    hot = jnp.where(source == (2 * (target >> 4) + zi) * CY + y0, 1.0, 0.0).astype(BF16)
    hot = jnp.concatenate([hot] * 3, axis=0)
    return jnp.dot(parts, hot, preferred_element_type=F32)


def halo_row(g, y0):
    row = y0 + HALO + (g - 1) * CY
    return row if 0 <= row < YS else None


def coef_kernel(own, low, high, out, tiles, sems):
    pairs = ((low.at[EDGE], tiles.at[0]), (own, tiles.at[1]), (high.at[EDGE], tiles.at[2]))
    for copy in fetch(sems, pairs):
        copy.wait()
    strip = split(tiles[...].reshape(3 * CX, CX))
    for zi in range(2):
        for y0 in range(CY):
            part = placed(strip, zi, y0)
            for g in range(3):
                row = halo_row(g, y0)
                if row is not None:
                    out[zi, row] = part[g * CX : (g + 1) * CX, :]


def coefs(own, low, high):
    return pl.pallas_call(
        coef_kernel,
        out_shape=jax.ShapeDtypeStruct((2, YS, CX, CX), F32),
        in_specs=[hspec()] * 3,
        out_specs=vspec(),
        scratch_shapes=[VM((3, XT - 2, 8, CX), F32), pltpu.SemaphoreType.DMA((3,))],
        compiler_params=params(),
        name="coefs",
    )(*far(own, low, high))


def deposit_kernel(
    incoming, top_far, conduct_far, quiet_far, out, peaks, total, top, conduct, quiet, sems
):
    copies = fetch(sems, ((top_far, top), (conduct_far.at[0:2], conduct), (quiet_far, quiet)))
    sources = incoming.shape[0]
    group = 64
    place = lax.broadcasted_iota(jnp.int32, (CX, CX), 0).astype(F32).astype(BF16)
    zero = jnp.zeros((M, CX), BF16)
    total[...] = jnp.zeros_like(total)

    def one(g, carry):
        left = []
        right = []
        for s in range(group):
            source = g * group + s
            index = incoming[source, 32:40, :].astype(F32)
            for slot in range(CAP):
                heat = incoming[source, slot * M : (slot + 1) * M, :]
                layer = jnp.broadcast_to(index[slot : slot + 1, :], (M, CX)).astype(BF16)
                cell = jnp.broadcast_to(index[2 + slot : 3 + slot, :], (CX, CX)).astype(BF16)
                left.append(
                    jnp.concatenate(
                        [jnp.where(layer == h, heat, zero) for h in range(2 * CY)], axis=0
                    )
                )
                right.append(jnp.where(place == cell, 1.0, 0.0).astype(BF16))
        total[...] += lax.dot_general(
            jnp.concatenate(left, axis=1),
            jnp.concatenate(right, axis=1),
            NT,
            preferred_element_type=F32,
        )
        return carry

    lax.fori_loop(0, sources // group, one, 0)
    for zi in range(2):
        out[zi] = (0.5 * total[zi * CX : (zi + 1) * CX, :]).T
    for copy in copies:
        copy.wait()
    peak = quiet[...]
    for zi in range(2):
        c = 0.5 * conduct[zi]
        for m in range(M):
            value = top[m, zi] + 0.5 * total[pl.ds(zi * CX + m, CY, stride=M), :]
            peak = jnp.maximum(peak, c + c * (value * value))
    send_row(whole_peak(peak), peaks)


def send_row(row, out):
    for d in range(0, out.shape[0], 8):
        out[d : d + 8, 0, :] = row


def deposit(incoming, top, conduct, quiet):
    devices = incoming.shape[0]
    return pl.pallas_call(
        deposit_kernel,
        out_shape=[
            kept((2, CX, CX)),
            jax.ShapeDtypeStruct((devices, 1, CX), F32),
        ],
        in_specs=[vspec()] + [hspec()] * 3,
        out_specs=[vspec()] * 2,
        scratch_shapes=[
            VM((2 * CY * M, CX), F32),
            VM(top.shape, F32),
            VM((2, CY, CX), F32),
            VM(quiet.shape, F32),
            pltpu.SemaphoreType.DMA((3,)),
        ],
        compiler_params=params(),
        name="deposit",
    )(incoming, *far(top, conduct, quiet))


def whole_peak(value):
    return jnp.broadcast_to(jnp.max(value, axis=(0, 1), keepdims=True), (8, CX))


def step_of(peak):
    return SHARE / (12.0 * peak + COOL)


def tile(t):
    return slice(8 * t, 8 * t + 8)


def half_conductance(c, u):
    return c + c * (u * u)


def segments(inside, first, end):
    parts = []
    if first < HALO:
        parts.append((first, HALO, False, inside[2]))
    parts.append((max(first, HALO), min(end, HALO + CY), True, None))
    if end > HALO + CY:
        parts.append((HALO + CY, end, False, inside[3]))
    return parts


def mask_of(inside, row_mask, t):
    if t == 0:
        return inside[0] if row_mask is None else inside[0] * row_mask
    if t == XT - 1:
        return inside[1] if row_mask is None else inside[1] * row_mask
    return row_mask


def sweep(field, half, above, inside, first, end, emit, carry):
    lane = lanes()
    row = rows()
    last_row = row == 7
    first_row = row == 0
    inner_lane = lane < CX - M
    outer_lane = lane >= M
    cooling = jnp.where(lane < M, COOL, 0.0)

    for zi in range(2):
        for t in range(XT):
            s = tile(t)
            above[zi, t] = (half[zi, first - 1, s, :] + half[zi, first, s, :]) * (
                field[zi, first, s, :] - field[zi, first - 1, s, :]
            )

    def line(own, row_mask, y, state):
        for t in range(XT):
            s = tile(t)
            us = [field[zi, y, s, :] for zi in range(2)]
            hs = [half[zi, y, s, :] for zi in range(2)]
            change = []
            for zi in range(2):
                u, h = us[zi], hs[zi]
                if t < XT - 1:
                    after = slice(8 * t + 1, 8 * t + 9)
                    u_after, h_after = field[zi, y, after, :], half[zi, y, after, :]
                else:
                    u_after = jnp.where(last_row, u, pltpu.roll(u, 7, axis=0))
                    h_after = pltpu.roll(h, 7, axis=0)
                if t:
                    before = slice(8 * t - 1, 8 * t + 7)
                    u_before, h_before = field[zi, y, before, :], half[zi, y, before, :]
                else:
                    u_before = jnp.where(first_row, u, pltpu.roll(u, 1, axis=0))
                    h_before = pltpu.roll(h, 1, axis=0)
                total = (h + h_after) * (u_after - u) + (h + h_before) * (u_before - u)
                across = (h + half[zi, y + 1, s, :]) * (field[zi, y + 1, s, :] - u)
                total = total + (across - above[zi, t])
                above[zi, t] = across
                change.append(total)
            within = (hs[0] + hs[1]) * (us[1] - us[0])
            between = (hs[1] + pltpu.roll(hs[0], CX - M, axis=1)) * (
                pltpu.roll(us[0], CX - M, axis=1) - us[1]
            )
            between = jnp.where(inner_lane, between, 0.0)
            below = (hs[0] + pltpu.roll(hs[1], M, axis=1)) * (us[0] - pltpu.roll(us[1], M, axis=1))
            below = jnp.where(outer_lane, below, 0.0)
            change[0] = change[0] + (within - below) - cooling * us[0]
            change[1] = change[1] + (between - within)
            state = emit(y, t, us, change, own, mask_of(inside, row_mask, t), state)
        return state

    for start, stop, own, row_mask in segments(inside, first, end):
        carry = lax.fori_loop(start, stop, functools.partial(line, own, row_mask), carry)
    return carry


def advance(field, half, coef, above, inside, step, first, end, put):
    def emit(y, t, us, change, own, mask, peak):
        part = step if mask is None else step * mask
        for zi in range(2):
            value = us[zi] + part * change[zi]
            after = half_conductance(coef[zi, y, tile(t), :], value)
            put(zi, y, t, value, after)
            if own and 0 < t < XT - 1:
                peak = jnp.maximum(peak, after)
        return peak

    return sweep(field, half, above, inside, first, end, emit, jnp.zeros((8, CX), F32))


def propose(field, half, coef, above, inside, guess, first, end, changes, peak, late, out):
    def emit(y, t, us, change, own, mask, best):
        for zi in range(2):
            moved = change[zi] if mask is None else change[zi] * mask
            changes[zi, y, tile(t), :] = moved
            if own and 0 < t < XT - 1:
                c = coef[zi, y, tile(t), :]
                rank = half_conductance(c, us[zi] + guess * moved)
                better = rank > best[0]
                best = tuple(
                    jnp.where(better, new, old)
                    for new, old in zip((rank, us[zi], moved, c), best)
                )
        return best

    best = sweep(
        field, half, above, inside, first, end, emit, (jnp.zeros((8, CX), F32),) * 4
    )
    for shift, axis in ((4, 0), (2, 0), (1, 0), (64, 1), (32, 1)):
        other = tuple(pltpu.roll(part, shift, axis=axis) for part in best)
        better = other[0] > best[0]
        best = tuple(jnp.where(better, new, old) for new, old in zip(other, best))
    part = lanes() >> 4
    chunk = jnp.where(part == 6, whole_peak(peak), whole_peak(late))
    for place, value in ((2, best[3]), (1, best[2]), (0, best[1])):
        chunk = jnp.where((part >> 1) == place, value, chunk)
    send_row(chunk, out)


def gather_rows(parts):
    return [parts[d : d + 8, 0, :] for d in range(0, parts.shape[0], 8)]


def largest(values):
    most = values[0]
    for value in values[1:]:
        most = jnp.maximum(most, value)
    return most


def agree(parts):
    part = lanes() >> 4
    rows_of = gather_rows(parts)
    most = largest(rows_of)
    now = whole_peak(jnp.where(part == 6, most, 0.0))
    late = whole_peak(jnp.where(part == 7, most, 0.0))
    step = step_of(now)
    then = jnp.zeros((8, CX), F32)
    for value in rows_of:
        moved = pltpu.roll(value, CX - 32, axis=1)
        c = pltpu.roll(value, CX - 64, axis=1)
        then = jnp.maximum(then, half_conductance(c, value + step * moved))
    return now, whole_peak(jnp.where(part < 2, then, 0.0)), late


def differs(late, used):
    return jnp.where(late > used * (1.0 + TOLERANCE), 1.0, 0.0)


def heated_kernel(
    inside, peaks, left, right, coef_main, own_far, low_far, high_far,
    heat_low_far, heat_own_far, heat_high_far,
    out, coef, changes, parts, start, half, next_half, above,
    own, low, high, heat_low, heat_own, heat_high, sems,
):
    copies = fetch(
        sems,
        [
            (heat_low_far, heat_low),
            (low_far.at[0:EDGE], low),
            (heat_own_far, heat_own),
            (own_far, own),
            (heat_high_far, heat_high),
            (high_far.at[0:EDGE], high),
        ],
    )
    top = lanes() < M

    strip = split(
        jnp.concatenate([side[SIDE + g] for g in range(3) for side in (left, right)], axis=0)
    )
    for zi in range(2):
        for y0 in range(CY):
            part = placed(strip, zi, y0)
            for g in range(3):
                at = halo_row(g, y0)
                if at is not None:
                    coef[zi, at, tile(0), :] = part[16 * g : 16 * g + 8, :]
                    coef[zi, at, tile(XT - 1), :] = part[16 * g + 8 : 16 * g + 16, :]

    def row(g, heat, tile_of, y0, yy):
        shift = (CX - 16 * y0) % CX
        for zi in range(2):
            for t in range(XT):
                if t == 0:
                    prior, add = left[zi * YS + yy], left[SIDE + 3 + 2 * g + zi]
                elif t == XT - 1:
                    prior, add = right[zi * YS + yy], right[SIDE + 3 + 2 * g + zi]
                else:
                    prior, add = tile_of(zi, t - 1), heat[zi, tile(t - 1), :]
                if shift:
                    add = pltpu.roll(add, shift, axis=1)
                value = prior + jnp.where(top, add, 0.0)
                if 0 < t < XT - 1:
                    c = coef_main[zi, yy, tile(t - 1), :]
                    coef[zi, yy, tile(t), :] = c
                else:
                    c = coef[zi, yy, tile(t), :]
                after = half_conductance(c, value)
                start[zi, yy, tile(t), :] = value
                half[zi, yy, tile(t), :] = after

    def edge(ref, y):
        return lambda zi, t: ref[zi * HALO + y, t]

    for copy in copies[0:2]:
        copy.wait()
    for y in range(HALO):
        row(0, heat_low, edge(low, y), y + CY - HALO, y)
    for copy in copies[2:4]:
        copy.wait()
    for y in range(CY):
        row(1, heat_own, lambda zi, t: own[zi, y, tile(t), :], y, y + HALO)
    for copy in copies[4:6]:
        copy.wait()
    for y in range(HALO):
        row(2, heat_high, edge(high, y), y, y + HALO + CY)

    def put(zi, y, t, value, after):
        out[zi, y, tile(t), :] = value
        next_half[zi, y, tile(t), :] = after

    step = step_of(whole_peak(largest(gather_rows(peaks))))
    peak = advance(start, half, coef, above, inside, step, 1, YS - 1, put)
    guess = jnp.minimum(step_of(whole_peak(peak)), 2.0 * step)
    zero = jnp.zeros((8, CX), F32)
    propose(
        out, next_half, coef, above, inside, guess, 2, YS - 2, changes, peak, zero, parts
    )


ROW = (2, XT, 8, CX)


def smem():
    return pl.BlockSpec(memory_space=pltpu.SMEM)


def heated(inside, prior, halos, heat, coef, peaks):
    near = [inside, peaks, *halos, coef]
    operands = far(*prior, *heat)
    edge = VM((EDGE, XT - 2, 8, CX), F32)
    return pl.pallas_call(
        heated_kernel,
        out_shape=[WIDE, WIDE, WIDE, jax.ShapeDtypeStruct(peaks.shape, F32)],
        in_specs=[smem()] + [vspec()] * 4 + [hspec()] * len(operands),
        out_specs=[vspec()] * 4,
        scratch_shapes=[VM(WIDE.shape, F32)] * 3
        + [VM(ROW, F32), VM(OWN.shape, F32), edge, edge]
        + [VM(part.shape, F32) for part in heat]
        + [pltpu.SemaphoreType.DMA((6,))],
        compiler_params=params(),
        name="heated",
    )(*near, *operands)


def first_of_pair(field, changes, coef, step, first, end, out, half):
    def line(y, peak):
        top = jnp.zeros((8, CX), F32)
        for zi in range(2):
            for t in range(XT):
                value = field[zi, y, tile(t), :] + step * changes[zi, y, tile(t), :]
                after = half_conductance(coef[zi, y, tile(t), :], value)
                out[zi, y, tile(t), :] = value
                half[zi, y, tile(t), :] = after
                if 0 < t < XT - 1:
                    top = jnp.maximum(top, after)
        own = jnp.where((y >= HALO) & (y < HALO + CY), 1.0, 0.0)
        return jnp.maximum(peak, own * top)

    return lax.fori_loop(first, end, line, jnp.zeros((8, CX), F32))


def pair_kernel(
    number, inside, field, changes, coef, parts,
    out, out_changes, out_parts, status, middle, half, next_half, above,
):
    now, then, _ = agree(parts)
    status[...] = jnp.where(rows() == 0, then, 0.0)
    seen = first_of_pair(
        field, changes, coef, step_of(now), number + 1, YS - 1 - number, middle, half
    )

    def put(zi, y, t, value, after):
        out[zi, y, tile(t), :] = value
        next_half[zi, y, tile(t), :] = after

    step = step_of(then)
    peak = advance(
        middle, half, coef, above, inside, step, number + 2, YS - 2 - number, put
    )
    guess = jnp.minimum(step_of(whole_peak(peak)), 1.2 * step)
    propose(
        out, next_half, coef, above, inside, guess, number + 3, YS - 3 - number,
        out_changes, peak, seen, out_parts,
    )


STATUS = jax.ShapeDtypeStruct((8, CX), F32)


def pair(number, inside, field, changes, coef, parts):
    operands = [inside, field, changes, coef, parts]
    return pl.pallas_call(
        functools.partial(pair_kernel, number),
        out_shape=[WIDE, WIDE, jax.ShapeDtypeStruct(parts.shape, F32), STATUS],
        in_specs=[smem()] + [vspec()] * 4,
        out_specs=[vspec()] * 4,
        scratch_shapes=[VM(WIDE.shape, F32)] * 3 + [VM(ROW, F32)],
        compiler_params=params(),
        name=f"pair_{number}",
    )(*operands)


def closing(
    field, half, above, inside, weight, data, peak, late, out, out_changes, sums, flat
):
    def emit(y, t, us, change, own, mask, state):
        if 0 < t < XT - 1:
            for zi in range(2):
                out[zi, y - HALO, tile(t - 1), :] = us[zi]
                out_changes[zi, y - HALO, tile(t - 1), :] = change[zi]
        return state

    sweep(field, half, above, inside, HALO, HALO + CY, emit, 0)
    lefts, rights = [], []
    for y in range(CY):
        w = weight[y : y + 1, :]
        for m in range(M):
            flat[m : m + 1, :] = data[m, y : y + 1, :]
        means = []
        spreads = []
        for part in (out, out_changes):
            seen = 2.0 * part[0, y].T[0:M, :]
            mean = jnp.mean(seen, axis=0, keepdims=True)
            means.append(mean)
            spreads.append(seen - mean)
        lefts.append(jnp.concatenate(spreads + means + [jnp.zeros((6, CX), F32)], axis=0))
        rights.append(jnp.concatenate([part * w for part in spreads] + [flat[...]], axis=0))
    grams = lax.dot_general(
        jnp.concatenate(lefts, axis=1),
        jnp.concatenate(rights, axis=1),
        NT,
        precision=lax.Precision.HIGHEST,
        preferred_element_type=F32,
    )
    grams = jnp.concatenate([grams, jnp.zeros((5 * CY, CX - 3 * M), F32)], axis=1)
    tall = lax.broadcasted_iota(jnp.int32, (M, CX), 0)
    wide = lax.broadcasted_iota(jnp.int32, (M, CX), 1)
    first, second, means = grams[0:M], grams[M : 2 * M], grams[2 * M : 2 * M + 8]

    def block(part, at):
        return jnp.where(wide < M, pltpu.roll(part, (CX - M * at) % CX, axis=1), 0.0)

    def lone(part, row, at):
        moved = pltpu.roll(part, (CX - M * at) % CX, axis=1) if at else part
        return jnp.broadcast_to(moved[row : row + 1, :], (M, CX))

    tops = [
        lone(means, 0, 1) + lone(means, 1, 0),
        lone(means, 0, 0),
        lone(means, 1, 1),
    ]
    blocks = [
        jnp.where(tall < wide, block(first, 0), block(second, 1)),
        block(first, 1) + block(second, 0),
        block(first, 2),
        block(second, 2),
    ]
    scalar = jnp.where(wide == 0, whole_peak(peak)[0:1], whole_peak(late)[0:1])
    blocks[0] = jnp.where(tall == wide, scalar, blocks[0])
    for i, top in enumerate(tops):
        blocks[i + 1] = jnp.where(tall == 0, jnp.where(wide < M, top, 0.0), blocks[i + 1])
    packed = blocks[0]
    for i in range(1, 4):
        packed = packed + pltpu.roll(blocks[i], M * i, axis=1)
    packed = packed[0:8] + pltpu.roll(packed[8:16], CX // 2, axis=1)
    for d in range(sums.shape[0]):
        sums[d] = packed


def last_kernel(
    inside, field, changes, coef, parts, status, weight_far, data_far,
    out, out_changes, sums, out_status,
    middle, half, near, near_half, above, flat, weight, data, sems,
):
    copies = fetch(sems, ((weight_far, weight), (data_far, data)))
    number = SUBSTEPS - 3
    now, then, late = agree(parts)
    bad = differs(late[0:1], status[0:1, :])
    out_status[...] = jnp.where(rows() == 0, then, bad)
    seen = first_of_pair(
        field, changes, coef, step_of(now), number + 1, YS - 1 - number, middle, half
    )

    def put(zi, y, t, value, after):
        near[zi, y, tile(t), :] = value
        near_half[zi, y, tile(t), :] = after

    peak = advance(
        middle, half, coef, above, inside, step_of(then), number + 2, YS - 2 - number, put
    )
    for copy in copies:
        copy.wait()
    closing(
        near, near_half, above, inside, weight, data, peak, seen, out, out_changes, sums, flat
    )


def sums_shape(devices):
    return jax.ShapeDtypeStruct((devices, 8, CX), F32)


def last(inside, field, changes, coef, parts, status, pixels):
    operands = [inside, field, changes, coef, parts, status, *far(*pixels)]
    return pl.pallas_call(
        last_kernel,
        out_shape=[OWN, OWN, sums_shape(parts.shape[0]), STATUS],
        in_specs=[smem()] + [vspec()] * 5 + [hspec()] * 2,
        out_specs=[vspec()] * 4,
        scratch_shapes=[VM(WIDE.shape, F32)] * 4
        + [VM(ROW, F32), VM((M, CX), F32)]
        + [VM(part.shape, F32) for part in pixels]
        + [pltpu.SemaphoreType.DMA((2,))],
        compiler_params=params(),
        name="last_pair",
    )(*operands)


def fill_half(field, coef, half, first, end):
    def fill(y, carry):
        for zi in range(2):
            half[zi, y] = half_conductance(coef[zi, y], field[zi, y])
        return carry

    lax.fori_loop(first, end, fill, 0)


def single_kernel(number, inside, field, coef, peaks, out, out_peaks, half, above):
    step = step_of(whole_peak(largest(gather_rows(peaks))))
    fill_half(field, coef, half, number, YS - number)

    def put(zi, y, t, value, after):
        out[zi, y, tile(t), :] = value

    peak = advance(field, half, coef, above, inside, step, number + 1, YS - 1 - number, put)
    send_row(whole_peak(peak), out_peaks)


def single(number, inside, field, coef, peaks):
    return pl.pallas_call(
        functools.partial(single_kernel, number),
        out_shape=[WIDE, jax.ShapeDtypeStruct(peaks.shape, F32)],
        in_specs=[smem()] + [vspec()] * 3,
        out_specs=[vspec()] * 2,
        scratch_shapes=[VM(WIDE.shape, F32), VM(ROW, F32)],
        compiler_params=params(),
        name=f"single_{number}",
    )(inside, field, coef, peaks)


def closing_kernel(
    inside, field, coef, peaks, weight, data, out, out_changes, sums, half, above, flat
):
    fill_half(field, coef, half, HALO - 1, HALO + CY + 1)
    peak = peaks[0:8, 0, :]
    closing(
        field, half, above, inside, weight, data, peak, jnp.zeros((8, CX), F32),
        out, out_changes, sums, flat,
    )


def close(inside, field, coef, peaks, pixels):
    operands = [inside, field, coef, peaks, *pixels]
    return pl.pallas_call(
        closing_kernel,
        out_shape=[OWN, OWN, sums_shape(peaks.shape[0])],
        in_specs=[smem()] + [vspec()] * (len(operands) - 1),
        out_specs=[vspec()] * 3,
        scratch_shapes=[VM(WIDE.shape, F32), VM(ROW, F32), VM((M, CX), F32)],
        compiler_params=params(),
        name="closing",
    )(*operands)


def pixel_kernel(cell, observed, variance, noise, weight, data):
    pixels = cell.shape[1]
    place = cell[...]
    var = variance[...]
    inverse = 1.0 / var
    values = (observed[...] + noise[...] * jnp.sqrt(var)) * inverse
    stack = jnp.concatenate([values, jnp.broadcast_to(inverse, (8, pixels))], axis=0)
    width = place >> 7
    hot = jnp.where(
        lax.broadcasted_iota(jnp.int32, (CX, pixels), 0) == (place & 127), 1.0, 0.0
    ).astype(F32)
    for y in range(CY):
        part = lax.dot_general(
            jnp.where(width == y, stack, 0.0),
            hot,
            NT,
            precision=lax.Precision.HIGHEST,
            preferred_element_type=F32,
        )
        weight[y : y + 1, :] = part[M : M + 1, :]
        for m in range(M):
            data[m, y : y + 1, :] = part[m : m + 1, :]


def pixel_sums(cell, observed, variance, noise):
    return pl.pallas_call(
        pixel_kernel,
        out_shape=[kept((CY, CX)), kept((M, CY, CX))],
        in_specs=[vspec()] * 4,
        out_specs=[vspec()] * 2,
        compiler_params=params(),
        name="pixels",
    )(cell, observed, variance, noise)


def update_kernel(sums, field, changes, status, out, flag):
    total = sums[0]
    most = total
    for d in range(1, sums.shape[0]):
        total = total + sums[d]
        most = jnp.maximum(most, sums[d])
    step = step_of(jnp.broadcast_to(most[0:1, 0:1], (1, CX)))
    late = jnp.broadcast_to(most[1:2, 1:2], (1, CX))
    bad = jnp.maximum(status[1:2, :], differs(late, status[0:1, :]))
    flag[0] = jnp.where(jnp.max(bad) > 0.0, 1, 0)

    tall = lax.broadcasted_iota(jnp.int32, (M, CX), 0)
    wide = lax.broadcasted_iota(jnp.int32, (M, CX), 1)
    packed = jnp.concatenate([total, pltpu.roll(total, CX // 2, axis=1)], axis=0)

    def block(at):
        return jnp.where(wide < M, pltpu.roll(packed, (CX - M * at) % CX, axis=1), 0.0)

    def whole(part):
        rest = jnp.where(tall == 0, 0.0, part)
        first = -jnp.sum(rest, axis=0, keepdims=True)
        return jnp.where(tall == 0, first, rest), part[0:1, :]

    def balanced(part):
        part = jnp.where((tall == wide) | (wide >= M), 0.0, part)
        return jnp.where(tall == wide, -jnp.sum(part, axis=1, keepdims=True), part)

    corner = block(0)
    mirror = jnp.concatenate([corner, jnp.zeros((CX - M, CX), F32)], axis=0).T[0:M, :]
    square = balanced(jnp.where(tall < wide, corner, mirror))
    square_c = balanced(jnp.where(tall > wide, corner, mirror))
    mixed, mean_1 = whole(block(1))
    data, mean_0 = whole(block(2))
    data_c, mean_2 = whole(block(3))
    cross = square + step * (mixed + step * square_c)
    mean = mean_0 + step * (mean_1 + step * mean_2)
    mean = jnp.sum(jnp.where(tall == wide, mean, 0.0), axis=1, keepdims=True)
    target = jnp.where(wide < M, data + step * data_c - cross - mean, 0.0)
    system = jnp.where(tall == wide, cross + (M - 1.0), cross)
    columns = [jnp.broadcast_to(system[:, i : i + 1], (M, CX)) for i in range(M)]
    for i in range(M):
        pivot = 1.0 / columns[i][i : i + 1, :]
        factor = jnp.where(tall == i, 0.0, columns[i] * pivot)
        for j in range(i + 1, M):
            columns[j] = columns[j] - factor * columns[j][i : i + 1, :]
        target = target - factor * target[i : i + 1, :]
    for i in range(M):
        target = jnp.where(tall == i, target / columns[i], target)
    mixing = target - jnp.mean(target, axis=0, keepdims=True)
    mixing = jnp.where(wide < M, mixing + jnp.where(tall == wide, 1.0, 0.0), 0.0)
    for shift in (16, 32, 64):
        mixing = mixing + pltpu.roll(mixing, shift, axis=1)
    mixing = jnp.concatenate([mixing] * ZG, axis=0)
    tall = lax.broadcasted_iota(jnp.int32, (CX, CX), 0)
    wide = lax.broadcasted_iota(jnp.int32, (CX, CX), 1)
    mixing = jnp.where((tall >> 4) == (wide >> 4), 2.0 * mixing, 0.0).T
    mixing_high = mixing.astype(BF16)
    mixing_low = (mixing - mixing_high.astype(F32)).astype(BF16)
    mixing = jnp.concatenate([mixing_high, mixing_low, mixing_high], axis=1)
    for zi in range(2):
        for y in range(CY):
            prior = field[zi, y] + step * changes[zi, y]
            high = prior.astype(BF16)
            low = (prior - high.astype(F32)).astype(BF16)
            part = lax.dot_general(
                mixing,
                jnp.concatenate([high, high, low], axis=1),
                NT,
                preferred_element_type=F32,
            )
            for group in range(ZG):
                for m0 in (0, 8):
                    at = group * M + m0
                    out[m0 : m0 + 8, 2 * group + zi, y, :] = part[at : at + 8, :]


def update(sums, field, changes, status):
    return pl.pallas_call(
        update_kernel,
        out_shape=[
            jax.ShapeDtypeStruct((M, NZ, CY, CX), F32),
            jax.ShapeDtypeStruct((1,), jnp.int32),
        ],
        in_specs=[vspec()] * 4,
        out_specs=[vspec(), smem()],
        compiler_params=params(),
        name="update",
    )(sums, field, changes, status)


def exchange(parts):
    return lax.all_to_all(parts, BOTH, split_axis=0, concat_axis=0, tiled=True)


def move(part, axis, ahead):
    count = lax.axis_size(axis)
    pairs = [(i, i + 1) if ahead else (i + 1, i) for i in range(count - 1)]
    return lax.ppermute(part, axis, pairs)


def on_device(
    state_prior,
    conductivity,
    heat_input,
    owner_tile,
    voxel_list,
    pixel_cell,
    observed,
    pixel_variance,
    pixel_noise,
):
    devices = lax.axis_size("gx") * lax.axis_size("gy")
    pixels = pixel_cell.shape[0]
    gx, gy = lax.axis_index("gx"), lax.axis_index("gy")
    inside = jnp.stack(
        [gx > 0, gx < lax.axis_size("gx") - 1, gy > 0, gy < lax.axis_size("gy") - 1]
    ).astype(F32)
    incoming = exchange(pack(owner_tile.reshape(-1), heat_input, voxel_list, devices))
    turned_c, to_high, to_low = rims(state_prior, conductivity)
    low, high = move(to_high, "gy", True), move(to_low, "gy", False)
    state_prior, turned_c = lax.optimization_barrier((state_prior, turned_c))
    own, edge_left, edge_right, top, quiet = relayout(state_prior, conductivity)
    seen = pixel_sums(
        pixel_cell.reshape(1, pixels),
        observed.reshape(1, pixels),
        pixel_variance.reshape(1, pixels),
        pixel_noise,
    )
    incoming, own, top, inside, *seen = lax.optimization_barrier(
        (incoming, own, top, inside, *seen)
    )
    heat, peaks = deposit(incoming, top, conductivity, quiet)
    heat_low, heat_high = move(heat, "gy", True), move(heat, "gy", False)
    low, high, heat_low, heat_high, peaks = lax.optimization_barrier(
        (low, high, heat_low, heat_high, exchange(peaks))
    )
    to_left, to_right = sides(
        edge_left, edge_right, turned_c, low, high, heat_low, heat, heat_high
    )
    left, right = move(to_right, "gx", True), move(to_left, "gx", False)
    start, coef, changes, parts = heated(
        inside,
        (own, low, high),
        (left, right),
        (heat_low, heat, heat_high),
        coefs(turned_c, low, high),
        peaks,
    )
    field, changes, parts, status = pair(1, inside, start, changes, coef, exchange(parts))
    field, changes, sums, status = last(
        inside, field, changes, coef, exchange(parts), status, seen
    )
    result, flag = update(exchange(sums), field, changes, status)

    def again():
        peak = coef * (1.0 + start * start)
        peaks = jnp.full((devices, 1, CX), jnp.max(peak[:, HALO : HALO + CY, 8 : XS - 8]))
        field = start
        for number in range(1, SUBSTEPS - 1):
            field, peaks = single(number, inside, field, coef, exchange(peaks))
        field, changes, sums = close(inside, field, coef, peaks, seen)
        return update(exchange(sums), field, changes, jnp.ones((8, CX), F32))[0]

    return lax.cond(flag[0] > 0, again, lambda: result)


def solution(mesh):
    in_specs = (
        P(None, None, "gy", "gx"),
        P(None, "gy", "gx"),
        P(None, BOTH, None),
        P(BOTH, None),
        P(BOTH, None),
        P(BOTH),
        P(BOTH),
        P(BOTH),
        P(None, BOTH),
    )
    out_specs = P(None, None, "gy", "gx")
    return jax.shard_map(
        on_device, mesh=mesh, in_specs=in_specs, out_specs=out_specs, check_vma=False
    )
```

```python
import functools

import jax
import jax.numpy as jnp
from jax import lax
from jax.experimental import pallas as pl
from jax.experimental.pallas import tpu as pltpu
from jax.sharding import PartitionSpec as P

SUBSTEPS = 6
CAP = 2
COOL = 0.1
SHARE = 0.9
F32 = jnp.float32
BF16 = jnp.bfloat16
VM = pltpu.VMEM
LIMIT = 32 * 1024 * 1024
NT = (((1,), (1,)), ((), ()))
BOTH = ("gx", "gy")

M, NZ, CY, CX = 16, 16, 8, 128
ROWS = 40


def vspec():
    return pl.BlockSpec(memory_space=pltpu.VMEM)


def hspec():
    return pl.BlockSpec(memory_space=pltpu.HBM)


def far(*arrays):
    return [pltpu.with_memory_space_constraint(array, pltpu.HBM) for array in arrays]


def kept(shape):
    return pltpu.HBM(tuple(shape), F32)


def fetch(sems, pairs):
    copies = [
        pltpu.make_async_copy(source, target, sems.at[i])
        for i, (source, target) in enumerate(pairs)
    ]
    for copy in copies:
        copy.start()
    return copies


def params():
    return pltpu.CompilerParams(vmem_limit_bytes=LIMIT)


def lanes():
    return lax.broadcasted_iota(jnp.int32, (CY, CX), 1)


def rows():
    return lax.broadcasted_iota(jnp.int32, (CY, CX), 0)


PARTS = 4


def pack_kernel(
    owner_far, heat_far, voxel_far, out_far,
    out, owner, heat, voxel, wide, high, low, inverse, sems, out_sems,
):
    copies = fetch(sems, ((owner_far, owner), (heat_far, heat), (voxel_far, voxel)))
    blocks = owner.shape[0]
    devices = out.shape[0]

    def clear(i, carry):
        inverse[i] = blocks
        return carry

    lax.fori_loop(0, devices * CAP, clear, 0, unroll=16)
    copies[0].wait()

    def place(b, carry):
        base = owner[b] * CAP
        base = base + jnp.where(inverse[base] != blocks, 1, 0)
        inverse[base] = b
        return carry

    lax.fori_loop(0, blocks, place, 0, unroll=8)
    copies[1].wait()
    copies[2].wait()

    def widen(m, carry):
        wide[m, 0:blocks, :] = heat[m].astype(F32)
        wide[m, blocks:, :] = jnp.zeros((8, CX), F32)
        return carry

    lax.fori_loop(0, M, widen, 0)
    cells = voxel[...]
    high[0:blocks, :] = (cells >> 7).astype(F32)
    high[blocks:, :] = jnp.zeros((8, CX), F32)
    low[0:blocks, :] = (cells & 127).astype(F32)
    low[blocks:, :] = jnp.zeros((8, CX), F32)
    row = rows()

    def emit(d, carry):
        first = inverse[d * CAP]
        second = inverse[d * CAP + 1]
        index = jnp.where(
            row == 0,
            high[pl.ds(first, 1), :],
            jnp.where(
                row == 1,
                high[pl.ds(second, 1), :],
                jnp.where(
                    row == 2,
                    low[pl.ds(first, 1), :],
                    jnp.where(row == 3, low[pl.ds(second, 1), :], 0.0),
                ),
            ),
        )
        chunk = jnp.concatenate(
            [
                wide[:, pl.ds(first, 1), :].reshape(M, CX),
                wide[:, pl.ds(second, 1), :].reshape(M, CX),
                index,
            ],
            axis=0,
        )
        out[d] = chunk.astype(BF16)
        return carry

    share = devices // PARTS
    sent = []
    for part in range(PARTS):
        lax.fori_loop(part * share, (part + 1) * share, emit, 0, unroll=16)
        at = pl.ds(part * share, share)
        copy = pltpu.make_async_copy(out.at[at], out_far.at[at], out_sems.at[part])
        copy.start()
        sent.append(copy)
    for copy in sent:
        copy.wait()


def pack(owner, heat, voxel, devices):
    blocks = owner.shape[0]
    return pl.pallas_call(
        pack_kernel,
        out_shape=pltpu.HBM((devices, ROWS, CX), BF16),
        in_specs=[hspec()] * 3,
        out_specs=hspec(),
        scratch_shapes=[
            VM((devices, ROWS, CX), BF16),
            pltpu.SMEM((blocks,), jnp.int32),
            VM((M, blocks, CX), BF16),
            VM((blocks, CX), jnp.int32),
            VM((M, blocks + 8, CX), F32),
            VM((blocks + 8, CX), F32),
            VM((blocks + 8, CX), F32),
            pltpu.SMEM((devices * CAP,), jnp.int32),
            pltpu.SemaphoreType.DMA((3,)),
            pltpu.SemaphoreType.DMA((PARTS,)),
        ],
        compiler_params=params(),
        name="pack",
    )(*far(owner, heat, voxel))


HALO = 6
YS = CY + 2 * HALO
XT = CX // 8 + 2
ZG = NZ // 2
TOLERANCE = 1e-6
OWN = jax.ShapeDtypeStruct((2, CY, CX, CX), F32)
XS = 8 * XT
WIDE = jax.ShapeDtypeStruct((2, YS, XS, CX), F32)
EDGE = 2 * HALO
SIDE = 2 * YS


def layout_block(state, zi, y):
    parts = [state[m0 : m0 + 8, 2 * group + zi, y, :] for group in range(ZG) for m0 in (0, 8)]
    return (0.5 * jnp.concatenate(parts, axis=0)).T


def rim_kernel(state, conduct, turned_c, to_high, to_low):
    turned = (0.5 * conduct[...].reshape(CX, CX)).T.reshape(XT - 2, 8, CX)
    turned_c[...] = turned
    to_high[EDGE] = turned
    to_low[EDGE] = turned
    for zi in range(2):
        for y in range(CY):
            turned = layout_block(state, zi, y).reshape(XT - 2, 8, CX)
            if y >= CY - HALO:
                to_high[zi * HALO + y - (CY - HALO)] = turned
            if y < HALO:
                to_low[zi * HALO + y] = turned


def rims(state, conduct):
    edge = kept((EDGE + 1, XT - 2, 8, CX))
    return pl.pallas_call(
        rim_kernel,
        out_shape=[kept((XT - 2, 8, CX)), edge, edge],
        in_specs=[vspec()] * 2,
        out_specs=[vspec()] * 3,
        compiler_params=params(),
        name="rims",
    )(state, conduct)


def relayout_kernel(state, conduct, own, edge_left, edge_right, top, quiet):
    peak = jnp.zeros((8, CX), F32)
    for zi in range(2):
        for y in range(CY):
            turned = layout_block(state, zi, y)
            own[zi, y] = turned
            edge_left[zi * CY + y] = turned[0:8]
            edge_right[zi * CY + y] = turned[CX - 8 :]
    for z in range(2, NZ):
        c = 0.5 * conduct[z]
        for m in range(M):
            value = 0.5 * state[m, z]
            peak = jnp.maximum(peak, c + c * (value * value))
    quiet[...] = peak
    for m in range(M):
        for zi in range(2):
            top[m, zi] = 0.5 * state[m, zi]


def relayout(state, conduct):
    side = kept((2 * CY, 8, CX))
    return pl.pallas_call(
        relayout_kernel,
        out_shape=[kept(OWN.shape), side, side, kept((M, 2, CY, CX)), kept((8, CX))],
        in_specs=[vspec()] * 2,
        out_specs=[vspec()] * 5,
        compiler_params=params(),
        name="relayout",
    )(state, conduct)


def side_kernel(
    edge_left, edge_right, turned_c, low, high, heat_low, heat_own, heat_high,
    to_left, to_right, sems,
):
    pairs = []
    for out, edge, t in ((to_left, edge_left, 0), (to_right, edge_right, XT - 3)):
        for zi in range(2):
            at, rows_at = zi * YS, slice(zi * HALO, zi * HALO + HALO)
            pairs += [
                (low.at[rows_at, t], out.at[at : at + HALO]),
                (edge.at[zi * CY : zi * CY + CY], out.at[at + HALO : at + HALO + CY]),
                (high.at[rows_at, t], out.at[at + HALO + CY : at + YS]),
            ]
            for g, heat in enumerate((heat_low, heat_own, heat_high)):
                pairs.append((heat.at[zi, 8 * t : 8 * t + 8, :], out.at[SIDE + 3 + 2 * g + zi]))
        for g, part in enumerate((low.at[EDGE, t], turned_c.at[t], high.at[EDGE, t])):
            pairs.append((part, out.at[SIDE + g]))
    for copy in fetch(sems, pairs):
        copy.wait()


def sides(*operands):
    shape = jax.ShapeDtypeStruct((SIDE + 9, 8, CX), F32)
    return pl.pallas_call(
        side_kernel,
        out_shape=[shape, shape],
        in_specs=[hspec()] * len(operands),
        out_specs=[vspec()] * 2,
        scratch_shapes=[pltpu.SemaphoreType.DMA((30,))],
        compiler_params=params(),
        name="sides",
    )(*far(*operands))


def split(strip):
    parts = []
    for _ in range(3):
        part = strip.astype(BF16)
        parts.append(part)
        strip = strip - part.astype(F32)
    return jnp.concatenate(parts, axis=1)


def placed(parts, zi, y0):
    source = lax.broadcasted_iota(jnp.int32, (CX, CX), 0)
    target = lax.broadcasted_iota(jnp.int32, (CX, CX), 1)
    hot = jnp.where(source == (2 * (target >> 4) + zi) * CY + y0, 1.0, 0.0).astype(BF16)
    hot = jnp.concatenate([hot] * 3, axis=0)
    return jnp.dot(parts, hot, preferred_element_type=F32)


def halo_row(g, y0):
    row = y0 + HALO + (g - 1) * CY
    return row if 0 <= row < YS else None


def coef_kernel(own, low, high, out, tiles, sems):
    pairs = ((low.at[EDGE], tiles.at[0]), (own, tiles.at[1]), (high.at[EDGE], tiles.at[2]))
    for copy in fetch(sems, pairs):
        copy.wait()
    strip = split(tiles[...].reshape(3 * CX, CX))
    for zi in range(2):
        for y0 in range(CY):
            part = placed(strip, zi, y0)
            for g in range(3):
                row = halo_row(g, y0)
                if row is not None:
                    out[zi, row] = part[g * CX : (g + 1) * CX, :]


def coefs(own, low, high):
    return pl.pallas_call(
        coef_kernel,
        out_shape=jax.ShapeDtypeStruct((2, YS, CX, CX), F32),
        in_specs=[hspec()] * 3,
        out_specs=vspec(),
        scratch_shapes=[VM((3, XT - 2, 8, CX), F32), pltpu.SemaphoreType.DMA((3,))],
        compiler_params=params(),
        name="coefs",
    )(*far(own, low, high))


def deposit_kernel(
    incoming, top_far, conduct_far, quiet_far, out, peaks, total, top, conduct, quiet, sems
):
    copies = fetch(sems, ((top_far, top), (conduct_far.at[0:2], conduct), (quiet_far, quiet)))
    sources = incoming.shape[0]
    group = 64
    place = lax.broadcasted_iota(jnp.int32, (CX, CX), 0).astype(F32).astype(BF16)
    zero = jnp.zeros((M, CX), BF16)
    total[...] = jnp.zeros_like(total)

    def one(g, carry):
        left = []
        right = []
        for s in range(group):
            source = g * group + s
            index = incoming[source, 32:40, :].astype(F32)
            for slot in range(CAP):
                heat = incoming[source, slot * M : (slot + 1) * M, :]
                layer = jnp.broadcast_to(index[slot : slot + 1, :], (M, CX)).astype(BF16)
                cell = jnp.broadcast_to(index[2 + slot : 3 + slot, :], (CX, CX)).astype(BF16)
                left.append(
                    jnp.concatenate(
                        [jnp.where(layer == h, heat, zero) for h in range(2 * CY)], axis=0
                    )
                )
                right.append(jnp.where(place == cell, 1.0, 0.0).astype(BF16))
        total[...] += lax.dot_general(
            jnp.concatenate(left, axis=1),
            jnp.concatenate(right, axis=1),
            NT,
            preferred_element_type=F32,
        )
        return carry

    lax.fori_loop(0, sources // group, one, 0)
    for zi in range(2):
        out[zi] = (0.5 * total[zi * CX : (zi + 1) * CX, :]).T
    for copy in copies:
        copy.wait()
    peak = quiet[...]
    for zi in range(2):
        c = 0.5 * conduct[zi]
        for m in range(M):
            value = top[m, zi] + 0.5 * total[pl.ds(zi * CX + m, CY, stride=M), :]
            peak = jnp.maximum(peak, c + c * (value * value))
    send_row(whole_peak(peak), peaks)


def send_row(row, out):
    for d in range(0, out.shape[0], 8):
        out[d : d + 8, 0, :] = row


def deposit(incoming, top, conduct, quiet):
    devices = incoming.shape[0]
    return pl.pallas_call(
        deposit_kernel,
        out_shape=[
            kept((2, CX, CX)),
            jax.ShapeDtypeStruct((devices, 1, CX), F32),
        ],
        in_specs=[vspec()] + [hspec()] * 3,
        out_specs=[vspec()] * 2,
        scratch_shapes=[
            VM((2 * CY * M, CX), F32),
            VM(top.shape, F32),
            VM((2, CY, CX), F32),
            VM(quiet.shape, F32),
            pltpu.SemaphoreType.DMA((3,)),
        ],
        compiler_params=params(),
        name="deposit",
    )(incoming, *far(top, conduct, quiet))


def whole_peak(value):
    return jnp.broadcast_to(jnp.max(value, axis=(0, 1), keepdims=True), (8, CX))


def step_of(peak):
    return SHARE / (12.0 * peak + COOL)


def tile(t):
    return slice(8 * t, 8 * t + 8)


def half_conductance(c, u):
    return c + c * (u * u)


def segments(inside, first, end):
    parts = []
    if first < HALO:
        parts.append((first, HALO, False, inside[2]))
    parts.append((max(first, HALO), min(end, HALO + CY), True, None))
    if end > HALO + CY:
        parts.append((HALO + CY, end, False, inside[3]))
    return parts


def mask_of(inside, row_mask, t):
    if t == 0:
        return inside[0] if row_mask is None else inside[0] * row_mask
    if t == XT - 1:
        return inside[1] if row_mask is None else inside[1] * row_mask
    return row_mask


def sweep(field, half, above, inside, first, end, emit, carry, unroll=1):
    lane = lanes()
    row = rows()
    last_row = row == 7
    first_row = row == 0
    inner_lane = lane < CX - M
    outer_lane = lane >= M
    cooling = jnp.where(lane < M, COOL, 0.0)

    for zi in range(2):
        for t in range(XT):
            s = tile(t)
            above[zi, t] = (half[zi, first - 1, s, :] + half[zi, first, s, :]) * (
                field[zi, first, s, :] - field[zi, first - 1, s, :]
            )

    def line(own, row_mask, y, state):
        for t in range(XT):
            s = tile(t)
            us = [field[zi, y, s, :] for zi in range(2)]
            hs = [half[zi, y, s, :] for zi in range(2)]
            change = []
            for zi in range(2):
                u, h = us[zi], hs[zi]
                if t < XT - 1:
                    after = slice(8 * t + 1, 8 * t + 9)
                    u_after, h_after = field[zi, y, after, :], half[zi, y, after, :]
                else:
                    u_after = jnp.where(last_row, u, pltpu.roll(u, 7, axis=0))
                    h_after = pltpu.roll(h, 7, axis=0)
                if t:
                    before = slice(8 * t - 1, 8 * t + 7)
                    u_before, h_before = field[zi, y, before, :], half[zi, y, before, :]
                else:
                    u_before = jnp.where(first_row, u, pltpu.roll(u, 1, axis=0))
                    h_before = pltpu.roll(h, 1, axis=0)
                total = (h + h_after) * (u_after - u) + (h + h_before) * (u_before - u)
                across = (h + half[zi, y + 1, s, :]) * (field[zi, y + 1, s, :] - u)
                total = total + (across - above[zi, t])
                above[zi, t] = across
                change.append(total)
            within = (hs[0] + hs[1]) * (us[1] - us[0])
            between = (hs[1] + pltpu.roll(hs[0], CX - M, axis=1)) * (
                pltpu.roll(us[0], CX - M, axis=1) - us[1]
            )
            between = jnp.where(inner_lane, between, 0.0)
            below = (hs[0] + pltpu.roll(hs[1], M, axis=1)) * (us[0] - pltpu.roll(us[1], M, axis=1))
            below = jnp.where(outer_lane, below, 0.0)
            change[0] = change[0] + (within - below) - cooling * us[0]
            change[1] = change[1] + (between - within)
            state = emit(y, t, us, change, own, mask_of(inside, row_mask, t), state)
        return state

    for start, stop, own, row_mask in segments(inside, first, end):
        carry = lax.fori_loop(
            start, stop, functools.partial(line, own, row_mask), carry, unroll=unroll
        )
    return carry


def advance(field, half, coef, above, inside, step, first, end, put, unroll=2):
    def emit(y, t, us, change, own, mask, peak):
        part = step if mask is None else step * mask
        for zi in range(2):
            value = us[zi] + part * change[zi]
            after = half_conductance(coef[zi, y, tile(t), :], value)
            put(zi, y, t, value, after)
            if own and 0 < t < XT - 1:
                peak = jnp.maximum(peak, after)
        return peak

    zero = jnp.zeros((8, CX), F32)
    return sweep(field, half, above, inside, first, end, emit, zero, unroll=unroll)


def propose(field, half, coef, above, inside, guess, first, end, changes, peak, late, out):
    def emit(y, t, us, change, own, mask, best):
        for zi in range(2):
            moved = change[zi] if mask is None else change[zi] * mask
            changes[zi, y, tile(t), :] = moved
            if own and 0 < t < XT - 1:
                c = coef[zi, y, tile(t), :]
                rank = half_conductance(c, us[zi] + guess * moved)
                better = rank > best[0]
                best = tuple(
                    jnp.where(better, new, old)
                    for new, old in zip((rank, us[zi], moved, c), best)
                )
        return best

    best = sweep(
        field, half, above, inside, first, end, emit, (jnp.zeros((8, CX), F32),) * 4,
        unroll=1,
    )
    for shift, axis in ((4, 0), (2, 0), (1, 0), (64, 1), (32, 1)):
        other = tuple(pltpu.roll(part, shift, axis=axis) for part in best)
        better = other[0] > best[0]
        best = tuple(jnp.where(better, new, old) for new, old in zip(other, best))
    part = lanes() >> 4
    chunk = jnp.where(part == 6, whole_peak(peak), whole_peak(late))
    for place, value in ((2, best[3]), (1, best[2]), (0, best[1])):
        chunk = jnp.where((part >> 1) == place, value, chunk)
    send_row(chunk, out)


def gather_rows(parts):
    return [parts[d : d + 8, 0, :] for d in range(0, parts.shape[0], 8)]


def largest(values):
    most = values[0]
    for value in values[1:]:
        most = jnp.maximum(most, value)
    return most


def agree(parts):
    part = lanes() >> 4
    rows_of = gather_rows(parts)
    most = largest(rows_of)
    now = whole_peak(jnp.where(part == 6, most, 0.0))
    late = whole_peak(jnp.where(part == 7, most, 0.0))
    step = step_of(now)
    then = jnp.zeros((8, CX), F32)
    for value in rows_of:
        moved = pltpu.roll(value, CX - 32, axis=1)
        c = pltpu.roll(value, CX - 64, axis=1)
        then = jnp.maximum(then, half_conductance(c, value + step * moved))
    return now, whole_peak(jnp.where(part < 2, then, 0.0)), late


def differs(late, used):
    return jnp.where(late > used * (1.0 + TOLERANCE), 1.0, 0.0)


def heated_kernel(
    inside, peaks, left, right, coef_main, own_far, low_far, high_far,
    heat_low_far, heat_own_far, heat_high_far,
    out, coef, changes, parts, start, half, next_half, above,
    own, low, high, heat_low, heat_own, heat_high, sems,
):
    copies = fetch(
        sems,
        [
            (heat_low_far, heat_low),
            (low_far.at[0:EDGE], low),
            (heat_own_far, heat_own),
            (own_far, own),
            (heat_high_far, heat_high),
            (high_far.at[0:EDGE], high),
        ],
    )
    top = lanes() < M

    strip = split(
        jnp.concatenate([side[SIDE + g] for g in range(3) for side in (left, right)], axis=0)
    )
    for zi in range(2):
        for y0 in range(CY):
            part = placed(strip, zi, y0)
            for g in range(3):
                at = halo_row(g, y0)
                if at is not None:
                    coef[zi, at, tile(0), :] = part[16 * g : 16 * g + 8, :]
                    coef[zi, at, tile(XT - 1), :] = part[16 * g + 8 : 16 * g + 16, :]

    def row(g, heat, tile_of, y0, yy):
        shift = (CX - 16 * y0) % CX
        for zi in range(2):
            for t in range(XT):
                if t == 0:
                    prior, add = left[zi * YS + yy], left[SIDE + 3 + 2 * g + zi]
                elif t == XT - 1:
                    prior, add = right[zi * YS + yy], right[SIDE + 3 + 2 * g + zi]
                else:
                    prior, add = tile_of(zi, t - 1), heat[zi, tile(t - 1), :]
                if shift:
                    add = pltpu.roll(add, shift, axis=1)
                value = prior + jnp.where(top, add, 0.0)
                if 0 < t < XT - 1:
                    c = coef_main[zi, yy, tile(t - 1), :]
                    coef[zi, yy, tile(t), :] = c
                else:
                    c = coef[zi, yy, tile(t), :]
                after = half_conductance(c, value)
                start[zi, yy, tile(t), :] = value
                half[zi, yy, tile(t), :] = after

    def edge(ref, y):
        return lambda zi, t: ref[zi * HALO + y, t]

    for copy in copies[0:2]:
        copy.wait()
    for y in range(HALO):
        row(0, heat_low, edge(low, y), y + CY - HALO, y)
    for copy in copies[2:4]:
        copy.wait()
    for y in range(CY):
        row(1, heat_own, lambda zi, t: own[zi, y, tile(t), :], y, y + HALO)
    for copy in copies[4:6]:
        copy.wait()
    for y in range(HALO):
        row(2, heat_high, edge(high, y), y, y + HALO + CY)

    def put(zi, y, t, value, after):
        out[zi, y, tile(t), :] = value
        next_half[zi, y, tile(t), :] = after

    step = step_of(whole_peak(largest(gather_rows(peaks))))
    peak = advance(start, half, coef, above, inside, step, 1, YS - 1, put, unroll=4)
    guess = jnp.minimum(step_of(whole_peak(peak)), 2.0 * step)
    zero = jnp.zeros((8, CX), F32)
    propose(
        out, next_half, coef, above, inside, guess, 2, YS - 2, changes, peak, zero, parts
    )


ROW = (2, XT, 8, CX)


def smem():
    return pl.BlockSpec(memory_space=pltpu.SMEM)


def heated(inside, prior, halos, heat, coef, peaks):
    near = [inside, peaks, *halos, coef]
    operands = far(*prior, *heat)
    edge = VM((EDGE, XT - 2, 8, CX), F32)
    return pl.pallas_call(
        heated_kernel,
        out_shape=[WIDE, WIDE, WIDE, jax.ShapeDtypeStruct(peaks.shape, F32)],
        in_specs=[smem()] + [vspec()] * 4 + [hspec()] * len(operands),
        out_specs=[vspec()] * 4,
        scratch_shapes=[VM(WIDE.shape, F32)] * 3
        + [VM(ROW, F32), VM(OWN.shape, F32), edge, edge]
        + [VM(part.shape, F32) for part in heat]
        + [pltpu.SemaphoreType.DMA((6,))],
        compiler_params=params(),
        name="heated",
    )(*near, *operands)


def first_of_pair(field, changes, coef, step, first, end, out, half):
    def line(y, peak):
        top = jnp.zeros((8, CX), F32)
        for zi in range(2):
            for t in range(XT):
                value = field[zi, y, tile(t), :] + step * changes[zi, y, tile(t), :]
                after = half_conductance(coef[zi, y, tile(t), :], value)
                out[zi, y, tile(t), :] = value
                half[zi, y, tile(t), :] = after
                if 0 < t < XT - 1:
                    top = jnp.maximum(top, after)
        own = jnp.where((y >= HALO) & (y < HALO + CY), 1.0, 0.0)
        return jnp.maximum(peak, own * top)

    return lax.fori_loop(first, end, line, jnp.zeros((8, CX), F32), unroll=2)


def pair_kernel(
    number, inside, field, changes, coef, parts,
    out, out_changes, out_parts, status, middle, half, next_half, above,
):
    now, then, _ = agree(parts)
    status[...] = jnp.where(rows() == 0, then, 0.0)
    seen = first_of_pair(
        field, changes, coef, step_of(now), number + 1, YS - 1 - number, middle, half
    )

    def put(zi, y, t, value, after):
        out[zi, y, tile(t), :] = value
        next_half[zi, y, tile(t), :] = after

    step = step_of(then)
    peak = advance(
        middle, half, coef, above, inside, step, number + 2, YS - 2 - number, put
    )
    guess = jnp.minimum(step_of(whole_peak(peak)), 1.2 * step)
    propose(
        out, next_half, coef, above, inside, guess, number + 3, YS - 3 - number,
        out_changes, peak, seen, out_parts,
    )


STATUS = jax.ShapeDtypeStruct((8, CX), F32)


def pair(number, inside, field, changes, coef, parts):
    operands = [inside, field, changes, coef, parts]
    return pl.pallas_call(
        functools.partial(pair_kernel, number),
        out_shape=[WIDE, WIDE, jax.ShapeDtypeStruct(parts.shape, F32), STATUS],
        in_specs=[smem()] + [vspec()] * 4,
        out_specs=[vspec()] * 4,
        scratch_shapes=[VM(WIDE.shape, F32)] * 3 + [VM(ROW, F32)],
        compiler_params=params(),
        name=f"pair_{number}",
    )(*operands)


def closing(
    field, half, above, inside, weight, data, peak, late, out, out_changes, sums, flat
):
    def emit(y, t, us, change, own, mask, state):
        if 0 < t < XT - 1:
            for zi in range(2):
                out[zi, y - HALO, tile(t - 1), :] = us[zi]
                out_changes[zi, y - HALO, tile(t - 1), :] = change[zi]
        return state

    sweep(field, half, above, inside, HALO, HALO + CY, emit, 0, unroll=4)
    lefts, rights = [], []
    for y in range(CY):
        w = weight[y : y + 1, :]
        for m in range(M):
            flat[m : m + 1, :] = data[m, y : y + 1, :]
        means = []
        spreads = []
        for part in (out, out_changes):
            seen = 2.0 * part[0, y].T[0:M, :]
            mean = jnp.mean(seen, axis=0, keepdims=True)
            means.append(mean)
            spreads.append(seen - mean)
        lefts.append(jnp.concatenate(spreads + means + [jnp.zeros((6, CX), F32)], axis=0))
        rights.append(jnp.concatenate([part * w for part in spreads] + [flat[...]], axis=0))
    grams = lax.dot_general(
        jnp.concatenate(lefts, axis=1),
        jnp.concatenate(rights, axis=1),
        NT,
        precision=lax.Precision.HIGHEST,
        preferred_element_type=F32,
    )
    grams = jnp.concatenate([grams, jnp.zeros((5 * CY, CX - 3 * M), F32)], axis=1)
    tall = lax.broadcasted_iota(jnp.int32, (M, CX), 0)
    wide = lax.broadcasted_iota(jnp.int32, (M, CX), 1)
    first, second, means = grams[0:M], grams[M : 2 * M], grams[2 * M : 2 * M + 8]

    def block(part, at):
        return jnp.where(wide < M, pltpu.roll(part, (CX - M * at) % CX, axis=1), 0.0)

    def lone(part, row, at):
        moved = pltpu.roll(part, (CX - M * at) % CX, axis=1) if at else part
        return jnp.broadcast_to(moved[row : row + 1, :], (M, CX))

    tops = [
        lone(means, 0, 1) + lone(means, 1, 0),
        lone(means, 0, 0),
        lone(means, 1, 1),
    ]
    blocks = [
        jnp.where(tall < wide, block(first, 0), block(second, 1)),
        block(first, 1) + block(second, 0),
        block(first, 2),
        block(second, 2),
    ]
    scalar = jnp.where(wide == 0, whole_peak(peak)[0:1], whole_peak(late)[0:1])
    blocks[0] = jnp.where(tall == wide, scalar, blocks[0])
    for i, top in enumerate(tops):
        blocks[i + 1] = jnp.where(tall == 0, jnp.where(wide < M, top, 0.0), blocks[i + 1])
    packed = blocks[0]
    for i in range(1, 4):
        packed = packed + pltpu.roll(blocks[i], M * i, axis=1)
    packed = packed[0:8] + pltpu.roll(packed[8:16], CX // 2, axis=1)
    for d in range(sums.shape[0]):
        sums[d] = packed


def last_kernel(
    inside, field, changes, coef, parts, status, weight_far, data_far,
    out, out_changes, sums, out_status,
    middle, half, near, near_half, above, flat, weight, data, sems,
):
    copies = fetch(sems, ((weight_far, weight), (data_far, data)))
    number = SUBSTEPS - 3
    now, then, late = agree(parts)
    bad = differs(late[0:1], status[0:1, :])
    out_status[...] = jnp.where(rows() == 0, then, bad)
    seen = first_of_pair(
        field, changes, coef, step_of(now), number + 1, YS - 1 - number, middle, half
    )

    def put(zi, y, t, value, after):
        near[zi, y, tile(t), :] = value
        near_half[zi, y, tile(t), :] = after

    peak = advance(
        middle, half, coef, above, inside, step_of(then), number + 2, YS - 2 - number, put
    )
    for copy in copies:
        copy.wait()
    closing(
        near, near_half, above, inside, weight, data, peak, seen, out, out_changes, sums, flat
    )


def sums_shape(devices):
    return jax.ShapeDtypeStruct((devices, 8, CX), F32)


def last(inside, field, changes, coef, parts, status, pixels):
    operands = [inside, field, changes, coef, parts, status, *far(*pixels)]
    return pl.pallas_call(
        last_kernel,
        out_shape=[OWN, OWN, sums_shape(parts.shape[0]), STATUS],
        in_specs=[smem()] + [vspec()] * 5 + [hspec()] * 2,
        out_specs=[vspec()] * 4,
        scratch_shapes=[VM(WIDE.shape, F32)] * 4
        + [VM(ROW, F32), VM((M, CX), F32)]
        + [VM(part.shape, F32) for part in pixels]
        + [pltpu.SemaphoreType.DMA((2,))],
        compiler_params=params(),
        name="last_pair",
    )(*operands)


def fill_half(field, coef, half, first, end):
    def fill(y, carry):
        for zi in range(2):
            half[zi, y] = half_conductance(coef[zi, y], field[zi, y])
        return carry

    lax.fori_loop(first, end, fill, 0)


def single_kernel(number, inside, field, coef, peaks, out, out_peaks, half, above):
    step = step_of(whole_peak(largest(gather_rows(peaks))))
    fill_half(field, coef, half, number, YS - number)

    def put(zi, y, t, value, after):
        out[zi, y, tile(t), :] = value

    peak = advance(field, half, coef, above, inside, step, number + 1, YS - 1 - number, put)
    send_row(whole_peak(peak), out_peaks)


def single(number, inside, field, coef, peaks):
    return pl.pallas_call(
        functools.partial(single_kernel, number),
        out_shape=[WIDE, jax.ShapeDtypeStruct(peaks.shape, F32)],
        in_specs=[smem()] + [vspec()] * 3,
        out_specs=[vspec()] * 2,
        scratch_shapes=[VM(WIDE.shape, F32), VM(ROW, F32)],
        compiler_params=params(),
        name=f"single_{number}",
    )(inside, field, coef, peaks)


def closing_kernel(
    inside, field, coef, peaks, weight, data, out, out_changes, sums, half, above, flat
):
    fill_half(field, coef, half, HALO - 1, HALO + CY + 1)
    peak = peaks[0:8, 0, :]
    closing(
        field, half, above, inside, weight, data, peak, jnp.zeros((8, CX), F32),
        out, out_changes, sums, flat,
    )


def close(inside, field, coef, peaks, pixels):
    operands = [inside, field, coef, peaks, *pixels]
    return pl.pallas_call(
        closing_kernel,
        out_shape=[OWN, OWN, sums_shape(peaks.shape[0])],
        in_specs=[smem()] + [vspec()] * (len(operands) - 1),
        out_specs=[vspec()] * 3,
        scratch_shapes=[VM(WIDE.shape, F32), VM(ROW, F32), VM((M, CX), F32)],
        compiler_params=params(),
        name="closing",
    )(*operands)


def pixel_kernel(cell, observed, variance, noise, weight, data):
    pixels = cell.shape[1]
    place = cell[...]
    var = variance[...]
    inverse = 1.0 / var
    values = (observed[...] + noise[...] * jnp.sqrt(var)) * inverse
    stack = jnp.concatenate([values, jnp.broadcast_to(inverse, (8, pixels))], axis=0)
    width = place >> 7
    hot = jnp.where(
        lax.broadcasted_iota(jnp.int32, (CX, pixels), 0) == (place & 127), 1.0, 0.0
    ).astype(F32)
    for y in range(CY):
        part = lax.dot_general(
            jnp.where(width == y, stack, 0.0),
            hot,
            NT,
            precision=lax.Precision.HIGHEST,
            preferred_element_type=F32,
        )
        weight[y : y + 1, :] = part[M : M + 1, :]
        for m in range(M):
            data[m, y : y + 1, :] = part[m : m + 1, :]


def pixel_sums(cell, observed, variance, noise):
    return pl.pallas_call(
        pixel_kernel,
        out_shape=[kept((CY, CX)), kept((M, CY, CX))],
        in_specs=[vspec()] * 4,
        out_specs=[vspec()] * 2,
        compiler_params=params(),
        name="pixels",
    )(cell, observed, variance, noise)


def update_kernel(sums, field, changes, status, out, flag):
    total = sums[0]
    most = total
    for d in range(1, sums.shape[0]):
        total = total + sums[d]
        most = jnp.maximum(most, sums[d])
    step = step_of(jnp.broadcast_to(most[0:1, 0:1], (1, CX)))
    late = jnp.broadcast_to(most[1:2, 1:2], (1, CX))
    bad = jnp.maximum(status[1:2, :], differs(late, status[0:1, :]))
    flag[0] = jnp.where(jnp.max(bad) > 0.0, 1, 0)

    tall = lax.broadcasted_iota(jnp.int32, (M, CX), 0)
    wide = lax.broadcasted_iota(jnp.int32, (M, CX), 1)
    packed = jnp.concatenate([total, pltpu.roll(total, CX // 2, axis=1)], axis=0)

    def block(at):
        return jnp.where(wide < M, pltpu.roll(packed, (CX - M * at) % CX, axis=1), 0.0)

    def whole(part):
        rest = jnp.where(tall == 0, 0.0, part)
        first = -jnp.sum(rest, axis=0, keepdims=True)
        return jnp.where(tall == 0, first, rest), part[0:1, :]

    def balanced(part):
        part = jnp.where((tall == wide) | (wide >= M), 0.0, part)
        return jnp.where(tall == wide, -jnp.sum(part, axis=1, keepdims=True), part)

    corner = block(0)
    mirror = jnp.concatenate([corner, jnp.zeros((CX - M, CX), F32)], axis=0).T[0:M, :]
    square = balanced(jnp.where(tall < wide, corner, mirror))
    square_c = balanced(jnp.where(tall > wide, corner, mirror))
    mixed, mean_1 = whole(block(1))
    data, mean_0 = whole(block(2))
    data_c, mean_2 = whole(block(3))
    cross = square + step * (mixed + step * square_c)
    mean = mean_0 + step * (mean_1 + step * mean_2)
    mean = jnp.sum(jnp.where(tall == wide, mean, 0.0), axis=1, keepdims=True)
    target = jnp.where(wide < M, data + step * data_c - cross - mean, 0.0)
    system = jnp.where(tall == wide, cross + (M - 1.0), cross)
    columns = [jnp.broadcast_to(system[:, i : i + 1], (M, CX)) for i in range(M)]
    for i in range(M):
        pivot = 1.0 / columns[i][i : i + 1, :]
        factor = jnp.where(tall == i, 0.0, columns[i] * pivot)
        for j in range(i + 1, M):
            columns[j] = columns[j] - factor * columns[j][i : i + 1, :]
        target = target - factor * target[i : i + 1, :]
    for i in range(M):
        target = jnp.where(tall == i, target / columns[i], target)
    mixing = target - jnp.mean(target, axis=0, keepdims=True)
    mixing = jnp.where(wide < M, mixing + jnp.where(tall == wide, 1.0, 0.0), 0.0)
    for shift in (16, 32, 64):
        mixing = mixing + pltpu.roll(mixing, shift, axis=1)
    mixing = jnp.concatenate([mixing] * ZG, axis=0)
    tall = lax.broadcasted_iota(jnp.int32, (CX, CX), 0)
    wide = lax.broadcasted_iota(jnp.int32, (CX, CX), 1)
    mixing = jnp.where((tall >> 4) == (wide >> 4), 2.0 * mixing, 0.0).T
    mixing_high = mixing.astype(BF16)
    mixing_low = (mixing - mixing_high.astype(F32)).astype(BF16)
    mixing = jnp.concatenate([mixing_high, mixing_low, mixing_high], axis=1)
    for zi in range(2):
        for y in range(CY):
            prior = field[zi, y] + step * changes[zi, y]
            high = prior.astype(BF16)
            low = (prior - high.astype(F32)).astype(BF16)
            part = lax.dot_general(
                mixing,
                jnp.concatenate([high, high, low], axis=1),
                NT,
                preferred_element_type=F32,
            )
            for group in range(ZG):
                for m0 in (0, 8):
                    at = group * M + m0
                    out[m0 : m0 + 8, 2 * group + zi, y, :] = part[at : at + 8, :]


def update(sums, field, changes, status):
    return pl.pallas_call(
        update_kernel,
        out_shape=[
            jax.ShapeDtypeStruct((M, NZ, CY, CX), F32),
            jax.ShapeDtypeStruct((1,), jnp.int32),
        ],
        in_specs=[vspec()] * 4,
        out_specs=[vspec(), smem()],
        compiler_params=params(),
        name="update",
    )(sums, field, changes, status)


def exchange(parts):
    return lax.all_to_all(parts, BOTH, split_axis=0, concat_axis=0, tiled=True)


def move(part, axis, ahead):
    count = lax.axis_size(axis)
    pairs = [(i, i + 1) if ahead else (i + 1, i) for i in range(count - 1)]
    return lax.ppermute(part, axis, pairs)


def on_device(
    state_prior,
    conductivity,
    heat_input,
    owner_tile,
    voxel_list,
    pixel_cell,
    observed,
    pixel_variance,
    pixel_noise,
):
    devices = lax.axis_size("gx") * lax.axis_size("gy")
    pixels = pixel_cell.shape[0]
    gx, gy = lax.axis_index("gx"), lax.axis_index("gy")
    inside = jnp.stack(
        [gx > 0, gx < lax.axis_size("gx") - 1, gy > 0, gy < lax.axis_size("gy") - 1]
    ).astype(F32)
    incoming = exchange(pack(owner_tile.reshape(-1), heat_input, voxel_list, devices))
    turned_c, to_high, to_low = rims(state_prior, conductivity)
    low, high = move(to_high, "gy", True), move(to_low, "gy", False)
    state_prior, turned_c = lax.optimization_barrier((state_prior, turned_c))
    own, edge_left, edge_right, top, quiet = relayout(state_prior, conductivity)
    seen = pixel_sums(
        pixel_cell.reshape(1, pixels),
        observed.reshape(1, pixels),
        pixel_variance.reshape(1, pixels),
        pixel_noise,
    )
    incoming, own, top, inside, *seen = lax.optimization_barrier(
        (incoming, own, top, inside, *seen)
    )
    heat, peaks = deposit(incoming, top, conductivity, quiet)
    heat_low, heat_high = move(heat, "gy", True), move(heat, "gy", False)
    low, high, heat_low, heat_high, peaks = lax.optimization_barrier(
        (low, high, heat_low, heat_high, exchange(peaks))
    )
    to_left, to_right = sides(
        edge_left, edge_right, turned_c, low, high, heat_low, heat, heat_high
    )
    left, right = move(to_right, "gx", True), move(to_left, "gx", False)
    start, coef, changes, parts = heated(
        inside,
        (own, low, high),
        (left, right),
        (heat_low, heat, heat_high),
        coefs(turned_c, low, high),
        peaks,
    )
    field, changes, parts, status = pair(1, inside, start, changes, coef, exchange(parts))
    field, changes, sums, status = last(
        inside, field, changes, coef, exchange(parts), status, seen
    )
    result, flag = update(exchange(sums), field, changes, status)

    def again():
        peak = coef * (1.0 + start * start)
        peaks = jnp.full((devices, 1, CX), jnp.max(peak[:, HALO : HALO + CY, 8 : XS - 8]))
        field = start
        for number in range(1, SUBSTEPS - 1):
            field, peaks = single(number, inside, field, coef, exchange(peaks))
        field, changes, sums = close(inside, field, coef, peaks, seen)
        return update(exchange(sums), field, changes, jnp.ones((8, CX), F32))[0]

    return lax.cond(flag[0] > 0, again, lambda: result)


def solution(mesh):
    in_specs = (
        P(None, None, "gy", "gx"),
        P(None, "gy", "gx"),
        P(None, BOTH, None),
        P(BOTH, None),
        P(BOTH, None),
        P(BOTH),
        P(BOTH),
        P(BOTH),
        P(None, BOTH),
    )
    out_specs = P(None, None, "gy", "gx")
    return jax.shard_map(
        on_device, mesh=mesh, in_specs=in_specs, out_specs=out_specs, check_vma=False
    )
```

```python
import functools

import jax
import jax.numpy as jnp
from jax import lax
from jax.experimental import pallas as pl
from jax.experimental.pallas import tpu as pltpu
from jax.sharding import PartitionSpec as P

SUBSTEPS = 6
CAP = 2
COOL = 0.1
SHARE = 0.9
F32 = jnp.float32
BF16 = jnp.bfloat16
VM = pltpu.VMEM
LIMIT = 32 * 1024 * 1024
NT = (((1,), (1,)), ((), ()))
BOTH = ("gx", "gy")

M, NZ, CY, CX = 16, 16, 8, 128
ROWS = 40


def vspec():
    return pl.BlockSpec(memory_space=pltpu.VMEM)


def hspec():
    return pl.BlockSpec(memory_space=pltpu.HBM)


def far(*arrays):
    return [pltpu.with_memory_space_constraint(array, pltpu.HBM) for array in arrays]


def kept(shape):
    return pltpu.HBM(tuple(shape), F32)


def fetch(sems, pairs):
    copies = [
        pltpu.make_async_copy(source, target, sems.at[i])
        for i, (source, target) in enumerate(pairs)
    ]
    for copy in copies:
        copy.start()
    return copies


def params():
    return pltpu.CompilerParams(vmem_limit_bytes=LIMIT)


def lanes():
    return lax.broadcasted_iota(jnp.int32, (CY, CX), 1)


def rows():
    return lax.broadcasted_iota(jnp.int32, (CY, CX), 0)


PARTS = 4


def pack_kernel(
    owner_far, heat_far, voxel_far, out_far,
    out, owner, heat, voxel, wide, high, low, inverse, sems, out_sems,
):
    copies = fetch(sems, ((owner_far, owner), (heat_far, heat), (voxel_far, voxel)))
    blocks = owner.shape[0]
    devices = out.shape[0]

    def clear(i, carry):
        inverse[i] = blocks
        return carry

    lax.fori_loop(0, devices * CAP, clear, 0, unroll=16)
    copies[0].wait()

    def place(b, carry):
        base = owner[b] * CAP
        base = base + jnp.where(inverse[base] != blocks, 1, 0)
        inverse[base] = b
        return carry

    lax.fori_loop(0, blocks, place, 0, unroll=8)
    copies[1].wait()
    copies[2].wait()

    def widen(m, carry):
        wide[m, 0:blocks, :] = heat[m].astype(F32)
        wide[m, blocks:, :] = jnp.zeros((8, CX), F32)
        return carry

    lax.fori_loop(0, M, widen, 0)
    cells = voxel[...]
    high[0:blocks, :] = (cells >> 7).astype(F32)
    high[blocks:, :] = jnp.zeros((8, CX), F32)
    low[0:blocks, :] = (cells & 127).astype(F32)
    low[blocks:, :] = jnp.zeros((8, CX), F32)
    row = rows()

    def emit(d, carry):
        first = inverse[d * CAP]
        second = inverse[d * CAP + 1]
        index = jnp.where(
            row == 0,
            high[pl.ds(first, 1), :],
            jnp.where(
                row == 1,
                high[pl.ds(second, 1), :],
                jnp.where(
                    row == 2,
                    low[pl.ds(first, 1), :],
                    jnp.where(row == 3, low[pl.ds(second, 1), :], 0.0),
                ),
            ),
        )
        chunk = jnp.concatenate(
            [
                wide[:, pl.ds(first, 1), :].reshape(M, CX),
                wide[:, pl.ds(second, 1), :].reshape(M, CX),
                index,
            ],
            axis=0,
        )
        out[d] = chunk.astype(BF16)
        return carry

    share = devices // PARTS
    sent = []
    for part in range(PARTS):
        lax.fori_loop(part * share, (part + 1) * share, emit, 0, unroll=16)
        at = pl.ds(part * share, share)
        copy = pltpu.make_async_copy(out.at[at], out_far.at[at], out_sems.at[part])
        copy.start()
        sent.append(copy)
    for copy in sent:
        copy.wait()


def pack(owner, heat, voxel, devices):
    blocks = owner.shape[0]
    return pl.pallas_call(
        pack_kernel,
        out_shape=pltpu.HBM((devices, ROWS, CX), BF16),
        in_specs=[hspec()] * 3,
        out_specs=hspec(),
        scratch_shapes=[
            VM((devices, ROWS, CX), BF16),
            pltpu.SMEM((blocks,), jnp.int32),
            VM((M, blocks, CX), BF16),
            VM((blocks, CX), jnp.int32),
            VM((M, blocks + 8, CX), F32),
            VM((blocks + 8, CX), F32),
            VM((blocks + 8, CX), F32),
            pltpu.SMEM((devices * CAP,), jnp.int32),
            pltpu.SemaphoreType.DMA((3,)),
            pltpu.SemaphoreType.DMA((PARTS,)),
        ],
        compiler_params=params(),
        name="pack",
    )(*far(owner, heat, voxel))


HALO = 6
YS = CY + 2 * HALO
XT = CX // 8 + 2
ZG = NZ // 2
TOLERANCE = 1e-6
OWN = jax.ShapeDtypeStruct((2, CY, CX, CX), F32)
XS = 8 * XT
WIDE = jax.ShapeDtypeStruct((2, YS, XS, CX), F32)
EDGE = 2 * HALO
SIDE = 2 * YS


def layout_block(state, zi, y):
    parts = [state[m0 : m0 + 8, 2 * group + zi, y, :] for group in range(ZG) for m0 in (0, 8)]
    return (0.5 * jnp.concatenate(parts, axis=0)).T


def rim_kernel(state, conduct, turned_c, to_high, to_low):
    turned = (0.5 * conduct[...].reshape(CX, CX)).T.reshape(XT - 2, 8, CX)
    turned_c[...] = turned
    to_high[EDGE] = turned
    to_low[EDGE] = turned
    for zi in range(2):
        for y in range(CY):
            turned = layout_block(state, zi, y).reshape(XT - 2, 8, CX)
            if y >= CY - HALO:
                to_high[zi * HALO + y - (CY - HALO)] = turned
            if y < HALO:
                to_low[zi * HALO + y] = turned


def rims(state, conduct):
    edge = kept((EDGE + 1, XT - 2, 8, CX))
    return pl.pallas_call(
        rim_kernel,
        out_shape=[kept((XT - 2, 8, CX)), edge, edge],
        in_specs=[vspec()] * 2,
        out_specs=[vspec()] * 3,
        compiler_params=params(),
        name="rims",
    )(state, conduct)


def relayout_kernel(state, conduct, own, edge_left, edge_right, top, quiet):
    peak = jnp.zeros((8, CX), F32)
    for zi in range(2):
        for y in range(CY):
            turned = layout_block(state, zi, y)
            own[zi, y] = turned
            edge_left[zi * CY + y] = turned[0:8]
            edge_right[zi * CY + y] = turned[CX - 8 :]
    for z in range(2, NZ):
        c = 0.5 * conduct[z]
        for m in range(M):
            value = 0.5 * state[m, z]
            peak = jnp.maximum(peak, c + c * (value * value))
    quiet[...] = peak
    for m in range(M):
        for zi in range(2):
            top[m, zi] = 0.5 * state[m, zi]


def relayout(state, conduct):
    side = kept((2 * CY, 8, CX))
    return pl.pallas_call(
        relayout_kernel,
        out_shape=[kept(OWN.shape), side, side, kept((M, 2, CY, CX)), kept((8, CX))],
        in_specs=[vspec()] * 2,
        out_specs=[vspec()] * 5,
        compiler_params=params(),
        name="relayout",
    )(state, conduct)


def side_kernel(
    edge_left, edge_right, turned_c, low, high, heat_low, heat_own, heat_high,
    to_left, to_right, sems,
):
    pairs = []
    for out, edge, t in ((to_left, edge_left, 0), (to_right, edge_right, XT - 3)):
        for zi in range(2):
            at, rows_at = zi * YS, slice(zi * HALO, zi * HALO + HALO)
            pairs += [
                (low.at[rows_at, t], out.at[at : at + HALO]),
                (edge.at[zi * CY : zi * CY + CY], out.at[at + HALO : at + HALO + CY]),
                (high.at[rows_at, t], out.at[at + HALO + CY : at + YS]),
            ]
            for g, heat in enumerate((heat_low, heat_own, heat_high)):
                pairs.append((heat.at[zi, 8 * t : 8 * t + 8, :], out.at[SIDE + 3 + 2 * g + zi]))
        for g, part in enumerate((low.at[EDGE, t], turned_c.at[t], high.at[EDGE, t])):
            pairs.append((part, out.at[SIDE + g]))
    for copy in fetch(sems, pairs):
        copy.wait()


def sides(*operands):
    shape = jax.ShapeDtypeStruct((SIDE + 9, 8, CX), F32)
    return pl.pallas_call(
        side_kernel,
        out_shape=[shape, shape],
        in_specs=[hspec()] * len(operands),
        out_specs=[vspec()] * 2,
        scratch_shapes=[pltpu.SemaphoreType.DMA((30,))],
        compiler_params=params(),
        name="sides",
    )(*far(*operands))


def split(strip):
    parts = []
    for _ in range(3):
        part = strip.astype(BF16)
        parts.append(part)
        strip = strip - part.astype(F32)
    return jnp.concatenate(parts, axis=1)


def placed(parts, zi, y0):
    source = lax.broadcasted_iota(jnp.int32, (CX, CX), 0)
    target = lax.broadcasted_iota(jnp.int32, (CX, CX), 1)
    hot = jnp.where(source == (2 * (target >> 4) + zi) * CY + y0, 1.0, 0.0).astype(BF16)
    hot = jnp.concatenate([hot] * 3, axis=0)
    return jnp.dot(parts, hot, preferred_element_type=F32)


def halo_row(g, y0):
    row = y0 + HALO + (g - 1) * CY
    return row if 0 <= row < YS else None


def coef_kernel(own, low, high, out, tiles, sems):
    pairs = ((low.at[EDGE], tiles.at[0]), (own, tiles.at[1]), (high.at[EDGE], tiles.at[2]))
    for copy in fetch(sems, pairs):
        copy.wait()
    strip = split(tiles[...].reshape(3 * CX, CX))
    for zi in range(2):
        for y0 in range(CY):
            part = placed(strip, zi, y0)
            for g in range(3):
                row = halo_row(g, y0)
                if row is not None:
                    out[zi, row] = part[g * CX : (g + 1) * CX, :]


def coefs(own, low, high):
    return pl.pallas_call(
        coef_kernel,
        out_shape=jax.ShapeDtypeStruct((2, YS, CX, CX), F32),
        in_specs=[hspec()] * 3,
        out_specs=vspec(),
        scratch_shapes=[VM((3, XT - 2, 8, CX), F32), pltpu.SemaphoreType.DMA((3,))],
        compiler_params=params(),
        name="coefs",
    )(*far(own, low, high))


def deposit_kernel(
    incoming, top_far, conduct_far, quiet_far, out, peaks, total, top, conduct, quiet, sems
):
    copies = fetch(sems, ((top_far, top), (conduct_far.at[0:2], conduct), (quiet_far, quiet)))
    sources = incoming.shape[0]
    group = 128
    place = lax.broadcasted_iota(jnp.int32, (CX, CX), 0).astype(F32).astype(BF16)
    zero = jnp.zeros((M, CX), BF16)
    total[...] = jnp.zeros_like(total)

    def one(g, carry):
        left = []
        right = []
        for s in range(group):
            source = g * group + s
            index = incoming[source, 32:40, :].astype(F32)
            for slot in range(CAP):
                heat = incoming[source, slot * M : (slot + 1) * M, :]
                layer = jnp.broadcast_to(index[slot : slot + 1, :], (M, CX)).astype(BF16)
                cell = jnp.broadcast_to(index[2 + slot : 3 + slot, :], (CX, CX)).astype(BF16)
                left.append(
                    jnp.concatenate(
                        [jnp.where(layer == h, heat, zero) for h in range(2 * CY)], axis=0
                    )
                )
                right.append(jnp.where(place == cell, 1.0, 0.0).astype(BF16))
        total[...] += lax.dot_general(
            jnp.concatenate(left, axis=1),
            jnp.concatenate(right, axis=1),
            NT,
            preferred_element_type=F32,
        )
        return carry

    lax.fori_loop(0, sources // group, one, 0)
    for zi in range(2):
        out[zi] = (0.5 * total[zi * CX : (zi + 1) * CX, :]).T
    for copy in copies:
        copy.wait()
    peak = quiet[...]
    for zi in range(2):
        c = 0.5 * conduct[zi]
        for m in range(M):
            value = top[m, zi] + 0.5 * total[pl.ds(zi * CX + m, CY, stride=M), :]
            peak = jnp.maximum(peak, c + c * (value * value))
    send_row(whole_peak(peak), peaks)


def send_row(row, out):
    for d in range(0, out.shape[0], 8):
        out[d : d + 8, 0, :] = row


def deposit(incoming, top, conduct, quiet):
    devices = incoming.shape[0]
    return pl.pallas_call(
        deposit_kernel,
        out_shape=[
            kept((2, CX, CX)),
            jax.ShapeDtypeStruct((devices, 1, CX), F32),
        ],
        in_specs=[vspec()] + [hspec()] * 3,
        out_specs=[vspec()] * 2,
        scratch_shapes=[
            VM((2 * CY * M, CX), F32),
            VM(top.shape, F32),
            VM((2, CY, CX), F32),
            VM(quiet.shape, F32),
            pltpu.SemaphoreType.DMA((3,)),
        ],
        compiler_params=params(),
        name="deposit",
    )(incoming, *far(top, conduct, quiet))


def whole_peak(value):
    return jnp.broadcast_to(jnp.max(value, axis=(0, 1), keepdims=True), (8, CX))


def step_of(peak):
    return SHARE / (12.0 * peak + COOL)


def tile(t):
    return slice(8 * t, 8 * t + 8)


def half_conductance(c, u):
    return c + c * (u * u)


def segments(inside, first, end):
    parts = []
    if first < HALO:
        parts.append((first, HALO, False, inside[2]))
    parts.append((max(first, HALO), min(end, HALO + CY), True, None))
    if end > HALO + CY:
        parts.append((HALO + CY, end, False, inside[3]))
    return parts


def mask_of(inside, row_mask, t):
    if t == 0:
        return inside[0] if row_mask is None else inside[0] * row_mask
    if t == XT - 1:
        return inside[1] if row_mask is None else inside[1] * row_mask
    return row_mask


def sweep(field, half, above, inside, first, end, emit, carry, unroll=1):
    lane = lanes()
    row = rows()
    last_row = row == 7
    first_row = row == 0
    inner_lane = lane < CX - M
    outer_lane = lane >= M
    cooling = jnp.where(lane < M, COOL, 0.0)

    for zi in range(2):
        for t in range(XT):
            s = tile(t)
            above[zi, t] = (half[zi, first - 1, s, :] + half[zi, first, s, :]) * (
                field[zi, first, s, :] - field[zi, first - 1, s, :]
            )

    def line(own, row_mask, y, state):
        for t in range(XT):
            s = tile(t)
            us = [field[zi, y, s, :] for zi in range(2)]
            hs = [half[zi, y, s, :] for zi in range(2)]
            change = []
            for zi in range(2):
                u, h = us[zi], hs[zi]
                if t < XT - 1:
                    after = slice(8 * t + 1, 8 * t + 9)
                    u_after, h_after = field[zi, y, after, :], half[zi, y, after, :]
                else:
                    u_after = jnp.where(last_row, u, pltpu.roll(u, 7, axis=0))
                    h_after = pltpu.roll(h, 7, axis=0)
                if t:
                    before = slice(8 * t - 1, 8 * t + 7)
                    u_before, h_before = field[zi, y, before, :], half[zi, y, before, :]
                else:
                    u_before = jnp.where(first_row, u, pltpu.roll(u, 1, axis=0))
                    h_before = pltpu.roll(h, 1, axis=0)
                total = (h + h_after) * (u_after - u) + (h + h_before) * (u_before - u)
                across = (h + half[zi, y + 1, s, :]) * (field[zi, y + 1, s, :] - u)
                total = total + (across - above[zi, t])
                above[zi, t] = across
                change.append(total)
            within = (hs[0] + hs[1]) * (us[1] - us[0])
            between = (hs[1] + pltpu.roll(hs[0], CX - M, axis=1)) * (
                pltpu.roll(us[0], CX - M, axis=1) - us[1]
            )
            between = jnp.where(inner_lane, between, 0.0)
            below = (hs[0] + pltpu.roll(hs[1], M, axis=1)) * (us[0] - pltpu.roll(us[1], M, axis=1))
            below = jnp.where(outer_lane, below, 0.0)
            change[0] = change[0] + (within - below) - cooling * us[0]
            change[1] = change[1] + (between - within)
            state = emit(y, t, us, change, own, mask_of(inside, row_mask, t), state)
        return state

    for start, stop, own, row_mask in segments(inside, first, end):
        carry = lax.fori_loop(
            start, stop, functools.partial(line, own, row_mask), carry, unroll=unroll
        )
    return carry


def advance(field, half, coef, above, inside, step, first, end, put, unroll=2):
    def emit(y, t, us, change, own, mask, peak):
        part = step if mask is None else step * mask
        for zi in range(2):
            value = us[zi] + part * change[zi]
            after = half_conductance(coef[zi, y, tile(t), :], value)
            put(zi, y, t, value, after)
            if own and 0 < t < XT - 1:
                peak = jnp.maximum(peak, after)
        return peak

    zero = jnp.zeros((8, CX), F32)
    return sweep(field, half, above, inside, first, end, emit, zero, unroll=unroll)


def propose(field, half, coef, above, inside, guess, first, end, changes, peak, late, out):
    def emit(y, t, us, change, own, mask, best):
        for zi in range(2):
            moved = change[zi] if mask is None else change[zi] * mask
            changes[zi, y, tile(t), :] = moved
            if own and 0 < t < XT - 1:
                c = coef[zi, y, tile(t), :]
                rank = half_conductance(c, us[zi] + guess * moved)
                better = rank > best[0]
                best = tuple(
                    jnp.where(better, new, old)
                    for new, old in zip((rank, us[zi], moved, c), best)
                )
        return best

    best = sweep(
        field, half, above, inside, first, end, emit, (jnp.zeros((8, CX), F32),) * 4,
        unroll=1,
    )
    for shift, axis in ((4, 0), (2, 0), (1, 0), (64, 1), (32, 1)):
        other = tuple(pltpu.roll(part, shift, axis=axis) for part in best)
        better = other[0] > best[0]
        best = tuple(jnp.where(better, new, old) for new, old in zip(other, best))
    part = lanes() >> 4
    chunk = jnp.where(part == 6, whole_peak(peak), whole_peak(late))
    for place, value in ((2, best[3]), (1, best[2]), (0, best[1])):
        chunk = jnp.where((part >> 1) == place, value, chunk)
    send_row(chunk, out)


def gather_rows(parts):
    return [parts[d : d + 8, 0, :] for d in range(0, parts.shape[0], 8)]


def largest(values):
    most = values[0]
    for value in values[1:]:
        most = jnp.maximum(most, value)
    return most


def agree(parts):
    part = lanes() >> 4
    rows_of = gather_rows(parts)
    most = largest(rows_of)
    now = whole_peak(jnp.where(part == 6, most, 0.0))
    late = whole_peak(jnp.where(part == 7, most, 0.0))
    step = step_of(now)
    then = jnp.zeros((8, CX), F32)
    for value in rows_of:
        moved = pltpu.roll(value, CX - 32, axis=1)
        c = pltpu.roll(value, CX - 64, axis=1)
        then = jnp.maximum(then, half_conductance(c, value + step * moved))
    return now, whole_peak(jnp.where(part < 2, then, 0.0)), late


def differs(late, used):
    return jnp.where(late > used * (1.0 + TOLERANCE), 1.0, 0.0)


def heated_kernel(
    inside, peaks, left, right, coef_main, own_far, low_far, high_far,
    heat_low_far, heat_own_far, heat_high_far,
    out, coef, changes, parts, start, half, next_half, above,
    own, low, high, heat_low, heat_own, heat_high, sems,
):
    copies = fetch(
        sems,
        [
            (heat_low_far, heat_low),
            (low_far.at[0:EDGE], low),
            (heat_own_far, heat_own),
            (own_far, own),
            (heat_high_far, heat_high),
            (high_far.at[0:EDGE], high),
        ],
    )
    top = lanes() < M

    strip = split(
        jnp.concatenate([side[SIDE + g] for g in range(3) for side in (left, right)], axis=0)
    )
    for zi in range(2):
        for y0 in range(CY):
            part = placed(strip, zi, y0)
            for g in range(3):
                at = halo_row(g, y0)
                if at is not None:
                    coef[zi, at, tile(0), :] = part[16 * g : 16 * g + 8, :]
                    coef[zi, at, tile(XT - 1), :] = part[16 * g + 8 : 16 * g + 16, :]

    def row(g, heat, tile_of, y0, yy):
        shift = (CX - 16 * y0) % CX
        for zi in range(2):
            for t in range(XT):
                if t == 0:
                    prior, add = left[zi * YS + yy], left[SIDE + 3 + 2 * g + zi]
                elif t == XT - 1:
                    prior, add = right[zi * YS + yy], right[SIDE + 3 + 2 * g + zi]
                else:
                    prior, add = tile_of(zi, t - 1), heat[zi, tile(t - 1), :]
                if shift:
                    add = pltpu.roll(add, shift, axis=1)
                value = prior + jnp.where(top, add, 0.0)
                if 0 < t < XT - 1:
                    c = coef_main[zi, yy, tile(t - 1), :]
                    coef[zi, yy, tile(t), :] = c
                else:
                    c = coef[zi, yy, tile(t), :]
                after = half_conductance(c, value)
                start[zi, yy, tile(t), :] = value
                half[zi, yy, tile(t), :] = after

    def edge(ref, y):
        return lambda zi, t: ref[zi * HALO + y, t]

    for copy in copies[0:2]:
        copy.wait()
    for y in range(HALO):
        row(0, heat_low, edge(low, y), y + CY - HALO, y)
    for copy in copies[2:4]:
        copy.wait()
    for y in range(CY):
        row(1, heat_own, lambda zi, t: own[zi, y, tile(t), :], y, y + HALO)
    for copy in copies[4:6]:
        copy.wait()
    for y in range(HALO):
        row(2, heat_high, edge(high, y), y, y + HALO + CY)

    def put(zi, y, t, value, after):
        out[zi, y, tile(t), :] = value
        next_half[zi, y, tile(t), :] = after

    step = step_of(whole_peak(largest(gather_rows(peaks))))
    peak = advance(start, half, coef, above, inside, step, 1, YS - 1, put, unroll=4)
    guess = jnp.minimum(step_of(whole_peak(peak)), 2.0 * step)
    zero = jnp.zeros((8, CX), F32)
    propose(
        out, next_half, coef, above, inside, guess, 2, YS - 2, changes, peak, zero, parts
    )


ROW = (2, XT, 8, CX)


def smem():
    return pl.BlockSpec(memory_space=pltpu.SMEM)


def heated(inside, prior, halos, heat, coef, peaks):
    near = [inside, peaks, *halos, coef]
    operands = far(*prior, *heat)
    edge = VM((EDGE, XT - 2, 8, CX), F32)
    return pl.pallas_call(
        heated_kernel,
        out_shape=[WIDE, WIDE, WIDE, jax.ShapeDtypeStruct(peaks.shape, F32)],
        in_specs=[smem()] + [vspec()] * 4 + [hspec()] * len(operands),
        out_specs=[vspec()] * 4,
        scratch_shapes=[VM(WIDE.shape, F32)] * 3
        + [VM(ROW, F32), VM(OWN.shape, F32), edge, edge]
        + [VM(part.shape, F32) for part in heat]
        + [pltpu.SemaphoreType.DMA((6,))],
        compiler_params=params(),
        name="heated",
    )(*near, *operands)


def first_of_pair(field, changes, coef, step, first, end, out, half):
    def line(y, peak):
        top = jnp.zeros((8, CX), F32)
        for zi in range(2):
            for t in range(XT):
                value = field[zi, y, tile(t), :] + step * changes[zi, y, tile(t), :]
                after = half_conductance(coef[zi, y, tile(t), :], value)
                out[zi, y, tile(t), :] = value
                half[zi, y, tile(t), :] = after
                if 0 < t < XT - 1:
                    top = jnp.maximum(top, after)
        own = jnp.where((y >= HALO) & (y < HALO + CY), 1.0, 0.0)
        return jnp.maximum(peak, own * top)

    return lax.fori_loop(first, end, line, jnp.zeros((8, CX), F32), unroll=4)


def pair_kernel(
    number, inside, field, changes, coef, parts,
    out, out_changes, out_parts, status, middle, half, next_half, above,
):
    now, then, _ = agree(parts)
    status[...] = jnp.where(rows() == 0, then, 0.0)
    seen = first_of_pair(
        field, changes, coef, step_of(now), number + 1, YS - 1 - number, middle, half
    )

    def put(zi, y, t, value, after):
        out[zi, y, tile(t), :] = value
        next_half[zi, y, tile(t), :] = after

    step = step_of(then)
    peak = advance(
        middle, half, coef, above, inside, step, number + 2, YS - 2 - number, put
    )
    guess = jnp.minimum(step_of(whole_peak(peak)), 1.2 * step)
    propose(
        out, next_half, coef, above, inside, guess, number + 3, YS - 3 - number,
        out_changes, peak, seen, out_parts,
    )


STATUS = jax.ShapeDtypeStruct((8, CX), F32)


def pair(number, inside, field, changes, coef, parts):
    operands = [inside, field, changes, coef, parts]
    return pl.pallas_call(
        functools.partial(pair_kernel, number),
        out_shape=[WIDE, WIDE, jax.ShapeDtypeStruct(parts.shape, F32), STATUS],
        in_specs=[smem()] + [vspec()] * 4,
        out_specs=[vspec()] * 4,
        scratch_shapes=[VM(WIDE.shape, F32)] * 3 + [VM(ROW, F32)],
        compiler_params=params(),
        name=f"pair_{number}",
    )(*operands)


def closing(
    field, half, above, inside, weight, data, peak, late, out, out_changes, sums, flat
):
    def emit(y, t, us, change, own, mask, state):
        if 0 < t < XT - 1:
            for zi in range(2):
                out[zi, y - HALO, tile(t - 1), :] = us[zi]
                out_changes[zi, y - HALO, tile(t - 1), :] = change[zi]
        return state

    sweep(field, half, above, inside, HALO, HALO + CY, emit, 0, unroll=4)
    lefts, rights = [], []
    for y in range(CY):
        w = weight[y : y + 1, :]
        for m in range(M):
            flat[m : m + 1, :] = data[m, y : y + 1, :]
        means = []
        spreads = []
        for part in (out, out_changes):
            seen = 2.0 * part[0, y].T[0:M, :]
            mean = jnp.mean(seen, axis=0, keepdims=True)
            means.append(mean)
            spreads.append(seen - mean)
        lefts.append(jnp.concatenate(spreads + means + [jnp.zeros((6, CX), F32)], axis=0))
        rights.append(jnp.concatenate([part * w for part in spreads] + [flat[...]], axis=0))
    grams = lax.dot_general(
        jnp.concatenate(lefts, axis=1),
        jnp.concatenate(rights, axis=1),
        NT,
        precision=lax.Precision.HIGHEST,
        preferred_element_type=F32,
    )
    grams = jnp.concatenate([grams, jnp.zeros((5 * CY, CX - 3 * M), F32)], axis=1)
    tall = lax.broadcasted_iota(jnp.int32, (M, CX), 0)
    wide = lax.broadcasted_iota(jnp.int32, (M, CX), 1)
    first, second, means = grams[0:M], grams[M : 2 * M], grams[2 * M : 2 * M + 8]

    def block(part, at):
        return jnp.where(wide < M, pltpu.roll(part, (CX - M * at) % CX, axis=1), 0.0)

    def lone(part, row, at):
        moved = pltpu.roll(part, (CX - M * at) % CX, axis=1) if at else part
        return jnp.broadcast_to(moved[row : row + 1, :], (M, CX))

    tops = [
        lone(means, 0, 1) + lone(means, 1, 0),
        lone(means, 0, 0),
        lone(means, 1, 1),
    ]
    blocks = [
        jnp.where(tall < wide, block(first, 0), block(second, 1)),
        block(first, 1) + block(second, 0),
        block(first, 2),
        block(second, 2),
    ]
    scalar = jnp.where(wide == 0, whole_peak(peak)[0:1], whole_peak(late)[0:1])
    blocks[0] = jnp.where(tall == wide, scalar, blocks[0])
    for i, top in enumerate(tops):
        blocks[i + 1] = jnp.where(tall == 0, jnp.where(wide < M, top, 0.0), blocks[i + 1])
    packed = blocks[0]
    for i in range(1, 4):
        packed = packed + pltpu.roll(blocks[i], M * i, axis=1)
    packed = packed[0:8] + pltpu.roll(packed[8:16], CX // 2, axis=1)
    for d in range(sums.shape[0]):
        sums[d] = packed


def last_kernel(
    inside, field, changes, coef, parts, status, weight_far, data_far,
    out, out_changes, sums, out_status,
    middle, half, near, near_half, above, flat, weight, data, sems,
):
    copies = fetch(sems, ((weight_far, weight), (data_far, data)))
    number = SUBSTEPS - 3
    now, then, late = agree(parts)
    bad = differs(late[0:1], status[0:1, :])
    out_status[...] = jnp.where(rows() == 0, then, bad)
    seen = first_of_pair(
        field, changes, coef, step_of(now), number + 1, YS - 1 - number, middle, half
    )

    def put(zi, y, t, value, after):
        near[zi, y, tile(t), :] = value
        near_half[zi, y, tile(t), :] = after

    peak = advance(
        middle, half, coef, above, inside, step_of(then), number + 2, YS - 2 - number, put
    )
    for copy in copies:
        copy.wait()
    closing(
        near, near_half, above, inside, weight, data, peak, seen, out, out_changes, sums, flat
    )


def sums_shape(devices):
    return jax.ShapeDtypeStruct((devices, 8, CX), F32)


def last(inside, field, changes, coef, parts, status, pixels):
    operands = [inside, field, changes, coef, parts, status, *far(*pixels)]
    return pl.pallas_call(
        last_kernel,
        out_shape=[OWN, OWN, sums_shape(parts.shape[0]), STATUS],
        in_specs=[smem()] + [vspec()] * 5 + [hspec()] * 2,
        out_specs=[vspec()] * 4,
        scratch_shapes=[VM(WIDE.shape, F32)] * 4
        + [VM(ROW, F32), VM((M, CX), F32)]
        + [VM(part.shape, F32) for part in pixels]
        + [pltpu.SemaphoreType.DMA((2,))],
        compiler_params=params(),
        name="last_pair",
    )(*operands)


def fill_half(field, coef, half, first, end):
    def fill(y, carry):
        for zi in range(2):
            half[zi, y] = half_conductance(coef[zi, y], field[zi, y])
        return carry

    lax.fori_loop(first, end, fill, 0)


def single_kernel(number, inside, field, coef, peaks, out, out_peaks, half, above):
    step = step_of(whole_peak(largest(gather_rows(peaks))))
    fill_half(field, coef, half, number, YS - number)

    def put(zi, y, t, value, after):
        out[zi, y, tile(t), :] = value

    peak = advance(field, half, coef, above, inside, step, number + 1, YS - 1 - number, put)
    send_row(whole_peak(peak), out_peaks)


def single(number, inside, field, coef, peaks):
    return pl.pallas_call(
        functools.partial(single_kernel, number),
        out_shape=[WIDE, jax.ShapeDtypeStruct(peaks.shape, F32)],
        in_specs=[smem()] + [vspec()] * 3,
        out_specs=[vspec()] * 2,
        scratch_shapes=[VM(WIDE.shape, F32), VM(ROW, F32)],
        compiler_params=params(),
        name=f"single_{number}",
    )(inside, field, coef, peaks)


def closing_kernel(
    inside, field, coef, peaks, weight, data, out, out_changes, sums, half, above, flat
):
    fill_half(field, coef, half, HALO - 1, HALO + CY + 1)
    peak = peaks[0:8, 0, :]
    closing(
        field, half, above, inside, weight, data, peak, jnp.zeros((8, CX), F32),
        out, out_changes, sums, flat,
    )


def close(inside, field, coef, peaks, pixels):
    operands = [inside, field, coef, peaks, *pixels]
    return pl.pallas_call(
        closing_kernel,
        out_shape=[OWN, OWN, sums_shape(peaks.shape[0])],
        in_specs=[smem()] + [vspec()] * (len(operands) - 1),
        out_specs=[vspec()] * 3,
        scratch_shapes=[VM(WIDE.shape, F32), VM(ROW, F32), VM((M, CX), F32)],
        compiler_params=params(),
        name="closing",
    )(*operands)


def pixel_kernel(cell, observed, variance, noise, weight, data):
    pixels = cell.shape[1]
    place = cell[...]
    var = variance[...]
    inverse = 1.0 / var
    values = (observed[...] + noise[...] * jnp.sqrt(var)) * inverse
    stack = jnp.concatenate([values, jnp.broadcast_to(inverse, (8, pixels))], axis=0)
    width = place >> 7
    hot = jnp.where(
        lax.broadcasted_iota(jnp.int32, (CX, pixels), 0) == (place & 127), 1.0, 0.0
    ).astype(F32)
    for y in range(CY):
        part = lax.dot_general(
            jnp.where(width == y, stack, 0.0),
            hot,
            NT,
            precision=lax.Precision.HIGHEST,
            preferred_element_type=F32,
        )
        weight[y : y + 1, :] = part[M : M + 1, :]
        for m in range(M):
            data[m, y : y + 1, :] = part[m : m + 1, :]


def pixel_sums(cell, observed, variance, noise):
    return pl.pallas_call(
        pixel_kernel,
        out_shape=[kept((CY, CX)), kept((M, CY, CX))],
        in_specs=[vspec()] * 4,
        out_specs=[vspec()] * 2,
        compiler_params=params(),
        name="pixels",
    )(cell, observed, variance, noise)


def update_kernel(sums, field, changes, status, out, flag):
    total = sums[0]
    most = total
    for d in range(1, sums.shape[0]):
        total = total + sums[d]
        most = jnp.maximum(most, sums[d])
    step = step_of(jnp.broadcast_to(most[0:1, 0:1], (1, CX)))
    late = jnp.broadcast_to(most[1:2, 1:2], (1, CX))
    bad = jnp.maximum(status[1:2, :], differs(late, status[0:1, :]))
    flag[0] = jnp.where(jnp.max(bad) > 0.0, 1, 0)

    tall = lax.broadcasted_iota(jnp.int32, (M, CX), 0)
    wide = lax.broadcasted_iota(jnp.int32, (M, CX), 1)
    packed = jnp.concatenate([total, pltpu.roll(total, CX // 2, axis=1)], axis=0)

    def block(at):
        return jnp.where(wide < M, pltpu.roll(packed, (CX - M * at) % CX, axis=1), 0.0)

    def whole(part):
        rest = jnp.where(tall == 0, 0.0, part)
        first = -jnp.sum(rest, axis=0, keepdims=True)
        return jnp.where(tall == 0, first, rest), part[0:1, :]

    def balanced(part):
        part = jnp.where((tall == wide) | (wide >= M), 0.0, part)
        return jnp.where(tall == wide, -jnp.sum(part, axis=1, keepdims=True), part)

    corner = block(0)
    mirror = jnp.concatenate([corner, jnp.zeros((CX - M, CX), F32)], axis=0).T[0:M, :]
    square = balanced(jnp.where(tall < wide, corner, mirror))
    square_c = balanced(jnp.where(tall > wide, corner, mirror))
    mixed, mean_1 = whole(block(1))
    data, mean_0 = whole(block(2))
    data_c, mean_2 = whole(block(3))
    cross = square + step * (mixed + step * square_c)
    mean = mean_0 + step * (mean_1 + step * mean_2)
    mean = jnp.sum(jnp.where(tall == wide, mean, 0.0), axis=1, keepdims=True)
    target = jnp.where(wide < M, data + step * data_c - cross - mean, 0.0)
    system = jnp.where(tall == wide, cross + (M - 1.0), cross)
    columns = [jnp.broadcast_to(system[:, i : i + 1], (M, CX)) for i in range(M)]
    for i in range(M):
        pivot = 1.0 / columns[i][i : i + 1, :]
        factor = jnp.where(tall == i, 0.0, columns[i] * pivot)
        for j in range(i + 1, M):
            columns[j] = columns[j] - factor * columns[j][i : i + 1, :]
        target = target - factor * target[i : i + 1, :]
    for i in range(M):
        target = jnp.where(tall == i, target / columns[i], target)
    mixing = target - jnp.mean(target, axis=0, keepdims=True)
    mixing = jnp.where(wide < M, mixing + jnp.where(tall == wide, 1.0, 0.0), 0.0)
    for shift in (16, 32, 64):
        mixing = mixing + pltpu.roll(mixing, shift, axis=1)
    mixing = jnp.concatenate([mixing] * ZG, axis=0)
    tall = lax.broadcasted_iota(jnp.int32, (CX, CX), 0)
    wide = lax.broadcasted_iota(jnp.int32, (CX, CX), 1)
    mixing = jnp.where((tall >> 4) == (wide >> 4), 2.0 * mixing, 0.0).T
    mixing_high = mixing.astype(BF16)
    mixing_low = (mixing - mixing_high.astype(F32)).astype(BF16)
    mixing = jnp.concatenate([mixing_high, mixing_low, mixing_high], axis=1)
    for zi in range(2):
        for y in range(CY):
            prior = field[zi, y] + step * changes[zi, y]
            high = prior.astype(BF16)
            low = (prior - high.astype(F32)).astype(BF16)
            part = lax.dot_general(
                mixing,
                jnp.concatenate([high, high, low], axis=1),
                NT,
                preferred_element_type=F32,
            )
            for group in range(ZG):
                for m0 in (0, 8):
                    at = group * M + m0
                    out[m0 : m0 + 8, 2 * group + zi, y, :] = part[at : at + 8, :]


def update(sums, field, changes, status):
    return pl.pallas_call(
        update_kernel,
        out_shape=[
            jax.ShapeDtypeStruct((M, NZ, CY, CX), F32),
            jax.ShapeDtypeStruct((1,), jnp.int32),
        ],
        in_specs=[vspec()] * 4,
        out_specs=[vspec(), smem()],
        compiler_params=params(),
        name="update",
    )(sums, field, changes, status)


def exchange(parts):
    return lax.all_to_all(parts, BOTH, split_axis=0, concat_axis=0, tiled=True)


def move(part, axis, ahead):
    count = lax.axis_size(axis)
    pairs = [(i, i + 1) if ahead else (i + 1, i) for i in range(count - 1)]
    return lax.ppermute(part, axis, pairs)


def on_device(
    state_prior,
    conductivity,
    heat_input,
    owner_tile,
    voxel_list,
    pixel_cell,
    observed,
    pixel_variance,
    pixel_noise,
):
    devices = lax.axis_size("gx") * lax.axis_size("gy")
    pixels = pixel_cell.shape[0]
    gx, gy = lax.axis_index("gx"), lax.axis_index("gy")
    inside = jnp.stack(
        [gx > 0, gx < lax.axis_size("gx") - 1, gy > 0, gy < lax.axis_size("gy") - 1]
    ).astype(F32)
    incoming = exchange(pack(owner_tile.reshape(-1), heat_input, voxel_list, devices))
    turned_c, to_high, to_low = rims(state_prior, conductivity)
    low, high = move(to_high, "gy", True), move(to_low, "gy", False)
    state_prior, turned_c = lax.optimization_barrier((state_prior, turned_c))
    own, edge_left, edge_right, top, quiet = relayout(state_prior, conductivity)
    seen = pixel_sums(
        pixel_cell.reshape(1, pixels),
        observed.reshape(1, pixels),
        pixel_variance.reshape(1, pixels),
        pixel_noise,
    )
    incoming, own, top, inside, *seen = lax.optimization_barrier(
        (incoming, own, top, inside, *seen)
    )
    heat, peaks = deposit(incoming, top, conductivity, quiet)
    heat_low, heat_high = move(heat, "gy", True), move(heat, "gy", False)
    low, high, heat_low, heat_high, peaks = lax.optimization_barrier(
        (low, high, heat_low, heat_high, exchange(peaks))
    )
    to_left, to_right = sides(
        edge_left, edge_right, turned_c, low, high, heat_low, heat, heat_high
    )
    left, right = move(to_right, "gx", True), move(to_left, "gx", False)
    start, coef, changes, parts = heated(
        inside,
        (own, low, high),
        (left, right),
        (heat_low, heat, heat_high),
        coefs(turned_c, low, high),
        peaks,
    )
    field, changes, parts, status = pair(1, inside, start, changes, coef, exchange(parts))
    field, changes, sums, status = last(
        inside, field, changes, coef, exchange(parts), status, seen
    )
    result, flag = update(exchange(sums), field, changes, status)

    def again():
        peak = coef * (1.0 + start * start)
        peaks = jnp.full((devices, 1, CX), jnp.max(peak[:, HALO : HALO + CY, 8 : XS - 8]))
        field = start
        for number in range(1, SUBSTEPS - 1):
            field, peaks = single(number, inside, field, coef, exchange(peaks))
        field, changes, sums = close(inside, field, coef, peaks, seen)
        return update(exchange(sums), field, changes, jnp.ones((8, CX), F32))[0]

    return lax.cond(flag[0] > 0, again, lambda: result)


def solution(mesh):
    in_specs = (
        P(None, None, "gy", "gx"),
        P(None, "gy", "gx"),
        P(None, BOTH, None),
        P(BOTH, None),
        P(BOTH, None),
        P(BOTH),
        P(BOTH),
        P(BOTH),
        P(None, BOTH),
    )
    out_specs = P(None, None, "gy", "gx")
    return jax.shard_map(
        on_device, mesh=mesh, in_specs=in_specs, out_specs=out_specs, check_vma=False
    )
```
